32 devices in a mesh: shard: 4 (over z), context: 2 (over x), tensor: 4 (over y, core).
Axes of the slice: x: 2, y: 2, z: 4, core: 2. Of those that a mesh axis runs over, the one named last changes fastest.
Arguments:
- frames: bfloat16 [8, 1024, 1536], P('shard', ('context', 'tensor')), may hold values from -12 to 12
- text_states: bfloat16 [8, 64, 1536], P('shard'), may hold values from -6 to 6
- cotangent: bfloat16 [8, 1024, 1536], P('shard', ('context', 'tensor')), may hold values from -6 to 6
- norm_gain: float32 [3, 1536], replicated, may hold values from 0.1 to 1.9
- norm_bias: float32 [3, 1536], replicated, may hold values from -1.5 to 1.5
- self_qkv: bfloat16 [3, 1536, 1536], P(None, 'shard', 'tensor'), may hold values from -0.15625 to 0.15625
- self_out: bfloat16 [1536, 1536], P('shard', 'tensor'), may hold values from -1.75 to 1.75
- cross_qkv: bfloat16 [3, 1536, 1536], P(None, 'shard', 'tensor'), may hold values from -0.15625 to 0.15625
- cross_out: bfloat16 [1536, 1536], P('shard', 'tensor'), may hold values from -0.875 to 0.875
- mlp_up: bfloat16 [1536, 6144], P('shard', 'tensor'), may hold values from -0.20412415 to 0.20412415
- mlp_down: bfloat16 [1536, 6144], P('shard', 'tensor'), may hold values from -0.15625 to 0.15625
Outputs:
- layer_out: bfloat16 [8, 1024, 1536], P('shard', ('context', 'tensor'))
- grad_frames: float32 [8, 1024, 1536], P('shard', ('context', 'tensor'))
- grad_text: float32 [8, 64, 1536], P('shard', ('context', 'tensor'))
- grad_norm_gain: float32 [3, 1536], P(None, 'shard')
- grad_norm_bias: float32 [3, 1536], P(None, 'shard')
- grad_self_qkv: float32 [3, 1536, 1536], P(None, 'shard', 'tensor')
- grad_self_out: float32 [1536, 1536], P('shard', 'tensor')
- grad_cross_qkv: float32 [3, 1536, 1536], P(None, 'shard', 'tensor')
- grad_cross_out: float32 [1536, 1536], P('shard', 'tensor')
- grad_mlp_up: float32 [1536, 6144], P('shard', 'tensor')
- grad_mlp_down: float32 [1536, 6144], P('shard', 'tensor')
- rms: float32 [4], replicated
The draws below stay inside these ranges and needn't reach their ends.
All inputs are finite; a program needn't handle non-finite values.
Results may differ from the reference program's by a relative error of at most 0.019.
Values may be sent and summed in bfloat16 or wider, within the bound.
A program may use at most 192 MiB of HBM per device.

```python
import jax
import jax.numpy as jnp
from jax import lax

D = 1536
HEADS = 24
HEAD_DIM = 64
FF = 6144
TEXT = 64
CLIPS = 8
LENGTH = 1024


def draw_frames(key, part):
    first_key = jax.random.fold_in(key, 0)
    places = (jnp.arange(CLIPS)[:, None] * LENGTH + jnp.arange(LENGTH)[None, :]).astype(jnp.float32)
    growth = 1.0 + 2.0 * places / (CLIPS * LENGTH - 1)
    baseline = jnp.clip(jax.random.normal(first_key, (CLIPS, LENGTH, D), jnp.float32), -4.0, 4.0)
    return (baseline * growth[:, :, None]).astype(jnp.bfloat16)


def draw_mlp_up(key, part):
    first_key, second_key = jax.random.split(jax.random.fold_in(key, 7))
    entries = jnp.clip(jax.random.normal(first_key, (D, FF), jnp.float32), -4.5, 4.5)
    shared = 0.8 * jnp.clip(jax.random.normal(second_key, (1, FF), jnp.float32), -4.375, 4.375)
    return ((entries + shared) * D ** (-0.5)).astype(jnp.bfloat16)


def with_spikes(values, own_key, source, target, blocks, factor):
    def block_of(dim):
        return (jnp.arange(values.shape[dim]) // (values.shape[dim] // blocks)).reshape((-1,) + (1,) * (values.ndim - 1 - dim))

    first = jax.random.permutation(own_key, blocks)[block_of(target)]
    other_side = (block_of(target) + blocks // 2) % blocks
    return jnp.where((block_of(source) == first) | (block_of(source) == other_side), factor * values, values)


def steps_of(own_key, dims, cuts, smallest, top_value):
    gain = 1.0
    for position, shards_of in cuts:
        steps = jax.random.uniform(jax.random.fold_in(jax.random.fold_in(own_key, 6), position), (shards_of,), jnp.float32, smallest / len(cuts), top_value / len(cuts))
        gain = gain * jnp.repeat(jnp.exp(steps), dims[position] // shards_of).reshape((-1,) + (1,) * (len(dims) - 1 - position))
    return gain


def gaussian(rng, dims, spread, reach, cuts=(), held_as=jnp.bfloat16):
    array = spread * jax.random.normal(rng, dims, jnp.float32)
    if cuts:
        array = array * steps_of(rng, dims, cuts, -0.22, 0.18)
    return jnp.clip(array, -reach, reach).astype(held_as)


def noise_with(rng, extent, scale, most, cuts, heavy, dtype=jnp.bfloat16):
    array = scale * jax.random.normal(rng, extent, jnp.float32)
    if cuts:
        array = array * steps_of(rng, extent, cuts, -0.22, 0.18)
    return jnp.clip(with_spikes(array, jax.random.fold_in(rng, 3), *heavy), -most, most).astype(dtype)


def setup_inputs(seed: int = 0) -> dict:
    key_of = jax.random.split(jax.random.key(seed), 12)
    frames = draw_frames(jax.random.fold_in(key_of[11], 71), 0)
    text_states = gaussian(key_of[1], (CLIPS, TEXT, D), 1.0, 6.0, ((0, 4),))
    cotangent = noise_with(key_of[2], (CLIPS, LENGTH, D), 1.0, 6.0, ((0, 4), (1, 8)), (0, 2, 4, 2.0))
    norm_gain = jnp.clip(1.0 + 0.18 * jax.random.normal(key_of[3], (3, D), jnp.float32), 0.1, 1.9)
    norm_bias = gaussian(key_of[4], (3, D), 0.3, 1.5, (), jnp.float32)
    self_qkv = gaussian(key_of[5], (3, D, D), D ** -0.5, 0.15625, ((1, 4), (2, 4)))
    self_out = gaussian(key_of[6], (D, D), (max(D // 128, 1)) ** -0.5, 1.75, ((0, 4), (1, 4)))
    cross_qkv = gaussian(key_of[7], (3, D, D), D ** -0.5, 0.15625, ((1, 4), (2, 4)))
    cross_out = gaussian(key_of[8], (D, D), (max(D // 32, 1)) ** -0.5, 0.875, ((0, 4), (1, 4)))
    mlp_up = draw_mlp_up(jax.random.fold_in(key_of[11], 71), 0)
    mlp_down = gaussian(key_of[10], (D, FF), (max(FF // 4, 1)) ** -0.5, 0.15625, ((0, 4), (1, 4)))
    return dict(frames=frames, text_states=text_states, cotangent=cotangent, norm_gain=norm_gain, norm_bias=norm_bias, self_qkv=self_qkv, self_out=self_out, cross_qkv=cross_qkv, cross_out=cross_out, mlp_up=mlp_up, mlp_down=mlp_down)


@jax.custom_vjp
def low(v):
    return lax.optimization_barrier(v.astype(jnp.bfloat16)).astype(jnp.float32)

@jax.custom_vjp
def low_back(v):
    return v

def low_keep(v):
    return (low(v), None)

def low_pass(kept, grad):
    return (grad,)

def back_keep(v):
    return (v, None)

def back_low(kept, grad):
    return (low(grad),)
low.defvjp(low_keep, low_pass)
low_back.defvjp(back_keep, back_low)
epsilon = 1e-05
highest = lax.Precision.HIGHEST

def both_ways(operand):
    return low(low_back(operand))

def layer_norm(inputs, scaling, offset):
    average = lax.optimization_barrier(jnp.mean(inputs, axis=-1, keepdims=True))
    centred = inputs - average
    variance = lax.optimization_barrier(jnp.mean(centred * centred, axis=-1, keepdims=True))
    return centred * lax.rsqrt(variance + epsilon) * scaling + offset

def product(left_side, right_side):
    return jnp.dot(left_side, right_side, precision=highest)

def attention(query_rows, key_rows, value_rows, causal):
    row_count = query_rows.shape[0]
    key_count = key_rows.shape[0]
    query_heads = query_rows.reshape(row_count, HEADS, HEAD_DIM)
    key_heads = key_rows.reshape(key_count, HEADS, HEAD_DIM)
    value_heads = value_rows.reshape(key_count, HEADS, HEAD_DIM)
    scores = low_back(jnp.einsum('qhd,khd->hqk', query_heads, key_heads, precision=highest) * HEAD_DIM ** (-0.5))
    if causal:
        allowed = jnp.arange(key_count)[None, :] <= jnp.arange(row_count)[:, None]
        scores = jnp.where(allowed[None], scores, -1e+30)
    soft_weights = low(jax.nn.softmax(scores, axis=-1))
    mixture = jnp.einsum('hqk,khd->qhd', soft_weights, value_heads, precision=highest)
    return both_ways(mixture.reshape(row_count, HEADS * HEAD_DIM))

def clip_layer(clip_rows, clip_text, norm_gains, norm_offsets, self_inputs, self_output, cross_inputs, cross_output, up_weights, down_weights):
    normed = low(layer_norm(clip_rows, norm_gains[0], norm_offsets[0]))
    query_rows = both_ways(product(normed, self_inputs[0]))
    key_rows = both_ways(product(normed, self_inputs[1]))
    value_rows = both_ways(product(normed, self_inputs[2]))
    branch_one = low_back(product(attention(query_rows, key_rows, value_rows, True), self_output.T))
    stream_one = clip_rows + branch_one
    normed = low(layer_norm(stream_one, norm_gains[1], norm_offsets[1]))
    query_rows = both_ways(product(normed, cross_inputs[0]))
    text_keys = low(product(clip_text, cross_inputs[1]))
    text_values = low(product(clip_text, cross_inputs[2]))
    branch_two = low_back(product(attention(query_rows, text_keys, text_values, False), cross_output.T))
    stream_two = stream_one + branch_two
    normed = low(layer_norm(stream_two, norm_gains[2], norm_offsets[2]))
    pre_act = low_back(product(normed, up_weights))
    hidden = low(jax.nn.gelu(pre_act, approximate=False))
    branch_three = low_back(product(hidden, down_weights.T))
    result = stream_two + branch_three
    squares = jnp.stack([jnp.sum(result * result), jnp.sum(branch_one * branch_one), jnp.sum(branch_two * branch_two), jnp.sum(branch_three * branch_three)])
    return (result, squares)

def reference(frames, text_states, cotangent, norm_gain, norm_bias, self_qkv, self_out, cross_qkv, cross_out, mlp_up, mlp_down):

    def forward(frame_rows, text_rows, norm_gains, norm_offsets, self_inputs, self_output, cross_inputs, cross_output, up_weights, down_weights):

        def one_clip(pieces):
            return clip_layer(pieces[0], pieces[1], norm_gains, norm_offsets, self_inputs, self_output, cross_inputs, cross_output, up_weights, down_weights)
        results, squares = lax.map(jax.checkpoint(one_clip), (frame_rows, text_rows))
        return (results, lax.optimization_barrier(jnp.sum(squares, axis=0)))
    results, pullback, squares = jax.vjp(forward, frames.astype(jnp.float32), text_states.astype(jnp.float32), norm_gain.astype(jnp.float32), norm_bias.astype(jnp.float32), self_qkv.astype(jnp.float32), self_out.astype(jnp.float32), cross_qkv.astype(jnp.float32), cross_out.astype(jnp.float32), mlp_up.astype(jnp.float32), mlp_down.astype(jnp.float32), has_aux=True)
    grads = pullback(cotangent.astype(jnp.float32))
    stats = jnp.sqrt(squares / (CLIPS * LENGTH * D))
    return (results.astype(jnp.bfloat16), grads[0], grads[1], grads[2], grads[3], grads[4], grads[5], grads[6], grads[7], grads[8], grads[9], stats)
```

```python
from functools import partial

import jax
import jax.numpy as jnp
from jax import lax
from jax.experimental import pallas as pl
from jax.experimental.pallas import tpu as pltpu
from jax.sharding import PartitionSpec as P

HEAD_DIM = 64
EPS = 1e-05
MASKED = -1e30
MESH = pl.DeviceIdType.MESH
BF = jnp.bfloat16
F32 = jnp.float32
PLANE = ("context", "tensor")
VMEM_LIMIT = 60 * 2**20


def place():
    return (
        lax.axis_index("shard"),
        lax.axis_index("context"),
        lax.axis_index("tensor") // 2,
        lax.axis_index("tensor") % 2,
    )


def device(z, x, y, c):
    return (z, x, 2 * y + c)


def slot(x, y, c):
    return 4 * x + 2 * y + c


def enter(targets):
    barrier = pltpu.get_barrier_semaphore()
    for target in targets:
        pl.semaphore_signal(barrier, inc=1, device_id=target, device_id_type=MESH)
    pl.semaphore_wait(barrier, len(targets))


def gather_kernel(in_ref, out_ref, local_sem, send, recv):
    z, x, y, c = place()
    rows = in_ref.shape[0]
    half = rows // 2
    to_x, to_y, to_c = device(z, 1 - x, y, c), device(z, x, 1 - y, c), device(z, x, y, 1 - c)
    enter((to_x, to_y, to_c))
    me = slot(x, y, c)

    def remote(index, source, place_in, start, size, target):
        return pltpu.make_async_remote_copy(
            src_ref=source,
            dst_ref=out_ref.at[place_in, pl.ds(start, size)],
            send_sem=send.at[index],
            recv_sem=recv.at[index],
            device_id=target,
            device_id_type=MESH,
        )

    def part(index, owner, start, size, target):
        return remote(index, out_ref.at[owner, pl.ds(start, size)], owner, start, size, target)

    own = pltpu.make_async_copy(in_ref, out_ref.at[me], local_sem)
    own.start()
    from_x, from_y, from_d = slot(1 - x, y, c), slot(x, 1 - y, c), slot(1 - x, 1 - y, c)
    sends = [
        remote(0, in_ref, me, 0, rows, to_x),
        remote(1, in_ref, me, 0, rows, to_y),
        remote(2, in_ref, me, 0, rows, to_c),
    ]
    for copy in sends:
        copy.start()

    def arrived(index, owner, start, size):
        remote(index, in_ref.at[pl.ds(0, size)], owner, start, size, to_x).wait_recv()

    arrived(1, from_y, 0, rows)
    later = [part(3, from_y, 0, half, to_x), part(5, from_y, 0, rows, to_c)]
    for copy in later:
        copy.start()
    sends += later
    arrived(0, from_x, 0, rows)
    later = [part(4, from_x, half, half, to_y), part(6, from_x, 0, rows, to_c)]
    for copy in later:
        copy.start()
    sends += later
    arrived(3, from_d, 0, half)
    later = [part(7, from_d, 0, half, to_c)]
    later[0].start()
    sends += later
    arrived(4, from_d, half, half)
    later = [part(8, from_d, half, half, to_c)]
    later[0].start()
    sends += later
    arrived(2, slot(x, y, 1 - c), 0, rows)
    arrived(5, slot(x, 1 - y, 1 - c), 0, rows)
    arrived(6, slot(1 - x, y, 1 - c), 0, rows)
    arrived(7, slot(1 - x, 1 - y, 1 - c), 0, half)
    arrived(8, slot(1 - x, 1 - y, 1 - c), half, half)
    own.wait()
    for copy in sends:
        copy.wait_send()


def plane_gather(values, ident):
    rows, columns = values.shape
    return pl.pallas_call(
        gather_kernel,
        out_shape=jax.ShapeDtypeStruct((8, rows, columns), values.dtype),
        in_specs=[pl.BlockSpec(memory_space=pl.ANY)],
        out_specs=pl.BlockSpec(memory_space=pl.ANY),
        scratch_shapes=[
            pltpu.SemaphoreType.DMA,
            pltpu.SemaphoreType.DMA((9,)),
            pltpu.SemaphoreType.DMA((9,)),
        ],
        name="plane_gather",
        compiler_params=pltpu.CompilerParams(collective_id=ident, has_side_effects=True),
    )(values)


def scatter_kernel(in_ref, out_ref, mine, core, sums, relay, final, local_sem, send, recv):
    z, x, y, c = place()
    rows = out_ref.shape[0]
    half = rows // 2
    to_x, to_y, to_c = device(z, 1 - x, y, c), device(z, x, 1 - y, c), device(z, x, y, 1 - c)
    enter((to_x, to_y, to_c))
    chips = ((1 - x, 1 - y), (1 - x, y), (x, 1 - y), (x, y))

    def remote(index, source, target_ref, target):
        return pltpu.make_async_remote_copy(
            src_ref=source,
            dst_ref=target_ref,
            send_sem=send.at[index],
            recv_sem=recv.at[index],
            device_id=target,
            device_id_type=MESH,
        )

    sends = []
    loads = []
    for index, (cx, cy) in enumerate(chips):
        copy = remote(index, in_ref.at[slot(cx, cy, 1 - c)], core.at[index], to_c)
        copy.start()
        sends.append(copy)
        load = pltpu.make_async_copy(in_ref.at[slot(cx, cy, c)], mine.at[index], local_sem.at[index])
        load.start()
        loads.append(load)

    low, high = pl.ds(0, half), pl.ds(half, half)

    def pair(index, part):
        return mine[index, part].astype(F32) + core[index, part].astype(F32)

    def forward(index, source, target_ref, target):
        copy = remote(index, source, target_ref, target)
        copy.start()
        sends.append(copy)

    loads[0].wait()
    sends[0].wait_recv()
    sums[0, low] = pair(0, low).astype(BF)
    forward(4, sums.at[0, low], relay.at[0], to_x)
    sums[0, high] = pair(0, high).astype(BF)
    forward(5, sums.at[0, high], relay.at[1], to_y)
    loads[1].wait()
    sends[1].wait_recv()
    sums[1, low] = pair(1, low).astype(BF)
    forward(6, sums.at[1, low], final.at[0, low], to_x)
    loads[2].wait()
    sends[2].wait_recv()
    sums[2, high] = pair(2, high).astype(BF)
    forward(7, sums.at[2, high], final.at[1, high], to_y)
    loads[3].wait()
    sends[3].wait_recv()
    sends[5].wait_recv()
    sums[1, high] = (pair(1, high) + relay[1].astype(F32)).astype(BF)
    forward(8, sums.at[1, high], final.at[0, high], to_x)
    sends[4].wait_recv()
    sums[2, low] = (pair(2, low) + relay[0].astype(F32)).astype(BF)
    forward(9, sums.at[2, low], final.at[1, low], to_y)
    sends[6].wait_recv()
    sends[7].wait_recv()
    sends[8].wait_recv()
    sends[9].wait_recv()
    out_ref[...] = (
        mine[3].astype(F32) + core[3].astype(F32) + final[0].astype(F32) + final[1].astype(F32)
    )
    for copy in sends:
        copy.wait_send()


def plane_scatter(values, ident):
    _, rows, columns = values.shape
    return pl.pallas_call(
        scatter_kernel,
        out_shape=jax.ShapeDtypeStruct((rows, columns), F32),
        in_specs=[pl.BlockSpec(memory_space=pl.ANY)],
        out_specs=pl.BlockSpec(memory_space=pltpu.VMEM),
        scratch_shapes=[
            pltpu.VMEM((4, rows, columns), BF),
            pltpu.VMEM((4, rows, columns), BF),
            pltpu.VMEM((3, rows, columns), BF),
            pltpu.VMEM((2, rows // 2, columns), BF),
            pltpu.VMEM((2, rows, columns), BF),
            pltpu.SemaphoreType.DMA((4,)),
            pltpu.SemaphoreType.DMA((10,)),
            pltpu.SemaphoreType.DMA((10,)),
        ],
        name="plane_scatter",
        compiler_params=pltpu.CompilerParams(
            collective_id=ident, has_side_effects=True, vmem_limit_bytes=VMEM_LIMIT
        ),
    )(values)


def exchange_kernel(in_ref, out_ref, local_sem, send, recv):
    z, x, y, c = place()
    others = [
        (dx, dy, dc) for dx in range(2) for dy in range(2) for dc in range(2) if dx + dy + dc > 0
    ]
    spots = [((x + dx) % 2, (y + dy) % 2, (c + dc) % 2) for dx, dy, dc in others]
    enter([device(z, *spot) for spot in spots])
    me = slot(x, y, c)
    own = pltpu.make_async_copy(in_ref.at[me], out_ref.at[me], local_sem)
    own.start()
    sends = []
    for index, spot in enumerate(spots):
        copy = pltpu.make_async_remote_copy(
            src_ref=in_ref.at[slot(*spot)],
            dst_ref=out_ref.at[me],
            send_sem=send.at[index],
            recv_sem=recv.at[index],
            device_id=device(z, *spot),
            device_id_type=MESH,
        )
        copy.start()
        sends.append(copy)
    own.wait()
    for copy in sends:
        copy.wait()


def plane_exchange(values, ident):
    return pl.pallas_call(
        exchange_kernel,
        out_shape=jax.ShapeDtypeStruct(values.shape, values.dtype),
        in_specs=[pl.BlockSpec(memory_space=pl.ANY)],
        out_specs=pl.BlockSpec(memory_space=pl.ANY),
        scratch_shapes=[
            pltpu.SemaphoreType.DMA,
            pltpu.SemaphoreType.DMA((7,)),
            pltpu.SemaphoreType.DMA((7,)),
        ],
        name="plane_exchange",
        compiler_params=pltpu.CompilerParams(collective_id=ident, has_side_effects=True),
    )(values)


def dots(spec, *operands):
    return jnp.einsum(spec, *operands, preferred_element_type=F32)


def layer_norm(inputs, scaling, offset):
    average = jnp.mean(inputs, axis=-1, keepdims=True)
    centred = inputs - average
    variance = jnp.mean(centred * centred, axis=-1, keepdims=True)
    return centred * lax.rsqrt(variance + EPS) * scaling + offset


def self_forward(query, key, value):
    length = query.shape[0]
    scores = dots("qhd,khd->hqk", query, key) * HEAD_DIM ** (-0.5)
    spots = jnp.arange(length)
    scores = jnp.where((spots[None, :] <= spots[:, None])[None], scores, MASKED)
    top = jnp.max(scores, axis=-1, keepdims=True)
    weights = jnp.exp(scores - top)
    total = jnp.sum(weights, axis=-1, keepdims=True)
    mix = dots("hqk,khd->qhd", (weights / total).astype(BF), value)
    return mix.astype(BF), (top + jnp.log(total))[..., 0]


def self_backward(query, key, value, grad_mix, log_total):
    length = query.shape[0]
    scores = dots("qhd,khd->hqk", query, key) * HEAD_DIM ** (-0.5)
    spots = jnp.arange(length)
    scores = jnp.where((spots[None, :] <= spots[:, None])[None], scores, MASKED)
    weights = jnp.exp(scores - log_total[..., None])
    grad_weights = dots("qhd,khd->hqk", grad_mix, value)
    inner = jnp.sum(weights * grad_weights, axis=-1, keepdims=True)
    grad_scores = (weights * (grad_weights - inner)).astype(BF)
    grad_query = dots("hqk,khd->qhd", grad_scores, key) * HEAD_DIM ** (-0.5)
    grad_key = dots("hqk,qhd->khd", grad_scores, query) * HEAD_DIM ** (-0.5)
    grad_value = dots("hqk,qhd->khd", weights.astype(BF), grad_mix)
    return grad_query.astype(BF), grad_key.astype(BF), grad_value.astype(BF)


def on_device(
    frames,
    text_states,
    cotangent,
    norm_gain,
    norm_bias,
    self_qkv,
    self_out,
    cross_qkv,
    cross_out,
    mlp_up,
    mlp_down,
):
    clips, rows, width = frames.shape
    context = lax.axis_index("context")
    depth = self_qkv.shape[1]
    slices = width // depth
    columns = self_qkv.shape[2] // 2
    heads = columns // HEAD_DIM
    block = clips * rows
    texts = text_states.shape[1]

    def half(weight):
        size = weight.shape[-1] // 2
        return lax.dynamic_slice_in_dim(weight, context * size, size, weight.ndim - 1)

    def over_shard(weight, tiled=True):
        return lax.all_gather(weight, "shard", axis=0, tiled=tiled)

    qkv_part = half(self_qkv)
    w_qkv = over_shard(jnp.concatenate([qkv_part[0], qkv_part[1], qkv_part[2]], axis=-1))
    cross_part = half(cross_qkv)
    side = jnp.stack(
        [half(self_out), cross_part[0], half(cross_out), cross_part[1], cross_part[2]]
    )
    w_side = over_shard(side.transpose(0, 2, 1), tiled=False).transpose(1, 2, 0, 3)
    w_side = w_side.reshape(5, columns, width)
    w_up = over_shard(half(mlp_up))
    w_down = over_shard(half(mlp_down))

    stream_zero = frames.astype(F32)
    norm_one, norm_one_back = jax.vjp(layer_norm, stream_zero, norm_gain[0], norm_bias[0])
    all_one = plane_gather(norm_one.astype(BF).reshape(block, width), 0)
    flat_one = all_one.reshape(8 * block, width)
    qkv = dots("rd,de->re", flat_one, w_qkv).astype(BF)

    def by_clip(values):
        values = values.reshape(8, clips, rows, columns).transpose(1, 0, 2, 3)
        return values.reshape(clips, 8 * rows, heads, HEAD_DIM)

    def by_owner(values):
        values = values.reshape(clips, 8, rows, columns).transpose(1, 0, 2, 3)
        return values.reshape(8, block, columns)

    query, key, value = (by_clip(qkv[:, j * columns : (j + 1) * columns]) for j in range(3))
    mix, self_log = lax.map(lambda a: self_forward(*a), (query, key, value))
    mix = by_owner(mix)
    my_mix = plane_exchange(mix, 1)

    plane_w = plane_gather(w_side[:3].reshape(3 * columns, width), 2)
    plane_w = plane_w.reshape(8, 3, columns, width)
    w_out, w_query, w_cross = plane_w[:, 0], plane_w[:, 1], plane_w[:, 2]
    branch_one = dots("bre,bed->rd", my_mix, w_out).reshape(clips, rows, width)
    stream_one = stream_zero + branch_one
    norm_two, norm_two_back = jax.vjp(layer_norm, stream_one, norm_gain[1], norm_bias[1])
    low_two = norm_two.astype(BF)
    cross_q = dots("cfd,bed->cfbe", low_two, w_query).astype(BF)
    text_part = dots("cnd,ted->tcne", text_states, w_side[3:]).astype(BF)
    text_all = plane_gather(text_part.reshape(2 * clips * texts, columns), 3)
    text_all = text_all.reshape(8, 2, clips, texts, heads, HEAD_DIM)
    text_k, text_v = text_all[:, 0], text_all[:, 1]
    cross_q = cross_q.reshape(clips, rows, 8, heads, HEAD_DIM)
    scale = HEAD_DIM ** (-0.5)
    scores = dots("cfbhd,bcnhd->cbhfn", cross_q, text_k) * scale
    top = jnp.max(scores, axis=-1, keepdims=True)
    cross_full = jnp.exp(scores - top)
    cross_full = cross_full / jnp.sum(cross_full, axis=-1, keepdims=True)
    cross_probs = cross_full.astype(BF)
    cross_mix = dots("cbhfn,bcnhd->cfbhd", cross_probs, text_v).astype(BF)
    cross_mix = cross_mix.reshape(clips, rows, 8, columns)
    branch_two = dots("cfbe,bed->cfd", cross_mix, w_cross)
    stream_two = stream_one + branch_two

    norm_three, norm_three_back = jax.vjp(layer_norm, stream_two, norm_gain[2], norm_bias[2])
    all_three = plane_gather(norm_three.astype(BF).reshape(block, width), 4)
    flat_three = all_three.reshape(8 * block, width)
    pre_act = dots("rd,dh->rh", flat_three, w_up)
    hidden, gelu_back = jax.vjp(partial(jax.nn.gelu, approximate=False), pre_act)
    hidden_low = hidden.astype(BF)
    part_three = dots("rh,dh->rd", hidden_low, w_down).astype(BF)
    branch_three = plane_scatter(part_three.reshape(8, block, width), 5)
    branch_three = branch_three.reshape(clips, rows, width)
    stream_out = stream_two + branch_three
    squares = jnp.stack(
        [
            jnp.sum(stream_out * stream_out),
            jnp.sum(branch_one * branch_one),
            jnp.sum(branch_two * branch_two),
            jnp.sum(branch_three * branch_three),
        ]
    )

    flat_grad = plane_gather(cotangent.reshape(block, width), 6).reshape(8 * block, width)
    grad_hidden = dots("rd,dh->rh", flat_grad, w_down)
    grad_pre = gelu_back(grad_hidden)[0].astype(BF)
    part_norm = dots("rh,dh->rd", grad_pre, w_up).astype(BF)
    grad_normed = plane_scatter(part_norm.reshape(8, block, width), 7)

    def to_shard(part):
        return lax.psum_scatter(part.astype(BF), "shard", scatter_dimension=0, tiled=True)

    grad_down = to_shard(dots("rd,rh->dh", flat_grad, hidden_low))
    grad_up = to_shard(dots("rd,rh->dh", flat_three, grad_pre))
    grad_inner, gain_three, shift_three = norm_three_back(grad_normed.reshape(clips, rows, width))
    grad_two = cotangent.astype(F32) + grad_inner

    grad_low = grad_two.astype(BF)
    grad_cross_mix = dots("cfd,bed->cfbe", grad_low, w_cross).astype(BF)
    w_grad_cross = dots("cfd,cfbe->bed", grad_low, cross_mix)
    grad_heads = grad_cross_mix.reshape(clips, rows, 8, heads, HEAD_DIM)
    cross_dp = dots("cfbhd,bcnhd->cbhfn", grad_heads, text_v)
    inner = jnp.sum(cross_full * cross_dp, axis=-1, keepdims=True)
    grad_scores = (cross_full * (cross_dp - inner)).astype(BF)
    grad_cq = (dots("cbhfn,bcnhd->cfbhd", grad_scores, text_k) * scale).astype(BF)
    grad_text_k = dots("cbhfn,cfbhd->bcnhd", grad_scores, cross_q) * scale
    grad_text_v = dots("cbhfn,cfbhd->bcnhd", cross_probs, grad_heads)
    grad_cq = grad_cq.reshape(clips, rows, 8, columns)
    w_grad_query = dots("cfd,cfbe->bed", low_two, grad_cq)
    grad_normed = dots("cfbe,bed->cfd", grad_cq, w_query)
    grad_inner, gain_two, shift_two = norm_two_back(grad_normed)
    grad_one = grad_two + grad_inner

    grad_low = grad_one.astype(BF).reshape(block, width)
    grad_mix = dots("rd,bed->bre", grad_low, w_out).astype(BF)
    w_grad_out = dots("rd,bre->bed", grad_low, my_mix)
    grad_mix = by_clip(plane_exchange(grad_mix, 8))

    text_grads = jnp.stack([grad_text_k, grad_text_v], axis=1).astype(BF)
    text_grads = plane_scatter(text_grads.reshape(8, 2 * clips * texts, columns), 9)
    text_grads = text_grads.reshape(2, clips, texts, columns)
    text_grads_low = text_grads.astype(BF)
    w_grad_text = dots("cnd,tcne->ted", text_states, text_grads_low)
    grad_text = dots("tcne,ted->cnd", text_grads_low, w_side[3:])
    grad_text = grad_text.reshape(clips, 8, texts // 8, width).transpose(1, 0, 2, 3).astype(BF)
    grad_text = plane_scatter(grad_text.reshape(8, clips * texts // 8, width), 10)
    grad_text = grad_text.reshape(clips, texts // 8, width)

    grads = lax.map(lambda a: self_backward(*a), (query, key, value, grad_mix, self_log))
    grad_qkv = jnp.concatenate([by_owner(g) for g in grads], axis=-1).reshape(8 * block, -1)
    part_norm = dots("re,de->rd", grad_qkv, w_qkv).astype(BF)
    grad_w_qkv = to_shard(dots("rd,re->de", flat_one, grad_qkv))
    grad_normed = plane_scatter(part_norm.reshape(8, block, width), 11)
    grad_inner, gain_one, shift_one = norm_one_back(grad_normed.reshape(clips, rows, width))
    grad_frames = grad_one + grad_inner

    part_side = jnp.stack([w_grad_out, w_grad_query, w_grad_cross], axis=1).astype(BF)
    part_side = plane_scatter(part_side.reshape(8, 3 * columns, width), 12)
    part_side = jnp.concatenate([part_side.reshape(3, columns, width), w_grad_text], axis=0)
    part_side = part_side.reshape(5, columns, slices, depth).transpose(2, 0, 1, 3)
    grad_side = to_shard(part_side)[0]

    def whole(values):
        return lax.all_gather(values, "context", axis=values.ndim - 1, tiled=True).astype(F32)

    grad_up, grad_down = whole(grad_up), whole(grad_down)
    grad_self = jnp.stack([grad_w_qkv[:, j * columns : (j + 1) * columns] for j in range(3)])
    grad_side = grad_side.transpose(0, 2, 1)
    grad_all = whole(jnp.concatenate([grad_self, grad_side], axis=0))

    gains = jnp.stack([gain_one, gain_two, gain_three])
    shifts = jnp.stack([shift_one, shift_two, shift_three])
    gains, shifts, squares = lax.psum((gains, shifts, squares), ("shard",) + PLANE)
    start = lax.axis_index("shard") * depth
    grad_gain = lax.dynamic_slice_in_dim(gains, start, depth, 1)
    grad_shift = lax.dynamic_slice_in_dim(shifts, start, depth, 1)
    entries = float(clips * rows * width * lax.axis_size(("shard",) + PLANE))
    return (
        stream_out.astype(BF),
        grad_frames,
        grad_text,
        grad_gain,
        grad_shift,
        grad_all[:3],
        grad_all[3],
        jnp.stack([grad_all[4], grad_all[6], grad_all[7]]),
        grad_all[5],
        grad_up,
        grad_down,
        jnp.sqrt(squares / entries),
    )


def solution(mesh):
    rows = P("shard", PLANE, None)
    stack = P(None, "shard", "tensor")
    flat = P("shard", "tensor")
    return jax.shard_map(
        on_device,
        mesh=mesh,
        in_specs=(rows, P("shard"), rows, P(), P(), stack, flat, stack, flat, flat, flat),
        out_specs=(
            (rows, rows, rows, P(None, "shard"), P(None, "shard"))
            + (stack, flat, stack, flat, flat, flat, P())
        ),
        check_vma=False,
    )
```

```python
from functools import partial

import jax
import jax.numpy as jnp
from jax import lax
from jax.experimental import pallas as pl
from jax.experimental.pallas import tpu as pltpu
from jax.sharding import PartitionSpec as P

HEAD_DIM = 64
EPS = 1e-05
MASKED = -1e30
MESH = pl.DeviceIdType.MESH
BF = jnp.bfloat16
F32 = jnp.float32
PLANE = ("context", "tensor")
VMEM_LIMIT = 60 * 2**20


def place():
    return (
        lax.axis_index("shard"),
        lax.axis_index("context"),
        lax.axis_index("tensor") // 2,
        lax.axis_index("tensor") % 2,
    )


def device(z, x, y, c):
    return (z, x, 2 * y + c)


def slot(x, y, c):
    return 4 * x + 2 * y + c


def neighbours():
    z, x, y, c = place()
    return [device(z, 1 - x, y, c), device(z, x, 1 - y, c), device(z, x, y, 1 - c)]


def plane_spots():
    z, x, y, c = place()
    steps = [(a, b, d) for a in range(2) for b in range(2) for d in range(2) if a + b + d]
    return [((x + a) % 2, (y + b) % 2, (c + d) % 2) for a, b, d in steps]


def plane_others():
    z = lax.axis_index("shard")
    return [device(z, *spot) for spot in plane_spots()]


def enter(targets):
    barrier = pltpu.get_barrier_semaphore()
    for target in targets:
        pl.semaphore_signal(barrier, inc=1, device_id=target, device_id_type=MESH)
    pl.semaphore_wait(barrier, len(targets))


def remote_copy(source, target_ref, send, recv, target):
    return pltpu.make_async_remote_copy(
        src_ref=source,
        dst_ref=target_ref,
        send_sem=send,
        recv_sem=recv,
        device_id=target,
        device_id_type=MESH,
    )


class Gather:
    semaphores = 9

    def __init__(self, in_ref, out_ref, local_sem, send, recv):
        z, x, y, c = place()
        self.in_ref, self.out_ref, self.local_sem = in_ref, out_ref, local_sem
        self.send, self.recv = send, recv
        self.spot = (x, y, c)
        self.to_x, self.to_y, self.to_c = neighbours()
        self.rows = in_ref.shape[0]
        self.sends = []

    def go(self, index, owner, start, size, target, source=None):
        there = self.out_ref.at[owner, pl.ds(start, size)]
        copy = remote_copy(
            there if source is None else source,
            there,
            self.send.at[index],
            self.recv.at[index],
            target,
        )
        copy.start()
        self.sends.append(copy)

    def arrived(self, index, owner, start, size):
        there = self.out_ref.at[owner, pl.ds(start, size)]
        remote_copy(
            there, there, self.send.at[index], self.recv.at[index], self.to_x
        ).wait_recv()

    def start(self):
        me = slot(*self.spot)
        self.own = pltpu.make_async_copy(self.in_ref, self.out_ref.at[me], self.local_sem)
        self.own.start()
        for index, target in enumerate((self.to_x, self.to_y, self.to_c)):
            self.go(index, me, 0, self.rows, target, self.in_ref)

    def relay_y(self):
        x, y, c = self.spot
        owner = slot(x, 1 - y, c)
        self.arrived(1, owner, 0, self.rows)
        self.go(3, owner, 0, self.rows // 2, self.to_x)
        self.go(5, owner, 0, self.rows, self.to_c)

    def relay_x(self):
        x, y, c = self.spot
        half = self.rows // 2
        owner = slot(1 - x, y, c)
        self.arrived(0, owner, 0, self.rows)
        self.go(4, owner, half, half, self.to_y)
        self.go(6, owner, 0, self.rows, self.to_c)

    def relay_far(self):
        x, y, c = self.spot
        half = self.rows // 2
        owner = slot(1 - x, 1 - y, c)
        self.arrived(3, owner, 0, half)
        self.go(7, owner, 0, half, self.to_c)
        self.arrived(4, owner, half, half)
        self.go(8, owner, half, half, self.to_c)

    def finish(self):
        x, y, c = self.spot
        half = self.rows // 2
        self.arrived(2, slot(x, y, 1 - c), 0, self.rows)
        self.arrived(5, slot(x, 1 - y, 1 - c), 0, self.rows)
        self.arrived(6, slot(1 - x, y, 1 - c), 0, self.rows)
        self.arrived(7, slot(1 - x, 1 - y, 1 - c), 0, half)
        self.arrived(8, slot(1 - x, 1 - y, 1 - c), half, half)
        self.own.wait()
        for copy in self.sends:
            copy.wait_send()

    def rest(self):
        self.relay_y()
        self.relay_x()
        self.relay_far()
        self.finish()


class Scatter:
    semaphores = 10

    @staticmethod
    def scratch(rows, columns):
        return [
            pltpu.VMEM((4, rows, columns), BF),
            pltpu.VMEM((4, rows, columns), BF),
            pltpu.VMEM((3, rows, columns), BF),
            pltpu.VMEM((2, rows // 2, columns), BF),
            pltpu.VMEM((2, rows, columns), BF),
            pltpu.SemaphoreType.DMA((4,)),
            pltpu.SemaphoreType.DMA((10,)),
            pltpu.SemaphoreType.DMA((10,)),
        ]

    def __init__(self, in_ref, out_ref, mine, core, sums, relay, final, local_sem, send, recv):
        self.in_ref, self.out_ref = in_ref, out_ref
        self.mine, self.core, self.sums = mine, core, sums
        self.relay, self.final = relay, final
        self.local_sem, self.send, self.recv = local_sem, send, recv
        self.to_x, self.to_y, self.to_c = neighbours()
        rows = out_ref.shape[0]
        self.low, self.high = pl.ds(0, rows // 2), pl.ds(rows // 2, rows // 2)

    def forward(self, index, source, target_ref, target):
        copy = remote_copy(
            source, target_ref, self.send.at[index], self.recv.at[index], target
        )
        copy.start()
        self.sends.append(copy)

    def pair(self, index, part):
        return self.mine[index, part].astype(F32) + self.core[index, part].astype(F32)

    def start(self):
        z, x, y, c = place()
        self.sends, self.loads = [], []
        chips = ((1 - x, 1 - y), (1 - x, y), (x, 1 - y), (x, y))
        for index, (cx, cy) in enumerate(chips):
            self.forward(
                index, self.in_ref.at[slot(cx, cy, 1 - c)], self.core.at[index], self.to_c
            )
            load = pltpu.make_async_copy(
                self.in_ref.at[slot(cx, cy, c)], self.mine.at[index], self.local_sem.at[index]
            )
            load.start()
            self.loads.append(load)

    def ready(self, index):
        self.loads[index].wait()
        self.sends[index].wait_recv()

    def first(self):
        low, high, sums = self.low, self.high, self.sums
        self.ready(0)
        sums[0, low] = self.pair(0, low).astype(BF)
        self.forward(4, sums.at[0, low], self.relay.at[0], self.to_x)
        sums[0, high] = self.pair(0, high).astype(BF)
        self.forward(5, sums.at[0, high], self.relay.at[1], self.to_y)
        self.ready(1)
        sums[1, low] = self.pair(1, low).astype(BF)
        self.forward(6, sums.at[1, low], self.final.at[0, low], self.to_x)
        self.ready(2)
        sums[2, high] = self.pair(2, high).astype(BF)
        self.forward(7, sums.at[2, high], self.final.at[1, high], self.to_y)
        self.ready(3)

    def second(self):
        low, high, sums = self.low, self.high, self.sums
        self.sends[5].wait_recv()
        sums[1, high] = (self.pair(1, high) + self.relay[1].astype(F32)).astype(BF)
        self.forward(8, sums.at[1, high], self.final.at[0, high], self.to_x)
        self.sends[4].wait_recv()
        sums[2, low] = (self.pair(2, low) + self.relay[0].astype(F32)).astype(BF)
        self.forward(9, sums.at[2, low], self.final.at[1, low], self.to_y)

    def total(self):
        for index in (6, 7, 8, 9):
            self.sends[index].wait_recv()
        everything = self.pair(3, slice(None))
        return everything + self.final[0].astype(F32) + self.final[1].astype(F32)

    def finish(self):
        for copy in self.sends:
            copy.wait_send()


class Exchange:
    def __init__(self, in_ref, out_ref, local_sem, send, recv):
        self.in_ref, self.out_ref, self.local_sem = in_ref, out_ref, local_sem
        self.send, self.recv = send, recv
        z, x, y, c = place()
        self.me = slot(x, y, c)
        self.copies = []

    def start(self, piece, part):
        z = lax.axis_index("shard")
        own = pltpu.make_async_copy(
            self.in_ref.at[self.me, part], self.out_ref.at[self.me, part], self.local_sem.at[piece]
        )
        own.start()
        self.copies.append(own)
        for index, spot in enumerate(plane_spots()):
            copy = remote_copy(
                self.in_ref.at[slot(*spot), part],
                self.out_ref.at[self.me, part],
                self.send.at[piece, index],
                self.recv.at[piece, index],
                device(z, *spot),
            )
            copy.start()
            self.copies.append(copy)

    def finish(self, piece=None):
        copies = self.copies if piece is None else self.copies[8 * piece : 8 * piece + 8]
        for copy in copies:
            copy.wait()


ANY = pl.BlockSpec(memory_space=pl.ANY)
IN_VMEM = pl.BlockSpec(memory_space=pltpu.VMEM)


def call(kernel, name, outs, out_specs, in_specs, scratch, ident=None):
    return pl.pallas_call(
        kernel,
        out_shape=outs,
        in_specs=in_specs,
        out_specs=out_specs,
        scratch_shapes=scratch,
        name=name,
        compiler_params=pltpu.CompilerParams(
            collective_id=ident,
            has_side_effects=ident is not None,
            vmem_limit_bytes=VMEM_LIMIT,
        ),
    )


def shape(*dims, dtype=BF):
    return jax.ShapeDtypeStruct(dims, dtype)


def gather_scratch():
    return [
        pltpu.SemaphoreType.DMA,
        pltpu.SemaphoreType.DMA((9,)),
        pltpu.SemaphoreType.DMA((9,)),
    ]


def gather_kernel(*refs):
    enter(neighbours())
    job = Gather(*refs)
    job.start()
    job.rest()


def plane_gather(values, ident):
    rows, columns = values.shape
    outs = shape(8, rows, columns, dtype=values.dtype)
    return call(gather_kernel, "plane_gather", outs, ANY, [ANY], gather_scratch(), ident)(values)


def scatter_kernel(in_ref, out_ref, *scratch):
    enter(neighbours())
    job = Scatter(in_ref, out_ref, *scratch)
    job.start()
    job.first()
    job.second()
    out_ref[...] = job.total()
    job.finish()


def plane_scatter(values, ident):
    _, rows, columns = values.shape
    outs = shape(rows, columns, dtype=F32)
    scratch = Scatter.scratch(rows, columns)
    return call(scatter_kernel, "plane_scatter", outs, IN_VMEM, [ANY], scratch, ident)(values)


SIDE = 256


def nt(left, right):
    return lax.dot_general(left, right, (((1,), (1,)), ((), ())), preferred_element_type=F32)


def nn(left, right):
    return lax.dot_general(left, right, (((1,), (0,)), ((), ())), preferred_element_type=F32)


def turn(values):
    return jnp.transpose(values.astype(F32))


def causal(scores):
    keys = lax.broadcasted_iota(jnp.int32, scores.shape, 0)
    queries = lax.broadcasted_iota(jnp.int32, scores.shape, 1)
    return jnp.where(keys <= queries, scores, MASKED)


def forward_kernel(
    rows_ref, w_ref, cot_ref,
    qkv_ref, log_ref, mix_ref, mine_ref, cot_out,
    ex_local, ex_send, ex_recv, g_local, g_send, g_recv,
):
    enter(plane_others())
    side = Gather(cot_ref, cot_out, g_local, g_send, g_recv)
    side.start()
    blocks, both, _ = rows_ref.shape
    rows = both // 2
    width = mix_ref.shape[2]
    heads = width // HEAD_DIM
    length = blocks * rows
    step = SIDE // rows

    def project(block, carry):
        qkv_ref[block] = nn(rows_ref[block], w_ref[...]).astype(BF)
        return carry

    lax.fori_loop(0, blocks, project, 0)
    exchange = Exchange(mix_ref, mine_ref, ex_local, ex_send, ex_recv)
    for clip in range(2):
        part = pl.ds(clip * rows, rows)
        for head in range(heads):
            lanes = [pl.ds(j * width + head * HEAD_DIM, HEAD_DIM) for j in range(3)]
            key = qkv_ref[:, part, lanes[1]].reshape(length, HEAD_DIM)
            value = turn(qkv_ref[:, part, lanes[2]].reshape(length, HEAD_DIM)).astype(BF)
            for index in range(length // SIDE):
                spots = pl.ds(index * step, step)
                query = qkv_ref[spots, part, lanes[0]].reshape(SIDE, HEAD_DIM)
                query = query * jnp.asarray(HEAD_DIM ** (-0.5), BF)
                start = index * SIDE
                last = causal(nt(key[start : start + SIDE], query))
                top = jnp.max(last, axis=0, keepdims=True)
                if index:
                    early = nt(key[:start], query)
                    top = jnp.maximum(top, jnp.max(early, axis=0, keepdims=True))
                last = jnp.exp(last - top)
                total = jnp.sum(last, axis=0, keepdims=True)
                mix = nn(value[:, start : start + SIDE], last.astype(BF))
                if index:
                    early = jnp.exp(early - top)
                    total += jnp.sum(early, axis=0, keepdims=True)
                    mix += nn(value[:, :start], early.astype(BF))
                mix = jnp.transpose(mix / total).astype(BF).reshape(step, rows, HEAD_DIM)
                mix_ref[spots, part, pl.ds(head * HEAD_DIM, HEAD_DIM)] = mix
                log_ref[pl.ds(clip * heads + head, 1), pl.ds(start, SIDE)] = top + jnp.log(total)
        exchange.start(clip, part)
        if clip == 0:
            side.relay_y()
            side.relay_x()
    side.relay_far()
    exchange.finish()
    side.finish()


def attend_forward(rows, weights, cotangent, ident):
    blocks, block, width = rows.shape
    columns = weights.shape[1] // 3
    heads = columns // HEAD_DIM
    return call(
        forward_kernel,
        "attend_forward",
        (
            shape(blocks, block, 3 * columns),
            shape(2 * heads, blocks * block // 2, dtype=F32),
            shape(blocks, block, columns),
            shape(blocks, block, columns),
            shape(blocks, block, width),
        ),
        (IN_VMEM, IN_VMEM, IN_VMEM, ANY, ANY),
        [IN_VMEM, IN_VMEM, ANY],
        [
            pltpu.SemaphoreType.DMA((2,)),
            pltpu.SemaphoreType.DMA((2, 7)),
            pltpu.SemaphoreType.DMA((2, 7)),
        ]
        + gather_scratch(),
        ident,
    )(rows, weights, cotangent)


def backward_kernel(
    grad_ref, qkv_ref, mix_ref, log_ref, side_ref,
    out_ref, side_out,
    grad_all, query_turned, ex_local, ex_send, ex_recv, *scratch,
):
    enter(plane_others())
    exchange = Exchange(grad_ref, grad_all, ex_local, ex_send, ex_recv)
    blocks, both, width = mix_ref.shape
    rows = both // 2
    heads = width // HEAD_DIM
    length = blocks * rows
    step = SIDE // rows
    for clip in range(2):
        exchange.start(clip, pl.ds(clip * rows, rows))
    side = Scatter(side_ref, side_out, *scratch)
    side.start()
    side.first()
    for clip in range(2):
        exchange.finish(clip)
        part = pl.ds(clip * rows, rows)
        for head in range(heads):
            lanes = [pl.ds(j * width + head * HEAD_DIM, HEAD_DIM) for j in range(3)]
            query = qkv_ref[:, part, lanes[0]].reshape(length, HEAD_DIM)
            query = query * jnp.asarray(HEAD_DIM ** (-0.5), BF)
            key = qkv_ref[:, part, lanes[1]].reshape(length, HEAD_DIM)
            value = qkv_ref[:, part, lanes[2]].reshape(length, HEAD_DIM)
            key_turned = turn(key).astype(BF)
            here = pl.ds(head * HEAD_DIM, HEAD_DIM)
            grad = grad_all[:, part, here].reshape(length, HEAD_DIM)
            mixed = mix_ref[:, part, here].reshape(length, HEAD_DIM)
            inner = jnp.transpose(grad.astype(F32) * mixed.astype(F32))
            inner = jnp.sum(inner, axis=0, keepdims=True)
            logs = log_ref[pl.ds(clip * heads + head, 1), :]
            for index in range(length // SIDE):
                start = index * SIDE
                spots = pl.ds(index * step, step)
                k_part, v_part = key[start : start + SIDE], value[start : start + SIDE]
                scores = nt(k_part, query[start:])
                first = causal(scores[:, :SIDE])
                if start + SIDE < length:
                    scores = jnp.concatenate([first, scores[:, SIDE:]], axis=1)
                else:
                    scores = first
                weights = jnp.exp(scores - logs[:, start:])
                slopes = nt(v_part, grad[start:])
                slopes = (weights * (slopes - inner[:, start:])).astype(BF)
                grad_key = nn(slopes, query[start:]).astype(BF).reshape(step, rows, HEAD_DIM)
                grad_value = nn(weights.astype(BF), grad[start:]).astype(BF)
                out_ref[spots, part, lanes[1]] = grad_key
                out_ref[spots, part, lanes[2]] = grad_value.reshape(step, rows, HEAD_DIM)
                grad_query = nn(key_turned[:, start : start + SIDE], slopes)
                if index:
                    query_turned[:, start:] += grad_query
                else:
                    query_turned[...] = grad_query
            grad_query = jnp.transpose(query_turned[...]) * HEAD_DIM ** (-0.5)
            grad_query = grad_query.astype(BF).reshape(blocks, rows, HEAD_DIM)
            out_ref[:, part, lanes[0]] = grad_query
        if clip == 0:
            side.second()
    side_out[...] = side.total().astype(BF)
    side.finish()


def attend_backward(grad_mix, qkv, mix, logs, side, ident):
    blocks, block, columns = mix.shape
    _, rows, width = side.shape
    return call(
        backward_kernel,
        "attend_backward",
        (shape(blocks, block, 3 * columns), shape(rows, width)),
        (IN_VMEM, IN_VMEM),
        [ANY, IN_VMEM, IN_VMEM, IN_VMEM, ANY],
        [
            pltpu.VMEM((blocks, block, columns), BF),
            pltpu.VMEM((HEAD_DIM, blocks * block // 2), F32),
            pltpu.SemaphoreType.DMA((2,)),
            pltpu.SemaphoreType.DMA((2, 7)),
            pltpu.SemaphoreType.DMA((2, 7)),
        ]
        + Scatter.scratch(rows, width),
        ident,
    )(grad_mix, qkv, mix, logs, side)


def last_kernel(
    part_ref, frames_ref, gain_ref, grad_ref, stats_ref,
    out_ref, total_ref,
    mine, came, all_ref, st_send, st_recv, z_send, z_recv, *scratch,
):
    z = lax.axis_index("shard")
    shards = lax.axis_size("shard")
    others = [lax.rem(z + i, shards) for i in range(1, shards)]
    spot = place()[1:]
    enter(neighbours() + [device(other, *spot) for other in others])
    job = Scatter(part_ref, out_ref, *scratch)
    job.start()
    inputs = frames_ref[...].astype(F32)
    average = jnp.mean(inputs, axis=-1, keepdims=True)
    centred = inputs - average
    rate = lax.rsqrt(jnp.mean(centred * centred, axis=-1, keepdims=True) + EPS)
    job.first()
    job.second()
    grads = job.total()
    normed = centred * rate
    mine[0] = stats_ref[...]
    mine[0, 0:1] = jnp.sum(grads * normed, axis=0, keepdims=True)
    mine[0, 1:2] = jnp.sum(grads, axis=0, keepdims=True)
    sends = []
    for index, target in enumerate(reversed(neighbours())):
        copy = remote_copy(
            mine.at[index], came.at[index], st_send.at[index], st_recv.at[index], target
        )
        copy.start()
        sends.append(copy)
        if index == 0:
            scaled = grads * gain_ref[...]
            inner = jnp.mean(scaled * normed, axis=-1, keepdims=True)
            scaled = scaled - jnp.mean(scaled, axis=-1, keepdims=True) - normed * inner
            out_ref[...] = grad_ref[...] + rate * scaled
        copy.wait_recv()
        mine[index + 1] = mine[index] + came[index]
    for index, other in enumerate(others):
        copy = remote_copy(
            mine.at[3], all_ref.at[z], z_send.at[index], z_recv.at[index], device(other, *spot)
        )
        copy.start()
        sends.append(copy)
    all_ref[z] = mine[3]
    for copy in sends[3:]:
        copy.wait_recv()
    total = all_ref[0]
    for index in range(1, shards):
        total += all_ref[index]
    total_ref[...] = total
    for copy in sends:
        copy.wait_send()
    job.finish()


def last_step(part, frames, gain, grad, stats, shards, ident):
    _, rows, width = part.shape
    return call(
        last_kernel,
        "last_step",
        (shape(rows, width, dtype=F32), shape(8, width, dtype=F32)),
        (IN_VMEM, IN_VMEM),
        [ANY, IN_VMEM, IN_VMEM, IN_VMEM, IN_VMEM],
        [
            pltpu.VMEM((4, 8, width), F32),
            pltpu.VMEM((3, 8, width), F32),
            pltpu.VMEM((shards, 8, width), F32),
            pltpu.SemaphoreType.DMA((3,)),
            pltpu.SemaphoreType.DMA((3,)),
            pltpu.SemaphoreType.DMA((shards - 1,)),
            pltpu.SemaphoreType.DMA((shards - 1,)),
        ]
        + Scatter.scratch(rows, width),
        ident,
    )(part, frames, gain, grad, stats)


def dots(spec, *operands):
    return jnp.einsum(spec, *operands, preferred_element_type=F32)


def layer_norm(inputs, scaling, offset):
    average = jnp.mean(inputs, axis=-1, keepdims=True)
    centred = inputs - average
    variance = jnp.mean(centred * centred, axis=-1, keepdims=True)
    return centred * lax.rsqrt(variance + EPS) * scaling + offset


def on_device(
    frames,
    text_states,
    cotangent,
    norm_gain,
    norm_bias,
    self_qkv,
    self_out,
    cross_qkv,
    cross_out,
    mlp_up,
    mlp_down,
):
    clips, rows, width = frames.shape
    context = lax.axis_index("context")
    depth = self_qkv.shape[1]
    slices = width // depth
    columns = self_qkv.shape[2] // 2
    heads = columns // HEAD_DIM
    block = clips * rows
    texts = text_states.shape[1]

    def half(weight):
        size = weight.shape[-1] // 2
        return lax.dynamic_slice_in_dim(weight, context * size, size, weight.ndim - 1)

    def over_shard(weight, tiled=True):
        return lax.all_gather(weight, "shard", axis=0, tiled=tiled)

    qkv_part = half(self_qkv)
    w_qkv = over_shard(jnp.concatenate([qkv_part[0], qkv_part[1], qkv_part[2]], axis=-1))
    cross_part = half(cross_qkv)
    side = jnp.stack(
        [half(self_out), cross_part[0], half(cross_out), cross_part[1], cross_part[2]]
    )
    w_side = over_shard(side.transpose(0, 2, 1), tiled=False).transpose(1, 2, 0, 3)
    w_side = w_side.reshape(5, columns, width)
    w_up = over_shard(half(mlp_up))
    w_down = over_shard(half(mlp_down))

    stream_zero = frames.astype(F32)
    norm_one = layer_norm(stream_zero, norm_gain[0], norm_bias[0])
    all_one = plane_gather(norm_one.astype(BF).reshape(block, width), 0)
    flat_one = all_one.reshape(8 * block, width)
    qkv, self_log, mix, my_mix, all_grad = attend_forward(
        all_one, w_qkv, cotangent.reshape(block, width), 1
    )

    plane_w = plane_gather(w_side[:3].reshape(3 * columns, width), 2)
    plane_w = plane_w.reshape(8, 3, columns, width)
    w_out, w_query, w_cross = plane_w[:, 0], plane_w[:, 1], plane_w[:, 2]
    branch_one = dots("bre,bed->rd", my_mix, w_out).reshape(clips, rows, width)
    stream_one = stream_zero + branch_one
    norm_two, norm_two_back = jax.vjp(layer_norm, stream_one, norm_gain[1], norm_bias[1])
    low_two = norm_two.astype(BF)
    cross_q = dots("cfd,bed->cfbe", low_two, w_query).astype(BF)
    text_part = dots("cnd,ted->tcne", text_states, w_side[3:]).astype(BF)
    text_all = plane_gather(text_part.reshape(2 * clips * texts, columns), 3)
    text_all = text_all.reshape(8, 2, clips, texts, heads, HEAD_DIM)
    text_k, text_v = text_all[:, 0], text_all[:, 1]
    cross_q = cross_q.reshape(clips, rows, 8, heads, HEAD_DIM)
    scale = HEAD_DIM ** (-0.5)
    scores = dots("cfbhd,bcnhd->cbhfn", cross_q, text_k) * scale
    top = jnp.max(scores, axis=-1, keepdims=True)
    cross_full = jnp.exp(scores - top)
    cross_full = cross_full / jnp.sum(cross_full, axis=-1, keepdims=True)
    cross_probs = cross_full.astype(BF)
    cross_mix = dots("cbhfn,bcnhd->cfbhd", cross_probs, text_v).astype(BF)
    cross_mix = cross_mix.reshape(clips, rows, 8, columns)
    branch_two = dots("cfbe,bed->cfd", cross_mix, w_cross)
    stream_two = stream_one + branch_two

    norm_three, norm_three_back = jax.vjp(layer_norm, stream_two, norm_gain[2], norm_bias[2])
    all_three = plane_gather(norm_three.astype(BF).reshape(block, width), 4)
    flat_three = all_three.reshape(8 * block, width)
    pre_act = dots("rd,dh->rh", flat_three, w_up)
    hidden, gelu_back = jax.vjp(partial(jax.nn.gelu, approximate=False), pre_act)
    hidden_low = hidden.astype(BF)
    part_three = dots("rh,dh->rd", hidden_low, w_down).astype(BF)
    branch_three = plane_scatter(part_three.reshape(8, block, width), 5)
    branch_three = branch_three.reshape(clips, rows, width)
    stream_out = stream_two + branch_three
    squares = jnp.stack(
        [
            jnp.sum(stream_out * stream_out),
            jnp.sum(branch_one * branch_one),
            jnp.sum(branch_two * branch_two),
            jnp.sum(branch_three * branch_three),
        ]
    )

    flat_grad = all_grad.reshape(8 * block, width)
    grad_hidden = dots("rd,dh->rh", flat_grad, w_down)
    grad_pre = gelu_back(grad_hidden)[0].astype(BF)
    part_norm = dots("rh,dh->rd", grad_pre, w_up).astype(BF)
    grad_normed = plane_scatter(part_norm.reshape(8, block, width), 7)

    def to_shard(part):
        return lax.psum_scatter(part.astype(BF), "shard", scatter_dimension=0, tiled=True)

    grad_down = to_shard(dots("rd,rh->dh", flat_grad, hidden_low))
    grad_up = to_shard(dots("rd,rh->dh", flat_three, grad_pre))
    grad_inner, gain_three, shift_three = norm_three_back(grad_normed.reshape(clips, rows, width))
    grad_two = cotangent.astype(F32) + grad_inner

    grad_low = grad_two.astype(BF)
    grad_cross_mix = dots("cfd,bed->cfbe", grad_low, w_cross).astype(BF)
    w_grad_cross = dots("cfd,cfbe->bed", grad_low, cross_mix)
    grad_heads = grad_cross_mix.reshape(clips, rows, 8, heads, HEAD_DIM)
    cross_dp = dots("cfbhd,bcnhd->cbhfn", grad_heads, text_v)
    inner = jnp.sum(cross_full * cross_dp, axis=-1, keepdims=True)
    grad_scores = (cross_full * (cross_dp - inner)).astype(BF)
    grad_cq = (dots("cbhfn,bcnhd->cfbhd", grad_scores, text_k) * scale).astype(BF)
    grad_text_k = dots("cbhfn,cfbhd->bcnhd", grad_scores, cross_q) * scale
    grad_text_v = dots("cbhfn,cfbhd->bcnhd", cross_probs, grad_heads)
    grad_cq = grad_cq.reshape(clips, rows, 8, columns)
    w_grad_query = dots("cfd,cfbe->bed", low_two, grad_cq)
    grad_normed = dots("cfbe,bed->cfd", grad_cq, w_query)
    grad_inner, gain_two, shift_two = norm_two_back(grad_normed)
    grad_one = grad_two + grad_inner

    grad_low = grad_one.astype(BF).reshape(block, width)
    grad_mix = dots("rd,bed->bre", grad_low, w_out).astype(BF)
    w_grad_out = dots("rd,bre->bed", grad_low, my_mix)

    text_grads = jnp.stack([grad_text_k, grad_text_v], axis=1).astype(BF)
    text_grads = plane_scatter(text_grads.reshape(8, 2 * clips * texts, columns), 9)
    text_grads = text_grads.reshape(2, clips, texts, columns)
    text_grads_low = text_grads.astype(BF)
    w_grad_text = dots("cnd,tcne->ted", text_states, text_grads_low)
    grad_text = dots("tcne,ted->cnd", text_grads_low, w_side[3:])
    grad_text = grad_text.reshape(clips, 8, texts // 8, width).transpose(1, 0, 2, 3).astype(BF)
    grad_text = plane_scatter(grad_text.reshape(8, clips * texts // 8, width), 10)
    grad_text = grad_text.reshape(clips, texts // 8, width)

    part_side = jnp.stack([w_grad_out, w_grad_query, w_grad_cross], axis=1).astype(BF)
    part_side = part_side.reshape(8, 3 * columns, width)
    grad_qkv, part_side = attend_backward(grad_mix, qkv, mix, self_log, part_side, 8)
    grad_qkv = grad_qkv.reshape(8 * block, 3 * columns)
    part_norm = dots("re,de->rd", grad_qkv, w_qkv).astype(BF)
    grad_w_qkv = to_shard(dots("rd,re->de", flat_one, grad_qkv))
    nothing = jnp.zeros((1, width), F32)
    stats = [nothing, nothing] + [
        v[None] for v in (gain_two, shift_two, gain_three, shift_three)
    ]
    stats.append(jnp.pad(squares, (0, width - 4))[None])
    grad_frames, totals = last_step(
        part_norm.reshape(8, block, width),
        frames.reshape(block, width),
        norm_gain[0][None],
        grad_one.reshape(block, width),
        jnp.concatenate(stats + [nothing], axis=0),
        lax.axis_size("shard"),
        11,
    )
    grad_frames = grad_frames.reshape(clips, rows, width)

    part_side = part_side.reshape(3, columns, width)
    part_side = jnp.concatenate([part_side, w_grad_text.astype(BF)], axis=0)
    part_side = part_side.reshape(5, columns, slices, depth).transpose(2, 0, 1, 3)
    grad_side = to_shard(part_side)[0]

    def whole(values):
        return lax.all_gather(values, "context", axis=values.ndim - 1, tiled=True).astype(F32)

    grad_up, grad_down = whole(grad_up), whole(grad_down)
    grad_self = jnp.stack([grad_w_qkv[:, j * columns : (j + 1) * columns] for j in range(3)])
    grad_side = grad_side.transpose(0, 2, 1)
    grad_all = whole(jnp.concatenate([grad_self, grad_side], axis=0))

    gains = jnp.stack([totals[0], totals[2], totals[4]])
    shifts = jnp.stack([totals[1], totals[3], totals[5]])
    squares = totals[6, :4]
    start = lax.axis_index("shard") * depth
    grad_gain = lax.dynamic_slice_in_dim(gains, start, depth, 1)
    grad_shift = lax.dynamic_slice_in_dim(shifts, start, depth, 1)
    entries = float(clips * rows * width * lax.axis_size(("shard",) + PLANE))
    return (
        stream_out.astype(BF),
        grad_frames,
        grad_text,
        grad_gain,
        grad_shift,
        grad_all[:3],
        grad_all[3],
        jnp.stack([grad_all[4], grad_all[6], grad_all[7]]),
        grad_all[5],
        grad_up,
        grad_down,
        jnp.sqrt(squares / entries),
    )


def solution(mesh):
    rows = P("shard", PLANE, None)
    stack = P(None, "shard", "tensor")
    flat = P("shard", "tensor")
    return jax.shard_map(
        on_device,
        mesh=mesh,
        in_specs=(rows, P("shard"), rows, P(), P(), stack, flat, stack, flat, flat, flat),
        out_specs=(
            (rows, rows, rows, P(None, "shard"), P(None, "shard"))
            + (stack, flat, stack, flat, flat, flat, P())
        ),
        check_vma=False,
    )
```

```python
from functools import partial

import jax
import jax.numpy as jnp
from jax import lax
from jax.experimental import pallas as pl
from jax.experimental.pallas import tpu as pltpu
from jax.sharding import PartitionSpec as P

HEAD_DIM = 64
EPS = 1e-05
MASKED = -1e30
MESH = pl.DeviceIdType.MESH
BF = jnp.bfloat16
F32 = jnp.float32
PLANE = ("context", "tensor")
VMEM_LIMIT = 60 * 2**20


def place():
    return (
        lax.axis_index("shard"),
        lax.axis_index("context"),
        lax.axis_index("tensor") // 2,
        lax.axis_index("tensor") % 2,
    )


def device(z, x, y, c):
    return (z, x, 2 * y + c)


def slot(x, y, c):
    return 4 * x + 2 * y + c


def neighbours():
    z, x, y, c = place()
    return [device(z, 1 - x, y, c), device(z, x, 1 - y, c), device(z, x, y, 1 - c)]


def plane_spots():
    z, x, y, c = place()
    steps = [(a, b, d) for a in range(2) for b in range(2) for d in range(2) if a + b + d]
    return [((x + a) % 2, (y + b) % 2, (c + d) % 2) for a, b, d in steps]


def plane_others():
    z = lax.axis_index("shard")
    return [device(z, *spot) for spot in plane_spots()]


def enter(targets):
    barrier = pltpu.get_barrier_semaphore()
    for target in targets:
        pl.semaphore_signal(barrier, inc=1, device_id=target, device_id_type=MESH)
    pl.semaphore_wait(barrier, len(targets))


def remote_copy(source, target_ref, send, recv, target):
    return pltpu.make_async_remote_copy(
        src_ref=source,
        dst_ref=target_ref,
        send_sem=send,
        recv_sem=recv,
        device_id=target,
        device_id_type=MESH,
    )


class Gather:
    semaphores = 9

    def __init__(self, in_ref, out_ref, local_sem, send, recv):
        z, x, y, c = place()
        self.in_ref, self.out_ref, self.local_sem = in_ref, out_ref, local_sem
        self.send, self.recv = send, recv
        self.spot = (x, y, c)
        self.to_x, self.to_y, self.to_c = neighbours()
        self.rows = in_ref.shape[0]
        self.sends = []

    def go(self, index, owner, start, size, target, source=None):
        there = self.out_ref.at[owner, pl.ds(start, size)]
        copy = remote_copy(
            there if source is None else source,
            there,
            self.send.at[index],
            self.recv.at[index],
            target,
        )
        copy.start()
        self.sends.append(copy)

    def arrived(self, index, owner, start, size):
        there = self.out_ref.at[owner, pl.ds(start, size)]
        remote_copy(
            there, there, self.send.at[index], self.recv.at[index], self.to_x
        ).wait_recv()

    def start(self):
        me = slot(*self.spot)
        self.own = pltpu.make_async_copy(self.in_ref, self.out_ref.at[me], self.local_sem)
        self.own.start()
        for index, target in enumerate((self.to_x, self.to_y, self.to_c)):
            self.go(index, me, 0, self.rows, target, self.in_ref)

    def relay_y(self):
        x, y, c = self.spot
        owner = slot(x, 1 - y, c)
        self.arrived(1, owner, 0, self.rows)
        self.go(3, owner, 0, self.rows // 2, self.to_x)
        self.go(5, owner, 0, self.rows, self.to_c)

    def relay_x(self):
        x, y, c = self.spot
        half = self.rows // 2
        owner = slot(1 - x, y, c)
        self.arrived(0, owner, 0, self.rows)
        self.go(4, owner, half, half, self.to_y)
        self.go(6, owner, 0, self.rows, self.to_c)

    def relay_far(self):
        x, y, c = self.spot
        half = self.rows // 2
        owner = slot(1 - x, 1 - y, c)
        self.arrived(3, owner, 0, half)
        self.go(7, owner, 0, half, self.to_c)
        self.arrived(4, owner, half, half)
        self.go(8, owner, half, half, self.to_c)

    def finish(self):
        x, y, c = self.spot
        half = self.rows // 2
        self.arrived(2, slot(x, y, 1 - c), 0, self.rows)
        self.arrived(5, slot(x, 1 - y, 1 - c), 0, self.rows)
        self.arrived(6, slot(1 - x, y, 1 - c), 0, self.rows)
        self.arrived(7, slot(1 - x, 1 - y, 1 - c), 0, half)
        self.arrived(8, slot(1 - x, 1 - y, 1 - c), half, half)
        self.own.wait()
        for copy in self.sends:
            copy.wait_send()

    def rest(self):
        self.relay_y()
        self.relay_x()
        self.relay_far()
        self.finish()


class Scatter:
    @staticmethod
    def scratch(rows, columns):
        return [
            pltpu.VMEM((4, rows, columns), BF),
            pltpu.VMEM((2, rows // 2, columns), BF),
            pltpu.VMEM((2, rows, columns), BF),
            pltpu.SemaphoreType.DMA((10,)),
            pltpu.SemaphoreType.DMA((10,)),
        ]

    def __init__(self, part_ref, core, relay, final, send, recv):
        self.part_ref, self.core, self.relay, self.final = part_ref, core, relay, final
        self.send, self.recv = send, recv
        self.to_x, self.to_y, self.to_c = neighbours()
        z, x, y, c = place()
        chips = ((1 - x, 1 - y), (1 - x, y), (x, 1 - y), (x, y))
        self.mine = [slot(*chip, c) for chip in chips]
        self.theirs = [slot(*chip, 1 - c) for chip in chips]
        rows = part_ref.shape[1]
        self.low, self.high = pl.ds(0, rows // 2), pl.ds(rows // 2, rows // 2)
        self.sends = []

    def forward(self, index, source, target_ref, target):
        copy = remote_copy(
            source, target_ref, self.send.at[index], self.recv.at[index], target
        )
        copy.start()
        self.sends.append(copy)

    def arrived(self, index, ref):
        remote_copy(ref, ref, self.send.at[index], self.recv.at[index], self.to_c).wait_recv()

    def pass_core(self, index):
        source = self.part_ref.at[self.theirs[index]]
        self.forward(index, source, self.core.at[index], self.to_c)

    def add(self, index, part, more=None):
        mine = self.mine[index]
        total = self.part_ref[mine, part].astype(F32) + self.core[index, part].astype(F32)
        if more is not None:
            total += more.astype(F32)
        self.part_ref[mine, part] = total.astype(BF)
        return self.part_ref.at[mine, part]

    def far(self):
        self.arrived(0, self.core.at[0])
        self.forward(4, self.add(0, self.low), self.relay.at[0], self.to_x)
        self.forward(5, self.add(0, self.high), self.relay.at[1], self.to_y)

    def near(self):
        self.arrived(1, self.core.at[1])
        self.forward(6, self.add(1, self.low), self.final.at[0, self.low], self.to_x)
        self.arrived(2, self.core.at[2])
        self.forward(7, self.add(2, self.high), self.final.at[1, self.high], self.to_y)

    def second(self):
        low, high, final, relay = self.low, self.high, self.final, self.relay
        self.arrived(5, relay.at[1])
        self.forward(8, self.add(1, high, relay[1]), final.at[0, high], self.to_x)
        self.arrived(4, relay.at[0])
        self.forward(9, self.add(2, low, relay[0]), final.at[1, low], self.to_y)

    def total(self):
        self.arrived(3, self.core.at[3])
        self.arrived(6, self.final.at[0, self.low])
        self.arrived(7, self.final.at[1, self.high])
        self.arrived(8, self.final.at[0, self.high])
        self.arrived(9, self.final.at[1, self.low])
        total = self.part_ref[self.mine[3]].astype(F32) + self.core[3].astype(F32)
        return total + self.final[0].astype(F32) + self.final[1].astype(F32)

    def finish(self):
        for copy in self.sends:
            copy.wait_send()


class LoadedScatter(Scatter):
    @staticmethod
    def scratch(rows, columns):
        return [
            pltpu.VMEM((4, rows, columns), BF),
            pltpu.SemaphoreType.DMA((4,)),
        ] + Scatter.scratch(rows, columns)

    def __init__(self, in_ref, part_ref, local_sem, *scratch):
        super().__init__(part_ref, *scratch)
        self.in_ref, self.local_sem = in_ref, local_sem

    def start(self):
        self.loads = []
        for index, (mine, theirs) in enumerate(zip(self.mine, self.theirs)):
            source = self.in_ref.at[theirs]
            self.forward(index, source, self.core.at[index], self.to_c)
            load = pltpu.make_async_copy(
                self.in_ref.at[mine], self.part_ref.at[index], self.local_sem.at[index]
            )
            load.start()
            self.loads.append(load)
        self.mine = (0, 1, 2, 3)

    def first(self):
        for load in self.loads:
            load.wait()
        self.far()
        self.near()


class Exchange:
    def __init__(self, in_ref, out_ref, local_sem, send, recv):
        self.in_ref, self.out_ref, self.local_sem = in_ref, out_ref, local_sem
        self.send, self.recv = send, recv
        z, x, y, c = place()
        self.me = slot(x, y, c)
        self.copies = []

    def start(self, piece, part):
        z = lax.axis_index("shard")
        own = pltpu.make_async_copy(
            self.in_ref.at[self.me, part], self.out_ref.at[self.me, part], self.local_sem.at[piece]
        )
        own.start()
        self.copies.append(own)
        for index, spot in enumerate(plane_spots()):
            copy = remote_copy(
                self.in_ref.at[slot(*spot), part],
                self.out_ref.at[self.me, part],
                self.send.at[piece, index],
                self.recv.at[piece, index],
                device(z, *spot),
            )
            copy.start()
            self.copies.append(copy)

    def finish(self, piece=None):
        copies = self.copies if piece is None else self.copies[8 * piece : 8 * piece + 8]
        for copy in copies:
            copy.wait()


ANY = pl.BlockSpec(memory_space=pl.ANY)
IN_VMEM = pl.BlockSpec(memory_space=pltpu.VMEM)


def call(kernel, name, outs, out_specs, in_specs, scratch, ident, micros):
    return pl.pallas_call(
        kernel,
        out_shape=outs,
        in_specs=in_specs,
        out_specs=out_specs,
        scratch_shapes=scratch,
        name=name,
        cost_estimate=pl.CostEstimate(
            flops=micros * 10**9, bytes_accessed=micros * 10**6, transcendentals=0
        ),
        compiler_params=pltpu.CompilerParams(
            collective_id=ident, has_side_effects=True, vmem_limit_bytes=VMEM_LIMIT
        ),
    )


def shape(*dims, dtype=BF):
    return jax.ShapeDtypeStruct(dims, dtype)


def gather_scratch():
    return [
        pltpu.SemaphoreType.DMA,
        pltpu.SemaphoreType.DMA((9,)),
        pltpu.SemaphoreType.DMA((9,)),
    ]


def gather_kernel(count, *refs):
    enter(neighbours())
    jobs = []
    for index in range(count):
        scratch = refs[2 * count + 3 * index : 2 * count + 3 * index + 3]
        jobs.append(Gather(refs[index], refs[count + index], *scratch))
    for job in jobs:
        job.start()
    for job in jobs:
        job.relay_y()
        job.relay_x()
    for job in jobs:
        job.relay_far()
    for job in jobs:
        job.finish()


def plane_gather(arrays, ident, micros):
    count = len(arrays)
    outs = tuple(shape(8, *values.shape, dtype=values.dtype) for values in arrays)
    kernel = partial(gather_kernel, count)
    scratch = gather_scratch() * count
    any_space = [ANY] * count
    return call(kernel, "plane_gather", outs, tuple(any_space), any_space, scratch, ident, micros)(
        *arrays
    )


def scatter_kernel(in_ref, out_ref, *scratch):
    enter(neighbours())
    job = LoadedScatter(in_ref, *scratch)
    job.start()
    job.first()
    job.second()
    out_ref[...] = job.total()
    job.finish()


def plane_scatter(values, ident, micros):
    _, rows, columns = values.shape
    outs = shape(rows, columns, dtype=F32)
    scratch = LoadedScatter.scratch(rows, columns)
    return call(
        scatter_kernel, "plane_scatter", outs, IN_VMEM, [ANY], scratch, ident, micros
    )(values)


def feed_kernel(
    own_ref, grad_ref, up_ref, down_ref,
    normed_out, branch_out, up_out, down_out,
    rows_ref, grads_ref, hidden_ref, slope_ref, part_a, part_b,
    load_sem, g_local, g_send, g_recv, *scratch,
):
    enter(neighbours())
    gather = Gather(own_ref, rows_ref, g_local, g_send, g_recv)
    gather.start()
    blocks, _, width = rows_ref.shape
    loads = []
    for block in range(blocks):
        load = pltpu.make_async_copy(grad_ref.at[block], grads_ref.at[block], load_sem.at[block])
        load.start()
        loads.append(load)
    for load in loads:
        load.wait()

    def early(block, carry):
        slope_ref[block] = nn(grads_ref[block], down_ref[...]).astype(BF)
        return carry

    lax.fori_loop(0, blocks, early, 0)

    def middle(block):
        before = nn(rows_ref[block], up_ref[...])
        share = 0.5 + 0.5 * lax.erf(before * (0.5**0.5))
        hidden_ref[block] = (before * share).astype(BF)
        slope = share + before * (jnp.exp(-0.5 * before * before) * (2.0 * jnp.pi) ** (-0.5))
        slope = (slope_ref[block].astype(F32) * slope).astype(BF)
        slope_ref[block] = slope
        part_a[block] = nt(slope, up_ref[...]).astype(BF)

    size = len(scratch) // 2
    first = Scatter(part_a, *scratch[:size])
    other = Scatter(part_b, *scratch[size:])
    x, y, c = gather.spot

    def pair(cx, cy):
        def one(index, carry):
            middle(slot(cx, cy, 0) + index)
            return carry

        lax.fori_loop(0, 2, one, 0)

    gather.own.wait()
    gather.arrived(2, slot(x, y, 1 - c), 0, gather.rows)
    pair(x, y)
    first.pass_core(3)
    gather.relay_y()
    gather.relay_x()
    gather.arrived(6, slot(1 - x, y, 1 - c), 0, gather.rows)
    pair(1 - x, y)
    first.pass_core(1)
    gather.arrived(5, slot(x, 1 - y, 1 - c), 0, gather.rows)
    pair(x, 1 - y)
    first.pass_core(2)
    gather.relay_far()
    first.near()
    gather.arrived(7, slot(1 - x, 1 - y, 1 - c), 0, gather.rows // 2)
    gather.arrived(8, slot(1 - x, 1 - y, 1 - c), gather.rows // 2, gather.rows // 2)
    pair(1 - x, 1 - y)
    first.pass_core(0)
    first.far()
    for copy in gather.sends:
        copy.wait_send()

    def branch(block, carry):
        part_b[block] = nt(hidden_ref[block], down_ref[...]).astype(BF)
        return carry

    lax.fori_loop(0, blocks, branch, 0)
    for index in range(4):
        other.pass_core(index)
    first.second()
    other.far()
    other.near()
    tile = 256
    hidden_width = hidden_ref.shape[2]

    def weight(left_ref, right_ref, out_ref):
        def one(index, carry):
            lanes = pl.ds(pl.multiple_of(index * tile, tile), tile)
            left = left_ref[:, :, lanes].reshape(-1, tile)
            right = right_ref[...].reshape(-1, hidden_width)
            out_ref[lanes, :] = lax.dot_general(
                left, right, (((0,), (0,)), ((), ())), preferred_element_type=F32
            ).astype(BF)
            return carry

        lax.fori_loop(0, width // tile, one, 0)

    weight(grads_ref, hidden_ref, down_out)
    normed_out[...] = first.total()
    other.second()
    weight(rows_ref, slope_ref, up_out)
    branch_out[...] = other.total()
    first.finish()
    other.finish()


def feed_forward(own, grads, w_up, w_down, ident):
    rows, width = own.shape
    hidden = w_up.shape[1]
    outs = (
        shape(rows, width, dtype=F32),
        shape(rows, width, dtype=F32),
        shape(width, hidden),
        shape(width, hidden),
    )
    scratch = [
        pltpu.VMEM((8, rows, width), BF),
        pltpu.VMEM((8, rows, width), BF),
        pltpu.VMEM((8, rows, hidden), BF),
        pltpu.VMEM((8, rows, hidden), BF),
        pltpu.VMEM((8, rows, width), BF),
        pltpu.VMEM((8, rows, width), BF),
        pltpu.SemaphoreType.DMA((8,)),
    ]
    return call(
        feed_kernel,
        "feed_forward",
        outs,
        (IN_VMEM,) * 4,
        [ANY, ANY, IN_VMEM, IN_VMEM],
        scratch + gather_scratch() + Scatter.scratch(rows, width) * 2,
        ident,
        90,
    )(own, grads, w_up, w_down)


SIDE = 256


def nt(left, right):
    return lax.dot_general(left, right, (((1,), (1,)), ((), ())), preferred_element_type=F32)


def nn(left, right):
    return lax.dot_general(left, right, (((1,), (0,)), ((), ())), preferred_element_type=F32)


def turn(values):
    return jnp.transpose(values.astype(F32))


def causal(scores):
    keys = lax.broadcasted_iota(jnp.int32, scores.shape, 0)
    queries = lax.broadcasted_iota(jnp.int32, scores.shape, 1)
    return jnp.where(keys <= queries, scores, MASKED)


def forward_kernel(
    rows_ref, w_ref, cot_ref,
    qkv_ref, log_ref, mix_ref, mine_ref, cot_out,
    ex_local, ex_send, ex_recv, g_local, g_send, g_recv,
):
    enter(plane_others())
    side = Gather(cot_ref, cot_out, g_local, g_send, g_recv)
    side.start()
    blocks, both, _ = rows_ref.shape
    rows = both // 2
    width = mix_ref.shape[2]
    heads = width // HEAD_DIM
    length = blocks * rows
    step = SIDE // rows

    def project(block, carry):
        qkv_ref[block] = nn(rows_ref[block], w_ref[...]).astype(BF)
        return carry

    lax.fori_loop(0, blocks, project, 0)
    exchange = Exchange(mix_ref, mine_ref, ex_local, ex_send, ex_recv)
    for clip in range(2):
        part = pl.ds(clip * rows, rows)
        for head in range(heads):
            lanes = [pl.ds(j * width + head * HEAD_DIM, HEAD_DIM) for j in range(3)]
            key = qkv_ref[:, part, lanes[1]].reshape(length, HEAD_DIM)
            value = turn(qkv_ref[:, part, lanes[2]].reshape(length, HEAD_DIM)).astype(BF)
            for index in range(length // SIDE):
                spots = pl.ds(index * step, step)
                query = qkv_ref[spots, part, lanes[0]].reshape(SIDE, HEAD_DIM)
                query = query * jnp.asarray(HEAD_DIM ** (-0.5), BF)
                start = index * SIDE
                last = causal(nt(key[start : start + SIDE], query))
                top = jnp.max(last, axis=0, keepdims=True)
                if index:
                    early = nt(key[:start], query)
                    top = jnp.maximum(top, jnp.max(early, axis=0, keepdims=True))
                last = jnp.exp(last - top)
                total = jnp.sum(last, axis=0, keepdims=True)
                mix = nn(value[:, start : start + SIDE], last.astype(BF))
                if index:
                    early = jnp.exp(early - top)
                    total += jnp.sum(early, axis=0, keepdims=True)
                    mix += nn(value[:, :start], early.astype(BF))
                mix = jnp.transpose(mix / total).astype(BF).reshape(step, rows, HEAD_DIM)
                mix_ref[spots, part, pl.ds(head * HEAD_DIM, HEAD_DIM)] = mix
                log_ref[pl.ds(clip * heads + head, 1), pl.ds(start, SIDE)] = top + jnp.log(total)
        exchange.start(clip, part)
        if clip == 0:
            side.relay_y()
            side.relay_x()
    side.relay_far()
    exchange.finish()
    side.finish()


def attend_forward(rows, weights, cotangent, ident):
    blocks, block, width = rows.shape
    columns = weights.shape[1] // 3
    heads = columns // HEAD_DIM
    return call(
        forward_kernel,
        "attend_forward",
        (
            shape(blocks, block, 3 * columns),
            shape(2 * heads, blocks * block // 2, dtype=F32),
            shape(blocks, block, columns),
            shape(blocks, block, columns),
            shape(blocks, block, width),
        ),
        (IN_VMEM, IN_VMEM, IN_VMEM, ANY, ANY),
        [IN_VMEM, IN_VMEM, ANY],
        [
            pltpu.SemaphoreType.DMA((2,)),
            pltpu.SemaphoreType.DMA((2, 7)),
            pltpu.SemaphoreType.DMA((2, 7)),
        ]
        + gather_scratch(),
        ident,
        45,
    )(rows, weights, cotangent)


def backward_kernel(
    grad_ref, qkv_ref, mix_ref, log_ref, side_ref, text_ref,
    out_ref, side_out, text_out,
    grad_all, query_turned, ex_local, ex_send, ex_recv, *scratch,
):
    enter(plane_others())
    exchange = Exchange(grad_ref, grad_all, ex_local, ex_send, ex_recv)
    blocks, both, width = mix_ref.shape
    rows = both // 2
    heads = width // HEAD_DIM
    length = blocks * rows
    step = SIDE // rows
    for clip in range(2):
        exchange.start(clip, pl.ds(clip * rows, rows))
    size = len(scratch) // 2
    text = LoadedScatter(text_ref, *scratch[size:])
    text.start()
    text.first()
    side = LoadedScatter(side_ref, *scratch[:size])
    side.start()
    side.first()
    for clip in range(2):
        exchange.finish(clip)
        part = pl.ds(clip * rows, rows)
        for head in range(heads):
            lanes = [pl.ds(j * width + head * HEAD_DIM, HEAD_DIM) for j in range(3)]
            query = qkv_ref[:, part, lanes[0]].reshape(length, HEAD_DIM)
            query = query * jnp.asarray(HEAD_DIM ** (-0.5), BF)
            key = qkv_ref[:, part, lanes[1]].reshape(length, HEAD_DIM)
            value = qkv_ref[:, part, lanes[2]].reshape(length, HEAD_DIM)
            key_turned = turn(key).astype(BF)
            here = pl.ds(head * HEAD_DIM, HEAD_DIM)
            grad = grad_all[:, part, here].reshape(length, HEAD_DIM)
            mixed = mix_ref[:, part, here].reshape(length, HEAD_DIM)
            inner = jnp.transpose(grad.astype(F32) * mixed.astype(F32))
            inner = jnp.sum(inner, axis=0, keepdims=True)
            logs = log_ref[pl.ds(clip * heads + head, 1), :]
            for index in range(length // SIDE):
                start = index * SIDE
                spots = pl.ds(index * step, step)
                k_part, v_part = key[start : start + SIDE], value[start : start + SIDE]
                scores = nt(k_part, query[start:])
                first = causal(scores[:, :SIDE])
                if start + SIDE < length:
                    scores = jnp.concatenate([first, scores[:, SIDE:]], axis=1)
                else:
                    scores = first
                weights = jnp.exp(scores - logs[:, start:])
                slopes = nt(v_part, grad[start:])
                slopes = (weights * (slopes - inner[:, start:])).astype(BF)
                grad_key = nn(slopes, query[start:]).astype(BF).reshape(step, rows, HEAD_DIM)
                grad_value = nn(weights.astype(BF), grad[start:]).astype(BF)
                out_ref[spots, part, lanes[1]] = grad_key
                out_ref[spots, part, lanes[2]] = grad_value.reshape(step, rows, HEAD_DIM)
                grad_query = nn(key_turned[:, start : start + SIDE], slopes)
                if index:
                    query_turned[:, start:] += grad_query
                else:
                    query_turned[...] = grad_query
            grad_query = jnp.transpose(query_turned[...]) * HEAD_DIM ** (-0.5)
            grad_query = grad_query.astype(BF).reshape(blocks, rows, HEAD_DIM)
            out_ref[:, part, lanes[0]] = grad_query
        if clip == 0:
            text.second()
            side.second()
    text_out[...] = text.total()
    side_out[...] = side.total().astype(BF)
    text.finish()
    side.finish()


def attend_backward(grad_mix, qkv, mix, logs, side, text, ident):
    blocks, block, columns = mix.shape
    _, rows, width = side.shape
    text_shape = text.shape[1:]
    return call(
        backward_kernel,
        "attend_backward",
        (shape(blocks, block, 3 * columns), shape(rows, width), shape(*text_shape, dtype=F32)),
        (IN_VMEM, IN_VMEM, IN_VMEM),
        [ANY, IN_VMEM, IN_VMEM, IN_VMEM, ANY, ANY],
        [
            pltpu.VMEM((blocks, block, columns), BF),
            pltpu.VMEM((HEAD_DIM, blocks * block // 2), F32),
            pltpu.SemaphoreType.DMA((2,)),
            pltpu.SemaphoreType.DMA((2, 7)),
            pltpu.SemaphoreType.DMA((2, 7)),
        ]
        + LoadedScatter.scratch(rows, width)
        + LoadedScatter.scratch(*text_shape),
        ident,
        75,
    )(grad_mix, qkv, mix, logs, side, text)


def last_kernel(
    part_ref, frames_ref, gain_ref, grad_ref, stats_ref, text_ref,
    out_ref, total_ref, text_out,
    mine, came, all_ref, st_send, st_recv, z_send, z_recv, *scratch,
):
    z = lax.axis_index("shard")
    shards = lax.axis_size("shard")
    others = [lax.rem(z + i, shards) for i in range(1, shards)]
    spot = place()[1:]
    enter(neighbours() + [device(other, *spot) for other in others])
    size = len(scratch) // 2
    text = LoadedScatter(text_ref, *scratch[size:])
    text.start()
    job = LoadedScatter(part_ref, *scratch[:size])
    job.start()
    inputs = frames_ref[...].astype(F32)
    average = jnp.mean(inputs, axis=-1, keepdims=True)
    centred = inputs - average
    rate = lax.rsqrt(jnp.mean(centred * centred, axis=-1, keepdims=True) + EPS)
    text.first()
    job.first()
    text.second()
    job.second()
    text_out[...] = text.total()
    grads = job.total()
    normed = centred * rate
    mine[0] = stats_ref[...]
    mine[0, 0:1] = jnp.sum(grads * normed, axis=0, keepdims=True)
    mine[0, 1:2] = jnp.sum(grads, axis=0, keepdims=True)
    sends = []
    for index, target in enumerate(reversed(neighbours())):
        copy = remote_copy(
            mine.at[index], came.at[index], st_send.at[index], st_recv.at[index], target
        )
        copy.start()
        sends.append(copy)
        if index == 0:
            scaled = grads * gain_ref[...]
            inner = jnp.mean(scaled * normed, axis=-1, keepdims=True)
            scaled = scaled - jnp.mean(scaled, axis=-1, keepdims=True) - normed * inner
            out_ref[...] = grad_ref[...] + rate * scaled
        copy.wait_recv()
        mine[index + 1] = mine[index] + came[index]
    for index, other in enumerate(others):
        copy = remote_copy(
            mine.at[3], all_ref.at[z], z_send.at[index], z_recv.at[index], device(other, *spot)
        )
        copy.start()
        sends.append(copy)
    all_ref[z] = mine[3]
    for copy in sends[3:]:
        copy.wait_recv()
    total = all_ref[0]
    for index in range(1, shards):
        total += all_ref[index]
    total_ref[...] = total
    for copy in sends:
        copy.wait_send()
    text.finish()
    job.finish()


def last_step(part, frames, gain, grad, stats, text, shards, ident):
    _, rows, width = part.shape
    return call(
        last_kernel,
        "last_step",
        (
            shape(rows, width, dtype=F32),
            shape(8, width, dtype=F32),
            shape(*text.shape[1:], dtype=F32),
        ),
        (IN_VMEM, IN_VMEM, IN_VMEM),
        [ANY, IN_VMEM, IN_VMEM, IN_VMEM, IN_VMEM, ANY],
        [
            pltpu.VMEM((4, 8, width), F32),
            pltpu.VMEM((3, 8, width), F32),
            pltpu.VMEM((shards, 8, width), F32),
            pltpu.SemaphoreType.DMA((3,)),
            pltpu.SemaphoreType.DMA((3,)),
            pltpu.SemaphoreType.DMA((shards - 1,)),
            pltpu.SemaphoreType.DMA((shards - 1,)),
        ]
        + LoadedScatter.scratch(rows, width)
        + LoadedScatter.scratch(*text.shape[1:]),
        ident,
        50,
    )(part, frames, gain, grad, stats, text)


def dots(spec, *operands):
    return jnp.einsum(spec, *operands, preferred_element_type=F32)


def layer_norm(inputs, scaling, offset):
    average = jnp.mean(inputs, axis=-1, keepdims=True)
    centred = inputs - average
    variance = jnp.mean(centred * centred, axis=-1, keepdims=True)
    return centred * lax.rsqrt(variance + EPS) * scaling + offset


def on_device(
    frames,
    text_states,
    cotangent,
    norm_gain,
    norm_bias,
    self_qkv,
    self_out,
    cross_qkv,
    cross_out,
    mlp_up,
    mlp_down,
):
    clips, rows, width = frames.shape
    context = lax.axis_index("context")
    depth = self_qkv.shape[1]
    slices = width // depth
    columns = self_qkv.shape[2] // 2
    heads = columns // HEAD_DIM
    block = clips * rows
    texts = text_states.shape[1]

    def half(weight):
        size = weight.shape[-1] // 2
        return lax.dynamic_slice_in_dim(weight, context * size, size, weight.ndim - 1)

    def over_shard(weight, tiled=True):
        return lax.all_gather(weight, "shard", axis=0, tiled=tiled)

    qkv_part = half(self_qkv)
    w_qkv = over_shard(jnp.concatenate([qkv_part[0], qkv_part[1], qkv_part[2]], axis=-1))
    cross_part = half(cross_qkv)
    side = jnp.stack(
        [half(self_out), cross_part[0], half(cross_out), cross_part[1], cross_part[2]]
    )
    w_side = over_shard(side.transpose(0, 2, 1), tiled=False).transpose(1, 2, 0, 3)
    w_side = w_side.reshape(5, columns, width)
    w_up = over_shard(half(mlp_up))
    w_down = over_shard(half(mlp_down))

    stream_zero = frames.astype(F32)
    norm_one = layer_norm(stream_zero, norm_gain[0], norm_bias[0])
    (all_one,) = plane_gather([norm_one.astype(BF).reshape(block, width)], 0, 33)
    flat_one = all_one.reshape(8 * block, width)
    qkv, self_log, mix, my_mix, all_grad = attend_forward(
        all_one, w_qkv, cotangent.reshape(block, width), 1
    )

    text_part = dots("cnd,ted->tcne", text_states, w_side[3:]).astype(BF)
    plane_w, text_all = plane_gather(
        [
            w_side[:3].reshape(3 * columns, width),
            text_part.reshape(2 * clips * texts, columns),
        ],
        2,
        65,
    )
    plane_w = plane_w.reshape(8, 3, columns, width)
    w_out, w_query, w_cross = plane_w[:, 0], plane_w[:, 1], plane_w[:, 2]
    branch_one = dots("bre,bed->rd", my_mix, w_out).reshape(clips, rows, width)
    stream_one = stream_zero + branch_one
    norm_two, norm_two_back = jax.vjp(layer_norm, stream_one, norm_gain[1], norm_bias[1])
    low_two = norm_two.astype(BF)
    cross_q = dots("cfd,bed->cfbe", low_two, w_query).astype(BF)
    text_all = text_all.reshape(8, 2, clips, texts, heads, HEAD_DIM)
    text_k, text_v = text_all[:, 0], text_all[:, 1]
    cross_q = cross_q.reshape(clips, rows, 8, heads, HEAD_DIM)
    scale = HEAD_DIM ** (-0.5)
    scores = dots("cfbhd,bcnhd->cbhfn", cross_q, text_k) * scale
    top = jnp.max(scores, axis=-1, keepdims=True)
    cross_full = jnp.exp(scores - top)
    cross_full = cross_full / jnp.sum(cross_full, axis=-1, keepdims=True)
    cross_probs = cross_full.astype(BF)
    cross_mix = dots("cbhfn,bcnhd->cfbhd", cross_probs, text_v).astype(BF)
    cross_mix = cross_mix.reshape(clips, rows, 8, columns)
    branch_two = dots("cfbe,bed->cfd", cross_mix, w_cross)
    stream_two = stream_one + branch_two

    norm_three, norm_three_back = jax.vjp(layer_norm, stream_two, norm_gain[2], norm_bias[2])
    grad_normed, branch_three, grad_up, grad_down = feed_forward(
        norm_three.astype(BF).reshape(block, width), all_grad, w_up, w_down, 4
    )
    branch_three = branch_three.reshape(clips, rows, width)
    stream_out = stream_two + branch_three
    squares = jnp.stack(
        [
            jnp.sum(stream_out * stream_out),
            jnp.sum(branch_one * branch_one),
            jnp.sum(branch_two * branch_two),
            jnp.sum(branch_three * branch_three),
        ]
    )

    def to_shard(part):
        return lax.psum_scatter(part.astype(BF), "shard", scatter_dimension=0, tiled=True)

    grad_down, grad_up = to_shard(grad_down), to_shard(grad_up)
    grad_inner, gain_three, shift_three = norm_three_back(grad_normed.reshape(clips, rows, width))
    grad_two = cotangent.astype(F32) + grad_inner

    grad_low = grad_two.astype(BF)
    grad_cross_mix = dots("cfd,bed->cfbe", grad_low, w_cross).astype(BF)
    w_grad_cross = dots("cfd,cfbe->bed", grad_low, cross_mix)
    grad_heads = grad_cross_mix.reshape(clips, rows, 8, heads, HEAD_DIM)
    cross_dp = dots("cfbhd,bcnhd->cbhfn", grad_heads, text_v)
    inner = jnp.sum(cross_full * cross_dp, axis=-1, keepdims=True)
    grad_scores = (cross_full * (cross_dp - inner)).astype(BF)
    grad_cq = (dots("cbhfn,bcnhd->cfbhd", grad_scores, text_k) * scale).astype(BF)
    grad_text_k = dots("cbhfn,cfbhd->bcnhd", grad_scores, cross_q) * scale
    grad_text_v = dots("cbhfn,cfbhd->bcnhd", cross_probs, grad_heads)
    grad_cq = grad_cq.reshape(clips, rows, 8, columns)
    w_grad_query = dots("cfd,cfbe->bed", low_two, grad_cq)
    grad_normed = dots("cfbe,bed->cfd", grad_cq, w_query)
    grad_inner, gain_two, shift_two = norm_two_back(grad_normed)
    grad_one = grad_two + grad_inner

    grad_low = grad_one.astype(BF).reshape(block, width)
    grad_mix = dots("rd,bed->bre", grad_low, w_out).astype(BF)
    w_grad_out = dots("rd,bre->bed", grad_low, my_mix)

    part_side = jnp.stack([w_grad_out, w_grad_query, w_grad_cross], axis=1).astype(BF)
    part_side = part_side.reshape(8, 3 * columns, width)
    text_grads = jnp.stack([grad_text_k, grad_text_v], axis=1).astype(BF)
    text_grads = text_grads.reshape(8, 2 * clips * texts, columns)
    grad_qkv, part_side, text_grads = attend_backward(
        grad_mix, qkv, mix, self_log, part_side, text_grads, 8
    )
    text_grads = text_grads.reshape(2, clips, texts, columns).astype(BF)
    w_grad_text = dots("cnd,tcne->ted", text_states, text_grads).astype(BF)
    part_side = jnp.concatenate([part_side, w_grad_text.reshape(2 * columns, width)], axis=0)
    part_side = part_side.reshape(5 * columns, slices, depth).transpose(1, 0, 2)
    grad_side = to_shard(part_side)
    grad_text = dots("tcne,ted->cnd", text_grads, w_side[3:])
    grad_text = grad_text.reshape(clips, 8, texts // 8, width).transpose(1, 0, 2, 3).astype(BF)
    grad_text = grad_text.reshape(8, clips * texts // 8, width)
    grad_qkv = grad_qkv.reshape(8 * block, 3 * columns)
    part_norm = dots("re,de->rd", grad_qkv, w_qkv).astype(BF)
    grad_w_qkv = to_shard(dots("rd,re->de", flat_one, grad_qkv))
    nothing = jnp.zeros((1, width), F32)
    stats = [nothing, nothing] + [
        v[None] for v in (gain_two, shift_two, gain_three, shift_three)
    ]
    stats.append(jnp.pad(squares, (0, width - 4))[None])
    grad_frames, totals, grad_text = last_step(
        part_norm.reshape(8, block, width),
        frames.reshape(block, width),
        norm_gain[0][None],
        grad_one.reshape(block, width),
        jnp.concatenate(stats + [nothing], axis=0),
        grad_text,
        lax.axis_size("shard"),
        11,
    )
    grad_frames = grad_frames.reshape(clips, rows, width)
    grad_text = grad_text.reshape(clips, texts // 8, width)

    grad_w_qkv, grad_side, totals = lax.optimization_barrier((grad_w_qkv, grad_side, totals))

    def whole(values):
        return lax.all_gather(values, "context", axis=values.ndim - 1, tiled=True).astype(F32)

    grad_up, grad_down = whole(grad_up), whole(grad_down)
    grad_self = jnp.stack([grad_w_qkv[:, j * columns : (j + 1) * columns] for j in range(3)])
    grad_side = grad_side.reshape(5, columns, depth).transpose(0, 2, 1)
    grad_all = whole(jnp.concatenate([grad_self, grad_side], axis=0))

    gains = jnp.stack([totals[0], totals[2], totals[4]])
    shifts = jnp.stack([totals[1], totals[3], totals[5]])
    squares = totals[6, :4]
    start = lax.axis_index("shard") * depth
    grad_gain = lax.dynamic_slice_in_dim(gains, start, depth, 1)
    grad_shift = lax.dynamic_slice_in_dim(shifts, start, depth, 1)
    entries = float(clips * rows * width * lax.axis_size(("shard",) + PLANE))
    return (
        stream_out.astype(BF),
        grad_frames,
        grad_text,
        grad_gain,
        grad_shift,
        grad_all[:3],
        grad_all[3],
        jnp.stack([grad_all[4], grad_all[6], grad_all[7]]),
        grad_all[5],
        grad_up,
        grad_down,
        jnp.sqrt(squares / entries),
    )


def solution(mesh):
    rows = P("shard", PLANE, None)
    stack = P(None, "shard", "tensor")
    flat = P("shard", "tensor")
    return jax.shard_map(
        on_device,
        mesh=mesh,
        in_specs=(rows, P("shard"), rows, P(), P(), stack, flat, stack, flat, flat, flat),
        out_specs=(
            (rows, rows, rows, P(None, "shard"), P(None, "shard"))
            + (stack, flat, stack, flat, flat, flat, P())
        ),
        check_vma=False,
    )
```

```python
from functools import partial

import jax
import jax.numpy as jnp
from jax import lax
from jax.experimental import pallas as pl
from jax.experimental.pallas import tpu as pltpu
from jax.sharding import PartitionSpec as P

HEAD_DIM = 64
EPS = 1e-05
MASKED = -1e30
MESH = pl.DeviceIdType.MESH
BF = jnp.bfloat16
F32 = jnp.float32
PLANE = ("context", "tensor")
VMEM_LIMIT = 60 * 2**20


def place():
    return (
        lax.axis_index("shard"),
        lax.axis_index("context"),
        lax.axis_index("tensor") // 2,
        lax.axis_index("tensor") % 2,
    )


def device(z, x, y, c):
    return (z, x, 2 * y + c)


def slot(x, y, c):
    return 4 * x + 2 * y + c


def neighbours():
    z, x, y, c = place()
    return [device(z, 1 - x, y, c), device(z, x, 1 - y, c), device(z, x, y, 1 - c)]


def plane_spots():
    z, x, y, c = place()
    steps = [(a, b, d) for a in range(2) for b in range(2) for d in range(2) if a + b + d]
    return [((x + a) % 2, (y + b) % 2, (c + d) % 2) for a, b, d in steps]


def plane_others():
    z = lax.axis_index("shard")
    return [device(z, *spot) for spot in plane_spots()]


def enter(targets):
    barrier = pltpu.get_barrier_semaphore()
    for target in targets:
        pl.semaphore_signal(barrier, inc=1, device_id=target, device_id_type=MESH)
    pl.semaphore_wait(barrier, len(targets))


def remote_copy(source, target_ref, send, recv, target):
    return pltpu.make_async_remote_copy(
        src_ref=source,
        dst_ref=target_ref,
        send_sem=send,
        recv_sem=recv,
        device_id=target,
        device_id_type=MESH,
    )


class Gather:
    semaphores = 9

    def __init__(self, in_ref, out_ref, local_sem, send, recv):
        z, x, y, c = place()
        self.in_ref, self.out_ref, self.local_sem = in_ref, out_ref, local_sem
        self.send, self.recv = send, recv
        self.spot = (x, y, c)
        self.to_x, self.to_y, self.to_c = neighbours()
        self.rows = in_ref.shape[0]
        self.sends = []

    def go(self, index, owner, start, size, target, source=None):
        there = self.out_ref.at[owner, pl.ds(start, size)]
        copy = remote_copy(
            there if source is None else source,
            there,
            self.send.at[index],
            self.recv.at[index],
            target,
        )
        copy.start()
        self.sends.append(copy)

    def arrived(self, index, owner, start, size):
        there = self.out_ref.at[owner, pl.ds(start, size)]
        remote_copy(
            there, there, self.send.at[index], self.recv.at[index], self.to_x
        ).wait_recv()

    def start(self):
        me = slot(*self.spot)
        self.own = pltpu.make_async_copy(self.in_ref, self.out_ref.at[me], self.local_sem)
        self.own.start()
        for index, target in enumerate((self.to_x, self.to_y, self.to_c)):
            self.go(index, me, 0, self.rows, target, self.in_ref)

    def relay_y(self):
        x, y, c = self.spot
        owner = slot(x, 1 - y, c)
        self.arrived(1, owner, 0, self.rows)
        self.go(3, owner, 0, self.rows // 2, self.to_x)
        self.go(5, owner, 0, self.rows, self.to_c)

    def relay_x(self):
        x, y, c = self.spot
        half = self.rows // 2
        owner = slot(1 - x, y, c)
        self.arrived(0, owner, 0, self.rows)
        self.go(4, owner, half, half, self.to_y)
        self.go(6, owner, 0, self.rows, self.to_c)

    def relay_far(self):
        x, y, c = self.spot
        half = self.rows // 2
        owner = slot(1 - x, 1 - y, c)
        self.arrived(3, owner, 0, half)
        self.go(7, owner, 0, half, self.to_c)
        self.arrived(4, owner, half, half)
        self.go(8, owner, half, half, self.to_c)

    def finish(self):
        x, y, c = self.spot
        half = self.rows // 2
        self.arrived(2, slot(x, y, 1 - c), 0, self.rows)
        self.arrived(5, slot(x, 1 - y, 1 - c), 0, self.rows)
        self.arrived(6, slot(1 - x, y, 1 - c), 0, self.rows)
        self.arrived(7, slot(1 - x, 1 - y, 1 - c), 0, half)
        self.arrived(8, slot(1 - x, 1 - y, 1 - c), half, half)
        self.own.wait()
        for copy in self.sends:
            copy.wait_send()

    def rest(self):
        self.relay_y()
        self.relay_x()
        self.relay_far()
        self.finish()


class Scatter:
    @staticmethod
    def scratch(rows, columns):
        return [
            pltpu.VMEM((4, rows, columns), BF),
            pltpu.VMEM((2, rows // 2, columns), BF),
            pltpu.VMEM((2, rows, columns), BF),
            pltpu.SemaphoreType.DMA((10,)),
            pltpu.SemaphoreType.DMA((10,)),
        ]

    def __init__(self, part_ref, core, relay, final, send, recv):
        self.part_ref, self.core, self.relay, self.final = part_ref, core, relay, final
        self.send, self.recv = send, recv
        self.to_x, self.to_y, self.to_c = neighbours()
        z, x, y, c = place()
        chips = ((1 - x, 1 - y), (1 - x, y), (x, 1 - y), (x, y))
        self.mine = [slot(*chip, c) for chip in chips]
        self.theirs = [slot(*chip, 1 - c) for chip in chips]
        rows = part_ref.shape[1]
        self.low, self.high = pl.ds(0, rows // 2), pl.ds(rows // 2, rows // 2)
        self.sends = []

    def forward(self, index, source, target_ref, target):
        copy = remote_copy(
            source, target_ref, self.send.at[index], self.recv.at[index], target
        )
        copy.start()
        self.sends.append(copy)

    def arrived(self, index, ref):
        remote_copy(ref, ref, self.send.at[index], self.recv.at[index], self.to_c).wait_recv()

    def pass_core(self, index):
        source = self.part_ref.at[self.theirs[index]]
        self.forward(index, source, self.core.at[index], self.to_c)

    def add(self, index, part, more=None):
        mine = self.mine[index]
        total = self.part_ref[mine, part].astype(F32) + self.core[index, part].astype(F32)
        if more is not None:
            total += more.astype(F32)
        self.part_ref[mine, part] = total.astype(BF)
        return self.part_ref.at[mine, part]

    def far(self):
        self.arrived(0, self.core.at[0])
        self.forward(4, self.add(0, self.low), self.relay.at[0], self.to_x)
        self.forward(5, self.add(0, self.high), self.relay.at[1], self.to_y)

    def near(self):
        self.arrived(1, self.core.at[1])
        self.forward(6, self.add(1, self.low), self.final.at[0, self.low], self.to_x)
        self.arrived(2, self.core.at[2])
        self.forward(7, self.add(2, self.high), self.final.at[1, self.high], self.to_y)

    def second(self):
        low, high, final, relay = self.low, self.high, self.final, self.relay
        self.arrived(5, relay.at[1])
        self.forward(8, self.add(1, high, relay[1]), final.at[0, high], self.to_x)
        self.arrived(4, relay.at[0])
        self.forward(9, self.add(2, low, relay[0]), final.at[1, low], self.to_y)

    def total(self):
        self.arrived(3, self.core.at[3])
        self.arrived(6, self.final.at[0, self.low])
        self.arrived(7, self.final.at[1, self.high])
        self.arrived(8, self.final.at[0, self.high])
        self.arrived(9, self.final.at[1, self.low])
        total = self.part_ref[self.mine[3]].astype(F32) + self.core[3].astype(F32)
        return total + self.final[0].astype(F32) + self.final[1].astype(F32)

    def finish(self):
        for copy in self.sends:
            copy.wait_send()


class LoadedScatter(Scatter):
    @staticmethod
    def scratch(rows, columns):
        return [
            pltpu.VMEM((4, rows, columns), BF),
            pltpu.SemaphoreType.DMA((4,)),
        ] + Scatter.scratch(rows, columns)

    def __init__(self, in_ref, part_ref, local_sem, *scratch):
        super().__init__(part_ref, *scratch)
        self.in_ref, self.local_sem = in_ref, local_sem

    def start(self):
        self.loads = []
        for index, (mine, theirs) in enumerate(zip(self.mine, self.theirs)):
            source = self.in_ref.at[theirs]
            self.forward(index, source, self.core.at[index], self.to_c)
            load = pltpu.make_async_copy(
                self.in_ref.at[mine], self.part_ref.at[index], self.local_sem.at[index]
            )
            load.start()
            self.loads.append(load)
        self.mine = (0, 1, 2, 3)

    def first(self):
        for load in self.loads:
            load.wait()
        self.far()
        self.near()


class Exchange:
    def __init__(self, in_ref, out_ref, local_sem, send, recv):
        self.in_ref, self.out_ref, self.local_sem = in_ref, out_ref, local_sem
        self.send, self.recv = send, recv
        z, x, y, c = place()
        self.me = slot(x, y, c)
        self.copies = []

    def start(self, piece, part):
        z = lax.axis_index("shard")
        own = pltpu.make_async_copy(
            self.in_ref.at[self.me, part], self.out_ref.at[self.me, part], self.local_sem.at[piece]
        )
        own.start()
        self.copies.append(own)
        for index, spot in enumerate(plane_spots()):
            copy = remote_copy(
                self.in_ref.at[slot(*spot), part],
                self.out_ref.at[self.me, part],
                self.send.at[piece, index],
                self.recv.at[piece, index],
                device(z, *spot),
            )
            copy.start()
            self.copies.append(copy)

    def finish(self, piece=None):
        copies = self.copies if piece is None else self.copies[8 * piece : 8 * piece + 8]
        for copy in copies:
            copy.wait()


ANY = pl.BlockSpec(memory_space=pl.ANY)
IN_VMEM = pl.BlockSpec(memory_space=pltpu.VMEM)


def call(kernel, name, outs, out_specs, in_specs, scratch, ident, micros):
    return pl.pallas_call(
        kernel,
        out_shape=outs,
        in_specs=in_specs,
        out_specs=out_specs,
        scratch_shapes=scratch,
        name=name,
        cost_estimate=pl.CostEstimate(
            flops=micros * 10**9, bytes_accessed=micros * 10**6, transcendentals=0
        ),
        compiler_params=pltpu.CompilerParams(
            collective_id=ident, has_side_effects=True, vmem_limit_bytes=VMEM_LIMIT
        ),
    )


def shape(*dims, dtype=BF):
    return jax.ShapeDtypeStruct(dims, dtype)


def gather_scratch():
    return [
        pltpu.SemaphoreType.DMA,
        pltpu.SemaphoreType.DMA((9,)),
        pltpu.SemaphoreType.DMA((9,)),
    ]


def gather_kernel(count, *refs):
    enter(neighbours())
    jobs = []
    for index in range(count):
        scratch = refs[2 * count + 3 * index : 2 * count + 3 * index + 3]
        jobs.append(Gather(refs[index], refs[count + index], *scratch))
    for job in jobs:
        job.start()
    for job in jobs:
        job.relay_y()
        job.relay_x()
    for job in jobs:
        job.relay_far()
    for job in jobs:
        job.finish()


def plane_gather(arrays, ident, micros):
    count = len(arrays)
    outs = tuple(shape(8, *values.shape, dtype=values.dtype) for values in arrays)
    kernel = partial(gather_kernel, count)
    scratch = gather_scratch() * count
    any_space = [ANY] * count
    return call(kernel, "plane_gather", outs, tuple(any_space), any_space, scratch, ident, micros)(
        *arrays
    )


def scatter_kernel(in_ref, out_ref, *scratch):
    enter(neighbours())
    job = LoadedScatter(in_ref, *scratch)
    job.start()
    job.first()
    job.second()
    out_ref[...] = job.total()
    job.finish()


def plane_scatter(values, ident, micros):
    _, rows, columns = values.shape
    outs = shape(rows, columns, dtype=F32)
    scratch = LoadedScatter.scratch(rows, columns)
    return call(
        scatter_kernel, "plane_scatter", outs, IN_VMEM, [ANY], scratch, ident, micros
    )(values)


def feed_kernel(
    own_ref, grad_ref, up_ref, down_ref,
    normed_out, branch_out, up_out, down_out,
    rows_ref, grads_ref, hidden_ref, slope_ref, part_a, part_b,
    load_sem, g_local, g_send, g_recv, *scratch,
):
    enter(neighbours())
    gather = Gather(own_ref, rows_ref, g_local, g_send, g_recv)
    gather.start()
    blocks, _, width = rows_ref.shape
    loads = []
    for block in range(blocks):
        load = pltpu.make_async_copy(grad_ref.at[block], grads_ref.at[block], load_sem.at[block])
        load.start()
        loads.append(load)
    for load in loads:
        load.wait()

    def early(block, carry):
        slope_ref[block] = nn(grads_ref[block], down_ref[...]).astype(BF)
        return carry

    lax.fori_loop(0, blocks, early, 0)

    def middle(block):
        before = nn(rows_ref[block], up_ref[...])
        share = 0.5 + 0.5 * lax.erf(before * (0.5**0.5))
        hidden_ref[block] = (before * share).astype(BF)
        slope = share + before * (jnp.exp(-0.5 * before * before) * (2.0 * jnp.pi) ** (-0.5))
        slope = (slope_ref[block].astype(F32) * slope).astype(BF)
        slope_ref[block] = slope
        part_a[block] = nt(slope, up_ref[...]).astype(BF)

    size = len(scratch) // 2
    first = Scatter(part_a, *scratch[:size])
    other = Scatter(part_b, *scratch[size:])
    x, y, c = gather.spot

    def pair(cx, cy):
        def one(index, carry):
            middle(slot(cx, cy, 0) + index)
            return carry

        lax.fori_loop(0, 2, one, 0)

    gather.own.wait()
    gather.arrived(2, slot(x, y, 1 - c), 0, gather.rows)
    pair(x, y)
    first.pass_core(3)
    gather.relay_y()
    gather.relay_x()
    gather.arrived(6, slot(1 - x, y, 1 - c), 0, gather.rows)
    pair(1 - x, y)
    first.pass_core(1)
    gather.arrived(5, slot(x, 1 - y, 1 - c), 0, gather.rows)
    pair(x, 1 - y)
    first.pass_core(2)
    gather.relay_far()
    first.near()
    gather.arrived(7, slot(1 - x, 1 - y, 1 - c), 0, gather.rows // 2)
    gather.arrived(8, slot(1 - x, 1 - y, 1 - c), gather.rows // 2, gather.rows // 2)
    pair(1 - x, 1 - y)
    first.pass_core(0)
    first.far()
    for copy in gather.sends:
        copy.wait_send()

    def branch(block, carry):
        part_b[block] = nt(hidden_ref[block], down_ref[...]).astype(BF)
        return carry

    lax.fori_loop(0, blocks, branch, 0)
    for index in range(4):
        other.pass_core(index)
    first.second()
    other.far()
    other.near()
    tile = 256
    hidden_width = hidden_ref.shape[2]

    def weight(left_ref, right_ref, out_ref):
        def one(index, carry):
            lanes = pl.ds(pl.multiple_of(index * tile, tile), tile)
            left = left_ref[:, :, lanes].reshape(-1, tile)
            right = right_ref[...].reshape(-1, hidden_width)
            out_ref[lanes, :] = lax.dot_general(
                left, right, (((0,), (0,)), ((), ())), preferred_element_type=F32
            ).astype(BF)
            return carry

        lax.fori_loop(0, width // tile, one, 0)

    weight(grads_ref, hidden_ref, down_out)
    normed_out[...] = first.total()
    other.second()
    weight(rows_ref, slope_ref, up_out)
    branch_out[...] = other.total()
    first.finish()
    other.finish()


def feed_forward(own, grads, w_up, w_down, ident):
    rows, width = own.shape
    hidden = w_up.shape[1]
    outs = (
        shape(rows, width, dtype=F32),
        shape(rows, width, dtype=F32),
        shape(width, hidden),
        shape(width, hidden),
    )
    scratch = [
        pltpu.VMEM((8, rows, width), BF),
        pltpu.VMEM((8, rows, width), BF),
        pltpu.VMEM((8, rows, hidden), BF),
        pltpu.VMEM((8, rows, hidden), BF),
        pltpu.VMEM((8, rows, width), BF),
        pltpu.VMEM((8, rows, width), BF),
        pltpu.SemaphoreType.DMA((8,)),
    ]
    return call(
        feed_kernel,
        "feed_forward",
        outs,
        (IN_VMEM,) * 4,
        [ANY, ANY, IN_VMEM, IN_VMEM],
        scratch + gather_scratch() + Scatter.scratch(rows, width) * 2,
        ident,
        90,
    )(own, grads, w_up, w_down)


SIDE = 256


def nt(left, right):
    return lax.dot_general(left, right, (((1,), (1,)), ((), ())), preferred_element_type=F32)


def nn(left, right):
    return lax.dot_general(left, right, (((1,), (0,)), ((), ())), preferred_element_type=F32)


def turn(values):
    return jnp.transpose(values.astype(F32))


def causal(scores):
    keys = lax.broadcasted_iota(jnp.int32, scores.shape, 0)
    queries = lax.broadcasted_iota(jnp.int32, scores.shape, 1)
    return jnp.where(keys <= queries, scores, MASKED)


def forward_kernel(
    rows_ref, w_ref, cot_ref,
    qkv_ref, log_ref, mix_ref, mine_ref, cot_out,
    ex_local, ex_send, ex_recv, g_local, g_send, g_recv,
):
    enter(plane_others())
    side = Gather(cot_ref, cot_out, g_local, g_send, g_recv)
    side.start()
    blocks, both, _ = rows_ref.shape
    rows = both // 2
    width = mix_ref.shape[2]
    heads = width // HEAD_DIM
    length = blocks * rows
    step = SIDE // rows

    def project(block, carry):
        qkv_ref[block] = nn(rows_ref[block], w_ref[...]).astype(BF)
        return carry

    lax.fori_loop(0, blocks, project, 0)
    exchange = Exchange(mix_ref, mine_ref, ex_local, ex_send, ex_recv)
    for clip in range(2):
        part = pl.ds(clip * rows, rows)
        for head in range(heads):
            lanes = [pl.ds(j * width + head * HEAD_DIM, HEAD_DIM) for j in range(3)]
            key = qkv_ref[:, part, lanes[1]].reshape(length, HEAD_DIM)
            value = turn(qkv_ref[:, part, lanes[2]].reshape(length, HEAD_DIM)).astype(BF)
            for index in range(length // SIDE):
                spots = pl.ds(index * step, step)
                query = qkv_ref[spots, part, lanes[0]].reshape(SIDE, HEAD_DIM)
                query = query * jnp.asarray(HEAD_DIM ** (-0.5), BF)
                start = index * SIDE
                last = causal(nt(key[start : start + SIDE], query))
                top = jnp.max(last, axis=0, keepdims=True)
                if index:
                    early = nt(key[:start], query)
                    top = jnp.maximum(top, jnp.max(early, axis=0, keepdims=True))
                last = jnp.exp(last - top)
                total = jnp.sum(last, axis=0, keepdims=True)
                mix = nn(value[:, start : start + SIDE], last.astype(BF))
                if index:
                    early = jnp.exp(early - top)
                    total += jnp.sum(early, axis=0, keepdims=True)
                    mix += nn(value[:, :start], early.astype(BF))
                mix = jnp.transpose(mix / total).astype(BF).reshape(step, rows, HEAD_DIM)
                mix_ref[spots, part, pl.ds(head * HEAD_DIM, HEAD_DIM)] = mix
                log_ref[pl.ds(clip * heads + head, 1), pl.ds(start, SIDE)] = top + jnp.log(total)
        exchange.start(clip, part)
        if clip == 0:
            side.relay_y()
            side.relay_x()
    side.relay_far()
    exchange.finish()
    side.finish()


def attend_forward(rows, weights, cotangent, ident):
    blocks, block, width = rows.shape
    columns = weights.shape[1] // 3
    heads = columns // HEAD_DIM
    return call(
        forward_kernel,
        "attend_forward",
        (
            shape(blocks, block, 3 * columns),
            shape(2 * heads, blocks * block // 2, dtype=F32),
            shape(blocks, block, columns),
            shape(blocks, block, columns),
            shape(blocks, block, width),
        ),
        (IN_VMEM, IN_VMEM, IN_VMEM, ANY, ANY),
        [IN_VMEM, IN_VMEM, ANY],
        [
            pltpu.SemaphoreType.DMA((2,)),
            pltpu.SemaphoreType.DMA((2, 7)),
            pltpu.SemaphoreType.DMA((2, 7)),
        ]
        + gather_scratch(),
        ident,
        45,
    )(rows, weights, cotangent)


def backward_kernel(
    grad_ref, qkv_ref, mix_ref, log_ref, side_ref, text_ref,
    out_ref, side_out, text_out,
    grad_all, query_turned, ex_local, ex_send, ex_recv, *scratch,
):
    enter(plane_others())
    exchange = Exchange(grad_ref, grad_all, ex_local, ex_send, ex_recv)
    blocks, both, width = mix_ref.shape
    rows = both // 2
    heads = width // HEAD_DIM
    length = blocks * rows
    step = SIDE // rows
    for clip in range(2):
        exchange.start(clip, pl.ds(clip * rows, rows))
    size = len(scratch) // 2
    text = LoadedScatter(text_ref, *scratch[size:])
    text.start()
    text.first()
    side = LoadedScatter(side_ref, *scratch[:size])
    side.start()
    side.first()
    for clip in range(2):
        exchange.finish(clip)
        part = pl.ds(clip * rows, rows)
        for head in range(heads):
            lanes = [pl.ds(j * width + head * HEAD_DIM, HEAD_DIM) for j in range(3)]
            query = qkv_ref[:, part, lanes[0]].reshape(length, HEAD_DIM)
            query = query * jnp.asarray(HEAD_DIM ** (-0.5), BF)
            key = qkv_ref[:, part, lanes[1]].reshape(length, HEAD_DIM)
            value = qkv_ref[:, part, lanes[2]].reshape(length, HEAD_DIM)
            key_turned = turn(key).astype(BF)
            here = pl.ds(head * HEAD_DIM, HEAD_DIM)
            grad = grad_all[:, part, here].reshape(length, HEAD_DIM)
            mixed = mix_ref[:, part, here].reshape(length, HEAD_DIM)
            inner = jnp.transpose(grad.astype(F32) * mixed.astype(F32))
            inner = jnp.sum(inner, axis=0, keepdims=True)
            logs = log_ref[pl.ds(clip * heads + head, 1), :]
            for index in range(length // SIDE):
                start = index * SIDE
                spots = pl.ds(index * step, step)
                k_part, v_part = key[start : start + SIDE], value[start : start + SIDE]
                scores = nt(k_part, query[start:])
                first = causal(scores[:, :SIDE])
                if start + SIDE < length:
                    scores = jnp.concatenate([first, scores[:, SIDE:]], axis=1)
                else:
                    scores = first
                weights = jnp.exp(scores - logs[:, start:])
                slopes = nt(v_part, grad[start:])
                slopes = (weights * (slopes - inner[:, start:])).astype(BF)
                grad_key = nn(slopes, query[start:]).astype(BF).reshape(step, rows, HEAD_DIM)
                grad_value = nn(weights.astype(BF), grad[start:]).astype(BF)
                out_ref[spots, part, lanes[1]] = grad_key
                out_ref[spots, part, lanes[2]] = grad_value.reshape(step, rows, HEAD_DIM)
                grad_query = nn(key_turned[:, start : start + SIDE], slopes)
                if index:
                    query_turned[:, start:] += grad_query
                else:
                    query_turned[...] = grad_query
            grad_query = jnp.transpose(query_turned[...]) * HEAD_DIM ** (-0.5)
            grad_query = grad_query.astype(BF).reshape(blocks, rows, HEAD_DIM)
            out_ref[:, part, lanes[0]] = grad_query
        if clip == 0:
            text.second()
            side.second()
    text_out[...] = text.total()
    side_out[...] = side.total().astype(BF)
    text.finish()
    side.finish()


def attend_backward(grad_mix, qkv, mix, logs, side, text, ident):
    blocks, block, columns = mix.shape
    _, rows, width = side.shape
    text_shape = text.shape[1:]
    return call(
        backward_kernel,
        "attend_backward",
        (shape(blocks, block, 3 * columns), shape(rows, width), shape(*text_shape, dtype=F32)),
        (IN_VMEM, IN_VMEM, IN_VMEM),
        [ANY, IN_VMEM, IN_VMEM, IN_VMEM, ANY, ANY],
        [
            pltpu.VMEM((blocks, block, columns), BF),
            pltpu.VMEM((HEAD_DIM, blocks * block // 2), F32),
            pltpu.SemaphoreType.DMA((2,)),
            pltpu.SemaphoreType.DMA((2, 7)),
            pltpu.SemaphoreType.DMA((2, 7)),
        ]
        + LoadedScatter.scratch(rows, width)
        + LoadedScatter.scratch(*text_shape),
        ident,
        75,
    )(grad_mix, qkv, mix, logs, side, text)


def last_kernel(
    part_ref, frames_ref, gain_ref, grad_ref, stats_ref, text_ref, qkv_ref, up_ref, down_ref,
    out_ref, total_ref, text_out, qkv_out, up_out, down_out,
    mine, came, all_ref, st_send, st_recv, z_send, z_recv,
    qkv_came, qkv_pair, up_pair, down_pair, q_send, q_recv, x_send, x_recv, *scratch,
):
    z = lax.axis_index("shard")
    shards = lax.axis_size("shard")
    others = [lax.rem(z + i, shards) for i in range(1, shards)]
    spot = place()[1:]
    context = spot[0]
    enter(neighbours() + [device(other, *spot) for other in others])
    size = len(scratch) // 2
    text = LoadedScatter(text_ref, *scratch[size:])
    text.start()
    job = LoadedScatter(part_ref, *scratch[:size])
    job.start()
    sends, moves = [], []
    for index, other in enumerate(others):
        copy = remote_copy(
            qkv_ref.at[other], qkv_came.at[index], q_send.at[index], q_recv.at[index],
            device(other, *spot),
        )
        copy.start()
        moves.append(copy)
    inputs = frames_ref[...].astype(F32)
    average = jnp.mean(inputs, axis=-1, keepdims=True)
    centred = inputs - average
    rate = lax.rsqrt(jnp.mean(centred * centred, axis=-1, keepdims=True) + EPS)
    text.first()
    job.first()
    text.second()
    job.second()
    to_x = neighbours()[0]
    pairs = []
    for index, (source, pair_ref) in enumerate(((up_ref, up_pair), (down_ref, down_pair))):
        copy = remote_copy(source, pair_ref, x_send.at[index], x_recv.at[index], to_x)
        copy.start()
        pairs.append(copy)
    text_out[...] = text.total()
    grads = job.total()
    normed = centred * rate
    mine[0] = stats_ref[...]
    mine[0, 0:1] = jnp.sum(grads * normed, axis=0, keepdims=True)
    mine[0, 1:2] = jnp.sum(grads, axis=0, keepdims=True)
    for index, target in enumerate(reversed(neighbours())):
        copy = remote_copy(
            mine.at[index], came.at[index], st_send.at[index], st_recv.at[index], target
        )
        copy.start()
        sends.append(copy)
        if index == 0:
            scaled = grads * gain_ref[...]
            inner = jnp.mean(scaled * normed, axis=-1, keepdims=True)
            scaled = scaled - jnp.mean(scaled, axis=-1, keepdims=True) - normed * inner
            out_ref[...] = grad_ref[...] + rate * scaled
        copy.wait_recv()
        mine[index + 1] = mine[index] + came[index]
    for index, other in enumerate(others):
        copy = remote_copy(
            mine.at[3], all_ref.at[z], z_send.at[index], z_recv.at[index], device(other, *spot)
        )
        copy.start()
        sends.append(copy)
    all_ref[z] = mine[3]
    total = qkv_ref[z].astype(F32)
    for index, copy in enumerate(moves):
        copy.wait_recv()
        total += qkv_came[index].astype(F32)
    qkv_pair[0] = total.astype(BF)
    copy = remote_copy(qkv_pair.at[0], qkv_pair.at[1], x_send.at[2], x_recv.at[2], to_x)
    copy.start()
    pairs.append(copy)
    for copy in sends[3:]:
        copy.wait_recv()
    total = all_ref[0]
    for index in range(1, shards):
        total += all_ref[index]
    total_ref[...] = total
    half = up_ref.shape[1]
    ours = pl.ds(pl.multiple_of(context * half, half), half)
    theirs = pl.ds(pl.multiple_of((1 - context) * half, half), half)
    for copy, source, pair_ref, target in (
        (pairs[0], up_ref, up_pair, up_out),
        (pairs[1], down_ref, down_pair, down_out),
    ):
        target[:, ours] = source[...].astype(F32)
        copy.wait_recv()
        target[:, theirs] = pair_ref[...].astype(F32)
    pairs[2].wait_recv()
    lead = jnp.where(context == 0, qkv_pair[0], qkv_pair[1]).astype(F32)
    trail = jnp.where(context == 0, qkv_pair[1], qkv_pair[0]).astype(F32)
    width = lead.shape[1] // 3
    for index in range(3):
        lanes = slice(index * width, (index + 1) * width)
        qkv_out[index, :, :width] = lead[:, lanes]
        qkv_out[index, :, width:] = trail[:, lanes]
    for copy in sends + moves + pairs:
        copy.wait_send()
    text.finish()
    job.finish()


def last_step(part, frames, gain, grad, stats, text, qkv, up, down, shards, ident):
    _, rows, width = part.shape
    depth, half = up.shape
    columns = qkv.shape[2]
    return call(
        last_kernel,
        "last_step",
        (
            shape(rows, width, dtype=F32),
            shape(8, width, dtype=F32),
            shape(*text.shape[1:], dtype=F32),
            shape(3, depth, 2 * columns // 3, dtype=F32),
            shape(depth, 2 * half, dtype=F32),
            shape(depth, 2 * half, dtype=F32),
        ),
        (IN_VMEM,) * 6,
        [ANY] + [IN_VMEM] * 4 + [ANY] + [IN_VMEM] * 3,
        [
            pltpu.VMEM((4, 8, width), F32),
            pltpu.VMEM((3, 8, width), F32),
            pltpu.VMEM((shards, 8, width), F32),
            pltpu.SemaphoreType.DMA((3,)),
            pltpu.SemaphoreType.DMA((3,)),
            pltpu.SemaphoreType.DMA((shards - 1,)),
            pltpu.SemaphoreType.DMA((shards - 1,)),
            pltpu.VMEM((shards - 1, depth, columns), BF),
            pltpu.VMEM((2, depth, columns), BF),
            pltpu.VMEM((depth, half), BF),
            pltpu.VMEM((depth, half), BF),
            pltpu.SemaphoreType.DMA((shards - 1,)),
            pltpu.SemaphoreType.DMA((shards - 1,)),
            pltpu.SemaphoreType.DMA((3,)),
            pltpu.SemaphoreType.DMA((3,)),
        ]
        + LoadedScatter.scratch(rows, width)
        + LoadedScatter.scratch(*text.shape[1:]),
        ident,
        65,
    )(part, frames, gain, grad, stats, text, qkv, up, down)


def dots(spec, *operands):
    return jnp.einsum(spec, *operands, preferred_element_type=F32)


def layer_norm(inputs, scaling, offset):
    average = jnp.mean(inputs, axis=-1, keepdims=True)
    centred = inputs - average
    variance = jnp.mean(centred * centred, axis=-1, keepdims=True)
    return centred * lax.rsqrt(variance + EPS) * scaling + offset


def on_device(
    frames,
    text_states,
    cotangent,
    norm_gain,
    norm_bias,
    self_qkv,
    self_out,
    cross_qkv,
    cross_out,
    mlp_up,
    mlp_down,
):
    clips, rows, width = frames.shape
    context = lax.axis_index("context")
    depth = self_qkv.shape[1]
    slices = width // depth
    columns = self_qkv.shape[2] // 2
    heads = columns // HEAD_DIM
    block = clips * rows
    texts = text_states.shape[1]

    def half(weight):
        size = weight.shape[-1] // 2
        return lax.dynamic_slice_in_dim(weight, context * size, size, weight.ndim - 1)

    def over_shard(weight, tiled=True):
        return lax.all_gather(weight, "shard", axis=0, tiled=tiled)

    qkv_part = half(self_qkv)
    w_qkv = over_shard(jnp.concatenate([qkv_part[0], qkv_part[1], qkv_part[2]], axis=-1))
    cross_part = half(cross_qkv)
    side = jnp.stack(
        [half(self_out), cross_part[0], half(cross_out), cross_part[1], cross_part[2]]
    )
    w_side = over_shard(side.transpose(0, 2, 1), tiled=False).transpose(1, 2, 0, 3)
    w_side = w_side.reshape(5, columns, width)
    w_up = over_shard(half(mlp_up))
    w_down = over_shard(half(mlp_down))

    stream_zero = frames.astype(F32)
    norm_one = layer_norm(stream_zero, norm_gain[0], norm_bias[0])
    (all_one,) = plane_gather([norm_one.astype(BF).reshape(block, width)], 0, 33)
    flat_one = all_one.reshape(8 * block, width)
    qkv, self_log, mix, my_mix, all_grad = attend_forward(
        all_one, w_qkv, cotangent.reshape(block, width), 1
    )

    text_part = dots("cnd,ted->tcne", text_states, w_side[3:]).astype(BF)
    plane_w, text_all = plane_gather(
        [
            w_side[:3].reshape(3 * columns, width),
            text_part.reshape(2 * clips * texts, columns),
        ],
        2,
        65,
    )
    plane_w = plane_w.reshape(8, 3, columns, width)
    w_out, w_query, w_cross = plane_w[:, 0], plane_w[:, 1], plane_w[:, 2]
    branch_one = dots("bre,bed->rd", my_mix, w_out).reshape(clips, rows, width)
    stream_one = stream_zero + branch_one
    norm_two, norm_two_back = jax.vjp(layer_norm, stream_one, norm_gain[1], norm_bias[1])
    low_two = norm_two.astype(BF)
    cross_q = dots("cfd,bed->cfbe", low_two, w_query).astype(BF)
    text_all = text_all.reshape(8, 2, clips, texts, heads, HEAD_DIM)
    text_k, text_v = text_all[:, 0], text_all[:, 1]
    cross_q = cross_q.reshape(clips, rows, 8, heads, HEAD_DIM)
    scale = HEAD_DIM ** (-0.5)
    scores = dots("cfbhd,bcnhd->cbhfn", cross_q, text_k) * scale
    top = jnp.max(scores, axis=-1, keepdims=True)
    cross_full = jnp.exp(scores - top)
    cross_full = cross_full / jnp.sum(cross_full, axis=-1, keepdims=True)
    cross_probs = cross_full.astype(BF)
    cross_mix = dots("cbhfn,bcnhd->cfbhd", cross_probs, text_v).astype(BF)
    cross_mix = cross_mix.reshape(clips, rows, 8, columns)
    branch_two = dots("cfbe,bed->cfd", cross_mix, w_cross)
    stream_two = stream_one + branch_two

    norm_three, norm_three_back = jax.vjp(layer_norm, stream_two, norm_gain[2], norm_bias[2])
    grad_normed, branch_three, grad_up, grad_down = feed_forward(
        norm_three.astype(BF).reshape(block, width), all_grad, w_up, w_down, 4
    )
    branch_three = branch_three.reshape(clips, rows, width)
    stream_out = stream_two + branch_three
    squares = jnp.stack(
        [
            jnp.sum(stream_out * stream_out),
            jnp.sum(branch_one * branch_one),
            jnp.sum(branch_two * branch_two),
            jnp.sum(branch_three * branch_three),
        ]
    )

    def to_shard(part):
        return lax.psum_scatter(part.astype(BF), "shard", scatter_dimension=0, tiled=True)

    grad_down, grad_up = to_shard(grad_down), to_shard(grad_up)
    grad_inner, gain_three, shift_three = norm_three_back(grad_normed.reshape(clips, rows, width))
    grad_two = cotangent.astype(F32) + grad_inner

    grad_low = grad_two.astype(BF)
    grad_cross_mix = dots("cfd,bed->cfbe", grad_low, w_cross).astype(BF)
    w_grad_cross = dots("cfd,cfbe->bed", grad_low, cross_mix)
    grad_heads = grad_cross_mix.reshape(clips, rows, 8, heads, HEAD_DIM)
    cross_dp = dots("cfbhd,bcnhd->cbhfn", grad_heads, text_v)
    inner = jnp.sum(cross_full * cross_dp, axis=-1, keepdims=True)
    grad_scores = (cross_full * (cross_dp - inner)).astype(BF)
    grad_cq = (dots("cbhfn,bcnhd->cfbhd", grad_scores, text_k) * scale).astype(BF)
    grad_text_k = dots("cbhfn,cfbhd->bcnhd", grad_scores, cross_q) * scale
    grad_text_v = dots("cbhfn,cfbhd->bcnhd", cross_probs, grad_heads)
    grad_cq = grad_cq.reshape(clips, rows, 8, columns)
    w_grad_query = dots("cfd,cfbe->bed", low_two, grad_cq)
    grad_normed = dots("cfbe,bed->cfd", grad_cq, w_query)
    grad_inner, gain_two, shift_two = norm_two_back(grad_normed)
    grad_one = grad_two + grad_inner

    grad_low = grad_one.astype(BF).reshape(block, width)
    grad_mix = dots("rd,bed->bre", grad_low, w_out).astype(BF)
    w_grad_out = dots("rd,bre->bed", grad_low, my_mix)

    part_side = jnp.stack([w_grad_out, w_grad_query, w_grad_cross], axis=1).astype(BF)
    part_side = part_side.reshape(8, 3 * columns, width)
    text_grads = jnp.stack([grad_text_k, grad_text_v], axis=1).astype(BF)
    text_grads = text_grads.reshape(8, 2 * clips * texts, columns)
    grad_qkv, part_side, text_grads = attend_backward(
        grad_mix, qkv, mix, self_log, part_side, text_grads, 8
    )
    grad_qkv, part_side, text_grads, grad_down, grad_up = lax.optimization_barrier(
        (grad_qkv, part_side, text_grads, grad_down, grad_up)
    )
    text_grads = text_grads.reshape(2, clips, texts, columns).astype(BF)
    w_grad_text = dots("cnd,tcne->ted", text_states, text_grads).astype(BF)
    part_side = jnp.concatenate([part_side, w_grad_text.reshape(2 * columns, width)], axis=0)
    part_side = part_side.reshape(5 * columns, slices, depth).transpose(1, 0, 2)
    grad_side = to_shard(part_side)
    grad_text = dots("tcne,ted->cnd", text_grads, w_side[3:])
    grad_text = grad_text.reshape(clips, 8, texts // 8, width).transpose(1, 0, 2, 3).astype(BF)
    grad_text = grad_text.reshape(8, clips * texts // 8, width)
    grad_qkv = grad_qkv.reshape(8 * block, 3 * columns)
    part_norm = dots("re,de->rd", grad_qkv, w_qkv).astype(BF)
    grad_w_qkv = dots("rd,re->de", flat_one, grad_qkv).astype(BF)
    nothing = jnp.zeros((1, width), F32)
    stats = [nothing, nothing] + [
        v[None] for v in (gain_two, shift_two, gain_three, shift_three)
    ]
    stats.append(jnp.pad(squares, (0, width - 4))[None])
    grad_frames, totals, grad_text, grad_w_qkv, grad_up, grad_down = last_step(
        part_norm.reshape(8, block, width),
        frames.reshape(block, width),
        norm_gain[0][None],
        grad_one.reshape(block, width),
        jnp.concatenate(stats + [nothing], axis=0),
        grad_text,
        grad_w_qkv.reshape(slices, depth, 3 * columns),
        grad_up,
        grad_down,
        slices,
        11,
    )
    grad_frames = grad_frames.reshape(clips, rows, width)
    grad_text = grad_text.reshape(clips, texts // 8, width)

    grad_side, totals = lax.optimization_barrier((grad_side, totals))

    def whole(values):
        return lax.all_gather(values, "context", axis=1, tiled=True)

    grad_side = whole(grad_side.reshape(5, columns, depth)).astype(F32).transpose(0, 2, 1)
    gains = jnp.stack([totals[0], totals[2], totals[4]])
    shifts = jnp.stack([totals[1], totals[3], totals[5]])
    squares = totals[6, :4]
    start = lax.axis_index("shard") * depth
    grad_gain = lax.dynamic_slice_in_dim(gains, start, depth, 1)
    grad_shift = lax.dynamic_slice_in_dim(shifts, start, depth, 1)
    entries = float(clips * rows * width * lax.axis_size(("shard",) + PLANE))
    return (
        stream_out.astype(BF),
        grad_frames,
        grad_text,
        grad_gain,
        grad_shift,
        grad_w_qkv,
        grad_side[0],
        jnp.stack([grad_side[1], grad_side[3], grad_side[4]]),
        grad_side[2],
        grad_up,
        grad_down,
        jnp.sqrt(squares / entries),
    )


def solution(mesh):
    rows = P("shard", PLANE, None)
    stack = P(None, "shard", "tensor")
    flat = P("shard", "tensor")
    return jax.shard_map(
        on_device,
        mesh=mesh,
        in_specs=(rows, P("shard"), rows, P(), P(), stack, flat, stack, flat, flat, flat),
        out_specs=(
            (rows, rows, rows, P(None, "shard"), P(None, "shard"))
            + (stack, flat, stack, flat, flat, flat, P())
        ),
        check_vma=False,
    )
```

```python
from functools import partial

import jax
import jax.numpy as jnp
from jax import lax
from jax.experimental import pallas as pl
from jax.experimental.pallas import tpu as pltpu
from jax.sharding import PartitionSpec as P

HEAD_DIM = 64
EPS = 1e-05
MASKED = -1e30
MESH = pl.DeviceIdType.MESH
BF = jnp.bfloat16
F32 = jnp.float32
PLANE = ("context", "tensor")
VMEM_LIMIT = 60 * 2**20


def place():
    return (
        lax.axis_index("shard"),
        lax.axis_index("context"),
        lax.axis_index("tensor") // 2,
        lax.axis_index("tensor") % 2,
    )


def device(z, x, y, c):
    return (z, x, 2 * y + c)


def slot(x, y, c):
    return 4 * x + 2 * y + c


def neighbours():
    z, x, y, c = place()
    return [device(z, 1 - x, y, c), device(z, x, 1 - y, c), device(z, x, y, 1 - c)]


def plane_spots():
    z, x, y, c = place()
    steps = [(a, b, d) for a in range(2) for b in range(2) for d in range(2) if a + b + d]
    return [((x + a) % 2, (y + b) % 2, (c + d) % 2) for a, b, d in steps]


def plane_others():
    z = lax.axis_index("shard")
    return [device(z, *spot) for spot in plane_spots()]


def enter(targets):
    barrier = pltpu.get_barrier_semaphore()
    for target in targets:
        pl.semaphore_signal(barrier, inc=1, device_id=target, device_id_type=MESH)
    pl.semaphore_wait(barrier, len(targets))


def remote_copy(source, target_ref, send, recv, target):
    return pltpu.make_async_remote_copy(
        src_ref=source,
        dst_ref=target_ref,
        send_sem=send,
        recv_sem=recv,
        device_id=target,
        device_id_type=MESH,
    )


class Gather:
    semaphores = 9

    def __init__(self, in_ref, out_ref, local_sem, send, recv):
        z, x, y, c = place()
        self.in_ref, self.out_ref, self.local_sem = in_ref, out_ref, local_sem
        self.send, self.recv = send, recv
        self.spot = (x, y, c)
        self.to_x, self.to_y, self.to_c = neighbours()
        self.rows = in_ref.shape[0]
        self.sends = []

    def go(self, index, owner, start, size, target, source=None):
        there = self.out_ref.at[owner, pl.ds(start, size)]
        copy = remote_copy(
            there if source is None else source,
            there,
            self.send.at[index],
            self.recv.at[index],
            target,
        )
        copy.start()
        self.sends.append(copy)

    def arrived(self, index, owner, start, size):
        there = self.out_ref.at[owner, pl.ds(start, size)]
        remote_copy(
            there, there, self.send.at[index], self.recv.at[index], self.to_x
        ).wait_recv()

    def start(self):
        me = slot(*self.spot)
        self.own = pltpu.make_async_copy(self.in_ref, self.out_ref.at[me], self.local_sem)
        self.own.start()
        for index, target in enumerate((self.to_x, self.to_y, self.to_c)):
            self.go(index, me, 0, self.rows, target, self.in_ref)

    def relay_y(self):
        x, y, c = self.spot
        owner = slot(x, 1 - y, c)
        self.arrived(1, owner, 0, self.rows)
        self.go(3, owner, 0, self.rows // 2, self.to_x)
        self.go(5, owner, 0, self.rows, self.to_c)

    def relay_x(self):
        x, y, c = self.spot
        half = self.rows // 2
        owner = slot(1 - x, y, c)
        self.arrived(0, owner, 0, self.rows)
        self.go(4, owner, half, half, self.to_y)
        self.go(6, owner, 0, self.rows, self.to_c)

    def relay_far(self):
        x, y, c = self.spot
        half = self.rows // 2
        owner = slot(1 - x, 1 - y, c)
        self.arrived(3, owner, 0, half)
        self.go(7, owner, 0, half, self.to_c)
        self.arrived(4, owner, half, half)
        self.go(8, owner, half, half, self.to_c)

    def finish(self):
        x, y, c = self.spot
        half = self.rows // 2
        self.arrived(2, slot(x, y, 1 - c), 0, self.rows)
        self.arrived(5, slot(x, 1 - y, 1 - c), 0, self.rows)
        self.arrived(6, slot(1 - x, y, 1 - c), 0, self.rows)
        self.arrived(7, slot(1 - x, 1 - y, 1 - c), 0, half)
        self.arrived(8, slot(1 - x, 1 - y, 1 - c), half, half)
        self.own.wait()
        for copy in self.sends:
            copy.wait_send()

    def rest(self):
        self.relay_y()
        self.relay_x()
        self.relay_far()
        self.finish()


class Scatter:
    @staticmethod
    def scratch(rows, columns):
        return [
            pltpu.VMEM((4, rows, columns), BF),
            pltpu.VMEM((2, rows // 2, columns), BF),
            pltpu.VMEM((2, rows, columns), BF),
            pltpu.SemaphoreType.DMA((10,)),
            pltpu.SemaphoreType.DMA((10,)),
        ]

    def __init__(self, part_ref, core, relay, final, send, recv):
        self.part_ref, self.core, self.relay, self.final = part_ref, core, relay, final
        self.send, self.recv = send, recv
        self.to_x, self.to_y, self.to_c = neighbours()
        z, x, y, c = place()
        chips = ((1 - x, 1 - y), (1 - x, y), (x, 1 - y), (x, y))
        self.mine = [slot(*chip, c) for chip in chips]
        self.theirs = [slot(*chip, 1 - c) for chip in chips]
        rows = part_ref.shape[1]
        self.low, self.high = pl.ds(0, rows // 2), pl.ds(rows // 2, rows // 2)
        self.sends = []

    def forward(self, index, source, target_ref, target):
        copy = remote_copy(
            source, target_ref, self.send.at[index], self.recv.at[index], target
        )
        copy.start()
        self.sends.append(copy)

    def arrived(self, index, ref):
        remote_copy(ref, ref, self.send.at[index], self.recv.at[index], self.to_c).wait_recv()

    def pass_core(self, index):
        source = self.part_ref.at[self.theirs[index]]
        self.forward(index, source, self.core.at[index], self.to_c)

    def add(self, index, part, more=None):
        mine = self.mine[index]
        total = self.part_ref[mine, part].astype(F32) + self.core[index, part].astype(F32)
        if more is not None:
            total += more.astype(F32)
        self.part_ref[mine, part] = total.astype(BF)
        return self.part_ref.at[mine, part]

    def far(self):
        self.arrived(0, self.core.at[0])
        self.forward(4, self.add(0, self.low), self.relay.at[0], self.to_x)
        self.forward(5, self.add(0, self.high), self.relay.at[1], self.to_y)

    def near(self):
        self.arrived(1, self.core.at[1])
        self.forward(6, self.add(1, self.low), self.final.at[0, self.low], self.to_x)
        self.arrived(2, self.core.at[2])
        self.forward(7, self.add(2, self.high), self.final.at[1, self.high], self.to_y)

    def second(self):
        low, high, final, relay = self.low, self.high, self.final, self.relay
        self.arrived(5, relay.at[1])
        self.forward(8, self.add(1, high, relay[1]), final.at[0, high], self.to_x)
        self.arrived(4, relay.at[0])
        self.forward(9, self.add(2, low, relay[0]), final.at[1, low], self.to_y)

    def wait(self):
        self.arrived(3, self.core.at[3])
        self.arrived(6, self.final.at[0, self.low])
        self.arrived(7, self.final.at[1, self.high])
        self.arrived(8, self.final.at[0, self.high])
        self.arrived(9, self.final.at[1, self.low])

    def value(self, part=slice(None)):
        total = self.part_ref[self.mine[3], part].astype(F32) + self.core[3, part].astype(F32)
        return total + self.final[0, part].astype(F32) + self.final[1, part].astype(F32)

    def total(self):
        self.wait()
        return self.value()

    def finish(self):
        for copy in self.sends:
            copy.wait_send()


class LoadedScatter(Scatter):
    @staticmethod
    def scratch(rows, columns):
        return [
            pltpu.VMEM((4, rows, columns), BF),
            pltpu.SemaphoreType.DMA((4,)),
        ] + Scatter.scratch(rows, columns)

    def __init__(self, in_ref, part_ref, local_sem, *scratch):
        super().__init__(part_ref, *scratch)
        self.in_ref, self.local_sem = in_ref, local_sem

    def start(self):
        self.loads = []
        for index, (mine, theirs) in enumerate(zip(self.mine, self.theirs)):
            source = self.in_ref.at[theirs]
            self.forward(index, source, self.core.at[index], self.to_c)
            load = pltpu.make_async_copy(
                self.in_ref.at[mine], self.part_ref.at[index], self.local_sem.at[index]
            )
            load.start()
            self.loads.append(load)
        self.mine = (0, 1, 2, 3)

    def first(self):
        for load in self.loads:
            load.wait()
        self.far()
        self.near()


class Exchange:
    def __init__(self, in_ref, out_ref, local_sem, send, recv):
        self.in_ref, self.out_ref, self.local_sem = in_ref, out_ref, local_sem
        self.send, self.recv = send, recv
        z, x, y, c = place()
        self.me = slot(x, y, c)
        self.copies = []

    def start(self, piece, part):
        z = lax.axis_index("shard")
        own = pltpu.make_async_copy(
            self.in_ref.at[self.me, part], self.out_ref.at[self.me, part], self.local_sem.at[piece]
        )
        own.start()
        self.copies.append(own)
        for index, spot in enumerate(plane_spots()):
            copy = remote_copy(
                self.in_ref.at[slot(*spot), part],
                self.out_ref.at[self.me, part],
                self.send.at[piece, index],
                self.recv.at[piece, index],
                device(z, *spot),
            )
            copy.start()
            self.copies.append(copy)

    def finish(self, piece=None):
        copies = self.copies if piece is None else self.copies[8 * piece : 8 * piece + 8]
        for copy in copies:
            copy.wait()


ANY = pl.BlockSpec(memory_space=pl.ANY)
IN_VMEM = pl.BlockSpec(memory_space=pltpu.VMEM)


def call(kernel, name, outs, out_specs, in_specs, scratch, ident, micros):
    return pl.pallas_call(
        kernel,
        out_shape=outs,
        in_specs=in_specs,
        out_specs=out_specs,
        scratch_shapes=scratch,
        name=name,
        cost_estimate=pl.CostEstimate(
            flops=micros * 10**9, bytes_accessed=micros * 10**6, transcendentals=0
        ),
        compiler_params=pltpu.CompilerParams(
            collective_id=ident, has_side_effects=True, vmem_limit_bytes=VMEM_LIMIT
        ),
    )


def shape(*dims, dtype=BF):
    return jax.ShapeDtypeStruct(dims, dtype)


def gather_scratch():
    return [
        pltpu.SemaphoreType.DMA,
        pltpu.SemaphoreType.DMA((9,)),
        pltpu.SemaphoreType.DMA((9,)),
    ]


def gather_kernel(count, *refs):
    enter(neighbours())
    jobs = []
    for index in range(count):
        scratch = refs[2 * count + 3 * index : 2 * count + 3 * index + 3]
        jobs.append(Gather(refs[index], refs[count + index], *scratch))
    for job in jobs:
        job.start()
    for job in jobs:
        job.relay_y()
        job.relay_x()
    for job in jobs:
        job.relay_far()
    for job in jobs:
        job.finish()


def plane_gather(arrays, ident, micros):
    count = len(arrays)
    outs = tuple(shape(8, *values.shape, dtype=values.dtype) for values in arrays)
    kernel = partial(gather_kernel, count)
    scratch = gather_scratch() * count
    any_space = [ANY] * count
    return call(kernel, "plane_gather", outs, tuple(any_space), any_space, scratch, ident, micros)(
        *arrays
    )


def scatter_kernel(in_ref, out_ref, *scratch):
    enter(neighbours())
    job = LoadedScatter(in_ref, *scratch)
    job.start()
    job.first()
    job.second()
    out_ref[...] = job.total()
    job.finish()


def plane_scatter(values, ident, micros):
    _, rows, columns = values.shape
    outs = shape(rows, columns, dtype=F32)
    scratch = LoadedScatter.scratch(rows, columns)
    return call(
        scatter_kernel, "plane_scatter", outs, IN_VMEM, [ANY], scratch, ident, micros
    )(values)


def feed_kernel(
    own_ref, grad_ref, up_ref, down_ref,
    normed_out, branch_out, up_out, down_out,
    rows_ref, grads_ref, hidden_ref, slope_ref, part_a, part_b,
    load_sem, store_sem, g_local, g_send, g_recv, *scratch,
):
    enter(neighbours())
    gather = Gather(own_ref, rows_ref, g_local, g_send, g_recv)
    gather.start()
    blocks, _, width = rows_ref.shape
    loads = []
    for block in range(blocks):
        load = pltpu.make_async_copy(grad_ref.at[block], grads_ref.at[block], load_sem.at[block])
        load.start()
        loads.append(load)
    for load in loads:
        load.wait()

    def early(block, carry):
        slope_ref[block] = nn(grads_ref[block], down_ref[...]).astype(BF)
        return carry

    lax.fori_loop(0, blocks, early, 0)

    def middle(block):
        before = nn(rows_ref[block], up_ref[...])
        share = 0.5 + 0.5 * lax.erf(before * (0.5**0.5))
        hidden_ref[block] = (before * share).astype(BF)
        slope = share + before * (jnp.exp(-0.5 * before * before) * (2.0 * jnp.pi) ** (-0.5))
        slope = (slope_ref[block].astype(F32) * slope).astype(BF)
        slope_ref[block] = slope
        part_a[block] = nt(slope, up_ref[...]).astype(BF)

    first = Scatter(part_a, *scratch)
    x, y, c = gather.spot

    def pair(cx, cy):
        def one(index, carry):
            middle(slot(cx, cy, 0) + index)
            return carry

        lax.fori_loop(0, 2, one, 0)

    gather.own.wait()
    gather.arrived(2, slot(x, y, 1 - c), 0, gather.rows)
    pair(x, y)
    first.pass_core(3)
    gather.relay_y()
    gather.relay_x()
    gather.arrived(6, slot(1 - x, y, 1 - c), 0, gather.rows)
    pair(1 - x, y)
    first.pass_core(1)
    gather.arrived(5, slot(x, 1 - y, 1 - c), 0, gather.rows)
    pair(x, 1 - y)
    first.pass_core(2)
    gather.relay_far()
    first.near()
    gather.arrived(7, slot(1 - x, 1 - y, 1 - c), 0, gather.rows // 2)
    gather.arrived(8, slot(1 - x, 1 - y, 1 - c), gather.rows // 2, gather.rows // 2)
    pair(1 - x, 1 - y)
    first.pass_core(0)
    first.far()
    for copy in gather.sends:
        copy.wait_send()

    def store(block):
        return pltpu.make_async_copy(part_b.at[block], branch_out.at[block], store_sem.at[block])

    def branch(block, carry):
        part_b[block] = nt(hidden_ref[block], down_ref[...]).astype(BF)
        store(block).start()
        return carry

    lax.fori_loop(0, blocks, branch, 0)
    first.second()
    tile = 256

    def weight(left_ref, right_ref, out_ref):
        right = right_ref[...].reshape(-1, right_ref.shape[2])

        def one(index, carry):
            lanes = pl.ds(pl.multiple_of(index * tile, tile), tile)
            left = left_ref[:, :, lanes].reshape(-1, tile)
            out_ref[lanes, :] = tn(left, right).astype(BF)
            return carry

        lax.fori_loop(0, width // tile, one, 0)

    weight(grads_ref, hidden_ref, down_out)
    weight(rows_ref, slope_ref, up_out)
    normed_out[...] = first.total()
    first.finish()
    for block in range(blocks):
        store(block).wait()


def feed_forward(own, grads, w_up, w_down, ident):
    rows, width = own.shape
    hidden = w_up.shape[1]
    outs = (
        shape(rows, width, dtype=F32),
        shape(8, rows, width),
        shape(width, hidden),
        shape(width, hidden),
    )
    scratch = [
        pltpu.VMEM((8, rows, width), BF),
        pltpu.VMEM((8, rows, width), BF),
        pltpu.VMEM((8, rows, hidden), BF),
        pltpu.VMEM((8, rows, hidden), BF),
        pltpu.VMEM((8, rows, width), BF),
        pltpu.VMEM((8, rows, width), BF),
        pltpu.SemaphoreType.DMA((8,)),
        pltpu.SemaphoreType.DMA((8,)),
    ]
    return call(
        feed_kernel,
        "feed_forward",
        outs,
        (IN_VMEM, ANY, IN_VMEM, IN_VMEM),
        [ANY, ANY, IN_VMEM, IN_VMEM],
        scratch + gather_scratch() + Scatter.scratch(rows, width),
        ident,
        70,
    )(own, grads, w_up, w_down)


SIDE = 256


def nt(left, right):
    return lax.dot_general(left, right, (((1,), (1,)), ((), ())), preferred_element_type=F32)


def nn(left, right):
    return lax.dot_general(left, right, (((1,), (0,)), ((), ())), preferred_element_type=F32)


def tn(left, right):
    return lax.dot_general(left, right, (((0,), (0,)), ((), ())), preferred_element_type=F32)


def turn(values):
    return jnp.transpose(values.astype(F32))


def causal(scores):
    keys = lax.broadcasted_iota(jnp.int32, scores.shape, 0)
    queries = lax.broadcasted_iota(jnp.int32, scores.shape, 1)
    return jnp.where(keys <= queries, scores, MASKED)


def forward_kernel(
    rows_ref, w_ref, cot_ref,
    qkv_ref, log_ref, mix_ref, mine_ref, cot_out,
    ex_local, ex_send, ex_recv, g_local, g_send, g_recv,
):
    enter(plane_others())
    side = Gather(cot_ref, cot_out, g_local, g_send, g_recv)
    side.start()
    blocks, both, _ = rows_ref.shape
    rows = both // 2
    width = mix_ref.shape[2]
    heads = width // HEAD_DIM
    length = blocks * rows
    step = SIDE // rows

    def project(block, carry):
        qkv_ref[block] = nn(rows_ref[block], w_ref[...]).astype(BF)
        return carry

    lax.fori_loop(0, blocks, project, 0)
    exchange = Exchange(mix_ref, mine_ref, ex_local, ex_send, ex_recv)
    for clip in range(2):
        part = pl.ds(clip * rows, rows)
        for head in range(heads):
            lanes = [pl.ds(j * width + head * HEAD_DIM, HEAD_DIM) for j in range(3)]
            key = qkv_ref[:, part, lanes[1]].reshape(length, HEAD_DIM)
            value = turn(qkv_ref[:, part, lanes[2]].reshape(length, HEAD_DIM)).astype(BF)
            for index in range(length // SIDE):
                spots = pl.ds(index * step, step)
                query = qkv_ref[spots, part, lanes[0]].reshape(SIDE, HEAD_DIM)
                query = query * jnp.asarray(HEAD_DIM ** (-0.5), BF)
                start = index * SIDE
                last = causal(nt(key[start : start + SIDE], query))
                top = jnp.max(last, axis=0, keepdims=True)
                if index:
                    early = nt(key[:start], query)
                    top = jnp.maximum(top, jnp.max(early, axis=0, keepdims=True))
                last = jnp.exp(last - top)
                total = jnp.sum(last, axis=0, keepdims=True)
                mix = nn(value[:, start : start + SIDE], last.astype(BF))
                if index:
                    early = jnp.exp(early - top)
                    total += jnp.sum(early, axis=0, keepdims=True)
                    mix += nn(value[:, :start], early.astype(BF))
                mix = jnp.transpose(mix / total).astype(BF).reshape(step, rows, HEAD_DIM)
                mix_ref[spots, part, pl.ds(head * HEAD_DIM, HEAD_DIM)] = mix
                log_ref[pl.ds(clip * heads + head, 1), pl.ds(start, SIDE)] = top + jnp.log(total)
        exchange.start(clip, part)
        if clip == 0:
            side.relay_y()
            side.relay_x()
    side.relay_far()
    exchange.finish()
    side.finish()


def attend_forward(rows, weights, cotangent, ident):
    blocks, block, width = rows.shape
    columns = weights.shape[1] // 3
    heads = columns // HEAD_DIM
    return call(
        forward_kernel,
        "attend_forward",
        (
            shape(blocks, block, 3 * columns),
            shape(2 * heads, blocks * block // 2, dtype=F32),
            shape(blocks, block, columns),
            shape(blocks, block, columns),
            shape(blocks, block, width),
        ),
        (IN_VMEM, IN_VMEM, IN_VMEM, ANY, ANY),
        [IN_VMEM, IN_VMEM, ANY],
        [
            pltpu.SemaphoreType.DMA((2,)),
            pltpu.SemaphoreType.DMA((2, 7)),
            pltpu.SemaphoreType.DMA((2, 7)),
        ]
        + gather_scratch(),
        ident,
        45,
    )(rows, weights, cotangent)


def backward_kernel(
    grad_ref, qkv_ref, mix_ref, log_ref, rows_ref, w_ref, side_ref, text_ref,
    part_out, w_out, side_out, text_out,
    out_ref, part_ref, store_sem, grad_all, query_turned, ex_local, ex_send, ex_recv, *scratch,
):
    enter(plane_others())
    exchange = Exchange(grad_ref, grad_all, ex_local, ex_send, ex_recv)
    blocks, both, width = mix_ref.shape
    rows = both // 2
    heads = width // HEAD_DIM
    length = blocks * rows
    step = SIDE // rows
    for clip in range(2):
        exchange.start(clip, pl.ds(clip * rows, rows))
    size = len(scratch) // 2
    text = LoadedScatter(text_ref, *scratch[size:])
    text.start()
    text.first()
    side = LoadedScatter(side_ref, *scratch[:size])
    side.start()
    side.first()
    for clip in range(2):
        exchange.finish(clip)
        part = pl.ds(clip * rows, rows)
        for head in range(heads):
            lanes = [pl.ds(j * width + head * HEAD_DIM, HEAD_DIM) for j in range(3)]
            query = qkv_ref[:, part, lanes[0]].reshape(length, HEAD_DIM)
            query = query * jnp.asarray(HEAD_DIM ** (-0.5), BF)
            key = qkv_ref[:, part, lanes[1]].reshape(length, HEAD_DIM)
            value = qkv_ref[:, part, lanes[2]].reshape(length, HEAD_DIM)
            key_turned = turn(key).astype(BF)
            here = pl.ds(head * HEAD_DIM, HEAD_DIM)
            grad = grad_all[:, part, here].reshape(length, HEAD_DIM)
            mixed = mix_ref[:, part, here].reshape(length, HEAD_DIM)
            inner = jnp.transpose(grad.astype(F32) * mixed.astype(F32))
            inner = jnp.sum(inner, axis=0, keepdims=True)
            logs = log_ref[pl.ds(clip * heads + head, 1), :]
            for index in range(length // SIDE):
                start = index * SIDE
                spots = pl.ds(index * step, step)
                k_part, v_part = key[start : start + SIDE], value[start : start + SIDE]
                scores = nt(k_part, query[start:])
                first = causal(scores[:, :SIDE])
                if start + SIDE < length:
                    scores = jnp.concatenate([first, scores[:, SIDE:]], axis=1)
                else:
                    scores = first
                weights = jnp.exp(scores - logs[:, start:])
                slopes = nt(v_part, grad[start:])
                slopes = (weights * (slopes - inner[:, start:])).astype(BF)
                grad_key = nn(slopes, query[start:]).astype(BF).reshape(step, rows, HEAD_DIM)
                grad_value = nn(weights.astype(BF), grad[start:]).astype(BF)
                out_ref[spots, part, lanes[1]] = grad_key
                out_ref[spots, part, lanes[2]] = grad_value.reshape(step, rows, HEAD_DIM)
                grad_query = nn(key_turned[:, start : start + SIDE], slopes)
                if index:
                    query_turned[:, start:] += grad_query
                else:
                    query_turned[...] = grad_query
            grad_query = jnp.transpose(query_turned[...]) * HEAD_DIM ** (-0.5)
            grad_query = grad_query.astype(BF).reshape(blocks, rows, HEAD_DIM)
            out_ref[:, part, lanes[0]] = grad_query
        if clip == 0:
            text.second()
            side.second()
    def store(block):
        return pltpu.make_async_copy(part_ref.at[block], part_out.at[block], store_sem.at[block])

    def project(block, carry):
        part_ref[block] = nt(out_ref[block], w_ref[...]).astype(BF)
        store(block).start()
        return carry

    lax.fori_loop(0, blocks, project, 0)
    tile = 256
    right = out_ref[...].reshape(blocks * both, 3 * width)

    def weight(index, carry):
        lanes = pl.ds(pl.multiple_of(index * tile, tile), tile)
        left = rows_ref[:, :, lanes].reshape(blocks * both, tile)
        w_out[lanes, :] = tn(left, right).astype(BF)
        return carry

    lax.fori_loop(0, w_out.shape[0] // tile, weight, 0)
    text_out[...] = text.total()
    side_out[...] = side.total().astype(BF)
    text.finish()
    side.finish()
    for block in range(blocks):
        store(block).wait()


def attend_backward(grad_mix, qkv, mix, logs, rows, weights, side, text, ident):
    blocks, block, columns = mix.shape
    _, side_rows, width = side.shape
    text_shape = text.shape[1:]
    return call(
        backward_kernel,
        "attend_backward",
        (
            shape(blocks, block, width),
            shape(width, 3 * columns),
            shape(side_rows, width),
            shape(*text_shape, dtype=F32),
        ),
        (ANY, IN_VMEM, IN_VMEM, IN_VMEM),
        [ANY] + [IN_VMEM] * 5 + [ANY, ANY],
        [
            pltpu.VMEM((blocks, block, 3 * columns), BF),
            pltpu.VMEM((blocks, block, width), BF),
            pltpu.SemaphoreType.DMA((8,)),
            pltpu.VMEM((blocks, block, columns), BF),
            pltpu.VMEM((HEAD_DIM, blocks * block // 2), F32),
            pltpu.SemaphoreType.DMA((2,)),
            pltpu.SemaphoreType.DMA((2, 7)),
            pltpu.SemaphoreType.DMA((2, 7)),
        ]
        + LoadedScatter.scratch(side_rows, width)
        + LoadedScatter.scratch(*text_shape),
        ident,
        45,
    )(grad_mix, qkv, mix, logs, rows, weights, side, text)


CHUNK = 64


def chunks(rows, body, carry=None):
    def one(index, carry):
        return body(pl.ds(pl.multiple_of(index * CHUNK, CHUNK), CHUNK), carry)

    return lax.fori_loop(0, rows // CHUNK, one, 0 if carry is None else carry)


def normalise(inputs):
    average = jnp.mean(inputs, axis=-1, keepdims=True)
    centred = inputs - average
    rate = lax.rsqrt(jnp.mean(centred * centred, axis=-1, keepdims=True) + EPS)
    return centred * rate, rate


def norm_back(grads, inputs, gain):
    normed, rate = normalise(inputs)
    scaled = grads * gain
    inner = jnp.mean(scaled * normed, axis=-1, keepdims=True)
    result = rate * (scaled - jnp.mean(scaled, axis=-1, keepdims=True) - normed * inner)
    sums = (
        jnp.sum(grads * normed, axis=0, keepdims=True),
        jnp.sum(grads, axis=0, keepdims=True),
    )
    return result, sums


def rows_back_kernel(
    normed_ref, cot_ref, one_ref, two_ref, query_ref, mix_ref, text_ref, my_mix_ref,
    gain_ref, bias_ref, w_ref, branch_ref,
    grad_ref, layer_ref, stats_ref, grad_mix_ref, out_ref, side_ref, text_out,
    w_cross, w_query, w_out, low_ref, two_low_ref, back_ref, grad_cm, grad_cq, w_sem,
    *scratch,
):
    enter(neighbours())
    cross_job = Scatter(w_cross, *scratch[:5])
    query_job = Scatter(w_query, *scratch[5:10])
    branch_job = LoadedScatter(branch_ref, *scratch[10:])
    branch_job.start()
    blocks, columns, width = w_out.shape
    rows = low_ref.shape[0]
    heads = columns // HEAD_DIM
    loads = []
    for index, buffer in ((2, w_cross), (1, w_query), (0, w_out)):
        load = pltpu.make_async_copy(
            w_ref.at[:, index], buffer, w_sem.at[index]
        )
        load.start()
        loads.append(load)
    nothing = (jnp.zeros((1, width), F32),) * 2

    def third(part, sums):
        back, more = norm_back(normed_ref[part], two_ref[part], gain_ref[2:3])
        total = cot_ref[part].astype(F32) + back
        grad_ref[part] = total
        low_ref[part] = total.astype(BF)
        normed, _ = normalise(one_ref[part])
        two_low_ref[part] = (normed * gain_ref[1:2] + bias_ref[1:2]).astype(BF)
        return sums[0] + more[0], sums[1] + more[1]

    gain_three, shift_three = chunks(rows, third, nothing)
    branch_job.first()
    loads[0].wait()

    def cross_weight(block, carry):
        grad_cm[block] = nt(low_ref[...], w_cross[block]).astype(BF)
        w_cross[block] = tn(mix_ref[block], low_ref[...]).astype(BF)
        return carry

    lax.fori_loop(0, blocks, cross_weight, 0)
    for index in range(4):
        cross_job.pass_core(index)
    half = rows // 2
    texts = text_ref.shape[1] // 4
    loads[1].wait()

    def cross(block, carry):
        for clip in range(2):
            part = pl.ds(clip * half, half)
            keys = pl.ds(clip * texts, texts)
            values = pl.ds((2 + clip) * texts, texts)
            for head in range(heads):
                here = pl.ds(head * HEAD_DIM, HEAD_DIM)
                query = query_ref[block, part, here] * jnp.asarray(HEAD_DIM ** (-0.5), BF)
                key, value = text_ref[block, keys, here], text_ref[block, values, here]
                grad = grad_cm[block, part, here]
                scores = nt(key, query)
                weights = jnp.exp(scores - jnp.max(scores, axis=0, keepdims=True))
                weights = weights / jnp.sum(weights, axis=0, keepdims=True)
                slopes = nt(value, grad)
                inner = jnp.sum(weights * slopes, axis=0, keepdims=True)
                slopes = (weights * (slopes - inner)).astype(BF)
                grad_query = jnp.transpose(nn(turn(key).astype(BF), slopes))
                grad_cq[block, part, here] = (grad_query * HEAD_DIM ** (-0.5)).astype(BF)
                text_out[block, keys, here] = nn(slopes, query).astype(BF)
                text_out[block, values, here] = nn(weights.astype(BF), grad).astype(BF)
        back = nn(grad_cq[block], w_query[block])
        back_ref[...] += back
        w_query[block] = tn(grad_cq[block], two_low_ref[...]).astype(BF)
        return carry

    back_ref[...] = jnp.zeros_like(back_ref)
    lax.fori_loop(0, blocks // 2, cross, 0)
    branch_job.second()
    cross_job.far()
    cross_job.near()
    lax.fori_loop(blocks // 2, blocks, cross, 0)
    for index in range(4):
        query_job.pass_core(index)

    def second(part, sums):
        back, more = norm_back(back_ref[part], one_ref[part], gain_ref[1:2])
        total = grad_ref[part] + back
        grad_ref[part] = total
        low_ref[part] = total.astype(BF)
        return sums[0] + more[0], sums[1] + more[1]

    gain_two, shift_two = chunks(rows, second, nothing)
    cross_job.second()
    query_job.far()
    query_job.near()
    loads[2].wait()

    def out_weight(block, carry):
        grad_mix_ref[block] = nt(low_ref[...], w_out[block]).astype(BF)
        out_ref[block] = tn(my_mix_ref[block], low_ref[...]).astype(BF)
        return carry

    lax.fori_loop(0, blocks, out_weight, 0)
    branch_job.wait()

    def last(part, sums):
        branch = branch_job.value(part)
        total = two_ref[part] + branch
        layer_ref[part] = total.astype(BF)
        return (
            sums[0] + jnp.sum(total * total, axis=0, keepdims=True),
            sums[1] + jnp.sum(branch * branch, axis=0, keepdims=True),
        )

    square_out, square_three = chunks(rows, last, nothing)
    rest = jnp.zeros((1, width), F32)
    for index, row in enumerate(
        (rest, rest, gain_two, shift_two, gain_three, shift_three, square_out, square_three)
    ):
        stats_ref[index : index + 1] = row
    query_job.second()
    side_ref[1] = cross_job.total().astype(BF)
    side_ref[0] = query_job.total().astype(BF)
    branch_job.finish()
    cross_job.finish()
    query_job.finish()


def rows_back(
    normed, cot, one, two, query, mix, text, my_mix, gain, bias, weights, branch, ident
):
    rows, width = cot.shape
    blocks, _, columns = my_mix.shape
    return call(
        rows_back_kernel,
        "rows_back",
        (
            shape(rows, width, dtype=F32),
            shape(rows, width),
            shape(8, width, dtype=F32),
            shape(*my_mix.shape),
            shape(blocks, columns, width),
            shape(2, columns, width),
            shape(*text.shape),
        ),
        (IN_VMEM,) * 7,
        [IN_VMEM] * 10 + [ANY, ANY],
        [pltpu.VMEM((blocks, columns, width), BF)] * 3
        + [
            pltpu.VMEM((rows, width), BF),
            pltpu.VMEM((rows, width), BF),
            pltpu.VMEM((rows, width), F32),
            pltpu.VMEM(my_mix.shape, BF),
            pltpu.VMEM(my_mix.shape, BF),
            pltpu.SemaphoreType.DMA((3,)),
        ]
        + Scatter.scratch(columns, width) * 2
        + LoadedScatter.scratch(rows, width),
        ident,
        65,
    )(normed, cot, one, two, query, mix, text, my_mix, gain, bias, weights, branch)


def last_kernel(
    part_ref, frames_ref, gain_ref, grad_ref, stats_ref, text_ref, qkv_ref, up_ref, down_ref,
    out_ref, total_ref, text_out, qkv_out, up_out, down_out,
    mine, came, all_ref, st_send, st_recv, z_send, z_recv,
    qkv_came, qkv_pair, up_pair, down_pair, q_send, q_recv, x_send, x_recv, *scratch,
):
    z = lax.axis_index("shard")
    shards = lax.axis_size("shard")
    others = [lax.rem(z + i, shards) for i in range(1, shards)]
    spot = place()[1:]
    context = spot[0]
    enter(neighbours() + [device(other, *spot) for other in others])
    size = len(scratch) // 2
    text = LoadedScatter(text_ref, *scratch[size:])
    text.start()
    job = LoadedScatter(part_ref, *scratch[:size])
    job.start()
    sends, moves = [], []
    for index, other in enumerate(others):
        copy = remote_copy(
            qkv_ref.at[other], qkv_came.at[index], q_send.at[index], q_recv.at[index],
            device(other, *spot),
        )
        copy.start()
        moves.append(copy)
    inputs = frames_ref[...].astype(F32)
    average = jnp.mean(inputs, axis=-1, keepdims=True)
    centred = inputs - average
    rate = lax.rsqrt(jnp.mean(centred * centred, axis=-1, keepdims=True) + EPS)
    text.first()
    job.first()
    text.second()
    job.second()
    to_x = neighbours()[0]
    pairs = []
    for index, (source, pair_ref) in enumerate(((up_ref, up_pair), (down_ref, down_pair))):
        copy = remote_copy(source, pair_ref, x_send.at[index], x_recv.at[index], to_x)
        copy.start()
        pairs.append(copy)
    text_out[...] = text.total()
    grads = job.total()
    normed = centred * rate
    mine[0] = stats_ref[...]
    mine[0, 0:1] = jnp.sum(grads * normed, axis=0, keepdims=True)
    mine[0, 1:2] = jnp.sum(grads, axis=0, keepdims=True)
    for index, target in enumerate(reversed(neighbours())):
        copy = remote_copy(
            mine.at[index], came.at[index], st_send.at[index], st_recv.at[index], target
        )
        copy.start()
        sends.append(copy)
        if index == 0:
            scaled = grads * gain_ref[...]
            inner = jnp.mean(scaled * normed, axis=-1, keepdims=True)
            scaled = scaled - jnp.mean(scaled, axis=-1, keepdims=True) - normed * inner
            out_ref[...] = grad_ref[...] + rate * scaled
        copy.wait_recv()
        mine[index + 1] = mine[index] + came[index]
    for index, other in enumerate(others):
        copy = remote_copy(
            mine.at[3], all_ref.at[z], z_send.at[index], z_recv.at[index], device(other, *spot)
        )
        copy.start()
        sends.append(copy)
    all_ref[z] = mine[3]
    total = qkv_ref[z].astype(F32)
    for index, copy in enumerate(moves):
        copy.wait_recv()
        total += qkv_came[index].astype(F32)
    qkv_pair[0] = total.astype(BF)
    copy = remote_copy(qkv_pair.at[0], qkv_pair.at[1], x_send.at[2], x_recv.at[2], to_x)
    copy.start()
    pairs.append(copy)
    for copy in sends[3:]:
        copy.wait_recv()
    total = all_ref[0]
    for index in range(1, shards):
        total += all_ref[index]
    total_ref[...] = total
    half = up_ref.shape[1]
    ours = pl.ds(pl.multiple_of(context * half, half), half)
    theirs = pl.ds(pl.multiple_of((1 - context) * half, half), half)
    for copy, source, pair_ref, target in (
        (pairs[0], up_ref, up_pair, up_out),
        (pairs[1], down_ref, down_pair, down_out),
    ):
        target[:, ours] = source[...].astype(F32)
        copy.wait_recv()
        target[:, theirs] = pair_ref[...].astype(F32)
    pairs[2].wait_recv()
    lead = jnp.where(context == 0, qkv_pair[0], qkv_pair[1]).astype(F32)
    trail = jnp.where(context == 0, qkv_pair[1], qkv_pair[0]).astype(F32)
    width = lead.shape[1] // 3
    for index in range(3):
        lanes = slice(index * width, (index + 1) * width)
        qkv_out[index, :, :width] = lead[:, lanes]
        qkv_out[index, :, width:] = trail[:, lanes]
    for copy in sends + moves + pairs:
        copy.wait_send()
    text.finish()
    job.finish()


def last_step(part, frames, gain, grad, stats, text, qkv, up, down, shards, ident):
    _, rows, width = part.shape
    depth, half = up.shape
    columns = qkv.shape[2]
    return call(
        last_kernel,
        "last_step",
        (
            shape(rows, width, dtype=F32),
            shape(16, width, dtype=F32),
            shape(*text.shape[1:], dtype=F32),
            shape(3, depth, 2 * columns // 3, dtype=F32),
            shape(depth, 2 * half, dtype=F32),
            shape(depth, 2 * half, dtype=F32),
        ),
        (IN_VMEM,) * 6,
        [ANY] + [IN_VMEM] * 4 + [ANY] + [IN_VMEM] * 3,
        [
            pltpu.VMEM((4, 16, width), F32),
            pltpu.VMEM((3, 16, width), F32),
            pltpu.VMEM((shards, 16, width), F32),
            pltpu.SemaphoreType.DMA((3,)),
            pltpu.SemaphoreType.DMA((3,)),
            pltpu.SemaphoreType.DMA((shards - 1,)),
            pltpu.SemaphoreType.DMA((shards - 1,)),
            pltpu.VMEM((shards - 1, depth, columns), BF),
            pltpu.VMEM((2, depth, columns), BF),
            pltpu.VMEM((depth, half), BF),
            pltpu.VMEM((depth, half), BF),
            pltpu.SemaphoreType.DMA((shards - 1,)),
            pltpu.SemaphoreType.DMA((shards - 1,)),
            pltpu.SemaphoreType.DMA((3,)),
            pltpu.SemaphoreType.DMA((3,)),
        ]
        + LoadedScatter.scratch(rows, width)
        + LoadedScatter.scratch(*text.shape[1:]),
        ident,
        65,
    )(part, frames, gain, grad, stats, text, qkv, up, down)


def dots(spec, *operands):
    return jnp.einsum(spec, *operands, preferred_element_type=F32)


def layer_norm(inputs, scaling, offset):
    average = jnp.mean(inputs, axis=-1, keepdims=True)
    centred = inputs - average
    variance = jnp.mean(centred * centred, axis=-1, keepdims=True)
    return centred * lax.rsqrt(variance + EPS) * scaling + offset


def on_device(
    frames,
    text_states,
    cotangent,
    norm_gain,
    norm_bias,
    self_qkv,
    self_out,
    cross_qkv,
    cross_out,
    mlp_up,
    mlp_down,
):
    clips, rows, width = frames.shape
    context = lax.axis_index("context")
    depth = self_qkv.shape[1]
    slices = width // depth
    columns = self_qkv.shape[2] // 2
    heads = columns // HEAD_DIM
    block = clips * rows
    texts = text_states.shape[1]

    def half(weight):
        size = weight.shape[-1] // 2
        return lax.dynamic_slice_in_dim(weight, context * size, size, weight.ndim - 1)

    def over_shard(weight, tiled=True):
        return lax.all_gather(weight, "shard", axis=0, tiled=tiled)

    qkv_part = half(self_qkv)
    w_qkv = over_shard(jnp.concatenate([qkv_part[0], qkv_part[1], qkv_part[2]], axis=-1))
    cross_part = half(cross_qkv)
    side = jnp.stack(
        [half(self_out), cross_part[0], half(cross_out), cross_part[1], cross_part[2]]
    )
    w_side = over_shard(side.transpose(0, 2, 1), tiled=False).transpose(1, 2, 0, 3)
    w_side = w_side.reshape(5, columns, width)
    w_up = over_shard(half(mlp_up))
    w_down = over_shard(half(mlp_down))

    stream_zero = frames.astype(F32).reshape(block, width)
    norm_one = layer_norm(stream_zero, norm_gain[0], norm_bias[0])
    (all_one,) = plane_gather([norm_one.astype(BF)], 0, 33)
    qkv, self_log, mix, my_mix, all_grad = attend_forward(
        all_one, w_qkv, cotangent.reshape(block, width), 1
    )

    text_part = dots("cnd,ted->tcne", text_states, w_side[3:]).astype(BF)
    plane_w, text_all = plane_gather(
        [
            w_side[:3].reshape(3 * columns, width),
            text_part.reshape(2 * clips * texts, columns),
        ],
        2,
        65,
    )
    plane_w = plane_w.reshape(8, 3, columns, width)
    w_out, w_query, w_cross = plane_w[:, 0], plane_w[:, 1], plane_w[:, 2]
    branch_one = dots("bre,bed->rd", my_mix, w_out)
    stream_one = stream_zero + branch_one
    norm_two = layer_norm(stream_one, norm_gain[1], norm_bias[1]).astype(BF)
    cross_q = dots("rd,bed->bre", norm_two, w_query).astype(BF)
    text_heads = text_all.reshape(8, 2, clips, texts, heads, HEAD_DIM)
    scale = HEAD_DIM ** (-0.5)
    queries = cross_q.reshape(8, clips, rows, heads, HEAD_DIM)
    scores = dots("bcfhd,bcnhd->cbhfn", queries, text_heads[:, 0]) * scale
    weights = jnp.exp(scores - jnp.max(scores, axis=-1, keepdims=True))
    weights = weights / jnp.sum(weights, axis=-1, keepdims=True)
    cross_mix = dots("cbhfn,bcnhd->bcfhd", weights.astype(BF), text_heads[:, 1]).astype(BF)
    cross_mix = cross_mix.reshape(8, block, columns)
    branch_two = dots("bre,bed->rd", cross_mix, w_cross)
    stream_two = stream_one + branch_two

    norm_three = layer_norm(stream_two, norm_gain[2], norm_bias[2]).astype(BF)
    grad_normed, part_three, grad_up, grad_down = feed_forward(
        norm_three, all_grad, w_up, w_down, 4
    )

    def to_shard(part):
        return lax.psum_scatter(part.astype(BF), "shard", scatter_dimension=0, tiled=True)

    grad_down, grad_up = to_shard(grad_down), to_shard(grad_up)
    grad_one, layer_out, stats, grad_mix, part_out, side, text_grads = rows_back(
        grad_normed,
        cotangent.reshape(block, width),
        stream_one,
        stream_two,
        cross_q,
        cross_mix,
        text_all,
        my_mix,
        norm_gain,
        norm_bias,
        plane_w,
        part_three,
        3,
    )

    def slice_shards(part):
        return part.reshape(-1, slices, depth).transpose(1, 0, 2)

    grad_cross = to_shard(slice_shards(side))
    part_norm, grad_w_qkv, grad_out, text_grads = attend_backward(
        grad_mix, qkv, mix, self_log, all_one, w_qkv, part_out, text_grads, 8
    )
    part_norm, grad_w_qkv, grad_out, text_grads, grad_down, grad_up = lax.optimization_barrier(
        (part_norm, grad_w_qkv, grad_out, text_grads, grad_down, grad_up)
    )
    text_grads = text_grads.reshape(2, clips, texts, columns).astype(BF)
    w_grad_text = dots("cnd,tcne->ted", text_states, text_grads).astype(BF)
    rest = jnp.concatenate([grad_out, w_grad_text.reshape(2 * columns, width)], axis=0)
    grad_rest = to_shard(slice_shards(rest))
    grad_text = dots("tcne,ted->cnd", text_grads, w_side[3:])
    grad_text = grad_text.reshape(clips, 8, texts // 8, width).transpose(1, 0, 2, 3).astype(BF)
    grad_text = grad_text.reshape(8, clips * texts // 8, width)
    squares = [jnp.sum(v * v, axis=0)[None] for v in (branch_one, branch_two)]
    grad_frames, totals, grad_text, grad_w_qkv, grad_up, grad_down = last_step(
        part_norm,
        frames.reshape(block, width),
        norm_gain[0][None],
        grad_one,
        jnp.concatenate([stats] + squares + [jnp.zeros((6, width), F32)], axis=0),
        grad_text,
        grad_w_qkv.reshape(slices, depth, 3 * columns),
        grad_up,
        grad_down,
        slices,
        11,
    )
    grad_frames = grad_frames.reshape(clips, rows, width)
    grad_text = grad_text.reshape(clips, texts // 8, width)

    grad_cross, grad_rest, totals = lax.optimization_barrier((grad_cross, grad_rest, totals))
    grad_side = jnp.concatenate([grad_cross, grad_rest], axis=1)

    def whole(values):
        return lax.all_gather(values, "context", axis=1, tiled=True)

    grad_side = whole(grad_side.reshape(5, columns, depth)).astype(F32).transpose(0, 2, 1)
    gains = jnp.stack([totals[0], totals[2], totals[4]])
    shifts = jnp.stack([totals[1], totals[3], totals[5]])
    squares = jnp.stack([totals[j].sum() for j in (6, 8, 9, 7)])
    start = lax.axis_index("shard") * depth
    grad_gain = lax.dynamic_slice_in_dim(gains, start, depth, 1)
    grad_shift = lax.dynamic_slice_in_dim(shifts, start, depth, 1)
    entries = float(clips * rows * width * lax.axis_size(("shard",) + PLANE))
    return (
        layer_out.reshape(clips, rows, width),
        grad_frames,
        grad_text,
        grad_gain,
        grad_shift,
        grad_w_qkv,
        grad_side[2],
        jnp.stack([grad_side[0], grad_side[3], grad_side[4]]),
        grad_side[1],
        grad_up,
        grad_down,
        jnp.sqrt(squares / entries),
    )


def solution(mesh):
    rows = P("shard", PLANE, None)
    stack = P(None, "shard", "tensor")
    flat = P("shard", "tensor")
    return jax.shard_map(
        on_device,
        mesh=mesh,
        in_specs=(rows, P("shard"), rows, P(), P(), stack, flat, stack, flat, flat, flat),
        out_specs=(
            (rows, rows, rows, P(None, "shard"), P(None, "shard"))
            + (stack, flat, stack, flat, flat, flat, P())
        ),
        check_vma=False,
    )
```

```python
from functools import partial

import jax
import jax.numpy as jnp
from jax import lax
from jax.experimental import pallas as pl
from jax.experimental.pallas import tpu as pltpu
from jax.sharding import PartitionSpec as P

HEAD_DIM = 64
EPS = 1e-05
MASKED = -1e30
MESH = pl.DeviceIdType.MESH
BF = jnp.bfloat16
F32 = jnp.float32
PLANE = ("context", "tensor")
VMEM_LIMIT = 60 * 2**20


def place():
    return (
        lax.axis_index("shard"),
        lax.axis_index("context"),
        lax.axis_index("tensor") // 2,
        lax.axis_index("tensor") % 2,
    )


def device(z, x, y, c):
    return (z, x, 2 * y + c)


def slot(x, y, c):
    return 4 * x + 2 * y + c


def neighbours():
    z, x, y, c = place()
    return [device(z, 1 - x, y, c), device(z, x, 1 - y, c), device(z, x, y, 1 - c)]


def plane_spots():
    z, x, y, c = place()
    steps = [(a, b, d) for a in range(2) for b in range(2) for d in range(2) if a + b + d]
    return [((x + a) % 2, (y + b) % 2, (c + d) % 2) for a, b, d in steps]


def plane_others():
    z = lax.axis_index("shard")
    return [device(z, *spot) for spot in plane_spots()]


def enter(targets):
    barrier = pltpu.get_barrier_semaphore()
    for target in targets:
        pl.semaphore_signal(barrier, inc=1, device_id=target, device_id_type=MESH)
    pl.semaphore_wait(barrier, len(targets))


def remote_copy(source, target_ref, send, recv, target):
    return pltpu.make_async_remote_copy(
        src_ref=source,
        dst_ref=target_ref,
        send_sem=send,
        recv_sem=recv,
        device_id=target,
        device_id_type=MESH,
    )


class Gather:
    semaphores = 9

    def __init__(self, in_ref, out_ref, local_sem, send, recv):
        z, x, y, c = place()
        self.in_ref, self.out_ref, self.local_sem = in_ref, out_ref, local_sem
        self.send, self.recv = send, recv
        self.spot = (x, y, c)
        self.to_x, self.to_y, self.to_c = neighbours()
        self.rows = in_ref.shape[0]
        self.sends = []

    def go(self, index, owner, start, size, target, source=None):
        there = self.out_ref.at[owner, pl.ds(start, size)]
        copy = remote_copy(
            there if source is None else source,
            there,
            self.send.at[index],
            self.recv.at[index],
            target,
        )
        copy.start()
        self.sends.append(copy)

    def arrived(self, index, owner, start, size):
        there = self.out_ref.at[owner, pl.ds(start, size)]
        remote_copy(
            there, there, self.send.at[index], self.recv.at[index], self.to_x
        ).wait_recv()

    def start(self):
        me = slot(*self.spot)
        self.own = pltpu.make_async_copy(self.in_ref, self.out_ref.at[me], self.local_sem)
        self.own.start()
        for index, target in enumerate((self.to_x, self.to_y, self.to_c)):
            self.go(index, me, 0, self.rows, target, self.in_ref)

    def relay_y(self):
        x, y, c = self.spot
        owner = slot(x, 1 - y, c)
        self.arrived(1, owner, 0, self.rows)
        self.go(3, owner, 0, self.rows // 2, self.to_x)
        self.go(5, owner, 0, self.rows, self.to_c)

    def relay_x(self):
        x, y, c = self.spot
        half = self.rows // 2
        owner = slot(1 - x, y, c)
        self.arrived(0, owner, 0, self.rows)
        self.go(4, owner, half, half, self.to_y)
        self.go(6, owner, 0, self.rows, self.to_c)

    def relay_far(self):
        x, y, c = self.spot
        half = self.rows // 2
        owner = slot(1 - x, 1 - y, c)
        self.arrived(3, owner, 0, half)
        self.go(7, owner, 0, half, self.to_c)
        self.arrived(4, owner, half, half)
        self.go(8, owner, half, half, self.to_c)

    def finish(self):
        x, y, c = self.spot
        half = self.rows // 2
        self.arrived(2, slot(x, y, 1 - c), 0, self.rows)
        self.arrived(5, slot(x, 1 - y, 1 - c), 0, self.rows)
        self.arrived(6, slot(1 - x, y, 1 - c), 0, self.rows)
        self.arrived(7, slot(1 - x, 1 - y, 1 - c), 0, half)
        self.arrived(8, slot(1 - x, 1 - y, 1 - c), half, half)
        self.own.wait()
        for copy in self.sends:
            copy.wait_send()

    def rest(self):
        self.relay_y()
        self.relay_x()
        self.relay_far()
        self.finish()


class Scatter:
    @staticmethod
    def scratch(rows, columns):
        return [
            pltpu.VMEM((4, rows, columns), BF),
            pltpu.VMEM((2, rows // 2, columns), BF),
            pltpu.VMEM((2, rows, columns), BF),
            pltpu.SemaphoreType.DMA((10,)),
            pltpu.SemaphoreType.DMA((10,)),
        ]

    def __init__(self, part_ref, core, relay, final, send, recv):
        self.part_ref, self.core, self.relay, self.final = part_ref, core, relay, final
        self.send, self.recv = send, recv
        self.to_x, self.to_y, self.to_c = neighbours()
        z, x, y, c = place()
        chips = ((1 - x, 1 - y), (1 - x, y), (x, 1 - y), (x, y))
        self.mine = [slot(*chip, c) for chip in chips]
        self.theirs = [slot(*chip, 1 - c) for chip in chips]
        rows = part_ref.shape[1]
        self.low, self.high = pl.ds(0, rows // 2), pl.ds(rows // 2, rows // 2)
        self.sends = []

    def forward(self, index, source, target_ref, target):
        copy = remote_copy(
            source, target_ref, self.send.at[index], self.recv.at[index], target
        )
        copy.start()
        self.sends.append(copy)

    def arrived(self, index, ref):
        remote_copy(ref, ref, self.send.at[index], self.recv.at[index], self.to_c).wait_recv()

    def pass_core(self, index):
        source = self.part_ref.at[self.theirs[index]]
        self.forward(index, source, self.core.at[index], self.to_c)

    def add(self, index, part, more=None):
        mine = self.mine[index]
        total = self.part_ref[mine, part].astype(F32) + self.core[index, part].astype(F32)
        if more is not None:
            total += more.astype(F32)
        self.part_ref[mine, part] = total.astype(BF)
        return self.part_ref.at[mine, part]

    def far(self):
        self.arrived(0, self.core.at[0])
        self.forward(4, self.add(0, self.low), self.relay.at[0], self.to_x)
        self.forward(5, self.add(0, self.high), self.relay.at[1], self.to_y)

    def near(self):
        self.arrived(1, self.core.at[1])
        self.forward(6, self.add(1, self.low), self.final.at[0, self.low], self.to_x)
        self.arrived(2, self.core.at[2])
        self.forward(7, self.add(2, self.high), self.final.at[1, self.high], self.to_y)

    def second(self):
        low, high, final, relay = self.low, self.high, self.final, self.relay
        self.arrived(5, relay.at[1])
        self.forward(8, self.add(1, high, relay[1]), final.at[0, high], self.to_x)
        self.arrived(4, relay.at[0])
        self.forward(9, self.add(2, low, relay[0]), final.at[1, low], self.to_y)

    def wait(self):
        self.arrived(3, self.core.at[3])
        self.arrived(6, self.final.at[0, self.low])
        self.arrived(7, self.final.at[1, self.high])
        self.arrived(8, self.final.at[0, self.high])
        self.arrived(9, self.final.at[1, self.low])

    def value(self, part=slice(None)):
        total = self.part_ref[self.mine[3], part].astype(F32) + self.core[3, part].astype(F32)
        return total + self.final[0, part].astype(F32) + self.final[1, part].astype(F32)

    def total(self):
        self.wait()
        return self.value()

    def finish(self):
        for copy in self.sends:
            copy.wait_send()


class LoadedScatter(Scatter):
    @staticmethod
    def scratch(rows, columns):
        return [
            pltpu.VMEM((4, rows, columns), BF),
            pltpu.SemaphoreType.DMA((4,)),
        ] + Scatter.scratch(rows, columns)

    def __init__(self, in_ref, part_ref, local_sem, *scratch):
        super().__init__(part_ref, *scratch)
        self.in_ref, self.local_sem = in_ref, local_sem

    def start(self):
        self.loads = []
        for index, (mine, theirs) in enumerate(zip(self.mine, self.theirs)):
            source = self.in_ref.at[theirs]
            self.forward(index, source, self.core.at[index], self.to_c)
            load = pltpu.make_async_copy(
                self.in_ref.at[mine], self.part_ref.at[index], self.local_sem.at[index]
            )
            load.start()
            self.loads.append(load)
        self.mine = (0, 1, 2, 3)

    def first(self):
        for load in self.loads:
            load.wait()
        self.far()
        self.near()


class Exchange:
    def __init__(self, in_ref, out_ref, local_sem, send, recv):
        self.in_ref, self.out_ref, self.local_sem = in_ref, out_ref, local_sem
        self.send, self.recv = send, recv
        z, x, y, c = place()
        self.me = slot(x, y, c)
        self.copies = []

    def start(self, piece, part):
        z = lax.axis_index("shard")
        own = pltpu.make_async_copy(
            self.in_ref.at[self.me, part], self.out_ref.at[self.me, part], self.local_sem.at[piece]
        )
        own.start()
        self.copies.append(own)
        for index, spot in enumerate(plane_spots()):
            copy = remote_copy(
                self.in_ref.at[slot(*spot), part],
                self.out_ref.at[self.me, part],
                self.send.at[piece, index],
                self.recv.at[piece, index],
                device(z, *spot),
            )
            copy.start()
            self.copies.append(copy)

    def finish(self, piece=None):
        copies = self.copies if piece is None else self.copies[8 * piece : 8 * piece + 8]
        for copy in copies:
            copy.wait()


ANY = pl.BlockSpec(memory_space=pl.ANY)
IN_VMEM = pl.BlockSpec(memory_space=pltpu.VMEM)


def call(kernel, name, outs, out_specs, in_specs, scratch, ident, micros):
    return pl.pallas_call(
        kernel,
        out_shape=outs,
        in_specs=in_specs,
        out_specs=out_specs,
        scratch_shapes=scratch,
        name=name,
        cost_estimate=pl.CostEstimate(
            flops=micros * 10**9, bytes_accessed=micros * 10**6, transcendentals=0
        ),
        compiler_params=pltpu.CompilerParams(
            collective_id=ident, has_side_effects=True, vmem_limit_bytes=VMEM_LIMIT
        ),
    )


def shape(*dims, dtype=BF):
    return jax.ShapeDtypeStruct(dims, dtype)


def gather_scratch():
    return [
        pltpu.SemaphoreType.DMA,
        pltpu.SemaphoreType.DMA((9,)),
        pltpu.SemaphoreType.DMA((9,)),
    ]


def shard_others():
    z, shards = lax.axis_index("shard"), lax.axis_size("shard")
    return [lax.rem(z + i, shards) for i in range(1, shards)]


def first_kernel(
    frames_ref, gain_ref, bias_ref, cot_ref, w_ref,
    rows_out, cot_out, w_out,
    normed_ref, w_sem, w_send, w_recv, *scratch,
):
    z = lax.axis_index("shard")
    spot = place()[1:]
    others = shard_others()
    enter(neighbours() + [device(other, *spot) for other in others])
    own = pltpu.make_async_copy(w_ref, w_out.at[z], w_sem)
    own.start()
    copies = []
    for index, other in enumerate(others):
        copy = remote_copy(
            w_ref, w_out.at[z], w_send.at[index], w_recv.at[index], device(other, *spot)
        )
        copy.start()
        copies.append(copy)

    def norm(part, carry):
        normed, _ = normalise(frames_ref[part].astype(F32))
        normed_ref[part] = (normed * gain_ref[0:1] + bias_ref[0:1]).astype(BF)
        return carry

    chunks(frames_ref.shape[0], norm)
    rows, grads = Gather(normed_ref, rows_out, *scratch[:3]), Gather(cot_ref, cot_out, *scratch[3:])
    rows.start()
    rows.relay_y()
    rows.relay_x()
    grads.start()
    rows.relay_far()
    rows.finish()
    grads.rest()
    own.wait()
    for copy in copies:
        copy.wait()


def first_step(frames, gain, bias, cotangent, w_qkv, shards, ident):
    rows, width = frames.shape
    return call(
        first_kernel,
        "first_step",
        (shape(8, rows, width), shape(8, rows, width), shape(shards, *w_qkv.shape)),
        (ANY, ANY, ANY),
        [IN_VMEM, IN_VMEM, IN_VMEM, ANY, ANY],
        [
            pltpu.VMEM((rows, width), BF),
            pltpu.SemaphoreType.DMA,
            pltpu.SemaphoreType.DMA((shards - 1,)),
            pltpu.SemaphoreType.DMA((shards - 1,)),
        ]
        + gather_scratch() * 2,
        ident,
        60,
    )(frames, gain, bias, cotangent, w_qkv)


def feed_kernel(
    own_ref, grad_ref, up_ref, down_ref,
    normed_out, branch_out, up_out, down_out,
    rows_ref, grads_ref, hidden_ref, slope_ref, part_a, part_b,
    load_sem, store_sem, g_local, g_send, g_recv, *scratch,
):
    enter(neighbours())
    gather = Gather(own_ref, rows_ref, g_local, g_send, g_recv)
    gather.start()
    blocks, _, width = rows_ref.shape
    loads = []
    for block in range(blocks):
        load = pltpu.make_async_copy(grad_ref.at[block], grads_ref.at[block], load_sem.at[block])
        load.start()
        loads.append(load)
    for load in loads:
        load.wait()

    def early(block, carry):
        slope_ref[block] = nn(grads_ref[block], down_ref[...]).astype(BF)
        return carry

    lax.fori_loop(0, blocks, early, 0)

    def middle(block):
        before = nn(rows_ref[block], up_ref[...])
        share = 0.5 + 0.5 * lax.erf(before * (0.5**0.5))
        hidden_ref[block] = (before * share).astype(BF)
        slope = share + before * (jnp.exp(-0.5 * before * before) * (2.0 * jnp.pi) ** (-0.5))
        slope = (slope_ref[block].astype(F32) * slope).astype(BF)
        slope_ref[block] = slope
        part_a[block] = nt(slope, up_ref[...]).astype(BF)

    first = Scatter(part_a, *scratch)
    x, y, c = gather.spot

    def pair(cx, cy):
        def one(index, carry):
            middle(slot(cx, cy, 0) + index)
            return carry

        lax.fori_loop(0, 2, one, 0)

    gather.own.wait()
    gather.arrived(2, slot(x, y, 1 - c), 0, gather.rows)
    pair(x, y)
    first.pass_core(3)
    gather.relay_y()
    gather.relay_x()
    gather.arrived(6, slot(1 - x, y, 1 - c), 0, gather.rows)
    pair(1 - x, y)
    first.pass_core(1)
    gather.arrived(5, slot(x, 1 - y, 1 - c), 0, gather.rows)
    pair(x, 1 - y)
    first.pass_core(2)
    gather.relay_far()
    first.near()
    gather.arrived(7, slot(1 - x, 1 - y, 1 - c), 0, gather.rows // 2)
    gather.arrived(8, slot(1 - x, 1 - y, 1 - c), gather.rows // 2, gather.rows // 2)
    pair(1 - x, 1 - y)
    first.pass_core(0)
    first.far()
    for copy in gather.sends:
        copy.wait_send()

    def store(block):
        return pltpu.make_async_copy(part_b.at[block], branch_out.at[block], store_sem.at[block])

    def branch(block, carry):
        part_b[block] = nt(hidden_ref[block], down_ref[...]).astype(BF)
        store(block).start()
        return carry

    lax.fori_loop(0, blocks, branch, 0)
    first.second()
    tile = 256

    def weight(left_ref, right_ref, out_ref):
        right = right_ref[...].reshape(-1, right_ref.shape[2])

        def one(index, carry):
            lanes = pl.ds(pl.multiple_of(index * tile, tile), tile)
            left = left_ref[:, :, lanes].reshape(-1, tile)
            out_ref[lanes, :] = tn(left, right).astype(BF)
            return carry

        lax.fori_loop(0, width // tile, one, 0)

    weight(grads_ref, hidden_ref, down_out)
    weight(rows_ref, slope_ref, up_out)
    normed_out[...] = first.total()
    first.finish()
    for block in range(blocks):
        store(block).wait()


def feed_forward(own, grads, w_up, w_down, ident):
    rows, width = own.shape
    hidden = w_up.shape[1]
    outs = (
        shape(rows, width, dtype=F32),
        shape(8, rows, width),
        shape(width, hidden),
        shape(width, hidden),
    )
    scratch = [
        pltpu.VMEM((8, rows, width), BF),
        pltpu.VMEM((8, rows, width), BF),
        pltpu.VMEM((8, rows, hidden), BF),
        pltpu.VMEM((8, rows, hidden), BF),
        pltpu.VMEM((8, rows, width), BF),
        pltpu.VMEM((8, rows, width), BF),
        pltpu.SemaphoreType.DMA((8,)),
        pltpu.SemaphoreType.DMA((8,)),
    ]
    return call(
        feed_kernel,
        "feed_forward",
        outs,
        (IN_VMEM, ANY, IN_VMEM, IN_VMEM),
        [ANY, ANY, IN_VMEM, IN_VMEM],
        scratch + gather_scratch() + Scatter.scratch(rows, width),
        ident,
        70,
    )(own, grads, w_up, w_down)


SIDE = 256


def nt(left, right):
    return lax.dot_general(left, right, (((1,), (1,)), ((), ())), preferred_element_type=F32)


def nn(left, right):
    return lax.dot_general(left, right, (((1,), (0,)), ((), ())), preferred_element_type=F32)


def tn(left, right):
    return lax.dot_general(left, right, (((0,), (0,)), ((), ())), preferred_element_type=F32)


def turn(values):
    return jnp.transpose(values.astype(F32))


def causal(scores):
    keys = lax.broadcasted_iota(jnp.int32, scores.shape, 0)
    queries = lax.broadcasted_iota(jnp.int32, scores.shape, 1)
    return jnp.where(keys <= queries, scores, MASKED)


def forward_kernel(
    rows_ref, w_ref, side_ref, text_in, frames_ref, gain_ref, bias_ref,
    qkv_ref, log_ref, mix_ref, mine_ref, one_ref, two_ref, query_ref, cross_ref, low_ref,
    text_ref, square_ref, plane_out,
    w_own, w_out, w_query, w_cross, sum_ref, two_low_ref, store_sem,
    ex_local, ex_send, ex_recv, *scratch,
):
    enter(plane_others())
    blocks, both, _ = rows_ref.shape
    rows = both // 2
    width = mix_ref.shape[2]
    features = two_low_ref.shape[1]
    heads = width // HEAD_DIM
    length = blocks * rows
    step = SIDE // rows
    depth = side_ref.shape[2]
    for index in range(side_ref.shape[0]):
        lanes = slice(index * depth, (index + 1) * depth)
        for kind in range(3):
            w_own[kind, :, lanes] = side_ref[index, kind * width : (kind + 1) * width]
    weights = (w_out, w_query, w_cross)
    jobs = [Gather(w_own.at[k], weights[k], *scratch[3 * k : 3 * k + 3]) for k in range(3)]
    text_job = Gather(text_in, text_ref, *scratch[9:])
    text_job.start()
    jobs[0].start()
    stores = []

    def keep(kind):
        copy = pltpu.make_async_copy(weights[kind], plane_out.at[kind], store_sem.at[kind])
        copy.start()
        stores.append(copy)

    def project(block, carry):
        qkv_ref[block] = nn(rows_ref[block], w_ref[...]).astype(BF)
        return carry

    lax.fori_loop(0, blocks, project, 0)
    exchange = Exchange(mix_ref, mine_ref, ex_local, ex_send, ex_recv)
    for clip in range(2):
        part = pl.ds(clip * rows, rows)
        for head in range(heads):
            lanes = [pl.ds(j * width + head * HEAD_DIM, HEAD_DIM) for j in range(3)]
            key = qkv_ref[:, part, lanes[1]].reshape(length, HEAD_DIM)
            value = turn(qkv_ref[:, part, lanes[2]].reshape(length, HEAD_DIM)).astype(BF)
            for index in range(length // SIDE):
                spots = pl.ds(index * step, step)
                query = qkv_ref[spots, part, lanes[0]].reshape(SIDE, HEAD_DIM)
                query = query * jnp.asarray(HEAD_DIM ** (-0.5), BF)
                start = index * SIDE
                last = causal(nt(key[start : start + SIDE], query))
                top = jnp.max(last, axis=0, keepdims=True)
                if index:
                    early = nt(key[:start], query)
                    top = jnp.maximum(top, jnp.max(early, axis=0, keepdims=True))
                last = jnp.exp(last - top)
                total = jnp.sum(last, axis=0, keepdims=True)
                mix = nn(value[:, start : start + SIDE], last.astype(BF))
                if index:
                    early = jnp.exp(early - top)
                    total += jnp.sum(early, axis=0, keepdims=True)
                    mix += nn(value[:, :start], early.astype(BF))
                mix = jnp.transpose(mix / total).astype(BF).reshape(step, rows, HEAD_DIM)
                mix_ref[spots, part, pl.ds(head * HEAD_DIM, HEAD_DIM)] = mix
                log_ref[pl.ds(clip * heads + head, 1), pl.ds(start, SIDE)] = top + jnp.log(total)
        exchange.start(clip, part)
        if clip == 0:
            jobs[0].relay_y()
            jobs[0].relay_x()
            jobs[1].start()
    text_job.relay_y()
    text_job.relay_x()
    jobs[0].relay_far()
    jobs[0].finish()
    keep(0)
    exchange.finish()

    def apply(values_ref, kind):
        sum_ref[...] = jnp.zeros_like(sum_ref)

        def one(block, carry):
            sum_ref[...] += nn(values_ref[block], weights[kind][block])
            return carry

        lax.fori_loop(0, blocks, one, 0)

    apply(mine_ref, 0)
    jobs[1].relay_y()
    jobs[1].relay_x()
    jobs[2].start()
    nothing = jnp.zeros((1, features), F32)

    def first(part, sums):
        branch = sum_ref[part]
        total = frames_ref[part].astype(F32) + branch
        one_ref[part] = total
        normed, _ = normalise(total)
        two_low_ref[part] = (normed * gain_ref[1:2] + bias_ref[1:2]).astype(BF)
        return sums + jnp.sum(branch * branch, axis=0, keepdims=True)

    square_one = chunks(both, first, nothing)
    text_job.relay_far()
    text_job.finish()
    jobs[1].relay_far()
    jobs[1].finish()
    keep(1)

    def ask(block, carry):
        query_ref[block] = nt(two_low_ref[...], w_query[block]).astype(BF)
        return carry

    lax.fori_loop(0, blocks, ask, 0)
    texts = text_ref.shape[1] // 4

    def cross(block, carry):
        for clip in range(2):
            part = pl.ds(clip * rows, rows)
            keys = pl.ds(clip * texts, texts)
            values = pl.ds((2 + clip) * texts, texts)
            for head in range(heads):
                here = pl.ds(head * HEAD_DIM, HEAD_DIM)
                query = query_ref[block, part, here] * jnp.asarray(HEAD_DIM ** (-0.5), BF)
                scores = nt(text_ref[block, keys, here], query)
                probs = jnp.exp(scores - jnp.max(scores, axis=0, keepdims=True))
                probs = probs / jnp.sum(probs, axis=0, keepdims=True)
                mix = nn(turn(text_ref[block, values, here]).astype(BF), probs.astype(BF))
                cross_ref[block, part, here] = jnp.transpose(mix).astype(BF)
        return carry

    lax.fori_loop(0, blocks // 2, cross, 0)
    jobs[2].relay_y()
    jobs[2].relay_x()
    lax.fori_loop(blocks // 2, blocks, cross, 0)
    jobs[2].relay_far()
    jobs[2].finish()
    keep(2)
    apply(cross_ref, 2)

    def second(part, sums):
        branch = sum_ref[part]
        total = one_ref[part] + branch
        two_ref[part] = total
        normed, _ = normalise(total)
        low_ref[part] = (normed * gain_ref[2:3] + bias_ref[2:3]).astype(BF)
        return sums + jnp.sum(branch * branch, axis=0, keepdims=True)

    square_two = chunks(both, second, nothing)
    square_ref[...] = jnp.zeros_like(square_ref)
    square_ref[0:1] = square_one
    square_ref[1:2] = square_two
    for copy in stores:
        copy.wait()


def attend_forward(rows, w_qkv, side, text, frames, gain, bias, ident):
    blocks, block, width = rows.shape
    columns = w_qkv.shape[1] // 3
    heads = columns // HEAD_DIM
    heads_shape = shape(blocks, block, columns)
    stream = shape(block, width, dtype=F32)
    return call(
        forward_kernel,
        "attend_forward",
        (
            shape(blocks, block, 3 * columns),
            shape(2 * heads, blocks * block // 2, dtype=F32),
            heads_shape,
            heads_shape,
            stream,
            stream,
            heads_shape,
            heads_shape,
            shape(block, width),
            shape(blocks, *text.shape),
            shape(8, width, dtype=F32),
            shape(3, blocks, columns, width),
        ),
        (IN_VMEM,) * 11 + (ANY,),
        [IN_VMEM] * 3 + [ANY] + [IN_VMEM] * 3,
        [pltpu.VMEM((3, columns, width), BF)]
        + [pltpu.VMEM((blocks, columns, width), BF)] * 3
        + [
            pltpu.VMEM((block, width), F32),
            pltpu.VMEM((block, width), BF),
            pltpu.SemaphoreType.DMA((3,)),
            pltpu.SemaphoreType.DMA((2,)),
            pltpu.SemaphoreType.DMA((2, 7)),
            pltpu.SemaphoreType.DMA((2, 7)),
        ]
        + gather_scratch() * 4,
        ident,
        80,
    )(rows, w_qkv, side, text, frames, gain, bias)


def backward_kernel(
    grad_ref, qkv_ref, mix_ref, log_ref, rows_ref, w_ref, side_ref, text_ref,
    part_out, w_out, side_out, text_out,
    out_ref, part_ref, store_sem, grad_all, query_turned, ex_local, ex_send, ex_recv, *scratch,
):
    enter(plane_others())
    exchange = Exchange(grad_ref, grad_all, ex_local, ex_send, ex_recv)
    blocks, both, width = mix_ref.shape
    rows = both // 2
    heads = width // HEAD_DIM
    length = blocks * rows
    step = SIDE // rows
    for clip in range(2):
        exchange.start(clip, pl.ds(clip * rows, rows))
    size = len(scratch) // 2
    text = LoadedScatter(text_ref, *scratch[size:])
    text.start()
    text.first()
    side = LoadedScatter(side_ref, *scratch[:size])
    side.start()
    side.first()
    for clip in range(2):
        exchange.finish(clip)
        part = pl.ds(clip * rows, rows)
        for head in range(heads):
            lanes = [pl.ds(j * width + head * HEAD_DIM, HEAD_DIM) for j in range(3)]
            query = qkv_ref[:, part, lanes[0]].reshape(length, HEAD_DIM)
            query = query * jnp.asarray(HEAD_DIM ** (-0.5), BF)
            key = qkv_ref[:, part, lanes[1]].reshape(length, HEAD_DIM)
            value = qkv_ref[:, part, lanes[2]].reshape(length, HEAD_DIM)
            key_turned = turn(key).astype(BF)
            here = pl.ds(head * HEAD_DIM, HEAD_DIM)
            grad = grad_all[:, part, here].reshape(length, HEAD_DIM)
            mixed = mix_ref[:, part, here].reshape(length, HEAD_DIM)
            inner = jnp.transpose(grad.astype(F32) * mixed.astype(F32))
            inner = jnp.sum(inner, axis=0, keepdims=True)
            logs = log_ref[pl.ds(clip * heads + head, 1), :]
            for index in range(length // SIDE):
                start = index * SIDE
                spots = pl.ds(index * step, step)
                k_part, v_part = key[start : start + SIDE], value[start : start + SIDE]
                scores = nt(k_part, query[start:])
                first = causal(scores[:, :SIDE])
                if start + SIDE < length:
                    scores = jnp.concatenate([first, scores[:, SIDE:]], axis=1)
                else:
                    scores = first
                weights = jnp.exp(scores - logs[:, start:])
                slopes = nt(v_part, grad[start:])
                slopes = (weights * (slopes - inner[:, start:])).astype(BF)
                grad_key = nn(slopes, query[start:]).astype(BF).reshape(step, rows, HEAD_DIM)
                grad_value = nn(weights.astype(BF), grad[start:]).astype(BF)
                out_ref[spots, part, lanes[1]] = grad_key
                out_ref[spots, part, lanes[2]] = grad_value.reshape(step, rows, HEAD_DIM)
                grad_query = nn(key_turned[:, start : start + SIDE], slopes)
                if index:
                    query_turned[:, start:] += grad_query
                else:
                    query_turned[...] = grad_query
            grad_query = jnp.transpose(query_turned[...]) * HEAD_DIM ** (-0.5)
            grad_query = grad_query.astype(BF).reshape(blocks, rows, HEAD_DIM)
            out_ref[:, part, lanes[0]] = grad_query
        if clip == 0:
            text.second()
            side.second()
    def store(block):
        return pltpu.make_async_copy(part_ref.at[block], part_out.at[block], store_sem.at[block])

    def project(block, carry):
        part_ref[block] = nt(out_ref[block], w_ref[...]).astype(BF)
        store(block).start()
        return carry

    lax.fori_loop(0, blocks, project, 0)
    tile = 256
    right = out_ref[...].reshape(blocks * both, 3 * width)

    def weight(index, carry):
        lanes = pl.ds(pl.multiple_of(index * tile, tile), tile)
        left = rows_ref[:, :, lanes].reshape(blocks * both, tile)
        w_out[lanes, :] = tn(left, right).astype(BF)
        return carry

    lax.fori_loop(0, w_out.shape[0] // tile, weight, 0)
    text_out[...] = text.total()
    side_out[...] = side.total().astype(BF)
    text.finish()
    side.finish()
    for block in range(blocks):
        store(block).wait()


def attend_backward(grad_mix, qkv, mix, logs, rows, weights, side, text, ident):
    blocks, block, columns = mix.shape
    _, side_rows, width = side.shape
    text_shape = text.shape[1:]
    return call(
        backward_kernel,
        "attend_backward",
        (
            shape(blocks, block, width),
            shape(width, 3 * columns),
            shape(side_rows, width),
            shape(*text_shape, dtype=F32),
        ),
        (ANY, IN_VMEM, IN_VMEM, IN_VMEM),
        [ANY] + [IN_VMEM] * 5 + [ANY, ANY],
        [
            pltpu.VMEM((blocks, block, 3 * columns), BF),
            pltpu.VMEM((blocks, block, width), BF),
            pltpu.SemaphoreType.DMA((8,)),
            pltpu.VMEM((blocks, block, columns), BF),
            pltpu.VMEM((HEAD_DIM, blocks * block // 2), F32),
            pltpu.SemaphoreType.DMA((2,)),
            pltpu.SemaphoreType.DMA((2, 7)),
            pltpu.SemaphoreType.DMA((2, 7)),
        ]
        + LoadedScatter.scratch(side_rows, width)
        + LoadedScatter.scratch(*text_shape),
        ident,
        45,
    )(grad_mix, qkv, mix, logs, rows, weights, side, text)


CHUNK = 64


def chunks(rows, body, carry=None):
    def one(index, carry):
        return body(pl.ds(pl.multiple_of(index * CHUNK, CHUNK), CHUNK), carry)

    return lax.fori_loop(0, rows // CHUNK, one, 0 if carry is None else carry)


def normalise(inputs):
    average = jnp.mean(inputs, axis=-1, keepdims=True)
    centred = inputs - average
    rate = lax.rsqrt(jnp.mean(centred * centred, axis=-1, keepdims=True) + EPS)
    return centred * rate, rate


def norm_back(grads, inputs, gain):
    normed, rate = normalise(inputs)
    scaled = grads * gain
    inner = jnp.mean(scaled * normed, axis=-1, keepdims=True)
    result = rate * (scaled - jnp.mean(scaled, axis=-1, keepdims=True) - normed * inner)
    sums = (
        jnp.sum(grads * normed, axis=0, keepdims=True),
        jnp.sum(grads, axis=0, keepdims=True),
    )
    return result, sums


def rows_back_kernel(
    normed_ref, cot_ref, one_ref, two_ref, query_ref, mix_ref, text_ref, my_mix_ref,
    gain_ref, bias_ref, w_ref, branch_ref,
    grad_ref, layer_ref, stats_ref, grad_mix_ref, out_ref, side_ref, text_out,
    w_cross, w_query, w_out, low_ref, two_low_ref, back_ref, grad_cm, grad_cq, w_sem,
    *scratch,
):
    enter(neighbours())
    cross_job = Scatter(w_cross, *scratch[:5])
    query_job = Scatter(w_query, *scratch[5:10])
    branch_job = LoadedScatter(branch_ref, *scratch[10:])
    branch_job.start()
    blocks, columns, width = w_out.shape
    rows = low_ref.shape[0]
    heads = columns // HEAD_DIM
    loads = []
    for index, buffer in ((2, w_cross), (1, w_query), (0, w_out)):
        load = pltpu.make_async_copy(
            w_ref.at[index], buffer, w_sem.at[index]
        )
        load.start()
        loads.append(load)
    nothing = (jnp.zeros((1, width), F32),) * 2

    def third(part, sums):
        back, more = norm_back(normed_ref[part], two_ref[part], gain_ref[2:3])
        total = cot_ref[part].astype(F32) + back
        grad_ref[part] = total
        low_ref[part] = total.astype(BF)
        normed, _ = normalise(one_ref[part])
        two_low_ref[part] = (normed * gain_ref[1:2] + bias_ref[1:2]).astype(BF)
        return sums[0] + more[0], sums[1] + more[1]

    gain_three, shift_three = chunks(rows, third, nothing)
    branch_job.first()
    loads[0].wait()

    def cross_weight(block, carry):
        grad_cm[block] = nt(low_ref[...], w_cross[block]).astype(BF)
        w_cross[block] = tn(mix_ref[block], low_ref[...]).astype(BF)
        return carry

    lax.fori_loop(0, blocks, cross_weight, 0)
    for index in range(4):
        cross_job.pass_core(index)
    half = rows // 2
    texts = text_ref.shape[1] // 4
    loads[1].wait()

    def cross(block, carry):
        for clip in range(2):
            part = pl.ds(clip * half, half)
            keys = pl.ds(clip * texts, texts)
            values = pl.ds((2 + clip) * texts, texts)
            for head in range(heads):
                here = pl.ds(head * HEAD_DIM, HEAD_DIM)
                query = query_ref[block, part, here] * jnp.asarray(HEAD_DIM ** (-0.5), BF)
                key, value = text_ref[block, keys, here], text_ref[block, values, here]
                grad = grad_cm[block, part, here]
                scores = nt(key, query)
                weights = jnp.exp(scores - jnp.max(scores, axis=0, keepdims=True))
                weights = weights / jnp.sum(weights, axis=0, keepdims=True)
                slopes = nt(value, grad)
                inner = jnp.sum(weights * slopes, axis=0, keepdims=True)
                slopes = (weights * (slopes - inner)).astype(BF)
                grad_query = jnp.transpose(nn(turn(key).astype(BF), slopes))
                grad_cq[block, part, here] = (grad_query * HEAD_DIM ** (-0.5)).astype(BF)
                text_out[block, keys, here] = nn(slopes, query).astype(BF)
                text_out[block, values, here] = nn(weights.astype(BF), grad).astype(BF)
        back = nn(grad_cq[block], w_query[block])
        back_ref[...] += back
        w_query[block] = tn(grad_cq[block], two_low_ref[...]).astype(BF)
        return carry

    back_ref[...] = jnp.zeros_like(back_ref)
    lax.fori_loop(0, blocks // 2, cross, 0)
    branch_job.second()
    cross_job.far()
    cross_job.near()
    lax.fori_loop(blocks // 2, blocks, cross, 0)
    for index in range(4):
        query_job.pass_core(index)

    def second(part, sums):
        back, more = norm_back(back_ref[part], one_ref[part], gain_ref[1:2])
        total = grad_ref[part] + back
        grad_ref[part] = total
        low_ref[part] = total.astype(BF)
        return sums[0] + more[0], sums[1] + more[1]

    gain_two, shift_two = chunks(rows, second, nothing)
    cross_job.second()
    query_job.far()
    query_job.near()
    loads[2].wait()

    def out_weight(block, carry):
        grad_mix_ref[block] = nt(low_ref[...], w_out[block]).astype(BF)
        out_ref[block] = tn(my_mix_ref[block], low_ref[...]).astype(BF)
        return carry

    lax.fori_loop(0, blocks, out_weight, 0)
    branch_job.wait()

    def last(part, sums):
        branch = branch_job.value(part)
        total = two_ref[part] + branch
        layer_ref[part] = total.astype(BF)
        return (
            sums[0] + jnp.sum(total * total, axis=0, keepdims=True),
            sums[1] + jnp.sum(branch * branch, axis=0, keepdims=True),
        )

    square_out, square_three = chunks(rows, last, nothing)
    rest = jnp.zeros((1, width), F32)
    for index, row in enumerate(
        (rest, rest, gain_two, shift_two, gain_three, shift_three, square_out, square_three)
    ):
        stats_ref[index : index + 1] = row
    query_job.second()
    side_ref[1] = cross_job.total().astype(BF)
    side_ref[0] = query_job.total().astype(BF)
    branch_job.finish()
    cross_job.finish()
    query_job.finish()


def rows_back(
    normed, cot, one, two, query, mix, text, my_mix, gain, bias, weights, branch, ident
):
    rows, width = cot.shape
    blocks, _, columns = my_mix.shape
    return call(
        rows_back_kernel,
        "rows_back",
        (
            shape(rows, width, dtype=F32),
            shape(rows, width),
            shape(8, width, dtype=F32),
            shape(*my_mix.shape),
            shape(blocks, columns, width),
            shape(2, columns, width),
            shape(*text.shape),
        ),
        (IN_VMEM,) * 7,
        [IN_VMEM] * 10 + [ANY, ANY],
        [pltpu.VMEM((blocks, columns, width), BF)] * 3
        + [
            pltpu.VMEM((rows, width), BF),
            pltpu.VMEM((rows, width), BF),
            pltpu.VMEM((rows, width), F32),
            pltpu.VMEM(my_mix.shape, BF),
            pltpu.VMEM(my_mix.shape, BF),
            pltpu.SemaphoreType.DMA((3,)),
        ]
        + Scatter.scratch(columns, width) * 2
        + LoadedScatter.scratch(rows, width),
        ident,
        65,
    )(normed, cot, one, two, query, mix, text, my_mix, gain, bias, weights, branch)


def last_kernel(
    part_ref, frames_ref, gain_ref, grad_ref, stats_ref, text_ref, qkv_ref, up_ref, down_ref,
    out_ref, total_ref, text_out, qkv_out, up_out, down_out,
    mine, came, all_ref, st_send, st_recv, z_send, z_recv,
    qkv_came, qkv_pair, up_pair, down_pair, q_send, q_recv, x_send, x_recv, *scratch,
):
    z = lax.axis_index("shard")
    shards = lax.axis_size("shard")
    others = [lax.rem(z + i, shards) for i in range(1, shards)]
    spot = place()[1:]
    context = spot[0]
    enter(neighbours() + [device(other, *spot) for other in others])
    size = len(scratch) // 2
    text = LoadedScatter(text_ref, *scratch[size:])
    text.start()
    job = LoadedScatter(part_ref, *scratch[:size])
    job.start()
    sends, moves = [], []
    for index, other in enumerate(others):
        copy = remote_copy(
            qkv_ref.at[other], qkv_came.at[index], q_send.at[index], q_recv.at[index],
            device(other, *spot),
        )
        copy.start()
        moves.append(copy)
    inputs = frames_ref[...].astype(F32)
    average = jnp.mean(inputs, axis=-1, keepdims=True)
    centred = inputs - average
    rate = lax.rsqrt(jnp.mean(centred * centred, axis=-1, keepdims=True) + EPS)
    text.first()
    job.first()
    text.second()
    job.second()
    to_x = neighbours()[0]
    pairs = []
    for index, (source, pair_ref) in enumerate(((up_ref, up_pair), (down_ref, down_pair))):
        copy = remote_copy(source, pair_ref, x_send.at[index], x_recv.at[index], to_x)
        copy.start()
        pairs.append(copy)
    text_out[...] = text.total()
    grads = job.total()
    normed = centred * rate
    mine[0] = stats_ref[...]
    mine[0, 0:1] = jnp.sum(grads * normed, axis=0, keepdims=True)
    mine[0, 1:2] = jnp.sum(grads, axis=0, keepdims=True)
    for index, target in enumerate(reversed(neighbours())):
        copy = remote_copy(
            mine.at[index], came.at[index], st_send.at[index], st_recv.at[index], target
        )
        copy.start()
        sends.append(copy)
        if index == 0:
            scaled = grads * gain_ref[...]
            inner = jnp.mean(scaled * normed, axis=-1, keepdims=True)
            scaled = scaled - jnp.mean(scaled, axis=-1, keepdims=True) - normed * inner
            out_ref[...] = grad_ref[...] + rate * scaled
        copy.wait_recv()
        mine[index + 1] = mine[index] + came[index]
    for index, other in enumerate(others):
        copy = remote_copy(
            mine.at[3], all_ref.at[z], z_send.at[index], z_recv.at[index], device(other, *spot)
        )
        copy.start()
        sends.append(copy)
    all_ref[z] = mine[3]
    total = qkv_ref[z].astype(F32)
    for index, copy in enumerate(moves):
        copy.wait_recv()
        total += qkv_came[index].astype(F32)
    qkv_pair[0] = total.astype(BF)
    copy = remote_copy(qkv_pair.at[0], qkv_pair.at[1], x_send.at[2], x_recv.at[2], to_x)
    copy.start()
    pairs.append(copy)
    for copy in sends[3:]:
        copy.wait_recv()
    total = all_ref[0]
    for index in range(1, shards):
        total += all_ref[index]
    total_ref[...] = total
    half = up_ref.shape[1]
    ours = pl.ds(pl.multiple_of(context * half, half), half)
    theirs = pl.ds(pl.multiple_of((1 - context) * half, half), half)
    for copy, source, pair_ref, target in (
        (pairs[0], up_ref, up_pair, up_out),
        (pairs[1], down_ref, down_pair, down_out),
    ):
        target[:, ours] = source[...].astype(F32)
        copy.wait_recv()
        target[:, theirs] = pair_ref[...].astype(F32)
    pairs[2].wait_recv()
    lead = jnp.where(context == 0, qkv_pair[0], qkv_pair[1]).astype(F32)
    trail = jnp.where(context == 0, qkv_pair[1], qkv_pair[0]).astype(F32)
    width = lead.shape[1] // 3
    for index in range(3):
        lanes = slice(index * width, (index + 1) * width)
        qkv_out[index, :, :width] = lead[:, lanes]
        qkv_out[index, :, width:] = trail[:, lanes]
    for copy in sends + moves + pairs:
        copy.wait_send()
    text.finish()
    job.finish()


def last_step(part, frames, gain, grad, stats, text, qkv, up, down, shards, ident):
    _, rows, width = part.shape
    depth, half = up.shape
    columns = qkv.shape[2]
    return call(
        last_kernel,
        "last_step",
        (
            shape(rows, width, dtype=F32),
            shape(16, width, dtype=F32),
            shape(*text.shape[1:], dtype=F32),
            shape(3, depth, 2 * columns // 3, dtype=F32),
            shape(depth, 2 * half, dtype=F32),
            shape(depth, 2 * half, dtype=F32),
        ),
        (IN_VMEM,) * 6,
        [ANY] + [IN_VMEM] * 4 + [ANY] + [IN_VMEM] * 3,
        [
            pltpu.VMEM((4, 16, width), F32),
            pltpu.VMEM((3, 16, width), F32),
            pltpu.VMEM((shards, 16, width), F32),
            pltpu.SemaphoreType.DMA((3,)),
            pltpu.SemaphoreType.DMA((3,)),
            pltpu.SemaphoreType.DMA((shards - 1,)),
            pltpu.SemaphoreType.DMA((shards - 1,)),
            pltpu.VMEM((shards - 1, depth, columns), BF),
            pltpu.VMEM((2, depth, columns), BF),
            pltpu.VMEM((depth, half), BF),
            pltpu.VMEM((depth, half), BF),
            pltpu.SemaphoreType.DMA((shards - 1,)),
            pltpu.SemaphoreType.DMA((shards - 1,)),
            pltpu.SemaphoreType.DMA((3,)),
            pltpu.SemaphoreType.DMA((3,)),
        ]
        + LoadedScatter.scratch(rows, width)
        + LoadedScatter.scratch(*text.shape[1:]),
        ident,
        65,
    )(part, frames, gain, grad, stats, text, qkv, up, down)


def dots(spec, *operands):
    return jnp.einsum(spec, *operands, preferred_element_type=F32)


def layer_norm(inputs, scaling, offset):
    average = jnp.mean(inputs, axis=-1, keepdims=True)
    centred = inputs - average
    variance = jnp.mean(centred * centred, axis=-1, keepdims=True)
    return centred * lax.rsqrt(variance + EPS) * scaling + offset


def on_device(
    frames,
    text_states,
    cotangent,
    norm_gain,
    norm_bias,
    self_qkv,
    self_out,
    cross_qkv,
    cross_out,
    mlp_up,
    mlp_down,
):
    clips, rows, width = frames.shape
    context = lax.axis_index("context")
    depth = self_qkv.shape[1]
    slices = width // depth
    columns = self_qkv.shape[2] // 2
    heads = columns // HEAD_DIM
    block = clips * rows
    texts = text_states.shape[1]

    def half(weight):
        size = weight.shape[-1] // 2
        return lax.dynamic_slice_in_dim(weight, context * size, size, weight.ndim - 1)

    def over_shard(weight, tiled=True):
        return lax.all_gather(weight, "shard", axis=0, tiled=tiled)

    cross_part = half(cross_qkv)
    side = jnp.concatenate([half(self_out), cross_part[0], half(cross_out)], axis=1)
    w_side = over_shard(side.transpose(1, 0), tiled=False)
    w_text = over_shard(jnp.concatenate([cross_part[1], cross_part[2]], axis=1))
    w_down = over_shard(half(mlp_down))
    w_up = over_shard(half(mlp_up))

    qkv_part = half(self_qkv)
    all_one, all_grad, w_qkv = first_step(
        frames.reshape(block, width),
        norm_gain,
        norm_bias,
        cotangent.reshape(block, width),
        jnp.concatenate([qkv_part[0], qkv_part[1], qkv_part[2]], axis=-1),
        slices,
        0,
    )
    w_qkv = w_qkv.reshape(width, 3 * columns)
    text_part = dots("cnd,de->cne", text_states, w_text).astype(BF)
    text_part = text_part.reshape(clips * texts, 2, columns).transpose(1, 0, 2)
    (
        qkv, self_log, mix, my_mix, stream_one, stream_two, cross_q, cross_mix, norm_three,
        text_all, squares, plane_w,
    ) = attend_forward(
        all_one,
        w_qkv,
        w_side,
        text_part.reshape(2 * clips * texts, columns),
        frames.reshape(block, width),
        norm_gain,
        norm_bias,
        1,
    )

    grad_normed, part_three, grad_up, grad_down = feed_forward(
        norm_three, all_grad, w_up, w_down, 4
    )

    def to_shard(part):
        return lax.psum_scatter(part.astype(BF), "shard", scatter_dimension=0, tiled=True)

    grad_down, grad_up = to_shard(grad_down), to_shard(grad_up)
    grad_one, layer_out, stats, grad_mix, part_out, side, text_grads = rows_back(
        grad_normed,
        cotangent.reshape(block, width),
        stream_one,
        stream_two,
        cross_q,
        cross_mix,
        text_all,
        my_mix,
        norm_gain,
        norm_bias,
        plane_w,
        part_three,
        3,
    )

    def slice_shards(part):
        return part.reshape(-1, slices, depth).transpose(1, 0, 2)

    grad_cross = to_shard(slice_shards(side))
    part_norm, grad_w_qkv, grad_out, text_grads = attend_backward(
        grad_mix, qkv, mix, self_log, all_one, w_qkv, part_out, text_grads, 8
    )
    (
        part_norm, grad_w_qkv, grad_out, text_grads, grad_down, grad_up, grad_cross
    ) = lax.optimization_barrier(
        (part_norm, grad_w_qkv, grad_out, text_grads, grad_down, grad_up, grad_cross)
    )
    text_grads = text_grads.reshape(2, clips, texts, columns).astype(BF)
    text_grads = text_grads.transpose(1, 2, 0, 3).reshape(clips, texts, 2 * columns)
    grad_w_text = to_shard(dots("cnd,cne->de", text_states, text_grads))
    grad_out = to_shard(slice_shards(grad_out))
    grad_text = dots("cne,de->cnd", text_grads, w_text)
    grad_text = grad_text.reshape(clips, 8, texts // 8, width).transpose(1, 0, 2, 3).astype(BF)
    grad_text = grad_text.reshape(8, clips * texts // 8, width)
    grad_frames, totals, grad_text, grad_w_qkv, grad_up, grad_down = last_step(
        part_norm,
        frames.reshape(block, width),
        norm_gain[0][None],
        grad_one,
        jnp.concatenate([stats, squares], axis=0),
        grad_text,
        grad_w_qkv.reshape(slices, depth, 3 * columns),
        grad_up,
        grad_down,
        slices,
        11,
    )
    grad_frames = grad_frames.reshape(clips, rows, width)
    grad_text = grad_text.reshape(clips, texts // 8, width)

    grad_cross, grad_out, grad_w_text, totals = lax.optimization_barrier(
        (grad_cross, grad_out, grad_w_text, totals)
    )
    grad_text_pair = [grad_w_text[None, :, k * columns : (k + 1) * columns] for k in range(2)]
    grad_side = jnp.concatenate([grad_cross, grad_out], axis=1).reshape(3, columns, depth)
    grad_side = jnp.concatenate([grad_side.transpose(0, 2, 1)] + grad_text_pair, axis=0)
    grad_side = lax.all_gather(grad_side, "context", axis=2, tiled=True).astype(F32)
    gains = jnp.stack([totals[0], totals[2], totals[4]])
    shifts = jnp.stack([totals[1], totals[3], totals[5]])
    squares = jnp.stack([totals[j].sum() for j in (6, 8, 9, 7)])
    start = lax.axis_index("shard") * depth
    grad_gain = lax.dynamic_slice_in_dim(gains, start, depth, 1)
    grad_shift = lax.dynamic_slice_in_dim(shifts, start, depth, 1)
    entries = float(clips * rows * width * lax.axis_size(("shard",) + PLANE))
    return (
        layer_out.reshape(clips, rows, width),
        grad_frames,
        grad_text,
        grad_gain,
        grad_shift,
        grad_w_qkv,
        grad_side[2],
        jnp.stack([grad_side[0], grad_side[3], grad_side[4]]),
        grad_side[1],
        grad_up,
        grad_down,
        jnp.sqrt(squares / entries),
    )


def solution(mesh):
    rows = P("shard", PLANE, None)
    stack = P(None, "shard", "tensor")
    flat = P("shard", "tensor")
    return jax.shard_map(
        on_device,
        mesh=mesh,
        in_specs=(rows, P("shard"), rows, P(), P(), stack, flat, stack, flat, flat, flat),
        out_specs=(
            (rows, rows, rows, P(None, "shard"), P(None, "shard"))
            + (stack, flat, stack, flat, flat, flat, P())
        ),
        check_vma=False,
    )
```

```python
from functools import partial

import jax
import jax.numpy as jnp
from jax import lax
from jax.experimental import pallas as pl
from jax.experimental.pallas import tpu as pltpu
from jax.sharding import PartitionSpec as P

HEAD_DIM = 64
EPS = 1e-05
MASKED = -1e30
MESH = pl.DeviceIdType.MESH
BF = jnp.bfloat16
F32 = jnp.float32
PLANE = ("context", "tensor")
VMEM_LIMIT = 60 * 2**20


def place():
    return (
        lax.axis_index("shard"),
        lax.axis_index("context"),
        lax.axis_index("tensor") // 2,
        lax.axis_index("tensor") % 2,
    )


def device(z, x, y, c):
    return (z, x, 2 * y + c)


def slot(x, y, c):
    return 4 * x + 2 * y + c


def neighbours():
    z, x, y, c = place()
    return [device(z, 1 - x, y, c), device(z, x, 1 - y, c), device(z, x, y, 1 - c)]


def plane_spots():
    z, x, y, c = place()
    steps = [(a, b, d) for a in range(2) for b in range(2) for d in range(2) if a + b + d]
    return [((x + a) % 2, (y + b) % 2, (c + d) % 2) for a, b, d in steps]


def plane_others():
    z = lax.axis_index("shard")
    return [device(z, *spot) for spot in plane_spots()]


def enter(targets):
    barrier = pltpu.get_barrier_semaphore()
    for target in targets:
        pl.semaphore_signal(barrier, inc=1, device_id=target, device_id_type=MESH)
    pl.semaphore_wait(barrier, len(targets))


def remote_copy(source, target_ref, send, recv, target):
    return pltpu.make_async_remote_copy(
        src_ref=source,
        dst_ref=target_ref,
        send_sem=send,
        recv_sem=recv,
        device_id=target,
        device_id_type=MESH,
    )


class Gather:
    semaphores = 9

    def __init__(self, in_ref, out_ref, local_sem, send, recv):
        z, x, y, c = place()
        self.in_ref, self.out_ref, self.local_sem = in_ref, out_ref, local_sem
        self.send, self.recv = send, recv
        self.spot = (x, y, c)
        self.to_x, self.to_y, self.to_c = neighbours()
        self.rows = in_ref.shape[0]
        self.sends = []

    def go(self, index, owner, start, size, target, source=None):
        there = self.out_ref.at[owner, pl.ds(start, size)]
        copy = remote_copy(
            there if source is None else source,
            there,
            self.send.at[index],
            self.recv.at[index],
            target,
        )
        copy.start()
        self.sends.append(copy)

    def arrived(self, index, owner, start, size):
        there = self.out_ref.at[owner, pl.ds(start, size)]
        remote_copy(
            there, there, self.send.at[index], self.recv.at[index], self.to_x
        ).wait_recv()

    def start(self):
        me = slot(*self.spot)
        self.own = pltpu.make_async_copy(self.in_ref, self.out_ref.at[me], self.local_sem)
        self.own.start()
        for index, target in enumerate((self.to_x, self.to_y, self.to_c)):
            self.go(index, me, 0, self.rows, target, self.in_ref)

    def relay_y(self):
        x, y, c = self.spot
        owner = slot(x, 1 - y, c)
        self.arrived(1, owner, 0, self.rows)
        self.go(3, owner, 0, self.rows // 2, self.to_x)
        self.go(5, owner, 0, self.rows, self.to_c)

    def relay_x(self):
        x, y, c = self.spot
        half = self.rows // 2
        owner = slot(1 - x, y, c)
        self.arrived(0, owner, 0, self.rows)
        self.go(4, owner, half, half, self.to_y)
        self.go(6, owner, 0, self.rows, self.to_c)

    def relay_far(self):
        x, y, c = self.spot
        half = self.rows // 2
        owner = slot(1 - x, 1 - y, c)
        self.arrived(3, owner, 0, half)
        self.go(7, owner, 0, half, self.to_c)
        self.arrived(4, owner, half, half)
        self.go(8, owner, half, half, self.to_c)

    def finish(self):
        x, y, c = self.spot
        half = self.rows // 2
        self.arrived(2, slot(x, y, 1 - c), 0, self.rows)
        self.arrived(5, slot(x, 1 - y, 1 - c), 0, self.rows)
        self.arrived(6, slot(1 - x, y, 1 - c), 0, self.rows)
        self.arrived(7, slot(1 - x, 1 - y, 1 - c), 0, half)
        self.arrived(8, slot(1 - x, 1 - y, 1 - c), half, half)
        self.own.wait()
        for copy in self.sends:
            copy.wait_send()

    def rest(self):
        self.relay_y()
        self.relay_x()
        self.relay_far()
        self.finish()


class Scatter:
    @staticmethod
    def scratch(rows, columns):
        return [
            pltpu.VMEM((4, rows, columns), BF),
            pltpu.VMEM((2, rows // 2, columns), BF),
            pltpu.VMEM((2, rows, columns), BF),
            pltpu.SemaphoreType.DMA((10,)),
            pltpu.SemaphoreType.DMA((10,)),
        ]

    def __init__(self, part_ref, core, relay, final, send, recv):
        self.part_ref, self.core, self.relay, self.final = part_ref, core, relay, final
        self.send, self.recv = send, recv
        self.to_x, self.to_y, self.to_c = neighbours()
        z, x, y, c = place()
        chips = ((1 - x, 1 - y), (1 - x, y), (x, 1 - y), (x, y))
        self.mine = [slot(*chip, c) for chip in chips]
        self.theirs = [slot(*chip, 1 - c) for chip in chips]
        rows = part_ref.shape[1]
        self.low, self.high = pl.ds(0, rows // 2), pl.ds(rows // 2, rows // 2)
        self.sends = []

    def forward(self, index, source, target_ref, target):
        copy = remote_copy(
            source, target_ref, self.send.at[index], self.recv.at[index], target
        )
        copy.start()
        self.sends.append(copy)

    def arrived(self, index, ref):
        remote_copy(ref, ref, self.send.at[index], self.recv.at[index], self.to_c).wait_recv()

    def pass_core(self, index):
        source = self.part_ref.at[self.theirs[index]]
        self.forward(index, source, self.core.at[index], self.to_c)

    def add(self, index, part, more=None):
        mine = self.mine[index]
        total = self.part_ref[mine, part].astype(F32) + self.core[index, part].astype(F32)
        if more is not None:
            total += more.astype(F32)
        self.part_ref[mine, part] = total.astype(BF)
        return self.part_ref.at[mine, part]

    def far(self):
        self.arrived(0, self.core.at[0])
        self.forward(4, self.add(0, self.low), self.relay.at[0], self.to_x)
        self.forward(5, self.add(0, self.high), self.relay.at[1], self.to_y)

    def near(self):
        self.arrived(1, self.core.at[1])
        self.forward(6, self.add(1, self.low), self.final.at[0, self.low], self.to_x)
        self.arrived(2, self.core.at[2])
        self.forward(7, self.add(2, self.high), self.final.at[1, self.high], self.to_y)

    def second(self):
        low, high, final, relay = self.low, self.high, self.final, self.relay
        self.arrived(5, relay.at[1])
        self.forward(8, self.add(1, high, relay[1]), final.at[0, high], self.to_x)
        self.arrived(4, relay.at[0])
        self.forward(9, self.add(2, low, relay[0]), final.at[1, low], self.to_y)

    def wait(self):
        self.arrived(3, self.core.at[3])
        self.arrived(6, self.final.at[0, self.low])
        self.arrived(7, self.final.at[1, self.high])
        self.arrived(8, self.final.at[0, self.high])
        self.arrived(9, self.final.at[1, self.low])

    def value(self, part=slice(None)):
        total = self.part_ref[self.mine[3], part].astype(F32) + self.core[3, part].astype(F32)
        return total + self.final[0, part].astype(F32) + self.final[1, part].astype(F32)

    def total(self):
        self.wait()
        return self.value()

    def finish(self):
        for copy in self.sends:
            copy.wait_send()


class LoadedScatter(Scatter):
    @staticmethod
    def scratch(rows, columns):
        return [
            pltpu.VMEM((4, rows, columns), BF),
            pltpu.SemaphoreType.DMA((4,)),
        ] + Scatter.scratch(rows, columns)

    def __init__(self, in_ref, part_ref, local_sem, *scratch):
        super().__init__(part_ref, *scratch)
        self.in_ref, self.local_sem = in_ref, local_sem

    def start(self):
        self.loads = []
        for index, (mine, theirs) in enumerate(zip(self.mine, self.theirs)):
            source = self.in_ref.at[theirs]
            self.forward(index, source, self.core.at[index], self.to_c)
            load = pltpu.make_async_copy(
                self.in_ref.at[mine], self.part_ref.at[index], self.local_sem.at[index]
            )
            load.start()
            self.loads.append(load)
        self.mine = (0, 1, 2, 3)

    def first(self):
        for load in self.loads:
            load.wait()
        self.far()
        self.near()


class Exchange:
    def __init__(self, in_ref, out_ref, local_sem, send, recv):
        self.in_ref, self.out_ref, self.local_sem = in_ref, out_ref, local_sem
        self.send, self.recv = send, recv
        z, x, y, c = place()
        self.me = slot(x, y, c)
        self.copies = []

    def start(self, piece, part):
        z = lax.axis_index("shard")
        own = pltpu.make_async_copy(
            self.in_ref.at[self.me, part], self.out_ref.at[self.me, part], self.local_sem.at[piece]
        )
        own.start()
        self.copies.append(own)
        for index, spot in enumerate(plane_spots()):
            copy = remote_copy(
                self.in_ref.at[slot(*spot), part],
                self.out_ref.at[self.me, part],
                self.send.at[piece, index],
                self.recv.at[piece, index],
                device(z, *spot),
            )
            copy.start()
            self.copies.append(copy)

    def finish(self, piece=None):
        copies = self.copies if piece is None else self.copies[8 * piece : 8 * piece + 8]
        for copy in copies:
            copy.wait()


ANY = pl.BlockSpec(memory_space=pl.ANY)
IN_VMEM = pl.BlockSpec(memory_space=pltpu.VMEM)


def call(kernel, name, outs, out_specs, in_specs, scratch, ident, micros):
    return pl.pallas_call(
        kernel,
        out_shape=outs,
        in_specs=in_specs,
        out_specs=out_specs,
        scratch_shapes=scratch,
        name=name,
        cost_estimate=pl.CostEstimate(
            flops=micros * 10**9, bytes_accessed=micros * 10**6, transcendentals=0
        ),
        compiler_params=pltpu.CompilerParams(
            collective_id=ident, has_side_effects=True, vmem_limit_bytes=VMEM_LIMIT
        ),
    )


def shape(*dims, dtype=BF):
    return jax.ShapeDtypeStruct(dims, dtype)


def gather_scratch():
    return [
        pltpu.SemaphoreType.DMA,
        pltpu.SemaphoreType.DMA((9,)),
        pltpu.SemaphoreType.DMA((9,)),
    ]


def shard_others():
    z, shards = lax.axis_index("shard"), lax.axis_size("shard")
    return [lax.rem(z + i, shards) for i in range(1, shards)]


def spread(source_of, target_ref, send, recv, others, spot):
    z = lax.axis_index("shard")
    copies = []
    for index, other in enumerate(others):
        copy = remote_copy(
            source_of(other), target_ref.at[z], send.at[index], recv.at[index],
            device(other, *spot),
        )
        copy.start()
        copies.append(copy)
    return copies


def first_kernel(
    frames_ref, gain_ref, bias_ref, cot_ref, w_ref, text_ref, w_text_ref,
    rows_out, cot_out, w_out, text_all, text_out,
    normed_ref, part_ref, came_ref, sems, sends, recvs, *scratch,
):
    z = lax.axis_index("shard")
    spot = place()[1:]
    others = shard_others()
    enter(neighbours() + [device(other, *spot) for other in others])
    own = pltpu.make_async_copy(w_ref, w_out.at[z], sems.at[0])
    own.start()
    texts = spread(lambda other: text_ref.at[other], text_all, sends.at[0], recvs.at[0], others, spot)
    copies = spread(lambda other: w_ref, w_out, sends.at[1], recvs.at[1], others, spot)
    text_all[z] = text_ref[z]

    def norm(part, carry):
        normed, _ = normalise(frames_ref[part].astype(F32))
        normed_ref[part] = (normed * gain_ref[0:1] + bias_ref[0:1]).astype(BF)
        return carry

    chunks(frames_ref.shape[0], norm)
    rows, grads = Gather(normed_ref, rows_out, *scratch[:3]), Gather(cot_ref, cot_out, *scratch[3:])
    rows.start()
    for copy in texts:
        copy.wait_recv()

    def share(index, carry):
        part_ref[index] = nn(text_all[index], w_text_ref[...]).astype(BF)
        return carry

    lax.fori_loop(0, text_all.shape[0], share, 0)
    parts = spread(lambda other: part_ref.at[other], came_ref, sends.at[2], recvs.at[2], others, spot)
    came_ref[z] = part_ref[z]
    rows.relay_y()
    rows.relay_x()
    grads.start()
    for copy in parts:
        copy.wait_recv()
    total = came_ref[0].astype(F32)
    for index in range(1, came_ref.shape[0]):
        total += came_ref[index].astype(F32)
    text_out[...] = total.astype(BF)
    rows.relay_far()
    rows.finish()
    grads.rest()
    own.wait()
    for copy in copies:
        copy.wait_recv()
    for copy in texts + copies + parts:
        copy.wait_send()


def first_step(frames, gain, bias, cotangent, w_qkv, text, w_text, ident):
    rows, width = frames.shape
    shards, texts, depth = text.shape
    return call(
        first_kernel,
        "first_step",
        (
            shape(8, rows, width),
            shape(8, rows, width),
            shape(shards, *w_qkv.shape),
            shape(shards, texts, depth),
            shape(texts, w_text.shape[1]),
        ),
        (ANY, ANY, ANY, IN_VMEM, IN_VMEM),
        [IN_VMEM, IN_VMEM, IN_VMEM, ANY, ANY, IN_VMEM, IN_VMEM],
        [
            pltpu.VMEM((rows, width), BF),
            pltpu.VMEM((shards, texts, w_text.shape[1]), BF),
            pltpu.VMEM((shards, texts, w_text.shape[1]), BF),
            pltpu.SemaphoreType.DMA((1,)),
            pltpu.SemaphoreType.DMA((3, shards - 1)),
            pltpu.SemaphoreType.DMA((3, shards - 1)),
        ]
        + gather_scratch() * 2,
        ident,
        60,
    )(frames, gain, bias, cotangent, w_qkv, text, w_text)


def feed_kernel(
    own_ref, grad_ref, up_ref, down_ref,
    normed_out, branch_out, up_out, down_out,
    rows_ref, grads_ref, hidden_ref, slope_ref, part_a, part_b,
    load_sem, store_sem, g_local, g_send, g_recv, *scratch,
):
    enter(neighbours())
    gather = Gather(own_ref, rows_ref, g_local, g_send, g_recv)
    gather.start()
    blocks, _, width = rows_ref.shape
    loads = []
    for block in range(blocks):
        load = pltpu.make_async_copy(grad_ref.at[block], grads_ref.at[block], load_sem.at[block])
        load.start()
        loads.append(load)
    for load in loads:
        load.wait()

    def early(block, carry):
        slope_ref[block] = nn(grads_ref[block], down_ref[...]).astype(BF)
        return carry

    lax.fori_loop(0, blocks, early, 0)

    def middle(block):
        before = nn(rows_ref[block], up_ref[...])
        share = 0.5 + 0.5 * lax.erf(before * (0.5**0.5))
        hidden_ref[block] = (before * share).astype(BF)
        slope = share + before * (jnp.exp(-0.5 * before * before) * (2.0 * jnp.pi) ** (-0.5))
        slope = (slope_ref[block].astype(F32) * slope).astype(BF)
        slope_ref[block] = slope
        part_a[block] = nt(slope, up_ref[...]).astype(BF)

    first = Scatter(part_a, *scratch)
    x, y, c = gather.spot

    def pair(cx, cy):
        def one(index, carry):
            middle(slot(cx, cy, 0) + index)
            return carry

        lax.fori_loop(0, 2, one, 0)

    gather.own.wait()
    gather.arrived(2, slot(x, y, 1 - c), 0, gather.rows)
    pair(x, y)
    first.pass_core(3)
    gather.relay_y()
    gather.relay_x()
    gather.arrived(6, slot(1 - x, y, 1 - c), 0, gather.rows)
    pair(1 - x, y)
    first.pass_core(1)
    gather.arrived(5, slot(x, 1 - y, 1 - c), 0, gather.rows)
    pair(x, 1 - y)
    first.pass_core(2)
    gather.relay_far()
    first.near()
    gather.arrived(7, slot(1 - x, 1 - y, 1 - c), 0, gather.rows // 2)
    gather.arrived(8, slot(1 - x, 1 - y, 1 - c), gather.rows // 2, gather.rows // 2)
    pair(1 - x, 1 - y)
    first.pass_core(0)
    first.far()
    for copy in gather.sends:
        copy.wait_send()

    def store(block):
        return pltpu.make_async_copy(part_b.at[block], branch_out.at[block], store_sem.at[block])

    def branch(block, carry):
        part_b[block] = nt(hidden_ref[block], down_ref[...]).astype(BF)
        store(block).start()
        return carry

    lax.fori_loop(0, blocks, branch, 0)
    first.second()
    tile = 256

    def weight(left_ref, right_ref, out_ref):
        right = right_ref[...].reshape(-1, right_ref.shape[2])

        def one(index, carry):
            lanes = pl.ds(pl.multiple_of(index * tile, tile), tile)
            left = left_ref[:, :, lanes].reshape(-1, tile)
            out_ref[lanes, :] = tn(left, right).astype(BF)
            return carry

        lax.fori_loop(0, width // tile, one, 0)

    weight(grads_ref, hidden_ref, down_out)
    weight(rows_ref, slope_ref, up_out)
    normed_out[...] = first.total()
    first.finish()
    for block in range(blocks):
        store(block).wait()


def feed_forward(own, grads, w_up, w_down, ident):
    rows, width = own.shape
    hidden = w_up.shape[1]
    outs = (
        shape(rows, width, dtype=F32),
        shape(8, rows, width),
        shape(width, hidden),
        shape(width, hidden),
    )
    scratch = [
        pltpu.VMEM((8, rows, width), BF),
        pltpu.VMEM((8, rows, width), BF),
        pltpu.VMEM((8, rows, hidden), BF),
        pltpu.VMEM((8, rows, hidden), BF),
        pltpu.VMEM((8, rows, width), BF),
        pltpu.VMEM((8, rows, width), BF),
        pltpu.SemaphoreType.DMA((8,)),
        pltpu.SemaphoreType.DMA((8,)),
    ]
    return call(
        feed_kernel,
        "feed_forward",
        outs,
        (IN_VMEM, ANY, IN_VMEM, IN_VMEM),
        [ANY, ANY, IN_VMEM, IN_VMEM],
        scratch + gather_scratch() + Scatter.scratch(rows, width),
        ident,
        70,
    )(own, grads, w_up, w_down)


SIDE = 256


def nt(left, right):
    return lax.dot_general(left, right, (((1,), (1,)), ((), ())), preferred_element_type=F32)


def nn(left, right):
    return lax.dot_general(left, right, (((1,), (0,)), ((), ())), preferred_element_type=F32)


def tn(left, right):
    return lax.dot_general(left, right, (((0,), (0,)), ((), ())), preferred_element_type=F32)


def turn(values):
    return jnp.transpose(values.astype(F32))


def causal(scores):
    keys = lax.broadcasted_iota(jnp.int32, scores.shape, 0)
    queries = lax.broadcasted_iota(jnp.int32, scores.shape, 1)
    return jnp.where(keys <= queries, scores, MASKED)


def forward_kernel(
    rows_ref, w_ref, side_ref, text_in, frames_ref, gain_ref, bias_ref,
    qkv_ref, log_ref, mix_ref, mine_ref, one_ref, two_ref, query_ref, cross_ref, low_ref,
    text_ref, square_ref, plane_out,
    w_own, w_out, w_query, w_cross, sum_ref, two_low_ref, store_sem,
    ex_local, ex_send, ex_recv, *scratch,
):
    enter(plane_others())
    blocks, both, _ = rows_ref.shape
    rows = both // 2
    width = mix_ref.shape[2]
    features = two_low_ref.shape[1]
    heads = width // HEAD_DIM
    length = blocks * rows
    step = SIDE // rows
    depth = side_ref.shape[2]
    for index in range(side_ref.shape[0]):
        lanes = slice(index * depth, (index + 1) * depth)
        for kind in range(3):
            w_own[kind, :, lanes] = side_ref[index, kind * width : (kind + 1) * width]
    weights = (w_out, w_query, w_cross)
    jobs = [Gather(w_own.at[k], weights[k], *scratch[3 * k : 3 * k + 3]) for k in range(3)]
    text_job = Gather(text_in, text_ref, *scratch[9:])
    text_job.start()
    jobs[0].start()
    stores = []

    def keep(kind):
        copy = pltpu.make_async_copy(weights[kind], plane_out.at[kind], store_sem.at[kind])
        copy.start()
        stores.append(copy)

    def project(block, carry):
        qkv_ref[block] = nn(rows_ref[block], w_ref[...]).astype(BF)
        return carry

    lax.fori_loop(0, blocks, project, 0)
    exchange = Exchange(mix_ref, mine_ref, ex_local, ex_send, ex_recv)
    for clip in range(2):
        part = pl.ds(clip * rows, rows)
        for head in range(heads):
            lanes = [pl.ds(j * width + head * HEAD_DIM, HEAD_DIM) for j in range(3)]
            key = qkv_ref[:, part, lanes[1]].reshape(length, HEAD_DIM)
            value = turn(qkv_ref[:, part, lanes[2]].reshape(length, HEAD_DIM)).astype(BF)
            for index in range(length // SIDE):
                spots = pl.ds(index * step, step)
                query = qkv_ref[spots, part, lanes[0]].reshape(SIDE, HEAD_DIM)
                query = query * jnp.asarray(HEAD_DIM ** (-0.5), BF)
                start = index * SIDE
                last = causal(nt(key[start : start + SIDE], query))
                top = jnp.max(last, axis=0, keepdims=True)
                if index:
                    early = nt(key[:start], query)
                    top = jnp.maximum(top, jnp.max(early, axis=0, keepdims=True))
                last = jnp.exp(last - top)
                total = jnp.sum(last, axis=0, keepdims=True)
                mix = nn(value[:, start : start + SIDE], last.astype(BF))
                if index:
                    early = jnp.exp(early - top)
                    total += jnp.sum(early, axis=0, keepdims=True)
                    mix += nn(value[:, :start], early.astype(BF))
                mix = jnp.transpose(mix / total).astype(BF).reshape(step, rows, HEAD_DIM)
                mix_ref[spots, part, pl.ds(head * HEAD_DIM, HEAD_DIM)] = mix
                log_ref[pl.ds(clip * heads + head, 1), pl.ds(start, SIDE)] = top + jnp.log(total)
        exchange.start(clip, part)
        if clip == 0:
            jobs[0].relay_y()
            jobs[0].relay_x()
            text_job.relay_y()
            text_job.relay_x()
    jobs[1].start()
    jobs[0].relay_far()
    text_job.relay_far()
    jobs[0].finish()
    text_job.finish()
    keep(0)
    exchange.finish()

    def apply(values_ref, kind):
        sum_ref[...] = jnp.zeros_like(sum_ref)

        def one(block, carry):
            sum_ref[...] += nn(values_ref[block], weights[kind][block])
            return carry

        lax.fori_loop(0, blocks, one, 0)

    apply(mine_ref, 0)
    nothing = jnp.zeros((1, features), F32)

    def first(part, sums):
        branch = sum_ref[part]
        total = frames_ref[part].astype(F32) + branch
        one_ref[part] = total
        normed, _ = normalise(total)
        two_low_ref[part] = (normed * gain_ref[1:2] + bias_ref[1:2]).astype(BF)
        return sums + jnp.sum(branch * branch, axis=0, keepdims=True)

    square_one = chunks(both, first, nothing)
    jobs[1].relay_y()
    jobs[1].relay_x()
    jobs[2].start()
    jobs[1].relay_far()
    jobs[1].finish()
    keep(1)

    def ask(block, carry):
        query_ref[block] = nt(two_low_ref[...], w_query[block]).astype(BF)
        return carry

    lax.fori_loop(0, blocks, ask, 0)
    texts = text_ref.shape[1] // 2

    def cross(block, carry):
        for clip in range(2):
            part = pl.ds(clip * rows, rows)
            keys = pl.ds(clip * texts, texts)
            for head in range(heads):
                here = pl.ds(head * HEAD_DIM, HEAD_DIM)
                query = query_ref[block, part, here] * jnp.asarray(HEAD_DIM ** (-0.5), BF)
                there = pl.ds(width + head * HEAD_DIM, HEAD_DIM)
                scores = nt(text_ref[block, keys, here], query)
                probs = jnp.exp(scores - jnp.max(scores, axis=0, keepdims=True))
                probs = probs / jnp.sum(probs, axis=0, keepdims=True)
                mix = nn(turn(text_ref[block, keys, there]).astype(BF), probs.astype(BF))
                cross_ref[block, part, here] = jnp.transpose(mix).astype(BF)
        return carry

    lax.fori_loop(0, blocks // 2, cross, 0)
    jobs[2].relay_y()
    jobs[2].relay_x()
    lax.fori_loop(blocks // 2, blocks, cross, 0)
    jobs[2].relay_far()
    jobs[2].finish()
    keep(2)
    apply(cross_ref, 2)

    def second(part, sums):
        branch = sum_ref[part]
        total = one_ref[part] + branch
        two_ref[part] = total
        normed, _ = normalise(total)
        low_ref[part] = (normed * gain_ref[2:3] + bias_ref[2:3]).astype(BF)
        return sums + jnp.sum(branch * branch, axis=0, keepdims=True)

    square_two = chunks(both, second, nothing)
    square_ref[...] = jnp.zeros_like(square_ref)
    square_ref[0:1] = square_one
    square_ref[1:2] = square_two
    for copy in stores:
        copy.wait()


def attend_forward(rows, w_qkv, side, text, frames, gain, bias, ident):
    blocks, block, width = rows.shape
    columns = w_qkv.shape[1] // 3
    heads = columns // HEAD_DIM
    heads_shape = shape(blocks, block, columns)
    stream = shape(block, width, dtype=F32)
    return call(
        forward_kernel,
        "attend_forward",
        (
            shape(blocks, block, 3 * columns),
            shape(2 * heads, blocks * block // 2, dtype=F32),
            heads_shape,
            heads_shape,
            stream,
            stream,
            heads_shape,
            heads_shape,
            shape(block, width),
            shape(blocks, *text.shape),
            shape(8, width, dtype=F32),
            shape(3, blocks, columns, width),
        ),
        (IN_VMEM,) * 11 + (ANY,),
        [IN_VMEM] * 3 + [ANY] + [IN_VMEM] * 3,
        [pltpu.VMEM((3, columns, width), BF)]
        + [pltpu.VMEM((blocks, columns, width), BF)] * 3
        + [
            pltpu.VMEM((block, width), F32),
            pltpu.VMEM((block, width), BF),
            pltpu.SemaphoreType.DMA((3,)),
            pltpu.SemaphoreType.DMA((2,)),
            pltpu.SemaphoreType.DMA((2, 7)),
            pltpu.SemaphoreType.DMA((2, 7)),
        ]
        + gather_scratch() * 4,
        ident,
        80,
    )(rows, w_qkv, side, text, frames, gain, bias)


def beside(own_ref, copy, other_ref, out_ref):
    half = own_ref.shape[1]
    context = lax.axis_index("context")
    out_ref[:, pl.ds(pl.multiple_of(context * half, half), half)] = own_ref[...].astype(F32)
    copy.wait_recv()
    there = pl.ds(pl.multiple_of((1 - context) * half, half), half)
    out_ref[:, there] = other_ref[...].astype(F32)


def backward_kernel(
    grad_ref, qkv_ref, mix_ref, log_ref, rows_ref, w_ref, side_ref, text_ref, down_ref,
    part_out, w_out, side_out, text_out, down_out,
    out_ref, part_ref, store_sem, down_pair, pair_sem, grad_all, query_turned, ex_local, ex_send, ex_recv, *scratch,
):
    enter(plane_others())
    exchange = Exchange(grad_ref, grad_all, ex_local, ex_send, ex_recv)
    blocks, both, width = mix_ref.shape
    rows = both // 2
    heads = width // HEAD_DIM
    length = blocks * rows
    step = SIDE // rows
    for clip in range(2):
        exchange.start(clip, pl.ds(clip * rows, rows))
    size = len(scratch) // 2
    text = LoadedScatter(text_ref, *scratch[size:])
    text.start()
    text.first()
    side = LoadedScatter(side_ref, *scratch[:size])
    side.start()
    side.first()
    for clip in range(2):
        exchange.finish(clip)
        part = pl.ds(clip * rows, rows)
        for head in range(heads):
            lanes = [pl.ds(j * width + head * HEAD_DIM, HEAD_DIM) for j in range(3)]
            query = qkv_ref[:, part, lanes[0]].reshape(length, HEAD_DIM)
            query = query * jnp.asarray(HEAD_DIM ** (-0.5), BF)
            key = qkv_ref[:, part, lanes[1]].reshape(length, HEAD_DIM)
            value = qkv_ref[:, part, lanes[2]].reshape(length, HEAD_DIM)
            key_turned = turn(key).astype(BF)
            here = pl.ds(head * HEAD_DIM, HEAD_DIM)
            grad = grad_all[:, part, here].reshape(length, HEAD_DIM)
            mixed = mix_ref[:, part, here].reshape(length, HEAD_DIM)
            inner = jnp.transpose(grad.astype(F32) * mixed.astype(F32))
            inner = jnp.sum(inner, axis=0, keepdims=True)
            logs = log_ref[pl.ds(clip * heads + head, 1), :]
            for index in range(length // SIDE):
                start = index * SIDE
                spots = pl.ds(index * step, step)
                k_part, v_part = key[start : start + SIDE], value[start : start + SIDE]
                scores = nt(k_part, query[start:])
                first = causal(scores[:, :SIDE])
                if start + SIDE < length:
                    scores = jnp.concatenate([first, scores[:, SIDE:]], axis=1)
                else:
                    scores = first
                weights = jnp.exp(scores - logs[:, start:])
                slopes = nt(v_part, grad[start:])
                slopes = (weights * (slopes - inner[:, start:])).astype(BF)
                grad_key = nn(slopes, query[start:]).astype(BF).reshape(step, rows, HEAD_DIM)
                grad_value = nn(weights.astype(BF), grad[start:]).astype(BF)
                out_ref[spots, part, lanes[1]] = grad_key
                out_ref[spots, part, lanes[2]] = grad_value.reshape(step, rows, HEAD_DIM)
                grad_query = nn(key_turned[:, start : start + SIDE], slopes)
                if index:
                    query_turned[:, start:] += grad_query
                else:
                    query_turned[...] = grad_query
            grad_query = jnp.transpose(query_turned[...]) * HEAD_DIM ** (-0.5)
            grad_query = grad_query.astype(BF).reshape(blocks, rows, HEAD_DIM)
            out_ref[:, part, lanes[0]] = grad_query
        if clip == 0:
            text.second()
            side.second()
            to_x = neighbours()[0]
            pair = remote_copy(down_ref, down_pair, pair_sem.at[0], pair_sem.at[1], to_x)
            pair.start()

    def store(block):
        return pltpu.make_async_copy(part_ref.at[block], part_out.at[block], store_sem.at[block])

    def project(block, carry):
        part_ref[block] = nt(out_ref[block], w_ref[...]).astype(BF)
        store(block).start()
        return carry

    lax.fori_loop(0, blocks, project, 0)
    tile = 256
    right = out_ref[...].reshape(blocks * both, 3 * width)

    def weight(index, carry):
        lanes = pl.ds(pl.multiple_of(index * tile, tile), tile)
        left = rows_ref[:, :, lanes].reshape(blocks * both, tile)
        w_out[lanes, :] = tn(left, right).astype(BF)
        return carry

    lax.fori_loop(0, w_out.shape[0] // tile, weight, 0)
    text_out[...] = text.total().astype(BF)
    side_out[...] = side.total().astype(BF)
    text.finish()
    side.finish()
    beside(down_ref, pair, down_pair, down_out)
    pair.wait_send()
    for block in range(blocks):
        store(block).wait()


def attend_backward(grad_mix, qkv, mix, logs, rows, weights, side, text, down, ident):
    blocks, block, columns = mix.shape
    _, side_rows, width = side.shape
    text_shape = text.shape[1:]
    return call(
        backward_kernel,
        "attend_backward",
        (
            shape(blocks, block, width),
            shape(width, 3 * columns),
            shape(side_rows, width),
            shape(*text_shape),
            shape(down.shape[0], 2 * down.shape[1], dtype=F32),
        ),
        (ANY, IN_VMEM, IN_VMEM, IN_VMEM, IN_VMEM),
        [ANY] + [IN_VMEM] * 5 + [ANY, ANY, IN_VMEM],
        [
            pltpu.VMEM((blocks, block, 3 * columns), BF),
            pltpu.VMEM((blocks, block, width), BF),
            pltpu.SemaphoreType.DMA((8,)),
            pltpu.VMEM(down.shape, BF),
            pltpu.SemaphoreType.DMA((2,)),
            pltpu.VMEM((blocks, block, columns), BF),
            pltpu.VMEM((HEAD_DIM, blocks * block // 2), F32),
            pltpu.SemaphoreType.DMA((2,)),
            pltpu.SemaphoreType.DMA((2, 7)),
            pltpu.SemaphoreType.DMA((2, 7)),
        ]
        + LoadedScatter.scratch(side_rows, width)
        + LoadedScatter.scratch(*text_shape),
        ident,
        1,
    )(grad_mix, qkv, mix, logs, rows, weights, side, text, down)


CHUNK = 64


def chunks(rows, body, carry=None):
    def one(index, carry):
        return body(pl.ds(pl.multiple_of(index * CHUNK, CHUNK), CHUNK), carry)

    return lax.fori_loop(0, rows // CHUNK, one, 0 if carry is None else carry)


def normalise(inputs):
    average = jnp.mean(inputs, axis=-1, keepdims=True)
    centred = inputs - average
    rate = lax.rsqrt(jnp.mean(centred * centred, axis=-1, keepdims=True) + EPS)
    return centred * rate, rate


def norm_back(grads, inputs, gain):
    normed, rate = normalise(inputs)
    scaled = grads * gain
    inner = jnp.mean(scaled * normed, axis=-1, keepdims=True)
    result = rate * (scaled - jnp.mean(scaled, axis=-1, keepdims=True) - normed * inner)
    sums = (
        jnp.sum(grads * normed, axis=0, keepdims=True),
        jnp.sum(grads, axis=0, keepdims=True),
    )
    return result, sums


def rows_back_kernel(
    normed_ref, cot_ref, one_ref, two_ref, query_ref, mix_ref, text_ref, my_mix_ref,
    gain_ref, bias_ref, w_ref, branch_ref, up_ref,
    grad_ref, layer_ref, stats_ref, grad_mix_ref, out_ref, side_ref, text_out, up_came,
    w_cross, w_query, w_out, low_ref, two_low_ref, back_ref, grad_cm, grad_cq, w_sem,
    up_send, up_recv, *scratch,
):
    z = lax.axis_index("shard")
    spot = place()[1:]
    others = shard_others()
    enter(neighbours() + [device(other, *spot) for other in others])
    up_moves = spread(lambda other: up_ref.at[other], up_came, up_send, up_recv, others, spot)
    up_own = pltpu.make_async_copy(up_ref.at[z], up_came.at[z], w_sem.at[3])
    up_own.start()
    cross_job = Scatter(w_cross, *scratch[:5])
    query_job = Scatter(w_query, *scratch[5:10])
    branch_job = LoadedScatter(branch_ref, *scratch[10:])
    branch_job.start()
    blocks, columns, width = w_out.shape
    rows = low_ref.shape[0]
    heads = columns // HEAD_DIM
    loads = []
    for index, buffer in ((2, w_cross), (1, w_query), (0, w_out)):
        load = pltpu.make_async_copy(
            w_ref.at[index], buffer, w_sem.at[index]
        )
        load.start()
        loads.append(load)
    nothing = (jnp.zeros((1, width), F32),) * 2

    def third(part, sums):
        back, more = norm_back(normed_ref[part], two_ref[part], gain_ref[2:3])
        total = cot_ref[part].astype(F32) + back
        grad_ref[part] = total
        low_ref[part] = total.astype(BF)
        normed, _ = normalise(one_ref[part])
        two_low_ref[part] = (normed * gain_ref[1:2] + bias_ref[1:2]).astype(BF)
        return sums[0] + more[0], sums[1] + more[1]

    gain_three, shift_three = chunks(rows, third, nothing)
    branch_job.first()
    loads[0].wait()

    def cross_weight(block, carry):
        grad_cm[block] = nt(low_ref[...], w_cross[block]).astype(BF)
        w_cross[block] = tn(mix_ref[block], low_ref[...]).astype(BF)
        return carry

    lax.fori_loop(0, blocks, cross_weight, 0)
    for index in range(4):
        cross_job.pass_core(index)
    half = rows // 2
    texts = text_ref.shape[1] // 2
    loads[1].wait()

    def cross(block, carry):
        for clip in range(2):
            part = pl.ds(clip * half, half)
            keys = pl.ds(clip * texts, texts)
            for head in range(heads):
                here = pl.ds(head * HEAD_DIM, HEAD_DIM)
                query = query_ref[block, part, here] * jnp.asarray(HEAD_DIM ** (-0.5), BF)
                there = pl.ds(columns + head * HEAD_DIM, HEAD_DIM)
                key, value = text_ref[block, keys, here], text_ref[block, keys, there]
                grad = grad_cm[block, part, here]
                scores = nt(key, query)
                weights = jnp.exp(scores - jnp.max(scores, axis=0, keepdims=True))
                weights = weights / jnp.sum(weights, axis=0, keepdims=True)
                slopes = nt(value, grad)
                inner = jnp.sum(weights * slopes, axis=0, keepdims=True)
                slopes = (weights * (slopes - inner)).astype(BF)
                grad_query = jnp.transpose(nn(turn(key).astype(BF), slopes))
                grad_cq[block, part, here] = (grad_query * HEAD_DIM ** (-0.5)).astype(BF)
                text_out[block, keys, here] = nn(slopes, query).astype(BF)
                text_out[block, keys, there] = nn(weights.astype(BF), grad).astype(BF)
        back = nn(grad_cq[block], w_query[block])
        back_ref[...] += back
        w_query[block] = tn(grad_cq[block], two_low_ref[...]).astype(BF)
        return carry

    back_ref[...] = jnp.zeros_like(back_ref)
    lax.fori_loop(0, blocks // 2, cross, 0)
    branch_job.second()
    cross_job.far()
    cross_job.near()
    lax.fori_loop(blocks // 2, blocks, cross, 0)
    for index in range(4):
        query_job.pass_core(index)

    def second(part, sums):
        back, more = norm_back(back_ref[part], one_ref[part], gain_ref[1:2])
        total = grad_ref[part] + back
        grad_ref[part] = total
        low_ref[part] = total.astype(BF)
        return sums[0] + more[0], sums[1] + more[1]

    gain_two, shift_two = chunks(rows, second, nothing)
    cross_job.second()
    query_job.far()
    query_job.near()
    loads[2].wait()

    def out_weight(block, carry):
        grad_mix_ref[block] = nt(low_ref[...], w_out[block]).astype(BF)
        out_ref[block] = tn(my_mix_ref[block], low_ref[...]).astype(BF)
        return carry

    lax.fori_loop(0, blocks, out_weight, 0)
    branch_job.wait()

    def last(part, sums):
        branch = branch_job.value(part)
        total = two_ref[part] + branch
        layer_ref[part] = total.astype(BF)
        return (
            sums[0] + jnp.sum(total * total, axis=0, keepdims=True),
            sums[1] + jnp.sum(branch * branch, axis=0, keepdims=True),
        )

    square_out, square_three = chunks(rows, last, nothing)
    rest = jnp.zeros((1, width), F32)
    for index, row in enumerate(
        (rest, rest, gain_two, shift_two, gain_three, shift_three, square_out, square_three)
    ):
        stats_ref[index : index + 1] = row
    query_job.second()
    side_ref[1] = cross_job.total().astype(BF)
    side_ref[0] = query_job.total().astype(BF)
    branch_job.finish()
    cross_job.finish()
    query_job.finish()
    up_own.wait()
    for copy in up_moves:
        copy.wait()


def rows_back(
    normed, cot, one, two, query, mix, text, my_mix, gain, bias, weights, branch, up, ident
):
    rows, width = cot.shape
    blocks, _, columns = my_mix.shape
    return call(
        rows_back_kernel,
        "rows_back",
        (
            shape(rows, width, dtype=F32),
            shape(rows, width),
            shape(8, width, dtype=F32),
            shape(*my_mix.shape),
            shape(blocks, columns, width),
            shape(2, columns, width),
            shape(*text.shape),
            shape(*up.shape),
        ),
        (IN_VMEM,) * 7 + (ANY,),
        [IN_VMEM] * 10 + [ANY, ANY, ANY],
        [pltpu.VMEM((blocks, columns, width), BF)] * 3
        + [
            pltpu.VMEM((rows, width), BF),
            pltpu.VMEM((rows, width), BF),
            pltpu.VMEM((rows, width), F32),
            pltpu.VMEM(my_mix.shape, BF),
            pltpu.VMEM(my_mix.shape, BF),
            pltpu.SemaphoreType.DMA((4,)),
            pltpu.SemaphoreType.DMA((up.shape[0] - 1,)),
            pltpu.SemaphoreType.DMA((up.shape[0] - 1,)),
        ]
        + Scatter.scratch(columns, width) * 2
        + LoadedScatter.scratch(rows, width),
        ident,
        60,
    )(normed, cot, one, two, query, mix, text, my_mix, gain, bias, weights, branch, up)


def last_kernel(
    part_ref, frames_ref, gain_ref, grad_ref, stats_ref, qkv_ref, up_ref, cross_ref, out_w_ref,
    text_ref, text_in, w_text_ref,
    out_ref, total_ref, text_out, qkv_out, up_out, query_out, cross_out, self_out, key_out,
    mine, came, all_ref, st_send, st_recv, z_send, z_recv,
    qkv_came, out_came, text_came, text_part, text_mine, text_all,
    qkv_pair, up_mine, up_pair, cross_pair, out_pair, key_pair, x_send, x_recv, *scratch,
):
    z = lax.axis_index("shard")
    shards = lax.axis_size("shard")
    others = shard_others()
    spot = place()[1:]
    context = spot[0]
    enter(neighbours() + [device(other, *spot) for other in others])

    def over(index, source_of, target_ref):
        return spread(source_of, target_ref, z_send.at[index], z_recv.at[index], others, spot)

    text_moves = over(0, lambda other: text_ref, text_came)
    qkv_moves = over(1, lambda other: qkv_ref.at[other], qkv_came)
    out_moves = over(2, lambda other: out_w_ref.at[other], out_came)
    size = len(scratch) - 5
    text = Scatter(text_part, *scratch[size:])
    job = LoadedScatter(part_ref, *scratch[:size])
    job.start()
    inputs = frames_ref[...].astype(F32)
    average = jnp.mean(inputs, axis=-1, keepdims=True)
    centred = inputs - average
    rate = lax.rsqrt(jnp.mean(centred * centred, axis=-1, keepdims=True) + EPS)
    total = up_ref[0].astype(F32)
    for index in range(1, shards):
        total += up_ref[index].astype(F32)
    up_mine[...] = total.astype(BF)
    text_came[z] = text_ref[...]
    for copy in text_moves:
        copy.wait_recv()
    job.first()
    texts = text_ref.shape[0] // 2
    own = texts // 8

    def text_back(index, carry):
        grads = nt(text_came[index], w_text_ref[...])
        rows = pl.ds(pl.multiple_of(index * 2 * own, 2 * own), 2 * own)
        for block in range(8):
            pair = [grads[k * texts + block * own : k * texts + block * own + own] for k in range(2)]
            text_part[block, rows] = jnp.concatenate(pair, axis=0).astype(BF)
        return carry

    lax.fori_loop(0, shards, text_back, 0)
    for index in range(4):
        text.pass_core(index)
    key_grad = tn(text_in[0], text_came[0])
    for index in range(1, shards):
        key_grad += tn(text_in[index], text_came[index])
    key_pair[0] = key_grad.astype(BF)
    text.far()
    text.near()
    job.second()
    to_x = neighbours()[0]

    def swap(index, source, target_ref):
        copy = remote_copy(source, target_ref, x_send.at[index], x_recv.at[index], to_x)
        copy.start()
        return copy

    text.second()
    pairs = [swap(0, up_mine, up_pair), swap(1, cross_ref, cross_pair)]
    pairs.append(swap(2, key_pair.at[0], key_pair.at[1]))
    text.wait()
    for index in range(shards):
        rows = slice(index * 2 * own, (index + 1) * 2 * own)
        text_mine[index] = text.value(rows).astype(BF)
    text_moves += over(3, lambda other: text_mine.at[other], text_all)
    text_all[z] = text_mine[z]
    grads = job.total()
    normed = centred * rate
    mine[0] = stats_ref[...]
    mine[0, 0:1] = jnp.sum(grads * normed, axis=0, keepdims=True)
    mine[0, 1:2] = jnp.sum(grads, axis=0, keepdims=True)
    sends = []
    for index, target in enumerate(reversed(neighbours())):
        copy = remote_copy(
            mine.at[index], came.at[index], st_send.at[index], st_recv.at[index], target
        )
        copy.start()
        sends.append(copy)
        if index == 0:
            scaled = grads * gain_ref[...]
            inner = jnp.mean(scaled * normed, axis=-1, keepdims=True)
            scaled = scaled - jnp.mean(scaled, axis=-1, keepdims=True) - normed * inner
            out_ref[...] = grad_ref[...] + rate * scaled
        copy.wait_recv()
        mine[index + 1] = mine[index] + came[index]
    stat_moves = over(4, lambda other: mine.at[3], all_ref)
    all_ref[z] = mine[3]

    def collect(moves, source_ref, came_ref):
        came_ref[z] = source_ref[z]
        for copy in moves:
            copy.wait_recv()
        total = came_ref[0].astype(F32)
        for index in range(1, shards):
            total += came_ref[index].astype(F32)
        return total.astype(BF)

    qkv_pair[0] = collect(qkv_moves, qkv_ref, qkv_came)
    pairs.append(swap(3, qkv_pair.at[0], qkv_pair.at[1]))
    out_pair[0] = collect(out_moves, out_w_ref, out_came)
    pairs.append(swap(4, out_pair.at[0], out_pair.at[1]))
    for copy in text_moves[shards - 1 :] + stat_moves:
        copy.wait_recv()
    text_out[...] = text_all[...].astype(F32)
    total = all_ref[0]
    for index in range(1, shards):
        total += all_ref[index]
    total_ref[...] = total
    beside(up_mine, pairs[0], up_pair, up_out)

    def ordered(first, second):
        first, second = first.astype(F32), second.astype(F32)
        return jnp.where(context == 0, first, second), jnp.where(context == 0, second, first)

    pairs[1].wait_recv()
    lead, trail = ordered(cross_ref[...], cross_pair[...])
    width = lead.shape[0] // 2
    query_out[:, :width] = jnp.transpose(lead[:width])
    query_out[:, width:] = jnp.transpose(trail[:width])
    cross_out[:, :width] = jnp.transpose(lead[width:])
    cross_out[:, width:] = jnp.transpose(trail[width:])
    pairs[2].wait_recv()
    lead, trail = ordered(key_pair[0], key_pair[1])
    for index in range(2):
        lanes = slice(index * width, (index + 1) * width)
        key_out[index, :, :width] = lead[:, lanes]
        key_out[index, :, width:] = trail[:, lanes]
    pairs[3].wait_recv()
    lead, trail = ordered(qkv_pair[0], qkv_pair[1])
    for index in range(3):
        lanes = slice(index * width, (index + 1) * width)
        qkv_out[index, :, :width] = lead[:, lanes]
        qkv_out[index, :, width:] = trail[:, lanes]
    pairs[4].wait_recv()
    lead, trail = ordered(out_pair[0], out_pair[1])
    self_out[:, :width] = jnp.transpose(lead)
    self_out[:, width:] = jnp.transpose(trail)
    for copy in sends + text_moves + qkv_moves + out_moves + stat_moves + pairs:
        copy.wait_send()
    text.finish()
    job.finish()


def last_step(part, frames, gain, grad, stats, qkv, up, cross, out, text, text_in, w_text, ident):
    _, rows, width = part.shape
    shards, texts, depth = text_in.shape
    half = up.shape[2]
    columns = out.shape[1]
    own = texts // 8
    square = shape(depth, 2 * columns, dtype=F32)
    return call(
        last_kernel,
        "last_step",
        (
            shape(rows, width, dtype=F32),
            shape(16, width, dtype=F32),
            shape(shards, own, depth, dtype=F32),
            shape(3, depth, 2 * columns, dtype=F32),
            shape(depth, 2 * half, dtype=F32),
            square,
            square,
            square,
            shape(2, depth, 2 * columns, dtype=F32),
        ),
        (IN_VMEM,) * 9,
        [ANY] + [IN_VMEM] * 11,
        [
            pltpu.VMEM((4, 16, width), F32),
            pltpu.VMEM((3, 16, width), F32),
            pltpu.VMEM((shards, 16, width), F32),
            pltpu.SemaphoreType.DMA((3,)),
            pltpu.SemaphoreType.DMA((3,)),
            pltpu.SemaphoreType.DMA((5, shards - 1)),
            pltpu.SemaphoreType.DMA((5, shards - 1)),
            pltpu.VMEM((shards, depth, 3 * columns), BF),
            pltpu.VMEM((shards, columns, depth), BF),
            pltpu.VMEM((shards, texts, 2 * columns), BF),
            pltpu.VMEM((8, shards * own, depth), BF),
            pltpu.VMEM((shards, own, depth), BF),
            pltpu.VMEM((shards, own, depth), BF),
            pltpu.VMEM((2, depth, 3 * columns), BF),
            pltpu.VMEM((depth, half), BF),
            pltpu.VMEM((depth, half), BF),
            pltpu.VMEM((2 * columns, depth), BF),
            pltpu.VMEM((2, columns, depth), BF),
            pltpu.VMEM((2, depth, 2 * columns), BF),
            pltpu.SemaphoreType.DMA((5,)),
            pltpu.SemaphoreType.DMA((5,)),
        ]
        + LoadedScatter.scratch(rows, width)
        + Scatter.scratch(shards * own, depth),
        ident,
        65,
    )(part, frames, gain, grad, stats, qkv, up, cross, out, text, text_in, w_text)


def dots(spec, *operands):
    return jnp.einsum(spec, *operands, preferred_element_type=F32)


def layer_norm(inputs, scaling, offset):
    average = jnp.mean(inputs, axis=-1, keepdims=True)
    centred = inputs - average
    variance = jnp.mean(centred * centred, axis=-1, keepdims=True)
    return centred * lax.rsqrt(variance + EPS) * scaling + offset


def on_device(
    frames,
    text_states,
    cotangent,
    norm_gain,
    norm_bias,
    self_qkv,
    self_out,
    cross_qkv,
    cross_out,
    mlp_up,
    mlp_down,
):
    clips, rows, width = frames.shape
    context = lax.axis_index("context")
    depth = self_qkv.shape[1]
    slices = width // depth
    columns = self_qkv.shape[2] // 2
    heads = columns // HEAD_DIM
    block = clips * rows
    texts = text_states.shape[1]

    def half(weight):
        size = weight.shape[-1] // 2
        return lax.dynamic_slice_in_dim(weight, context * size, size, weight.ndim - 1)

    def over_shard(weight, tiled=True):
        return lax.all_gather(weight, "shard", axis=0, tiled=tiled)

    cross_part = half(cross_qkv)
    side = jnp.concatenate([half(self_out), cross_part[0], half(cross_out)], axis=1)
    w_side = over_shard(side.transpose(1, 0), tiled=False)
    w_text = jnp.concatenate([cross_part[1], cross_part[2]], axis=1)
    text_slices = text_states.reshape(clips * texts, slices, depth).transpose(1, 0, 2)
    w_down = over_shard(half(mlp_down))
    w_up = over_shard(half(mlp_up))

    qkv_part = half(self_qkv)
    all_one, all_grad, w_qkv, text_in, text_part = first_step(
        frames.reshape(block, width),
        norm_gain,
        norm_bias,
        cotangent.reshape(block, width),
        jnp.concatenate([qkv_part[0], qkv_part[1], qkv_part[2]], axis=-1),
        text_slices,
        w_text,
        0,
    )
    w_qkv = w_qkv.reshape(width, 3 * columns)
    (
        qkv, self_log, mix, my_mix, stream_one, stream_two, cross_q, cross_mix, norm_three,
        text_all, squares, plane_w,
    ) = attend_forward(
        all_one,
        w_qkv,
        w_side,
        text_part,
        frames.reshape(block, width),
        norm_gain,
        norm_bias,
        1,
    )

    grad_normed, part_three, grad_up, grad_down = feed_forward(
        norm_three, all_grad, w_up, w_down, 4
    )

    def to_shard(part):
        return lax.psum_scatter(part.astype(BF), "shard", scatter_dimension=0, tiled=True)

    grad_down = to_shard(grad_down)
    grad_one, layer_out, stats, grad_mix, part_out, side, text_grads, grad_up = rows_back(
        grad_normed,
        cotangent.reshape(block, width),
        stream_one,
        stream_two,
        cross_q,
        cross_mix,
        text_all,
        my_mix,
        norm_gain,
        norm_bias,
        plane_w,
        part_three,
        grad_up.reshape(slices, depth, -1),
        3,
    )

    def slice_shards(part):
        return part.reshape(-1, slices, depth).transpose(1, 0, 2)

    grad_cross = to_shard(slice_shards(side))[0]
    part_norm, grad_w_qkv, grad_out, text_grads, grad_down = attend_backward(
        grad_mix, qkv, mix, self_log, all_one, w_qkv, part_out, text_grads, grad_down, 8
    )
    (
        grad_frames, totals, grad_text, grad_w_qkv, grad_up, grad_query, grad_cross, grad_out,
        grad_keys,
    ) = last_step(
        part_norm,
        frames.reshape(block, width),
        norm_gain[0][None],
        grad_one,
        jnp.concatenate([stats, squares], axis=0),
        grad_w_qkv.reshape(slices, depth, 3 * columns),
        grad_up,
        grad_cross,
        slice_shards(grad_out),
        text_grads,
        text_in,
        w_text,
        11,
    )
    grad_frames = grad_frames.reshape(clips, rows, width)
    grad_text = grad_text.transpose(1, 0, 2).reshape(clips, texts // 8, width)

    gains = jnp.stack([totals[0], totals[2], totals[4]])
    shifts = jnp.stack([totals[1], totals[3], totals[5]])
    squares = jnp.stack([totals[j].sum() for j in (6, 8, 9, 7)])
    start = lax.axis_index("shard") * depth
    grad_gain = lax.dynamic_slice_in_dim(gains, start, depth, 1)
    grad_shift = lax.dynamic_slice_in_dim(shifts, start, depth, 1)
    entries = float(clips * rows * width * lax.axis_size(("shard",) + PLANE))
    return (
        layer_out.reshape(clips, rows, width),
        grad_frames,
        grad_text,
        grad_gain,
        grad_shift,
        grad_w_qkv,
        grad_out,
        jnp.concatenate([grad_query[None], grad_keys]),
        grad_cross,
        grad_up,
        grad_down,
        jnp.sqrt(squares / entries),
    )


def solution(mesh):
    rows = P("shard", PLANE, None)
    stack = P(None, "shard", "tensor")
    flat = P("shard", "tensor")
    return jax.shard_map(
        on_device,
        mesh=mesh,
        in_specs=(rows, P("shard"), rows, P(), P(), stack, flat, stack, flat, flat, flat),
        out_specs=(
            (rows, rows, rows, P(None, "shard"), P(None, "shard"))
            + (stack, flat, stack, flat, flat, flat, P())
        ),
        check_vma=False,
    )
```

```python
from functools import partial

import jax
import jax.numpy as jnp
from jax import lax
from jax.experimental import pallas as pl
from jax.experimental.pallas import tpu as pltpu
from jax.sharding import PartitionSpec as P

HEAD_DIM = 64
EPS = 1e-05
MASKED = -1e30
MESH = pl.DeviceIdType.MESH
BF = jnp.bfloat16
F32 = jnp.float32
PLANE = ("context", "tensor")
VMEM_LIMIT = 60 * 2**20


def place():
    return (
        lax.axis_index("shard"),
        lax.axis_index("context"),
        lax.axis_index("tensor") // 2,
        lax.axis_index("tensor") % 2,
    )


def device(z, x, y, c):
    return (z, x, 2 * y + c)


def slot(x, y, c):
    return 4 * x + 2 * y + c


def neighbours():
    z, x, y, c = place()
    return [device(z, 1 - x, y, c), device(z, x, 1 - y, c), device(z, x, y, 1 - c)]


def plane_spots():
    z, x, y, c = place()
    steps = [(a, b, d) for a in range(2) for b in range(2) for d in range(2) if a + b + d]
    return [((x + a) % 2, (y + b) % 2, (c + d) % 2) for a, b, d in steps]


def plane_others():
    z = lax.axis_index("shard")
    return [device(z, *spot) for spot in plane_spots()]


def enter(targets):
    barrier = pltpu.get_barrier_semaphore()
    for target in targets:
        pl.semaphore_signal(barrier, inc=1, device_id=target, device_id_type=MESH)
    pl.semaphore_wait(barrier, len(targets))


def remote_copy(source, target_ref, send, recv, target):
    return pltpu.make_async_remote_copy(
        src_ref=source,
        dst_ref=target_ref,
        send_sem=send,
        recv_sem=recv,
        device_id=target,
        device_id_type=MESH,
    )


class Gather:
    semaphores = 9

    def __init__(self, in_ref, out_ref, local_sem, send, recv):
        z, x, y, c = place()
        self.in_ref, self.out_ref, self.local_sem = in_ref, out_ref, local_sem
        self.send, self.recv = send, recv
        self.spot = (x, y, c)
        self.to_x, self.to_y, self.to_c = neighbours()
        self.rows = in_ref.shape[0]
        self.sends = []

    def go(self, index, owner, start, size, target, source=None):
        there = self.out_ref.at[owner, pl.ds(start, size)]
        copy = remote_copy(
            there if source is None else source,
            there,
            self.send.at[index],
            self.recv.at[index],
            target,
        )
        copy.start()
        self.sends.append(copy)

    def arrived(self, index, owner, start, size):
        there = self.out_ref.at[owner, pl.ds(start, size)]
        remote_copy(
            there, there, self.send.at[index], self.recv.at[index], self.to_x
        ).wait_recv()

    def start(self):
        me = slot(*self.spot)
        self.own = pltpu.make_async_copy(self.in_ref, self.out_ref.at[me], self.local_sem)
        self.own.start()
        for index, target in enumerate((self.to_x, self.to_y, self.to_c)):
            self.go(index, me, 0, self.rows, target, self.in_ref)

    def relay_y(self):
        x, y, c = self.spot
        owner = slot(x, 1 - y, c)
        self.arrived(1, owner, 0, self.rows)
        self.go(3, owner, 0, self.rows // 2, self.to_x)
        self.go(5, owner, 0, self.rows, self.to_c)

    def relay_x(self):
        x, y, c = self.spot
        half = self.rows // 2
        owner = slot(1 - x, y, c)
        self.arrived(0, owner, 0, self.rows)
        self.go(4, owner, half, half, self.to_y)
        self.go(6, owner, 0, self.rows, self.to_c)

    def relay_far(self):
        x, y, c = self.spot
        half = self.rows // 2
        owner = slot(1 - x, 1 - y, c)
        self.arrived(3, owner, 0, half)
        self.go(7, owner, 0, half, self.to_c)
        self.arrived(4, owner, half, half)
        self.go(8, owner, half, half, self.to_c)

    def finish(self):
        x, y, c = self.spot
        half = self.rows // 2
        self.arrived(2, slot(x, y, 1 - c), 0, self.rows)
        self.arrived(5, slot(x, 1 - y, 1 - c), 0, self.rows)
        self.arrived(6, slot(1 - x, y, 1 - c), 0, self.rows)
        self.arrived(7, slot(1 - x, 1 - y, 1 - c), 0, half)
        self.arrived(8, slot(1 - x, 1 - y, 1 - c), half, half)
        self.own.wait()
        for copy in self.sends:
            copy.wait_send()

    def rest(self):
        self.relay_y()
        self.relay_x()
        self.relay_far()
        self.finish()


class Scatter:
    @staticmethod
    def scratch(rows, columns):
        return [
            pltpu.VMEM((4, rows, columns), BF),
            pltpu.VMEM((2, rows // 2, columns), BF),
            pltpu.VMEM((2, rows, columns), BF),
            pltpu.SemaphoreType.DMA((10,)),
            pltpu.SemaphoreType.DMA((10,)),
        ]

    def __init__(self, part_ref, core, relay, final, send, recv):
        self.part_ref, self.core, self.relay, self.final = part_ref, core, relay, final
        self.send, self.recv = send, recv
        self.to_x, self.to_y, self.to_c = neighbours()
        z, x, y, c = place()
        chips = ((1 - x, 1 - y), (1 - x, y), (x, 1 - y), (x, y))
        self.mine = [slot(*chip, c) for chip in chips]
        self.theirs = [slot(*chip, 1 - c) for chip in chips]
        rows = part_ref.shape[1]
        self.low, self.high = pl.ds(0, rows // 2), pl.ds(rows // 2, rows // 2)
        self.sends = []

    def forward(self, index, source, target_ref, target):
        copy = remote_copy(
            source, target_ref, self.send.at[index], self.recv.at[index], target
        )
        copy.start()
        self.sends.append(copy)

    def arrived(self, index, ref):
        remote_copy(ref, ref, self.send.at[index], self.recv.at[index], self.to_c).wait_recv()

    def pass_core(self, index):
        source = self.part_ref.at[self.theirs[index]]
        self.forward(index, source, self.core.at[index], self.to_c)

    def add(self, index, part, more=None):
        mine = self.mine[index]
        total = self.part_ref[mine, part].astype(F32) + self.core[index, part].astype(F32)
        if more is not None:
            total += more.astype(F32)
        self.part_ref[mine, part] = total.astype(BF)
        return self.part_ref.at[mine, part]

    def far(self):
        self.arrived(0, self.core.at[0])
        self.forward(4, self.add(0, self.low), self.relay.at[0], self.to_x)
        self.forward(5, self.add(0, self.high), self.relay.at[1], self.to_y)

    def near(self):
        self.arrived(1, self.core.at[1])
        self.forward(6, self.add(1, self.low), self.final.at[0, self.low], self.to_x)
        self.arrived(2, self.core.at[2])
        self.forward(7, self.add(2, self.high), self.final.at[1, self.high], self.to_y)

    def second(self):
        low, high, final, relay = self.low, self.high, self.final, self.relay
        self.arrived(5, relay.at[1])
        self.forward(8, self.add(1, high, relay[1]), final.at[0, high], self.to_x)
        self.arrived(4, relay.at[0])
        self.forward(9, self.add(2, low, relay[0]), final.at[1, low], self.to_y)

    def wait(self):
        self.arrived(3, self.core.at[3])
        self.arrived(6, self.final.at[0, self.low])
        self.arrived(7, self.final.at[1, self.high])
        self.arrived(8, self.final.at[0, self.high])
        self.arrived(9, self.final.at[1, self.low])

    def value(self, part=slice(None)):
        total = self.part_ref[self.mine[3], part].astype(F32) + self.core[3, part].astype(F32)
        return total + self.final[0, part].astype(F32) + self.final[1, part].astype(F32)

    def total(self):
        self.wait()
        return self.value()

    def finish(self):
        for copy in self.sends:
            copy.wait_send()


class LoadedScatter(Scatter):
    @staticmethod
    def scratch(rows, columns):
        return [
            pltpu.VMEM((4, rows, columns), BF),
            pltpu.SemaphoreType.DMA((4,)),
        ] + Scatter.scratch(rows, columns)

    def __init__(self, in_ref, part_ref, local_sem, *scratch):
        super().__init__(part_ref, *scratch)
        self.in_ref, self.local_sem = in_ref, local_sem

    def start(self):
        self.loads = []
        for index, (mine, theirs) in enumerate(zip(self.mine, self.theirs)):
            source = self.in_ref.at[theirs]
            self.forward(index, source, self.core.at[index], self.to_c)
            load = pltpu.make_async_copy(
                self.in_ref.at[mine], self.part_ref.at[index], self.local_sem.at[index]
            )
            load.start()
            self.loads.append(load)
        self.mine = (0, 1, 2, 3)

    def first(self):
        for load in self.loads:
            load.wait()
        self.far()
        self.near()


class Exchange:
    def __init__(self, in_ref, out_ref, local_sem, send, recv):
        self.in_ref, self.out_ref, self.local_sem = in_ref, out_ref, local_sem
        self.send, self.recv = send, recv
        z, x, y, c = place()
        self.me = slot(x, y, c)
        self.copies = []

    def start(self, piece, part):
        z = lax.axis_index("shard")
        own = pltpu.make_async_copy(
            self.in_ref.at[self.me, part], self.out_ref.at[self.me, part], self.local_sem.at[piece]
        )
        own.start()
        self.copies.append(own)
        for index, spot in enumerate(plane_spots()):
            copy = remote_copy(
                self.in_ref.at[slot(*spot), part],
                self.out_ref.at[self.me, part],
                self.send.at[piece, index],
                self.recv.at[piece, index],
                device(z, *spot),
            )
            copy.start()
            self.copies.append(copy)

    def finish(self, piece=None):
        copies = self.copies if piece is None else self.copies[8 * piece : 8 * piece + 8]
        for copy in copies:
            copy.wait()


ANY = pl.BlockSpec(memory_space=pl.ANY)
IN_VMEM = pl.BlockSpec(memory_space=pltpu.VMEM)


def call(kernel, name, outs, out_specs, in_specs, scratch, ident, micros):
    return pl.pallas_call(
        kernel,
        out_shape=outs,
        in_specs=in_specs,
        out_specs=out_specs,
        scratch_shapes=scratch,
        name=name,
        cost_estimate=pl.CostEstimate(
            flops=micros * 10**9, bytes_accessed=micros * 10**6, transcendentals=0
        ),
        compiler_params=pltpu.CompilerParams(
            collective_id=ident, has_side_effects=True, vmem_limit_bytes=VMEM_LIMIT
        ),
    )


def shape(*dims, dtype=BF):
    return jax.ShapeDtypeStruct(dims, dtype)


def gather_scratch():
    return [
        pltpu.SemaphoreType.DMA,
        pltpu.SemaphoreType.DMA((9,)),
        pltpu.SemaphoreType.DMA((9,)),
    ]


def shard_others():
    z, shards = lax.axis_index("shard"), lax.axis_size("shard")
    return [lax.rem(z + i, shards) for i in range(1, shards)]


def spread(source_of, target_ref, send, recv, others, spot):
    z = lax.axis_index("shard")
    copies = []
    for index, other in enumerate(others):
        copy = remote_copy(
            source_of(other), target_ref.at[z], send.at[index], recv.at[index],
            device(other, *spot),
        )
        copy.start()
        copies.append(copy)
    return copies


def first_kernel(
    frames_ref, gain_ref, bias_ref, cot_ref, text_ref, w_text_ref,
    rows_out, cot_out, text_all, text_out,
    normed_ref, part_ref, came_ref, sends, recvs, *scratch,
):
    z = lax.axis_index("shard")
    spot = place()[1:]
    others = shard_others()
    enter(neighbours() + [device(other, *spot) for other in others])
    texts = spread(lambda other: text_ref.at[other], text_all, sends.at[0], recvs.at[0], others, spot)
    text_all[z] = text_ref[z]

    def norm(part, carry):
        normed, _ = normalise(frames_ref[part].astype(F32))
        normed_ref[part] = (normed * gain_ref[0:1] + bias_ref[0:1]).astype(BF)
        return carry

    chunks(frames_ref.shape[0], norm)
    rows, grads = Gather(normed_ref, rows_out, *scratch[:3]), Gather(cot_ref, cot_out, *scratch[3:])
    rows.start()
    for copy in texts:
        copy.wait_recv()

    def share(index, carry):
        part_ref[index] = nn(text_all[index], w_text_ref[...]).astype(BF)
        return carry

    lax.fori_loop(0, text_all.shape[0], share, 0)
    parts = spread(lambda other: part_ref.at[other], came_ref, sends.at[1], recvs.at[1], others, spot)
    came_ref[z] = part_ref[z]
    rows.relay_y()
    rows.relay_x()
    grads.start()
    rows.relay_far()
    rows.finish()
    grads.rest()
    for copy in parts:
        copy.wait_recv()
    total = came_ref[0].astype(F32)
    for index in range(1, came_ref.shape[0]):
        total += came_ref[index].astype(F32)
    text_out[...] = total.astype(BF)
    for copy in texts + parts:
        copy.wait_send()


def first_step(frames, gain, bias, cotangent, text, w_text, ident):
    rows, width = frames.shape
    shards, texts, depth = text.shape
    return call(
        first_kernel,
        "first_step",
        (
            shape(8, rows, width),
            shape(8, rows, width),
            shape(shards, texts, depth),
            shape(texts, w_text.shape[1]),
        ),
        (ANY, ANY, IN_VMEM, IN_VMEM),
        [IN_VMEM, IN_VMEM, IN_VMEM, ANY, IN_VMEM, IN_VMEM],
        [
            pltpu.VMEM((rows, width), BF),
            pltpu.VMEM((shards, texts, w_text.shape[1]), BF),
            pltpu.VMEM((shards, texts, w_text.shape[1]), BF),
            pltpu.SemaphoreType.DMA((2, shards - 1)),
            pltpu.SemaphoreType.DMA((2, shards - 1)),
        ]
        + gather_scratch() * 2,
        ident,
        60,
    )(frames, gain, bias, cotangent, text, w_text)


def feed_kernel(
    own_ref, grad_ref, w_ref,
    normed_out, branch_out, up_out, down_out,
    rows_ref, grads_ref, hidden_ref, slope_ref, part_a, part_b,
    load_sem, store_sem, g_local, g_send, g_recv, *scratch,
):
    enter(neighbours())
    gather = Gather(own_ref, rows_ref, g_local, g_send, g_recv)
    gather.start()
    hidden = hidden_ref.shape[2]
    up_ref, down_ref = w_ref.at[:, pl.ds(0, hidden)], w_ref.at[:, pl.ds(hidden, hidden)]
    blocks, _, width = rows_ref.shape
    loads = []
    for block in range(blocks):
        load = pltpu.make_async_copy(grad_ref.at[block], grads_ref.at[block], load_sem.at[block])
        load.start()
        loads.append(load)
    for load in loads:
        load.wait()

    def early(block, carry):
        slope_ref[block] = nn(grads_ref[block], down_ref[...]).astype(BF)
        return carry

    lax.fori_loop(0, blocks, early, 0)

    def middle(block):
        before = nn(rows_ref[block], up_ref[...])
        share = 0.5 + 0.5 * lax.erf(before * (0.5**0.5))
        hidden_ref[block] = (before * share).astype(BF)
        slope = share + before * (jnp.exp(-0.5 * before * before) * (2.0 * jnp.pi) ** (-0.5))
        slope = (slope_ref[block].astype(F32) * slope).astype(BF)
        slope_ref[block] = slope
        part_a[block] = nt(slope, up_ref[...]).astype(BF)

    first = Scatter(part_a, *scratch)
    x, y, c = gather.spot

    def pair(cx, cy):
        def one(index, carry):
            middle(slot(cx, cy, 0) + index)
            return carry

        lax.fori_loop(0, 2, one, 0)

    gather.own.wait()
    gather.arrived(2, slot(x, y, 1 - c), 0, gather.rows)
    pair(x, y)
    first.pass_core(3)
    gather.relay_y()
    gather.relay_x()
    gather.arrived(6, slot(1 - x, y, 1 - c), 0, gather.rows)
    pair(1 - x, y)
    first.pass_core(1)
    gather.arrived(5, slot(x, 1 - y, 1 - c), 0, gather.rows)
    pair(x, 1 - y)
    first.pass_core(2)
    gather.relay_far()
    first.near()
    gather.arrived(7, slot(1 - x, 1 - y, 1 - c), 0, gather.rows // 2)
    gather.arrived(8, slot(1 - x, 1 - y, 1 - c), gather.rows // 2, gather.rows // 2)
    pair(1 - x, 1 - y)
    first.pass_core(0)
    first.far()
    for copy in gather.sends:
        copy.wait_send()

    def store(block):
        return pltpu.make_async_copy(part_b.at[block], branch_out.at[block], store_sem.at[block])

    def branch(block, carry):
        part_b[block] = nt(hidden_ref[block], down_ref[...]).astype(BF)
        store(block).start()
        return carry

    lax.fori_loop(0, blocks, branch, 0)
    first.second()
    tile = 256

    def weight(left_ref, right_ref, out_ref):
        right = right_ref[...].reshape(-1, right_ref.shape[2])

        def one(index, carry):
            lanes = pl.ds(pl.multiple_of(index * tile, tile), tile)
            left = left_ref[:, :, lanes].reshape(-1, tile)
            out_ref[lanes, :] = tn(left, right).astype(BF)
            return carry

        lax.fori_loop(0, width // tile, one, 0)

    weight(grads_ref, hidden_ref, down_out)
    weight(rows_ref, slope_ref, up_out)
    normed_out[...] = first.total()
    first.finish()
    for block in range(blocks):
        store(block).wait()


def feed_forward(own, grads, weights, ident):
    rows, width = own.shape
    hidden = weights.shape[1] // 2
    outs = (
        shape(rows, width, dtype=F32),
        shape(8, rows, width),
        shape(width, hidden),
        shape(width, hidden),
    )
    scratch = [
        pltpu.VMEM((8, rows, width), BF),
        pltpu.VMEM((8, rows, width), BF),
        pltpu.VMEM((8, rows, hidden), BF),
        pltpu.VMEM((8, rows, hidden), BF),
        pltpu.VMEM((8, rows, width), BF),
        pltpu.VMEM((8, rows, width), BF),
        pltpu.SemaphoreType.DMA((8,)),
        pltpu.SemaphoreType.DMA((8,)),
    ]
    return call(
        feed_kernel,
        "feed_forward",
        outs,
        (IN_VMEM, ANY, IN_VMEM, IN_VMEM),
        [ANY, ANY, IN_VMEM],
        scratch + gather_scratch() + Scatter.scratch(rows, width),
        ident,
        70,
    )(own, grads, weights)


SIDE = 256


def nt(left, right):
    return lax.dot_general(left, right, (((1,), (1,)), ((), ())), preferred_element_type=F32)


def nn(left, right):
    return lax.dot_general(left, right, (((1,), (0,)), ((), ())), preferred_element_type=F32)


def tn(left, right):
    return lax.dot_general(left, right, (((0,), (0,)), ((), ())), preferred_element_type=F32)


def turn(values):
    return jnp.transpose(values.astype(F32))


def causal(scores):
    keys = lax.broadcasted_iota(jnp.int32, scores.shape, 0)
    queries = lax.broadcasted_iota(jnp.int32, scores.shape, 1)
    return jnp.where(keys <= queries, scores, MASKED)


def forward_kernel(
    rows_ref, side_ref, text_in, frames_ref, gain_ref, bias_ref,
    qkv_ref, log_ref, mix_ref, mine_ref, one_ref, two_ref, query_ref, cross_ref, low_ref,
    text_ref, square_ref, plane_out,
    w_own, w_out, w_query, w_cross, sum_ref, two_low_ref, store_sem,
    ex_local, ex_send, ex_recv, *scratch,
):
    enter(plane_others())
    blocks, both, _ = rows_ref.shape
    rows = both // 2
    width = mix_ref.shape[2]
    features = two_low_ref.shape[1]
    heads = width // HEAD_DIM
    length = blocks * rows
    step = SIDE // rows
    weights = (w_out, w_query, w_cross)

    def turn_own(kind):
        w_own[kind] = turn(side_ref[:, (3 + kind) * width : (4 + kind) * width]).astype(BF)

    turn_own(0)
    jobs = [Gather(w_own.at[k], weights[k], *scratch[3 * k : 3 * k + 3]) for k in range(3)]
    text_job = Gather(text_in, text_ref, *scratch[9:])
    text_job.start()
    jobs[0].start()
    stores = []

    def keep(kind):
        copy = pltpu.make_async_copy(weights[kind], plane_out.at[kind], store_sem.at[kind])
        copy.start()
        stores.append(copy)

    def project(block, carry):
        qkv_ref[block] = nn(rows_ref[block], side_ref[:, : 3 * width]).astype(BF)
        return carry

    lax.fori_loop(0, blocks, project, 0)
    turn_own(1)
    turn_own(2)
    exchange = Exchange(mix_ref, mine_ref, ex_local, ex_send, ex_recv)
    for clip in range(2):
        part = pl.ds(clip * rows, rows)
        for head in range(heads):
            lanes = [pl.ds(j * width + head * HEAD_DIM, HEAD_DIM) for j in range(3)]
            key = qkv_ref[:, part, lanes[1]].reshape(length, HEAD_DIM)
            value = turn(qkv_ref[:, part, lanes[2]].reshape(length, HEAD_DIM)).astype(BF)
            for index in range(length // SIDE):
                spots = pl.ds(index * step, step)
                query = qkv_ref[spots, part, lanes[0]].reshape(SIDE, HEAD_DIM)
                query = query * jnp.asarray(HEAD_DIM ** (-0.5), BF)
                start = index * SIDE
                last = causal(nt(key[start : start + SIDE], query))
                top = jnp.max(last, axis=0, keepdims=True)
                if index:
                    early = nt(key[:start], query)
                    top = jnp.maximum(top, jnp.max(early, axis=0, keepdims=True))
                last = jnp.exp(last - top)
                total = jnp.sum(last, axis=0, keepdims=True)
                mix = nn(value[:, start : start + SIDE], last.astype(BF))
                if index:
                    early = jnp.exp(early - top)
                    total += jnp.sum(early, axis=0, keepdims=True)
                    mix += nn(value[:, :start], early.astype(BF))
                mix = jnp.transpose(mix / total).astype(BF).reshape(step, rows, HEAD_DIM)
                mix_ref[spots, part, pl.ds(head * HEAD_DIM, HEAD_DIM)] = mix
                log_ref[pl.ds(clip * heads + head, 1), pl.ds(start, SIDE)] = top + jnp.log(total)
        exchange.start(clip, part)
        if clip == 0:
            jobs[0].relay_y()
            jobs[0].relay_x()
            text_job.relay_y()
            text_job.relay_x()
    jobs[1].start()
    jobs[0].relay_far()
    text_job.relay_far()
    jobs[0].finish()
    text_job.finish()
    keep(0)
    exchange.finish()

    def apply(values_ref, kind):
        sum_ref[...] = jnp.zeros_like(sum_ref)

        def one(block, carry):
            sum_ref[...] += nn(values_ref[block], weights[kind][block])
            return carry

        lax.fori_loop(0, blocks, one, 0)

    apply(mine_ref, 0)
    nothing = jnp.zeros((1, features), F32)

    def first(part, sums):
        branch = sum_ref[part]
        total = frames_ref[part].astype(F32) + branch
        one_ref[part] = total
        normed, _ = normalise(total)
        two_low_ref[part] = (normed * gain_ref[1:2] + bias_ref[1:2]).astype(BF)
        return sums + jnp.sum(branch * branch, axis=0, keepdims=True)

    square_one = chunks(both, first, nothing)
    jobs[1].relay_y()
    jobs[1].relay_x()
    jobs[2].start()
    jobs[1].relay_far()
    jobs[1].finish()
    keep(1)

    def ask(block, carry):
        query_ref[block] = nt(two_low_ref[...], w_query[block]).astype(BF)
        return carry

    lax.fori_loop(0, blocks, ask, 0)
    texts = text_ref.shape[1] // 2

    def cross(block, carry):
        for clip in range(2):
            part = pl.ds(clip * rows, rows)
            keys = pl.ds(clip * texts, texts)
            for head in range(heads):
                here = pl.ds(head * HEAD_DIM, HEAD_DIM)
                query = query_ref[block, part, here] * jnp.asarray(HEAD_DIM ** (-0.5), BF)
                there = pl.ds(width + head * HEAD_DIM, HEAD_DIM)
                scores = nt(text_ref[block, keys, here], query)
                probs = jnp.exp(scores - jnp.max(scores, axis=0, keepdims=True))
                probs = probs / jnp.sum(probs, axis=0, keepdims=True)
                mix = nn(turn(text_ref[block, keys, there]).astype(BF), probs.astype(BF))
                cross_ref[block, part, here] = jnp.transpose(mix).astype(BF)
        return carry

    lax.fori_loop(0, blocks // 2, cross, 0)
    jobs[2].relay_y()
    jobs[2].relay_x()
    lax.fori_loop(blocks // 2, blocks, cross, 0)
    jobs[2].relay_far()
    jobs[2].finish()
    keep(2)
    apply(cross_ref, 2)

    def second(part, sums):
        branch = sum_ref[part]
        total = one_ref[part] + branch
        two_ref[part] = total
        normed, _ = normalise(total)
        low_ref[part] = (normed * gain_ref[2:3] + bias_ref[2:3]).astype(BF)
        return sums + jnp.sum(branch * branch, axis=0, keepdims=True)

    square_two = chunks(both, second, nothing)
    square_ref[...] = jnp.zeros_like(square_ref)
    square_ref[0:1] = square_one
    square_ref[1:2] = square_two
    for copy in stores:
        copy.wait()


def attend_forward(rows, side, text, frames, gain, bias, ident):
    blocks, block, width = rows.shape
    columns = side.shape[1] // 6
    heads = columns // HEAD_DIM
    heads_shape = shape(blocks, block, columns)
    stream = shape(block, width, dtype=F32)
    return call(
        forward_kernel,
        "attend_forward",
        (
            shape(blocks, block, 3 * columns),
            shape(2 * heads, blocks * block // 2, dtype=F32),
            heads_shape,
            heads_shape,
            stream,
            stream,
            heads_shape,
            heads_shape,
            shape(block, width),
            shape(blocks, *text.shape),
            shape(8, width, dtype=F32),
            shape(3, blocks, columns, width),
        ),
        (IN_VMEM,) * 11 + (ANY,),
        [IN_VMEM] * 2 + [ANY] + [IN_VMEM] * 3,
        [pltpu.VMEM((3, columns, width), BF)]
        + [pltpu.VMEM((blocks, columns, width), BF)] * 3
        + [
            pltpu.VMEM((block, width), F32),
            pltpu.VMEM((block, width), BF),
            pltpu.SemaphoreType.DMA((4,)),
            pltpu.SemaphoreType.DMA((2,)),
            pltpu.SemaphoreType.DMA((2, 7)),
            pltpu.SemaphoreType.DMA((2, 7)),
        ]
        + gather_scratch() * 4,
        ident,
        80,
    )(rows, side, text, frames, gain, bias)


def beside(own_ref, copy, other_ref, out_ref):
    half = own_ref.shape[1]
    context = lax.axis_index("context")
    out_ref[:, pl.ds(pl.multiple_of(context * half, half), half)] = own_ref[...]
    copy.wait_recv()
    there = pl.ds(pl.multiple_of((1 - context) * half, half), half)
    out_ref[:, there] = other_ref[...]


def backward_kernel(
    grad_ref, qkv_ref, mix_ref, log_ref, rows_ref, w_ref, side_ref, text_ref, down_ref, up_ref,
    part_out, w_out, side_out, text_out, down_out, up_came,
    up_send, up_recv, out_ref, part_ref, store_sem, down_pair, pair_sem, grad_all, query_turned, ex_local, ex_send, ex_recv, *scratch,
):
    z = lax.axis_index("shard")
    spot = place()[1:]
    others = shard_others()
    enter(plane_others() + [device(other, *spot) for other in others])
    exchange = Exchange(grad_ref, grad_all, ex_local, ex_send, ex_recv)
    blocks, both, width = mix_ref.shape
    rows = both // 2
    heads = width // HEAD_DIM
    length = blocks * rows
    step = SIDE // rows
    for clip in range(2):
        exchange.start(clip, pl.ds(clip * rows, rows))
    some = pl.ds(up_came.shape[2], up_came.shape[2])
    up_moves = spread(
        lambda other: up_ref.at[other, :, some], up_came, up_send, up_recv, others, spot
    )
    up_own = pltpu.make_async_copy(up_ref.at[z, :, some], up_came.at[z], pair_sem.at[2])
    up_own.start()
    size = len(scratch) // 2
    text = LoadedScatter(text_ref, *scratch[size:])
    text.start()
    text.first()
    side = LoadedScatter(side_ref, *scratch[:size])
    side.start()
    side.first()
    for clip in range(2):
        exchange.finish(clip)
        part = pl.ds(clip * rows, rows)
        for head in range(heads):
            lanes = [pl.ds(j * width + head * HEAD_DIM, HEAD_DIM) for j in range(3)]
            query = qkv_ref[:, part, lanes[0]].reshape(length, HEAD_DIM)
            query = query * jnp.asarray(HEAD_DIM ** (-0.5), BF)
            key = qkv_ref[:, part, lanes[1]].reshape(length, HEAD_DIM)
            value = qkv_ref[:, part, lanes[2]].reshape(length, HEAD_DIM)
            key_turned = turn(key).astype(BF)
            here = pl.ds(head * HEAD_DIM, HEAD_DIM)
            grad = grad_all[:, part, here].reshape(length, HEAD_DIM)
            mixed = mix_ref[:, part, here].reshape(length, HEAD_DIM)
            inner = jnp.transpose(grad.astype(F32) * mixed.astype(F32))
            inner = jnp.sum(inner, axis=0, keepdims=True)
            logs = log_ref[pl.ds(clip * heads + head, 1), :]
            for index in range(length // SIDE):
                start = index * SIDE
                spots = pl.ds(index * step, step)
                k_part, v_part = key[start : start + SIDE], value[start : start + SIDE]
                scores = nt(k_part, query[start:])
                first = causal(scores[:, :SIDE])
                if start + SIDE < length:
                    scores = jnp.concatenate([first, scores[:, SIDE:]], axis=1)
                else:
                    scores = first
                weights = jnp.exp(scores - logs[:, start:])
                slopes = nt(v_part, grad[start:])
                slopes = (weights * (slopes - inner[:, start:])).astype(BF)
                grad_key = nn(slopes, query[start:]).astype(BF).reshape(step, rows, HEAD_DIM)
                grad_value = nn(weights.astype(BF), grad[start:]).astype(BF)
                out_ref[spots, part, lanes[1]] = grad_key
                out_ref[spots, part, lanes[2]] = grad_value.reshape(step, rows, HEAD_DIM)
                grad_query = nn(key_turned[:, start : start + SIDE], slopes)
                if index:
                    query_turned[:, start:] += grad_query
                else:
                    query_turned[...] = grad_query
            grad_query = jnp.transpose(query_turned[...]) * HEAD_DIM ** (-0.5)
            grad_query = grad_query.astype(BF).reshape(blocks, rows, HEAD_DIM)
            out_ref[:, part, lanes[0]] = grad_query
        if clip == 0:
            text.second()
            side.second()
            to_x = neighbours()[0]
            pair = remote_copy(down_ref, down_pair, pair_sem.at[0], pair_sem.at[1], to_x)
            pair.start()

    def store(block):
        return pltpu.make_async_copy(part_ref.at[block], part_out.at[block], store_sem.at[block])

    def project(block, carry):
        part_ref[block] = nt(out_ref[block], w_ref[:, : 3 * width]).astype(BF)
        store(block).start()
        return carry

    lax.fori_loop(0, blocks, project, 0)
    tile = 256
    right = out_ref[...].reshape(blocks * both, 3 * width)

    def weight(index, carry):
        lanes = pl.ds(pl.multiple_of(index * tile, tile), tile)
        left = rows_ref[:, :, lanes].reshape(blocks * both, tile)
        w_out[lanes, :] = tn(left, right).astype(BF)
        return carry

    lax.fori_loop(0, w_out.shape[0] // tile, weight, 0)
    text_out[...] = text.total().astype(BF)
    side_out[...] = side.total().astype(BF)
    text.finish()
    side.finish()
    beside(down_ref, pair, down_pair, down_out)
    pair.wait_send()
    up_own.wait()
    for copy in up_moves:
        copy.wait()
    for block in range(blocks):
        store(block).wait()


def attend_backward(grad_mix, qkv, mix, logs, rows, weights, side, text, down, up, ident):
    blocks, block, columns = mix.shape
    _, side_rows, width = side.shape
    text_shape = text.shape[1:]
    return call(
        backward_kernel,
        "attend_backward",
        (
            shape(blocks, block, width),
            shape(width, 3 * columns),
            shape(side_rows, width),
            shape(*text_shape),
            shape(down.shape[0], 2 * down.shape[1]),
            shape(*up.shape[:2], up.shape[2] // 2),
        ),
        (ANY, IN_VMEM, IN_VMEM, IN_VMEM, IN_VMEM, ANY),
        [ANY] + [IN_VMEM] * 5 + [ANY, ANY, IN_VMEM, ANY],
        [
            pltpu.SemaphoreType.DMA((up.shape[0] - 1,)),
            pltpu.SemaphoreType.DMA((up.shape[0] - 1,)),
            pltpu.VMEM((blocks, block, 3 * columns), BF),
            pltpu.VMEM((blocks, block, width), BF),
            pltpu.SemaphoreType.DMA((8,)),
            pltpu.VMEM(down.shape, BF),
            pltpu.SemaphoreType.DMA((3,)),
            pltpu.VMEM((blocks, block, columns), BF),
            pltpu.VMEM((HEAD_DIM, blocks * block // 2), F32),
            pltpu.SemaphoreType.DMA((2,)),
            pltpu.SemaphoreType.DMA((2, 7)),
            pltpu.SemaphoreType.DMA((2, 7)),
        ]
        + LoadedScatter.scratch(side_rows, width)
        + LoadedScatter.scratch(*text_shape),
        ident,
        1,
    )(grad_mix, qkv, mix, logs, rows, weights, side, text, down, up)


CHUNK = 64


def chunks(rows, body, carry=None):
    def one(index, carry):
        return body(pl.ds(pl.multiple_of(index * CHUNK, CHUNK), CHUNK), carry)

    return lax.fori_loop(0, rows // CHUNK, one, 0 if carry is None else carry)


def normalise(inputs):
    average = jnp.mean(inputs, axis=-1, keepdims=True)
    centred = inputs - average
    rate = lax.rsqrt(jnp.mean(centred * centred, axis=-1, keepdims=True) + EPS)
    return centred * rate, rate


def norm_back(grads, inputs, gain):
    normed, rate = normalise(inputs)
    scaled = grads * gain
    inner = jnp.mean(scaled * normed, axis=-1, keepdims=True)
    result = rate * (scaled - jnp.mean(scaled, axis=-1, keepdims=True) - normed * inner)
    sums = (
        jnp.sum(grads * normed, axis=0, keepdims=True),
        jnp.sum(grads, axis=0, keepdims=True),
    )
    return result, sums


def rows_back_kernel(
    normed_ref, cot_ref, one_ref, two_ref, query_ref, mix_ref, text_ref, my_mix_ref,
    gain_ref, bias_ref, w_ref, branch_ref, up_ref,
    grad_ref, layer_ref, stats_ref, grad_mix_ref, out_ref, side_ref, text_out, up_came,
    w_cross, w_query, w_out, low_ref, two_low_ref, back_ref, grad_cm, grad_cq, w_sem,
    up_send, up_recv, *scratch,
):
    z = lax.axis_index("shard")
    spot = place()[1:]
    others = shard_others()
    enter(neighbours() + [device(other, *spot) for other in others])
    some = pl.ds(0, up_came.shape[2])
    up_moves = spread(
        lambda other: up_ref.at[other, :, some], up_came, up_send, up_recv, others, spot
    )
    up_own = pltpu.make_async_copy(up_ref.at[z, :, some], up_came.at[z], w_sem.at[3])
    up_own.start()
    cross_job = Scatter(w_cross, *scratch[:5])
    query_job = Scatter(w_query, *scratch[5:10])
    branch_job = LoadedScatter(branch_ref, *scratch[10:])
    branch_job.start()
    blocks, columns, width = w_out.shape
    rows = low_ref.shape[0]
    heads = columns // HEAD_DIM
    loads = []
    for index, buffer in ((2, w_cross), (1, w_query), (0, w_out)):
        load = pltpu.make_async_copy(
            w_ref.at[index], buffer, w_sem.at[index]
        )
        load.start()
        loads.append(load)
    nothing = (jnp.zeros((1, width), F32),) * 2

    def third(part, sums):
        back, more = norm_back(normed_ref[part], two_ref[part], gain_ref[2:3])
        total = cot_ref[part].astype(F32) + back
        grad_ref[part] = total
        low_ref[part] = total.astype(BF)
        normed, _ = normalise(one_ref[part])
        two_low_ref[part] = (normed * gain_ref[1:2] + bias_ref[1:2]).astype(BF)
        return sums[0] + more[0], sums[1] + more[1]

    gain_three, shift_three = chunks(rows, third, nothing)
    branch_job.first()
    loads[0].wait()

    def cross_weight(block, carry):
        grad_cm[block] = nt(low_ref[...], w_cross[block]).astype(BF)
        w_cross[block] = tn(mix_ref[block], low_ref[...]).astype(BF)
        return carry

    lax.fori_loop(0, blocks, cross_weight, 0)
    for index in range(4):
        cross_job.pass_core(index)
    half = rows // 2
    texts = text_ref.shape[1] // 2
    loads[1].wait()

    def cross(block, carry):
        for clip in range(2):
            part = pl.ds(clip * half, half)
            keys = pl.ds(clip * texts, texts)
            for head in range(heads):
                here = pl.ds(head * HEAD_DIM, HEAD_DIM)
                query = query_ref[block, part, here] * jnp.asarray(HEAD_DIM ** (-0.5), BF)
                there = pl.ds(columns + head * HEAD_DIM, HEAD_DIM)
                key, value = text_ref[block, keys, here], text_ref[block, keys, there]
                grad = grad_cm[block, part, here]
                scores = nt(key, query)
                weights = jnp.exp(scores - jnp.max(scores, axis=0, keepdims=True))
                weights = weights / jnp.sum(weights, axis=0, keepdims=True)
                slopes = nt(value, grad)
                inner = jnp.sum(weights * slopes, axis=0, keepdims=True)
                slopes = (weights * (slopes - inner)).astype(BF)
                grad_query = jnp.transpose(nn(turn(key).astype(BF), slopes))
                grad_cq[block, part, here] = (grad_query * HEAD_DIM ** (-0.5)).astype(BF)
                text_out[block, keys, here] = nn(slopes, query).astype(BF)
                text_out[block, keys, there] = nn(weights.astype(BF), grad).astype(BF)
        back = nn(grad_cq[block], w_query[block])
        back_ref[...] += back
        w_query[block] = tn(grad_cq[block], two_low_ref[...]).astype(BF)
        return carry

    back_ref[...] = jnp.zeros_like(back_ref)
    branch_job.second()
    lax.fori_loop(0, blocks // 2, cross, 0)
    cross_job.far()
    cross_job.near()
    lax.fori_loop(blocks // 2, blocks, cross, 0)
    for index in range(4):
        query_job.pass_core(index)

    def second(part, sums):
        back, more = norm_back(back_ref[part], one_ref[part], gain_ref[1:2])
        total = grad_ref[part] + back
        grad_ref[part] = total
        low_ref[part] = total.astype(BF)
        return sums[0] + more[0], sums[1] + more[1]

    gain_two, shift_two = chunks(rows, second, nothing)
    cross_job.second()
    query_job.far()
    query_job.near()
    loads[2].wait()

    def out_weight(block, carry):
        grad_mix_ref[block] = nt(low_ref[...], w_out[block]).astype(BF)
        out_ref[block] = tn(my_mix_ref[block], low_ref[...]).astype(BF)
        return carry

    lax.fori_loop(0, blocks, out_weight, 0)
    branch_job.wait()

    def last(part, sums):
        branch = branch_job.value(part)
        total = two_ref[part] + branch
        layer_ref[part] = total.astype(BF)
        return (
            sums[0] + jnp.sum(total * total, axis=0, keepdims=True),
            sums[1] + jnp.sum(branch * branch, axis=0, keepdims=True),
        )

    square_out, square_three = chunks(rows, last, nothing)
    rest = jnp.zeros((1, width), F32)
    for index, row in enumerate(
        (rest, gain_two, gain_three, rest, shift_two, shift_three, square_out, square_three)
    ):
        stats_ref[index : index + 1] = row
    query_job.second()
    side_ref[1] = cross_job.total().astype(BF)
    side_ref[0] = query_job.total().astype(BF)
    branch_job.finish()
    cross_job.finish()
    query_job.finish()
    up_own.wait()
    for copy in up_moves:
        copy.wait()


def rows_back(
    normed, cot, one, two, query, mix, text, my_mix, gain, bias, weights, branch, up, ident
):
    rows, width = cot.shape
    blocks, _, columns = my_mix.shape
    return call(
        rows_back_kernel,
        "rows_back",
        (
            shape(rows, width, dtype=F32),
            shape(rows, width),
            shape(8, width, dtype=F32),
            shape(*my_mix.shape),
            shape(blocks, columns, width),
            shape(2, columns, width),
            shape(*text.shape),
            shape(*up.shape[:2], up.shape[2] // 2),
        ),
        (IN_VMEM,) * 7 + (ANY,),
        [IN_VMEM] * 10 + [ANY, ANY, ANY],
        [pltpu.VMEM((blocks, columns, width), BF)] * 3
        + [
            pltpu.VMEM((rows, width), BF),
            pltpu.VMEM((rows, width), BF),
            pltpu.VMEM((rows, width), F32),
            pltpu.VMEM(my_mix.shape, BF),
            pltpu.VMEM(my_mix.shape, BF),
            pltpu.SemaphoreType.DMA((4,)),
            pltpu.SemaphoreType.DMA((up.shape[0] - 1,)),
            pltpu.SemaphoreType.DMA((up.shape[0] - 1,)),
        ]
        + Scatter.scratch(columns, width) * 2
        + LoadedScatter.scratch(rows, width),
        ident,
        60,
    )(normed, cot, one, two, query, mix, text, my_mix, gain, bias, weights, branch, up)


def last_kernel(
    part_ref, frames_ref, gain_ref, grad_ref, stats_ref, qkv_ref, up_a, up_b, cross_ref, out_w_ref,
    text_ref, text_in, w_text_ref,
    out_ref, total_ref, text_out, qkv_out, up_out, cross_out, self_out, key_out,
    mine, came, all_ref, st_send, st_recv, z_send, z_recv,
    qkv_came, out_came, text_came, text_part, text_mine, text_all,
    qkv_pair, up_mine, up_pair, cross_pair, out_pair, key_pair, x_send, x_recv, *scratch,
):
    z = lax.axis_index("shard")
    shards = lax.axis_size("shard")
    others = shard_others()
    spot = place()[1:]
    context = spot[0]
    enter(neighbours() + [device(other, *spot) for other in others])

    def over(index, source_of, target_ref):
        return spread(source_of, target_ref, z_send.at[index], z_recv.at[index], others, spot)

    text_moves = over(0, lambda other: text_ref, text_came)
    qkv_moves = over(1, lambda other: qkv_ref.at[other], qkv_came)
    out_moves = over(2, lambda other: out_w_ref.at[other], out_came)
    size = len(scratch) - 5
    text = Scatter(text_part, *scratch[size:])
    job = LoadedScatter(part_ref, *scratch[:size])
    job.start()
    inputs = frames_ref[...].astype(F32)
    average = jnp.mean(inputs, axis=-1, keepdims=True)
    centred = inputs - average
    rate = lax.rsqrt(jnp.mean(centred * centred, axis=-1, keepdims=True) + EPS)
    for start, up_ref in ((0, up_a), (up_a.shape[2], up_b)):
        total = up_ref[0].astype(F32)
        for index in range(1, shards):
            total += up_ref[index].astype(F32)
        up_mine[:, start : start + up_ref.shape[2]] = total.astype(BF)
    text_came[z] = text_ref[...]
    for copy in text_moves:
        copy.wait_recv()
    job.first()
    texts = text_ref.shape[0] // 2
    own = texts // 8

    def text_back(index, carry):
        grads = nt(text_came[index], w_text_ref[...])
        rows = pl.ds(pl.multiple_of(index * 2 * own, 2 * own), 2 * own)
        for block in range(8):
            pair = [grads[k * texts + block * own : k * texts + block * own + own] for k in range(2)]
            text_part[block, rows] = jnp.concatenate(pair, axis=0).astype(BF)
        return carry

    lax.fori_loop(0, shards, text_back, 0)
    for index in range(4):
        text.pass_core(index)
    key_grad = tn(text_in[0], text_came[0])
    for index in range(1, shards):
        key_grad += tn(text_in[index], text_came[index])
    key_pair[0] = key_grad.astype(BF)
    text.far()
    text.near()
    job.second()
    to_x = neighbours()[0]

    def swap(index, source, target_ref):
        copy = remote_copy(source, target_ref, x_send.at[index], x_recv.at[index], to_x)
        copy.start()
        return copy

    text.second()
    grads = job.total()
    normed = centred * rate
    mine[0] = stats_ref[...]
    mine[0, 0:1] = jnp.sum(grads * normed, axis=0, keepdims=True)
    mine[0, 3:4] = jnp.sum(grads, axis=0, keepdims=True)
    sends = []
    for index, target in enumerate(neighbours()):
        copy = remote_copy(
            mine.at[index], came.at[index], st_send.at[index], st_recv.at[index], target
        )
        copy.start()
        sends.append(copy)
        if index == 0:
            pairs = [swap(0, up_mine, up_pair), swap(1, cross_ref, cross_pair)]
            pairs.append(swap(2, key_pair.at[0], key_pair.at[1]))
            text.wait()
            for block in range(shards):
                rows = slice(block * 2 * own, (block + 1) * 2 * own)
                text_mine[block] = text.value(rows).astype(BF)
            text_moves += over(3, lambda other: text_mine.at[other], text_all)
            text_all[z] = text_mine[z]
            scaled = grads * gain_ref[...]
            inner = jnp.mean(scaled * normed, axis=-1, keepdims=True)
            scaled = scaled - jnp.mean(scaled, axis=-1, keepdims=True) - normed * inner
            out_ref[...] = grad_ref[...] + rate * scaled
        copy.wait_recv()
        mine[index + 1] = mine[index] + came[index]
    stat_moves = over(4, lambda other: mine.at[3], all_ref)
    all_ref[z] = mine[3]

    def collect(moves, source_ref, came_ref):
        came_ref[z] = source_ref[z]
        for copy in moves:
            copy.wait_recv()
        total = came_ref[0].astype(F32)
        for index in range(1, shards):
            total += came_ref[index].astype(F32)
        return total.astype(BF)

    qkv_pair[0] = collect(qkv_moves, qkv_ref, qkv_came)
    pairs.append(swap(3, qkv_pair.at[0], qkv_pair.at[1]))
    out_pair[0] = collect(out_moves, out_w_ref, out_came)
    pairs.append(swap(4, out_pair.at[0], out_pair.at[1]))
    for copy in text_moves[shards - 1 :] + stat_moves:
        copy.wait_recv()
    text_out[...] = text_all[...].astype(F32)
    total = all_ref[0]
    for index in range(1, shards):
        total += all_ref[index]
    total_ref[...] = total
    beside(up_mine, pairs[0], up_pair, up_out)

    def ordered(first, second):
        return jnp.where(context == 0, first, second), jnp.where(context == 0, second, first)

    pairs[1].wait_recv()
    lead, trail = ordered(cross_ref[...], cross_pair[...])
    width = lead.shape[0] // 2
    for index in range(2):
        part = slice(index * width, (index + 1) * width)
        cross_out[index, :width] = lead[part]
        cross_out[index, width:] = trail[part]
    pairs[2].wait_recv()
    lead, trail = ordered(key_pair[0], key_pair[1])
    for index in range(2):
        lanes = slice(index * width, (index + 1) * width)
        key_out[index, :, :width] = lead[:, lanes]
        key_out[index, :, width:] = trail[:, lanes]
    pairs[3].wait_recv()
    lead, trail = ordered(qkv_pair[0], qkv_pair[1])
    for index in range(3):
        lanes = slice(index * width, (index + 1) * width)
        qkv_out[index, :, :width] = lead[:, lanes]
        qkv_out[index, :, width:] = trail[:, lanes]
    pairs[4].wait_recv()
    lead, trail = ordered(out_pair[0], out_pair[1])
    self_out[:width] = lead
    self_out[width:] = trail
    for copy in sends + text_moves + qkv_moves + out_moves + stat_moves + pairs:
        copy.wait_send()
    text.finish()
    job.finish()


def last_step(
    part, frames, gain, grad, stats, qkv, up_a, up_b, cross, out, text, text_in, w_text, ident
):
    _, rows, width = part.shape
    shards, texts, depth = text_in.shape
    half = 2 * up_a.shape[2]
    columns = out.shape[1]
    own = texts // 8
    return call(
        last_kernel,
        "last_step",
        (
            shape(rows, width, dtype=F32),
            shape(16, width, dtype=F32),
            shape(shards, own, depth, dtype=F32),
            shape(3, depth, 2 * columns),
            shape(depth, 2 * half),
            shape(2, 2 * columns, depth),
            shape(2 * columns, depth),
            shape(2, depth, 2 * columns),
        ),
        (IN_VMEM,) * 8,
        [ANY] + [IN_VMEM] * 12,
        [
            pltpu.VMEM((4, 16, width), F32),
            pltpu.VMEM((3, 16, width), F32),
            pltpu.VMEM((shards, 16, width), F32),
            pltpu.SemaphoreType.DMA((3,)),
            pltpu.SemaphoreType.DMA((3,)),
            pltpu.SemaphoreType.DMA((5, shards - 1)),
            pltpu.SemaphoreType.DMA((5, shards - 1)),
            pltpu.VMEM((shards, depth, 3 * columns), BF),
            pltpu.VMEM((shards, columns, depth), BF),
            pltpu.VMEM((shards, texts, 2 * columns), BF),
            pltpu.VMEM((8, shards * own, depth), BF),
            pltpu.VMEM((shards, own, depth), BF),
            pltpu.VMEM((shards, own, depth), BF),
            pltpu.VMEM((2, depth, 3 * columns), BF),
            pltpu.VMEM((depth, half), BF),
            pltpu.VMEM((depth, half), BF),
            pltpu.VMEM((2 * columns, depth), BF),
            pltpu.VMEM((2, columns, depth), BF),
            pltpu.VMEM((2, depth, 2 * columns), BF),
            pltpu.SemaphoreType.DMA((5,)),
            pltpu.SemaphoreType.DMA((5,)),
        ]
        + LoadedScatter.scratch(rows, width)
        + Scatter.scratch(shards * own, depth),
        ident,
        65,
    )(part, frames, gain, grad, stats, qkv, up_a, up_b, cross, out, text, text_in, w_text)


def dots(spec, *operands):
    return jnp.einsum(spec, *operands, preferred_element_type=F32)


def layer_norm(inputs, scaling, offset):
    average = jnp.mean(inputs, axis=-1, keepdims=True)
    centred = inputs - average
    variance = jnp.mean(centred * centred, axis=-1, keepdims=True)
    return centred * lax.rsqrt(variance + EPS) * scaling + offset


def on_device(
    frames,
    text_states,
    cotangent,
    norm_gain,
    norm_bias,
    self_qkv,
    self_out,
    cross_qkv,
    cross_out,
    mlp_up,
    mlp_down,
):
    clips, rows, width = frames.shape
    context = lax.axis_index("context")
    depth = self_qkv.shape[1]
    slices = width // depth
    columns = self_qkv.shape[2] // 2
    heads = columns // HEAD_DIM
    block = clips * rows
    texts = text_states.shape[1]

    def half(weight):
        size = weight.shape[-1] // 2
        return lax.dynamic_slice_in_dim(weight, context * size, size, weight.ndim - 1)

    def over_shard(weight, tiled=True):
        return lax.all_gather(weight, "shard", axis=0, tiled=tiled)

    cross_part = half(cross_qkv)
    qkv_part = half(self_qkv)
    early = [qkv_part[0], qkv_part[1], qkv_part[2], half(self_out), cross_part[0], half(cross_out)]
    w_early = over_shard(jnp.concatenate(early, axis=1))
    w_late = over_shard(jnp.concatenate([half(mlp_up), half(mlp_down)], axis=1))
    w_text = jnp.concatenate([cross_part[1], cross_part[2]], axis=1)
    text_slices = text_states.reshape(clips * texts, slices, depth).transpose(1, 0, 2)
    w_down = over_shard(half(mlp_down))

    all_one, all_grad, text_in, text_part = first_step(
        frames.reshape(block, width),
        norm_gain,
        norm_bias,
        cotangent.reshape(block, width),
        text_slices,
        w_text,
        0,
    )
    (
        qkv, self_log, mix, my_mix, stream_one, stream_two, cross_q, cross_mix, norm_three,
        text_all, squares, plane_w,
    ) = attend_forward(
        all_one,
        w_early,
        text_part,
        frames.reshape(block, width),
        norm_gain,
        norm_bias,
        1,
    )

    grad_normed, part_three, grad_up, grad_down = feed_forward(
        norm_three, all_grad, w_late, 4
    )

    def to_shard(part):
        return lax.psum_scatter(part.astype(BF), "shard", scatter_dimension=0, tiled=True)

    grad_down = to_shard(grad_down)
    grad_up = grad_up.reshape(slices, depth, -1)
    grad_one, layer_out, stats, grad_mix, part_out, side, text_grads, up_a = rows_back(
        grad_normed,
        cotangent.reshape(block, width),
        stream_one,
        stream_two,
        cross_q,
        cross_mix,
        text_all,
        my_mix,
        norm_gain,
        norm_bias,
        plane_w,
        part_three,
        grad_up,
        3,
    )

    def slice_shards(part):
        return part.reshape(-1, slices, depth).transpose(1, 0, 2)

    grad_cross = to_shard(slice_shards(side))[0]
    part_norm, grad_w_qkv, grad_out, text_grads, grad_down, up_b = attend_backward(
        grad_mix, qkv, mix, self_log, all_one, w_early, part_out, text_grads, grad_down, grad_up, 8
    )
    (
        grad_frames, totals, grad_text, grad_w_qkv, grad_up, grad_cross, grad_out, grad_keys,
    ) = last_step(
        part_norm,
        frames.reshape(block, width),
        norm_gain[0][None],
        grad_one,
        jnp.concatenate([stats, squares], axis=0),
        grad_w_qkv.reshape(slices, depth, 3 * columns),
        up_a,
        up_b,
        grad_cross,
        slice_shards(grad_out),
        text_grads,
        text_in,
        w_text,
        11,
    )
    grad_frames = grad_frames.reshape(clips, rows, width)
    grad_text = grad_text.transpose(1, 0, 2).reshape(clips, texts // 8, width)

    squares = totals[6:10].sum(axis=1)[jnp.array([0, 2, 3, 1])]
    start = lax.axis_index("shard") * depth
    grad_gain = lax.dynamic_slice_in_dim(totals[:3], start, depth, 1)
    grad_shift = lax.dynamic_slice_in_dim(totals[3:6], start, depth, 1)
    entries = float(clips * rows * width * lax.axis_size(("shard",) + PLANE))
    return (
        layer_out.reshape(clips, rows, width),
        grad_frames,
        grad_text,
        grad_gain,
        grad_shift,
        grad_w_qkv.astype(F32),
        grad_out.transpose(1, 0).astype(F32),
        jnp.concatenate([grad_cross[:1].transpose(0, 2, 1), grad_keys]).astype(F32),
        grad_cross[1].transpose(1, 0).astype(F32),
        grad_up.astype(F32),
        grad_down.astype(F32),
        jnp.sqrt(squares / entries),
    )


def solution(mesh):
    rows = P("shard", PLANE, None)
    stack = P(None, "shard", "tensor")
    flat = P("shard", "tensor")
    return jax.shard_map(
        on_device,
        mesh=mesh,
        in_specs=(rows, P("shard"), rows, P(), P(), stack, flat, stack, flat, flat, flat),
        out_specs=(
            (rows, rows, rows, P(None, "shard"), P(None, "shard"))
            + (stack, flat, stack, flat, flat, flat, P())
        ),
        check_vma=False,
    )
```

```python
from functools import partial

import jax
import jax.numpy as jnp
from jax import lax
from jax.experimental import pallas as pl
from jax.experimental.pallas import tpu as pltpu
from jax.sharding import PartitionSpec as P

HEAD_DIM = 64
EPS = 1e-05
MASKED = -1e30
MESH = pl.DeviceIdType.MESH
BF = jnp.bfloat16
F32 = jnp.float32
PLANE = ("context", "tensor")
VMEM_LIMIT = 60 * 2**20


def place():
    return (
        lax.axis_index("shard"),
        lax.axis_index("context"),
        lax.axis_index("tensor") // 2,
        lax.axis_index("tensor") % 2,
    )


def device(z, x, y, c):
    return (z, x, 2 * y + c)


def slot(x, y, c):
    return 4 * x + 2 * y + c


def neighbours():
    z, x, y, c = place()
    return [device(z, 1 - x, y, c), device(z, x, 1 - y, c), device(z, x, y, 1 - c)]


def plane_spots():
    z, x, y, c = place()
    steps = [(a, b, d) for a in range(2) for b in range(2) for d in range(2) if a + b + d]
    return [((x + a) % 2, (y + b) % 2, (c + d) % 2) for a, b, d in steps]


def plane_others():
    z = lax.axis_index("shard")
    return [device(z, *spot) for spot in plane_spots()]


def enter(targets):
    barrier = pltpu.get_barrier_semaphore()
    for target in targets:
        pl.semaphore_signal(barrier, inc=1, device_id=target, device_id_type=MESH)
    pl.semaphore_wait(barrier, len(targets))


def remote_copy(source, target_ref, send, recv, target):
    return pltpu.make_async_remote_copy(
        src_ref=source,
        dst_ref=target_ref,
        send_sem=send,
        recv_sem=recv,
        device_id=target,
        device_id_type=MESH,
    )


class Gather:
    semaphores = 9

    def __init__(self, in_ref, out_ref, local_sem, send, recv):
        z, x, y, c = place()
        self.in_ref, self.out_ref, self.local_sem = in_ref, out_ref, local_sem
        self.send, self.recv = send, recv
        self.spot = (x, y, c)
        self.to_x, self.to_y, self.to_c = neighbours()
        self.rows = in_ref.shape[0]
        self.sends = []

    def go(self, index, owner, start, size, target, source=None):
        there = self.out_ref.at[owner, pl.ds(start, size)]
        copy = remote_copy(
            there if source is None else source,
            there,
            self.send.at[index],
            self.recv.at[index],
            target,
        )
        copy.start()
        self.sends.append(copy)

    def arrived(self, index, owner, start, size):
        there = self.out_ref.at[owner, pl.ds(start, size)]
        remote_copy(
            there, there, self.send.at[index], self.recv.at[index], self.to_x
        ).wait_recv()

    def start(self):
        me = slot(*self.spot)
        self.own = pltpu.make_async_copy(self.in_ref, self.out_ref.at[me], self.local_sem)
        self.own.start()
        for index, target in enumerate((self.to_x, self.to_y, self.to_c)):
            self.go(index, me, 0, self.rows, target, self.in_ref)

    def relay_y(self):
        x, y, c = self.spot
        owner = slot(x, 1 - y, c)
        self.arrived(1, owner, 0, self.rows)
        self.go(3, owner, 0, self.rows // 2, self.to_x)
        self.go(5, owner, 0, self.rows, self.to_c)

    def relay_x(self):
        x, y, c = self.spot
        half = self.rows // 2
        owner = slot(1 - x, y, c)
        self.arrived(0, owner, 0, self.rows)
        self.go(4, owner, half, half, self.to_y)
        self.go(6, owner, 0, self.rows, self.to_c)

    def relay_far(self):
        x, y, c = self.spot
        half = self.rows // 2
        owner = slot(1 - x, 1 - y, c)
        self.arrived(3, owner, 0, half)
        self.go(7, owner, 0, half, self.to_c)
        self.arrived(4, owner, half, half)
        self.go(8, owner, half, half, self.to_c)

    def finish(self):
        x, y, c = self.spot
        half = self.rows // 2
        self.arrived(2, slot(x, y, 1 - c), 0, self.rows)
        self.arrived(5, slot(x, 1 - y, 1 - c), 0, self.rows)
        self.arrived(6, slot(1 - x, y, 1 - c), 0, self.rows)
        self.arrived(7, slot(1 - x, 1 - y, 1 - c), 0, half)
        self.arrived(8, slot(1 - x, 1 - y, 1 - c), half, half)
        self.own.wait()
        for copy in self.sends:
            copy.wait_send()

    def rest(self):
        self.relay_y()
        self.relay_x()
        self.relay_far()
        self.finish()


class Scatter:
    @staticmethod
    def scratch(rows, columns):
        return [
            pltpu.VMEM((4, rows, columns), BF),
            pltpu.VMEM((2, rows // 2, columns), BF),
            pltpu.VMEM((2, rows, columns), BF),
            pltpu.SemaphoreType.DMA((10,)),
            pltpu.SemaphoreType.DMA((10,)),
        ]

    def __init__(self, part_ref, core, relay, final, send, recv):
        self.part_ref, self.core, self.relay, self.final = part_ref, core, relay, final
        self.send, self.recv = send, recv
        self.to_x, self.to_y, self.to_c = neighbours()
        z, x, y, c = place()
        chips = ((1 - x, 1 - y), (1 - x, y), (x, 1 - y), (x, y))
        self.mine = [slot(*chip, c) for chip in chips]
        self.theirs = [slot(*chip, 1 - c) for chip in chips]
        rows = part_ref.shape[1]
        self.low, self.high = pl.ds(0, rows // 2), pl.ds(rows // 2, rows // 2)
        self.sends = []

    def forward(self, index, source, target_ref, target):
        copy = remote_copy(
            source, target_ref, self.send.at[index], self.recv.at[index], target
        )
        copy.start()
        self.sends.append(copy)

    def arrived(self, index, ref):
        remote_copy(ref, ref, self.send.at[index], self.recv.at[index], self.to_c).wait_recv()

    def pass_core(self, index):
        source = self.part_ref.at[self.theirs[index]]
        self.forward(index, source, self.core.at[index], self.to_c)

    def add(self, index, part, more=None):
        mine = self.mine[index]
        total = self.part_ref[mine, part].astype(F32) + self.core[index, part].astype(F32)
        if more is not None:
            total += more.astype(F32)
        self.part_ref[mine, part] = total.astype(BF)
        return self.part_ref.at[mine, part]

    def far(self):
        self.arrived(0, self.core.at[0])
        self.forward(4, self.add(0, self.low), self.relay.at[0], self.to_x)
        self.forward(5, self.add(0, self.high), self.relay.at[1], self.to_y)

    def near(self):
        self.arrived(1, self.core.at[1])
        self.forward(6, self.add(1, self.low), self.final.at[0, self.low], self.to_x)
        self.arrived(2, self.core.at[2])
        self.forward(7, self.add(2, self.high), self.final.at[1, self.high], self.to_y)

    def second(self):
        low, high, final, relay = self.low, self.high, self.final, self.relay
        self.arrived(5, relay.at[1])
        self.forward(8, self.add(1, high, relay[1]), final.at[0, high], self.to_x)
        self.arrived(4, relay.at[0])
        self.forward(9, self.add(2, low, relay[0]), final.at[1, low], self.to_y)

    def wait(self):
        self.arrived(3, self.core.at[3])
        self.arrived(6, self.final.at[0, self.low])
        self.arrived(7, self.final.at[1, self.high])
        self.arrived(8, self.final.at[0, self.high])
        self.arrived(9, self.final.at[1, self.low])

    def value(self, part=slice(None)):
        total = self.part_ref[self.mine[3], part].astype(F32) + self.core[3, part].astype(F32)
        return total + self.final[0, part].astype(F32) + self.final[1, part].astype(F32)

    def total(self):
        self.wait()
        return self.value()

    def finish(self):
        for copy in self.sends:
            copy.wait_send()


class LoadedScatter(Scatter):
    steep = False

    @staticmethod
    def scratch(rows, columns):
        return [
            pltpu.VMEM((4, rows, columns), BF),
            pltpu.SemaphoreType.DMA((4,)),
        ] + Scatter.scratch(rows, columns)

    def __init__(self, in_ref, part_ref, local_sem, *scratch):
        super().__init__(part_ref, *scratch)
        self.in_ref, self.local_sem = in_ref, local_sem

    def bring(self, index):
        source = self.in_ref.at[self.theirs[index]]
        self.forward(index, source, self.core.at[index], self.to_c)
        load = pltpu.make_async_copy(
            self.in_ref.at[self.blocks[index]], self.part_ref.at[index], self.local_sem.at[index]
        )
        load.start()
        self.loads.append(load)

    def start(self):
        self.loads = []
        self.blocks, self.mine = self.mine, (0, 1, 2, 3)
        for index in range(4):
            self.bring(index)

    def first(self):
        for load in self.loads:
            load.wait()
        if not self.steep:
            self.far()
            self.near()
            return
        self.arrived(0, self.core.at[0])
        self.forward(4, self.add(0, self.low), self.relay.at[0], self.to_y)
        self.forward(5, self.add(0, self.high), self.relay.at[1], self.to_y)
        self.arrived(2, self.core.at[2])
        self.forward(7, self.add(2, self.high), self.final.at[1, self.high], self.to_y)
        self.forward(9, self.add(2, self.low), self.final.at[1, self.low], self.to_y)

    def second(self):
        if not self.steep:
            super().second()
            return
        final, relay = self.final, self.relay
        self.arrived(1, self.core.at[1])
        self.arrived(4, relay.at[0])
        self.forward(6, self.add(1, self.low, relay[0]), final.at[0, self.low], self.to_x)
        self.arrived(5, relay.at[1])
        self.forward(8, self.add(1, self.high, relay[1]), final.at[0, self.high], self.to_x)


class SteepScatter(LoadedScatter):
    steep = True


class Exchange:
    def __init__(self, in_ref, out_ref, local_sem, send, recv):
        self.in_ref, self.out_ref, self.local_sem = in_ref, out_ref, local_sem
        self.send, self.recv = send, recv
        z, x, y, c = place()
        self.me = slot(x, y, c)
        self.copies = []

    def start(self, piece, part):
        z = lax.axis_index("shard")
        own = pltpu.make_async_copy(
            self.in_ref.at[self.me, part], self.out_ref.at[self.me, part], self.local_sem.at[piece]
        )
        own.start()
        self.copies.append(own)
        for index, spot in enumerate(plane_spots()):
            copy = remote_copy(
                self.in_ref.at[slot(*spot), part],
                self.out_ref.at[self.me, part],
                self.send.at[piece, index],
                self.recv.at[piece, index],
                device(z, *spot),
            )
            copy.start()
            self.copies.append(copy)

    def finish(self, piece=None):
        copies = self.copies if piece is None else self.copies[8 * piece : 8 * piece + 8]
        for copy in copies:
            copy.wait()


ANY = pl.BlockSpec(memory_space=pl.ANY)
IN_VMEM = pl.BlockSpec(memory_space=pltpu.VMEM)


def call(kernel, name, outs, out_specs, in_specs, scratch, ident, micros):
    return pl.pallas_call(
        kernel,
        out_shape=outs,
        in_specs=in_specs,
        out_specs=out_specs,
        scratch_shapes=scratch,
        name=name,
        cost_estimate=pl.CostEstimate(
            flops=micros * 10**9, bytes_accessed=micros * 10**6, transcendentals=0
        ),
        compiler_params=pltpu.CompilerParams(
            collective_id=ident, has_side_effects=True, vmem_limit_bytes=VMEM_LIMIT
        ),
    )


def shape(*dims, dtype=BF):
    return jax.ShapeDtypeStruct(dims, dtype)


def gather_scratch():
    return [
        pltpu.SemaphoreType.DMA,
        pltpu.SemaphoreType.DMA((9,)),
        pltpu.SemaphoreType.DMA((9,)),
    ]


def shard_others():
    z, shards = lax.axis_index("shard"), lax.axis_size("shard")
    return [lax.rem(z + i, shards) for i in range(1, shards)]


def spread(source_of, target_ref, send, recv, others, spot):
    z = lax.axis_index("shard")
    copies = []
    for index, other in enumerate(others):
        copy = remote_copy(
            source_of(other), target_ref.at[z], send.at[index], recv.at[index],
            device(other, *spot),
        )
        copy.start()
        copies.append(copy)
    return copies


def first_kernel(
    frames_ref, gain_ref, bias_ref, cot_ref, text_ref, w_text_ref,
    rows_out, cot_out, text_all, text_out,
    normed_ref, part_ref, came_ref, sends, recvs, *scratch,
):
    z = lax.axis_index("shard")
    spot = place()[1:]
    others = shard_others()
    enter(neighbours() + [device(other, *spot) for other in others])
    texts = spread(lambda other: text_ref.at[other], text_all, sends.at[0], recvs.at[0], others, spot)
    text_all[z] = text_ref[z]

    def norm(part, carry):
        normed, _ = normalise(frames_ref[part].astype(F32))
        normed_ref[part] = (normed * gain_ref[0:1] + bias_ref[0:1]).astype(BF)
        return carry

    chunks(frames_ref.shape[0], norm)
    rows, grads = Gather(normed_ref, rows_out, *scratch[:3]), Gather(cot_ref, cot_out, *scratch[3:])
    rows.start()
    for copy in texts:
        copy.wait_recv()

    def share(index, carry):
        part_ref[index] = nn(text_all[index], w_text_ref[...]).astype(BF)
        return carry

    lax.fori_loop(0, text_all.shape[0], share, 0)
    parts = spread(lambda other: part_ref.at[other], came_ref, sends.at[1], recvs.at[1], others, spot)
    came_ref[z] = part_ref[z]
    rows.relay_y()
    rows.relay_x()
    grads.start()
    rows.relay_far()
    rows.finish()
    grads.rest()
    for copy in parts:
        copy.wait_recv()
    total = came_ref[0].astype(F32)
    for index in range(1, came_ref.shape[0]):
        total += came_ref[index].astype(F32)
    text_out[...] = total.astype(BF)
    for copy in texts + parts:
        copy.wait_send()


def first_step(frames, gain, bias, cotangent, text, w_text, ident):
    rows, width = frames.shape
    shards, texts, depth = text.shape
    return call(
        first_kernel,
        "first_step",
        (
            shape(8, rows, width),
            shape(8, rows, width),
            shape(shards, texts, depth),
            shape(texts, w_text.shape[1]),
        ),
        (ANY, ANY, IN_VMEM, IN_VMEM),
        [IN_VMEM, IN_VMEM, IN_VMEM, ANY, IN_VMEM, IN_VMEM],
        [
            pltpu.VMEM((rows, width), BF),
            pltpu.VMEM((shards, texts, w_text.shape[1]), BF),
            pltpu.VMEM((shards, texts, w_text.shape[1]), BF),
            pltpu.SemaphoreType.DMA((2, shards - 1)),
            pltpu.SemaphoreType.DMA((2, shards - 1)),
        ]
        + gather_scratch() * 2,
        ident,
        60,
    )(frames, gain, bias, cotangent, text, w_text)


def feed_kernel(
    own_ref, grad_ref, w_ref,
    normed_out, branch_out, up_out, down_out,
    rows_ref, grads_ref, hidden_ref, slope_ref, part_a, part_b,
    load_sem, store_sem, g_local, g_send, g_recv, *scratch,
):
    enter(neighbours())
    gather = Gather(own_ref, rows_ref, g_local, g_send, g_recv)
    gather.start()
    hidden = hidden_ref.shape[2]
    up_ref, down_ref = w_ref.at[:, pl.ds(0, hidden)], w_ref.at[:, pl.ds(hidden, hidden)]
    blocks, _, width = rows_ref.shape
    loads = []
    for block in range(blocks):
        load = pltpu.make_async_copy(grad_ref.at[block], grads_ref.at[block], load_sem.at[block])
        load.start()
        loads.append(load)
    for load in loads:
        load.wait()

    def early(block, carry):
        slope_ref[block] = nn(grads_ref[block], down_ref[...]).astype(BF)
        return carry

    lax.fori_loop(0, blocks, early, 0)

    def middle(block):
        before = nn(rows_ref[block], up_ref[...])
        share = 0.5 + 0.5 * lax.erf(before * (0.5**0.5))
        hidden_ref[block] = (before * share).astype(BF)
        slope = share + before * (jnp.exp(-0.5 * before * before) * (2.0 * jnp.pi) ** (-0.5))
        slope = (slope_ref[block].astype(F32) * slope).astype(BF)
        slope_ref[block] = slope
        part_a[block] = nt(slope, up_ref[...]).astype(BF)

    first = Scatter(part_a, *scratch)
    x, y, c = gather.spot

    def pair(cx, cy):
        def one(index, carry):
            middle(slot(cx, cy, 0) + index)
            return carry

        lax.fori_loop(0, 2, one, 0)

    gather.own.wait()
    gather.arrived(2, slot(x, y, 1 - c), 0, gather.rows)
    pair(x, y)
    first.pass_core(3)
    gather.relay_y()
    gather.relay_x()
    gather.arrived(6, slot(1 - x, y, 1 - c), 0, gather.rows)
    pair(1 - x, y)
    first.pass_core(1)
    gather.arrived(5, slot(x, 1 - y, 1 - c), 0, gather.rows)
    pair(x, 1 - y)
    first.pass_core(2)
    gather.relay_far()
    first.near()
    gather.arrived(7, slot(1 - x, 1 - y, 1 - c), 0, gather.rows // 2)
    gather.arrived(8, slot(1 - x, 1 - y, 1 - c), gather.rows // 2, gather.rows // 2)
    pair(1 - x, 1 - y)
    first.pass_core(0)
    first.far()
    for copy in gather.sends:
        copy.wait_send()

    def store(block):
        return pltpu.make_async_copy(part_b.at[block], branch_out.at[block], store_sem.at[block])

    def branch(block, carry):
        part_b[block] = nt(hidden_ref[block], down_ref[...]).astype(BF)
        store(block).start()
        return carry

    lax.fori_loop(0, blocks, branch, 0)
    first.second()
    tile = 256

    def weight(left_ref, right_ref, out_ref):
        right = right_ref[...].reshape(-1, right_ref.shape[2])

        def one(index, carry):
            lanes = pl.ds(pl.multiple_of(index * tile, tile), tile)
            left = left_ref[:, :, lanes].reshape(-1, tile)
            out_ref[lanes, :] = tn(left, right).astype(BF)
            return carry

        lax.fori_loop(0, width // tile, one, 0)

    weight(grads_ref, hidden_ref, down_out)
    weight(rows_ref, slope_ref, up_out)
    normed_out[...] = first.total()
    first.finish()
    for block in range(blocks):
        store(block).wait()


def feed_forward(own, grads, weights, ident):
    rows, width = own.shape
    hidden = weights.shape[1] // 2
    outs = (
        shape(rows, width, dtype=F32),
        shape(8, rows, width),
        shape(width, hidden),
        shape(width, hidden),
    )
    scratch = [
        pltpu.VMEM((8, rows, width), BF),
        pltpu.VMEM((8, rows, width), BF),
        pltpu.VMEM((8, rows, hidden), BF),
        pltpu.VMEM((8, rows, hidden), BF),
        pltpu.VMEM((8, rows, width), BF),
        pltpu.VMEM((8, rows, width), BF),
        pltpu.SemaphoreType.DMA((8,)),
        pltpu.SemaphoreType.DMA((8,)),
    ]
    return call(
        feed_kernel,
        "feed_forward",
        outs,
        (IN_VMEM, ANY, IN_VMEM, IN_VMEM),
        [ANY, ANY, IN_VMEM],
        scratch + gather_scratch() + Scatter.scratch(rows, width),
        ident,
        70,
    )(own, grads, weights)


SIDE = 256


def nt(left, right):
    return lax.dot_general(left, right, (((1,), (1,)), ((), ())), preferred_element_type=F32)


def nn(left, right):
    return lax.dot_general(left, right, (((1,), (0,)), ((), ())), preferred_element_type=F32)


def tn(left, right):
    return lax.dot_general(left, right, (((0,), (0,)), ((), ())), preferred_element_type=F32)


def turn(values):
    return jnp.transpose(values.astype(F32))


def side_by_side(ref):
    return jnp.concatenate([ref[block] for block in range(ref.shape[0])], axis=1)


def all_rows(ref):
    return ref[...].reshape(-1, ref.shape[2])


def split_columns(values, ref):
    columns = ref.shape[2]
    for block in range(ref.shape[0]):
        ref[block] = values[:, block * columns : (block + 1) * columns].astype(BF)


def causal(scores):
    keys = lax.broadcasted_iota(jnp.int32, scores.shape, 0)
    queries = lax.broadcasted_iota(jnp.int32, scores.shape, 1)
    return jnp.where(keys <= queries, scores, MASKED)


def forward_kernel(
    rows_ref, side_ref, text_in, frames_ref, gain_ref, bias_ref,
    qkv_ref, log_ref, mix_ref, mine_ref, one_ref, two_ref, query_ref, cross_ref, low_ref,
    text_ref, square_ref, plane_out,
    w_own, w_out, w_query, w_cross, sum_ref, two_low_ref, store_sem,
    ex_local, ex_send, ex_recv, *scratch,
):
    enter(plane_others())
    blocks, both, _ = rows_ref.shape
    rows = both // 2
    width = mix_ref.shape[2]
    features = two_low_ref.shape[1]
    heads = width // HEAD_DIM
    length = blocks * rows
    step = SIDE // rows
    weights = (w_out, w_query, w_cross)

    def turn_own(kind):
        w_own[kind] = turn(side_ref[:, (3 + kind) * width : (4 + kind) * width]).astype(BF)

    turn_own(0)
    jobs = [Gather(w_own.at[k], weights[k], *scratch[3 * k : 3 * k + 3]) for k in range(3)]
    text_job = Gather(text_in, text_ref, *scratch[9:])
    text_job.start()
    jobs[0].start()
    stores = []

    def keep(kind):
        copy = pltpu.make_async_copy(weights[kind], plane_out.at[kind], store_sem.at[kind])
        copy.start()
        stores.append(copy)

    def project(block, carry):
        qkv_ref[block] = nn(rows_ref[block], side_ref[:, : 3 * width]).astype(BF)
        return carry

    lax.fori_loop(0, blocks, project, 0)
    turn_own(1)
    turn_own(2)
    exchange = Exchange(mix_ref, mine_ref, ex_local, ex_send, ex_recv)
    for clip in range(2):
        part = pl.ds(clip * rows, rows)
        for head in range(heads):
            lanes = [pl.ds(j * width + head * HEAD_DIM, HEAD_DIM) for j in range(3)]
            key = qkv_ref[:, part, lanes[1]].reshape(length, HEAD_DIM)
            value = turn(qkv_ref[:, part, lanes[2]].reshape(length, HEAD_DIM)).astype(BF)
            for index in range(length // SIDE):
                spots = pl.ds(index * step, step)
                query = qkv_ref[spots, part, lanes[0]].reshape(SIDE, HEAD_DIM)
                query = query * jnp.asarray(HEAD_DIM ** (-0.5), BF)
                start = index * SIDE
                last = causal(nt(key[start : start + SIDE], query))
                top = jnp.max(last, axis=0, keepdims=True)
                if index:
                    early = nt(key[:start], query)
                    top = jnp.maximum(top, jnp.max(early, axis=0, keepdims=True))
                last = jnp.exp(last - top)
                total = jnp.sum(last, axis=0, keepdims=True)
                mix = nn(value[:, start : start + SIDE], last.astype(BF))
                if index:
                    early = jnp.exp(early - top)
                    total += jnp.sum(early, axis=0, keepdims=True)
                    mix += nn(value[:, :start], early.astype(BF))
                mix = jnp.transpose(mix / total).astype(BF).reshape(step, rows, HEAD_DIM)
                mix_ref[spots, part, pl.ds(head * HEAD_DIM, HEAD_DIM)] = mix
                log_ref[pl.ds(clip * heads + head, 1), pl.ds(start, SIDE)] = top + jnp.log(total)
        exchange.start(clip, part)
        if clip == 0:
            jobs[0].relay_y()
            jobs[0].relay_x()
            text_job.relay_y()
            text_job.relay_x()
    jobs[1].start()
    jobs[0].relay_far()
    text_job.relay_far()
    jobs[0].finish()
    text_job.finish()
    keep(0)
    exchange.finish()

    def apply(values_ref, kind):
        sum_ref[...] = nn(side_by_side(values_ref), all_rows(weights[kind]))

    apply(mine_ref, 0)
    nothing = jnp.zeros((1, features), F32)

    def first(part, sums):
        branch = sum_ref[part]
        total = frames_ref[part].astype(F32) + branch
        one_ref[part] = total
        normed, _ = normalise(total)
        two_low_ref[part] = (normed * gain_ref[1:2] + bias_ref[1:2]).astype(BF)
        return sums + jnp.sum(branch * branch, axis=0, keepdims=True)

    square_one = chunks(both, first, nothing)
    jobs[1].relay_y()
    jobs[1].relay_x()
    jobs[2].start()
    jobs[1].relay_far()
    jobs[1].finish()
    keep(1)

    split_columns(nt(two_low_ref[...], all_rows(w_query)), query_ref)
    texts = text_ref.shape[1] // 2

    def cross(block, carry):
        for clip in range(2):
            part = pl.ds(clip * rows, rows)
            keys = pl.ds(clip * texts, texts)
            for head in range(heads):
                here = pl.ds(head * HEAD_DIM, HEAD_DIM)
                query = query_ref[block, part, here] * jnp.asarray(HEAD_DIM ** (-0.5), BF)
                there = pl.ds(width + head * HEAD_DIM, HEAD_DIM)
                scores = nt(text_ref[block, keys, here], query)
                probs = jnp.exp(scores - jnp.max(scores, axis=0, keepdims=True))
                probs = probs / jnp.sum(probs, axis=0, keepdims=True)
                mix = nn(turn(text_ref[block, keys, there]).astype(BF), probs.astype(BF))
                cross_ref[block, part, here] = jnp.transpose(mix).astype(BF)
        return carry

    lax.fori_loop(0, blocks // 2, cross, 0)
    jobs[2].relay_y()
    jobs[2].relay_x()
    lax.fori_loop(blocks // 2, blocks, cross, 0)
    jobs[2].relay_far()
    jobs[2].finish()
    keep(2)
    apply(cross_ref, 2)

    def second(part, sums):
        branch = sum_ref[part]
        total = one_ref[part] + branch
        two_ref[part] = total
        normed, _ = normalise(total)
        low_ref[part] = (normed * gain_ref[2:3] + bias_ref[2:3]).astype(BF)
        return sums + jnp.sum(branch * branch, axis=0, keepdims=True)

    square_two = chunks(both, second, nothing)
    square_ref[...] = jnp.zeros_like(square_ref)
    square_ref[0:1] = square_one
    square_ref[1:2] = square_two
    for copy in stores:
        copy.wait()


def attend_forward(rows, side, text, frames, gain, bias, ident):
    blocks, block, width = rows.shape
    columns = side.shape[1] // 6
    heads = columns // HEAD_DIM
    heads_shape = shape(blocks, block, columns)
    stream = shape(block, width, dtype=F32)
    return call(
        forward_kernel,
        "attend_forward",
        (
            shape(blocks, block, 3 * columns),
            shape(2 * heads, blocks * block // 2, dtype=F32),
            heads_shape,
            heads_shape,
            stream,
            stream,
            heads_shape,
            heads_shape,
            shape(block, width),
            shape(blocks, *text.shape),
            shape(8, width, dtype=F32),
            shape(3, blocks, columns, width),
        ),
        (IN_VMEM,) * 11 + (ANY,),
        [IN_VMEM] * 2 + [ANY] + [IN_VMEM] * 3,
        [pltpu.VMEM((3, columns, width), BF)]
        + [pltpu.VMEM((blocks, columns, width), BF)] * 3
        + [
            pltpu.VMEM((block, width), F32),
            pltpu.VMEM((block, width), BF),
            pltpu.SemaphoreType.DMA((4,)),
            pltpu.SemaphoreType.DMA((2,)),
            pltpu.SemaphoreType.DMA((2, 7)),
            pltpu.SemaphoreType.DMA((2, 7)),
        ]
        + gather_scratch() * 4,
        ident,
        80,
    )(rows, side, text, frames, gain, bias)


def beside(own_ref, copy, other_ref, out_ref):
    half = own_ref.shape[1]
    context = lax.axis_index("context")
    out_ref[:, pl.ds(pl.multiple_of(context * half, half), half)] = own_ref[...]
    copy.wait_recv()
    there = pl.ds(pl.multiple_of((1 - context) * half, half), half)
    out_ref[:, there] = other_ref[...]


def backward_kernel(
    grad_ref, qkv_ref, mix_ref, log_ref, rows_ref, w_ref, side_ref, text_ref, down_ref, up_ref,
    part_out, w_out, side_out, text_out, down_out, up_came,
    up_send, up_recv, out_ref, part_ref, store_sem, down_pair, pair_sem, grad_all, query_turned, ex_local, ex_send, ex_recv, *scratch,
):
    z = lax.axis_index("shard")
    spot = place()[1:]
    others = shard_others()
    enter(plane_others() + [device(other, *spot) for other in others])
    exchange = Exchange(grad_ref, grad_all, ex_local, ex_send, ex_recv)
    blocks, both, width = mix_ref.shape
    rows = both // 2
    heads = width // HEAD_DIM
    length = blocks * rows
    step = SIDE // rows
    for clip in range(2):
        exchange.start(clip, pl.ds(clip * rows, rows))
    some = pl.ds(up_came.shape[2], up_came.shape[2])
    up_moves = spread(
        lambda other: up_ref.at[other, :, some], up_came, up_send, up_recv, others, spot
    )
    up_own = pltpu.make_async_copy(up_ref.at[z, :, some], up_came.at[z], pair_sem.at[2])
    up_own.start()
    size = len(scratch) // 2
    text = LoadedScatter(text_ref, *scratch[size:])
    text.start()
    text.first()
    side = LoadedScatter(side_ref, *scratch[:size])
    side.start()
    side.first()
    for clip in range(2):
        exchange.finish(clip)
        part = pl.ds(clip * rows, rows)
        for head in range(heads):
            lanes = [pl.ds(j * width + head * HEAD_DIM, HEAD_DIM) for j in range(3)]
            query = qkv_ref[:, part, lanes[0]].reshape(length, HEAD_DIM)
            query = query * jnp.asarray(HEAD_DIM ** (-0.5), BF)
            key = qkv_ref[:, part, lanes[1]].reshape(length, HEAD_DIM)
            value = qkv_ref[:, part, lanes[2]].reshape(length, HEAD_DIM)
            key_turned = turn(key).astype(BF)
            here = pl.ds(head * HEAD_DIM, HEAD_DIM)
            grad = grad_all[:, part, here].reshape(length, HEAD_DIM)
            mixed = mix_ref[:, part, here].reshape(length, HEAD_DIM)
            inner = jnp.transpose(grad.astype(F32) * mixed.astype(F32))
            inner = jnp.sum(inner, axis=0, keepdims=True)
            logs = log_ref[pl.ds(clip * heads + head, 1), :]
            for index in range(length // SIDE):
                start = index * SIDE
                spots = pl.ds(index * step, step)
                k_part, v_part = key[start : start + SIDE], value[start : start + SIDE]
                scores = nt(k_part, query[start:])
                first = causal(scores[:, :SIDE])
                if start + SIDE < length:
                    scores = jnp.concatenate([first, scores[:, SIDE:]], axis=1)
                else:
                    scores = first
                weights = jnp.exp(scores - logs[:, start:])
                slopes = nt(v_part, grad[start:])
                slopes = (weights * (slopes - inner[:, start:])).astype(BF)
                grad_key = nn(slopes, query[start:]).astype(BF).reshape(step, rows, HEAD_DIM)
                grad_value = nn(weights.astype(BF), grad[start:]).astype(BF)
                out_ref[spots, part, lanes[1]] = grad_key
                out_ref[spots, part, lanes[2]] = grad_value.reshape(step, rows, HEAD_DIM)
                grad_query = nn(key_turned[:, start : start + SIDE], slopes)
                if index:
                    query_turned[:, start:] += grad_query
                else:
                    query_turned[...] = grad_query
            grad_query = jnp.transpose(query_turned[...]) * HEAD_DIM ** (-0.5)
            grad_query = grad_query.astype(BF).reshape(blocks, rows, HEAD_DIM)
            out_ref[:, part, lanes[0]] = grad_query
        if clip == 0:
            text.second()
            side.second()
            to_x = neighbours()[0]
            pair = remote_copy(down_ref, down_pair, pair_sem.at[0], pair_sem.at[1], to_x)
            pair.start()

    def store(block):
        return pltpu.make_async_copy(part_ref.at[block], part_out.at[block], store_sem.at[block])

    def project(block, carry):
        part_ref[block] = nt(out_ref[block], w_ref[:, : 3 * width]).astype(BF)
        store(block).start()
        return carry

    lax.fori_loop(0, blocks, project, 0)
    tile = 256
    right = out_ref[...].reshape(blocks * both, 3 * width)

    def weight(index, carry):
        lanes = pl.ds(pl.multiple_of(index * tile, tile), tile)
        left = rows_ref[:, :, lanes].reshape(blocks * both, tile)
        w_out[lanes, :] = tn(left, right).astype(BF)
        return carry

    lax.fori_loop(0, w_out.shape[0] // tile, weight, 0)
    text_out[...] = text.total().astype(BF)
    side_out[...] = side.total().astype(BF)
    text.finish()
    side.finish()
    beside(down_ref, pair, down_pair, down_out)
    pair.wait_send()
    up_own.wait()
    for copy in up_moves:
        copy.wait()
    for block in range(blocks):
        store(block).wait()


def attend_backward(grad_mix, qkv, mix, logs, rows, weights, side, text, down, up, ident):
    blocks, block, columns = mix.shape
    _, side_rows, width = side.shape
    text_shape = text.shape[1:]
    return call(
        backward_kernel,
        "attend_backward",
        (
            shape(blocks, block, width),
            shape(width, 3 * columns),
            shape(side_rows, width),
            shape(*text_shape),
            shape(down.shape[0], 2 * down.shape[1]),
            shape(*up.shape[:2], up.shape[2] // 2),
        ),
        (ANY, IN_VMEM, IN_VMEM, IN_VMEM, IN_VMEM, ANY),
        [ANY] + [IN_VMEM] * 5 + [ANY, ANY, IN_VMEM, ANY],
        [
            pltpu.SemaphoreType.DMA((up.shape[0] - 1,)),
            pltpu.SemaphoreType.DMA((up.shape[0] - 1,)),
            pltpu.VMEM((blocks, block, 3 * columns), BF),
            pltpu.VMEM((blocks, block, width), BF),
            pltpu.SemaphoreType.DMA((8,)),
            pltpu.VMEM(down.shape, BF),
            pltpu.SemaphoreType.DMA((3,)),
            pltpu.VMEM((blocks, block, columns), BF),
            pltpu.VMEM((HEAD_DIM, blocks * block // 2), F32),
            pltpu.SemaphoreType.DMA((2,)),
            pltpu.SemaphoreType.DMA((2, 7)),
            pltpu.SemaphoreType.DMA((2, 7)),
        ]
        + LoadedScatter.scratch(side_rows, width)
        + LoadedScatter.scratch(*text_shape),
        ident,
        1,
    )(grad_mix, qkv, mix, logs, rows, weights, side, text, down, up)


CHUNK = 64


def chunks(rows, body, carry=None):
    def one(index, carry):
        return body(pl.ds(pl.multiple_of(index * CHUNK, CHUNK), CHUNK), carry)

    return lax.fori_loop(0, rows // CHUNK, one, 0 if carry is None else carry)


def normalise(inputs):
    average = jnp.mean(inputs, axis=-1, keepdims=True)
    centred = inputs - average
    rate = lax.rsqrt(jnp.mean(centred * centred, axis=-1, keepdims=True) + EPS)
    return centred * rate, rate


def norm_back(grads, inputs, gain):
    normed, rate = normalise(inputs)
    scaled = grads * gain
    inner = jnp.mean(scaled * normed, axis=-1, keepdims=True)
    result = rate * (scaled - jnp.mean(scaled, axis=-1, keepdims=True) - normed * inner)
    sums = (
        jnp.sum(grads * normed, axis=0, keepdims=True),
        jnp.sum(grads, axis=0, keepdims=True),
    )
    return result, sums


def rows_back_kernel(
    normed_ref, cot_ref, one_ref, two_ref, query_ref, mix_ref, text_ref, my_mix_ref,
    gain_ref, bias_ref, w_ref, branch_ref, up_ref,
    grad_ref, layer_ref, stats_ref, grad_mix_ref, out_ref, side_ref, text_out, up_came,
    w_cross, w_query, w_out, low_ref, two_low_ref, back_ref, grad_cm, grad_cq, w_sem,
    up_send, up_recv, *scratch,
):
    z = lax.axis_index("shard")
    spot = place()[1:]
    others = shard_others()
    enter(neighbours() + [device(other, *spot) for other in others])
    some = pl.ds(0, up_came.shape[2])
    up_moves = spread(
        lambda other: up_ref.at[other, :, some], up_came, up_send, up_recv, others, spot
    )
    up_own = pltpu.make_async_copy(up_ref.at[z, :, some], up_came.at[z], w_sem.at[3])
    up_own.start()
    cross_job = Scatter(w_cross, *scratch[:5])
    query_job = Scatter(w_query, *scratch[5:10])
    branch_job = LoadedScatter(branch_ref, *scratch[10:])
    branch_job.start()
    blocks, columns, width = w_out.shape
    rows = low_ref.shape[0]
    heads = columns // HEAD_DIM
    loads = []
    for index, buffer in ((2, w_cross), (1, w_query), (0, w_out)):
        load = pltpu.make_async_copy(
            w_ref.at[index], buffer, w_sem.at[index]
        )
        load.start()
        loads.append(load)
    nothing = (jnp.zeros((1, width), F32),) * 2

    def third(part, sums):
        back, more = norm_back(normed_ref[part], two_ref[part], gain_ref[2:3])
        total = cot_ref[part].astype(F32) + back
        grad_ref[part] = total
        low_ref[part] = total.astype(BF)
        normed, _ = normalise(one_ref[part])
        two_low_ref[part] = (normed * gain_ref[1:2] + bias_ref[1:2]).astype(BF)
        return sums[0] + more[0], sums[1] + more[1]

    gain_three, shift_three = chunks(rows, third, nothing)
    branch_job.first()
    loads[0].wait()

    split_columns(nt(low_ref[...], all_rows(w_cross)), grad_cm)

    def cross_weight(block, carry):
        w_cross[block] = tn(mix_ref[block], low_ref[...]).astype(BF)
        return carry

    lax.fori_loop(0, blocks, cross_weight, 0)
    for index in range(4):
        cross_job.pass_core(index)
    half = rows // 2
    texts = text_ref.shape[1] // 2
    loads[1].wait()

    def cross(block, carry):
        for clip in range(2):
            part = pl.ds(clip * half, half)
            keys = pl.ds(clip * texts, texts)
            for head in range(heads):
                here = pl.ds(head * HEAD_DIM, HEAD_DIM)
                query = query_ref[block, part, here] * jnp.asarray(HEAD_DIM ** (-0.5), BF)
                there = pl.ds(columns + head * HEAD_DIM, HEAD_DIM)
                key, value = text_ref[block, keys, here], text_ref[block, keys, there]
                grad = grad_cm[block, part, here]
                scores = nt(key, query)
                weights = jnp.exp(scores - jnp.max(scores, axis=0, keepdims=True))
                weights = weights / jnp.sum(weights, axis=0, keepdims=True)
                slopes = nt(value, grad)
                inner = jnp.sum(weights * slopes, axis=0, keepdims=True)
                slopes = (weights * (slopes - inner)).astype(BF)
                grad_query = jnp.transpose(nn(turn(key).astype(BF), slopes))
                grad_cq[block, part, here] = (grad_query * HEAD_DIM ** (-0.5)).astype(BF)
                text_out[block, keys, here] = nn(slopes, query).astype(BF)
                text_out[block, keys, there] = nn(weights.astype(BF), grad).astype(BF)
        return carry

    def query_weight(block, carry):
        w_query[block] = tn(grad_cq[block], two_low_ref[...]).astype(BF)
        return carry

    branch_job.second()
    lax.fori_loop(0, blocks // 2, cross, 0)
    cross_job.far()
    cross_job.near()
    lax.fori_loop(blocks // 2, blocks, cross, 0)
    back_ref[...] = nn(side_by_side(grad_cq), all_rows(w_query))
    lax.fori_loop(0, blocks, query_weight, 0)
    for index in range(4):
        query_job.pass_core(index)

    def second(part, sums):
        back, more = norm_back(back_ref[part], one_ref[part], gain_ref[1:2])
        total = grad_ref[part] + back
        grad_ref[part] = total
        low_ref[part] = total.astype(BF)
        return sums[0] + more[0], sums[1] + more[1]

    gain_two, shift_two = chunks(rows, second, nothing)
    cross_job.second()
    query_job.far()
    query_job.near()
    loads[2].wait()

    split_columns(nt(low_ref[...], all_rows(w_out)), grad_mix_ref)

    def out_weight(block, carry):
        out_ref[block] = tn(my_mix_ref[block], low_ref[...]).astype(BF)
        return carry

    lax.fori_loop(0, blocks, out_weight, 0)
    branch_job.wait()

    def last(part, sums):
        branch = branch_job.value(part)
        total = two_ref[part] + branch
        layer_ref[part] = total.astype(BF)
        return (
            sums[0] + jnp.sum(total * total, axis=0, keepdims=True),
            sums[1] + jnp.sum(branch * branch, axis=0, keepdims=True),
        )

    square_out, square_three = chunks(rows, last, nothing)
    rest = jnp.zeros((1, width), F32)
    for index, row in enumerate(
        (rest, gain_two, gain_three, rest, shift_two, shift_three, square_out, square_three)
    ):
        stats_ref[index : index + 1] = row
    query_job.second()
    side_ref[1] = cross_job.total().astype(BF)
    side_ref[0] = query_job.total().astype(BF)
    branch_job.finish()
    cross_job.finish()
    query_job.finish()
    up_own.wait()
    for copy in up_moves:
        copy.wait()


def rows_back(
    normed, cot, one, two, query, mix, text, my_mix, gain, bias, weights, branch, up, ident
):
    rows, width = cot.shape
    blocks, _, columns = my_mix.shape
    return call(
        rows_back_kernel,
        "rows_back",
        (
            shape(rows, width, dtype=F32),
            shape(rows, width),
            shape(8, width, dtype=F32),
            shape(*my_mix.shape),
            shape(blocks, columns, width),
            shape(2, columns, width),
            shape(*text.shape),
            shape(*up.shape[:2], up.shape[2] // 2),
        ),
        (IN_VMEM,) * 7 + (ANY,),
        [IN_VMEM] * 10 + [ANY, ANY, ANY],
        [pltpu.VMEM((blocks, columns, width), BF)] * 3
        + [
            pltpu.VMEM((rows, width), BF),
            pltpu.VMEM((rows, width), BF),
            pltpu.VMEM((rows, width), F32),
            pltpu.VMEM(my_mix.shape, BF),
            pltpu.VMEM(my_mix.shape, BF),
            pltpu.SemaphoreType.DMA((4,)),
            pltpu.SemaphoreType.DMA((up.shape[0] - 1,)),
            pltpu.SemaphoreType.DMA((up.shape[0] - 1,)),
        ]
        + Scatter.scratch(columns, width) * 2
        + LoadedScatter.scratch(rows, width),
        ident,
        60,
    )(normed, cot, one, two, query, mix, text, my_mix, gain, bias, weights, branch, up)


def last_kernel(
    part_ref, frames_ref, gain_ref, grad_ref, stats_ref, qkv_ref, up_a, up_b, cross_ref, out_w_ref,
    text_ref, text_in, w_text_ref,
    out_ref, total_ref, text_out, qkv_out, up_out, cross_out, self_out, key_out,
    mine, came, all_ref, st_send, st_recv, z_send, z_recv,
    qkv_came, out_came, text_came, text_part, text_mine, text_all,
    qkv_pair, up_mine, up_pair, cross_pair, out_pair, key_pair, x_send, x_recv, q_send, q_recv,
    *scratch,
):
    z = lax.axis_index("shard")
    shards = lax.axis_size("shard")
    others = shard_others()
    spot = place()[1:]
    context = spot[0]
    enter(neighbours() + [device(other, *spot) for other in others])

    def collect(moves, source_ref, came_ref, rows=slice(None)):
        for copy in moves:
            copy.wait_recv()
        total = source_ref[z, rows].astype(F32)
        for other in others:
            total += came_ref[other, rows].astype(F32)
        return total.astype(BF)

    def over(index, source_of, target_ref):
        return spread(source_of, target_ref, z_send.at[index], z_recv.at[index], others, spot)

    text_moves = over(0, lambda other: text_ref, text_came)
    size = len(scratch) - 5
    text = Scatter(text_part, *scratch[size:])
    job = SteepScatter(part_ref, *scratch[:size])
    job.start()
    out_moves = over(2, lambda other: out_w_ref.at[other], out_came)
    third = qkv_ref.shape[1] // 3
    thirds = [pl.ds(index * third, third) for index in range(3)]
    qkv_moves = []

    def send_third(index):
        for step, other in enumerate(others):
            copy = remote_copy(
                qkv_ref.at[other, thirds[index]], qkv_came.at[z, thirds[index]],
                q_send.at[index, step], q_recv.at[index, step], device(other, *spot),
            )
            copy.start()
            qkv_moves.append(copy)

    def sum_third(index):
        moves = qkv_moves[index * len(others) : (index + 1) * len(others)]
        rows = thirds[index]
        qkv_pair[0, rows] = collect(moves, qkv_ref, qkv_came, rows)
        pairs.append(swap(4 + index, qkv_pair.at[0, rows], qkv_pair.at[1, rows]))

    send_third(0)
    to_x = neighbours()[0]

    def swap(index, source, target_ref):
        copy = remote_copy(source, target_ref, x_send.at[index], x_recv.at[index], to_x)
        copy.start()
        return copy

    cross_move = swap(1, cross_ref, cross_pair)
    job.first()
    for start, up_ref in ((0, up_a), (up_a.shape[2], up_b)):
        total = up_ref[0].astype(F32)
        for index in range(1, shards):
            total += up_ref[index].astype(F32)
        up_mine[:, start : start + up_ref.shape[2]] = total.astype(BF)
    pairs = [swap(0, up_mine, up_pair), cross_move]
    text_came[z] = text_ref[...]
    for copy in text_moves:
        copy.wait_recv()
    texts = text_ref.shape[0] // 2
    own = texts // 8

    def text_back(index, carry):
        grads = nt(text_came[index], w_text_ref[...])
        rows = pl.ds(pl.multiple_of(index * 2 * own, 2 * own), 2 * own)
        for block in range(8):
            pair = [grads[k * texts + block * own : k * texts + block * own + own] for k in range(2)]
            text_part[block, rows] = jnp.concatenate(pair, axis=0).astype(BF)
        return carry

    lax.fori_loop(0, shards, text_back, 0)
    for index in range(4):
        text.pass_core(index)
    key_grad = tn(text_in[0], text_came[0])
    for index in range(1, shards):
        key_grad += tn(text_in[index], text_came[index])
    key_pair[0] = key_grad.astype(BF)
    pairs.append(swap(2, key_pair.at[0], key_pair.at[1]))
    job.second()
    text.far()
    text.near()
    out_pair[0] = collect(out_moves, out_w_ref, out_came)
    pairs.append(swap(3, out_pair.at[0], out_pair.at[1]))
    send_third(1)
    text.second()
    job.wait()
    sum_third(0)
    send_third(2)

    def norm(part, sums):
        back, more = norm_back(job.value(part), frames_ref[part].astype(F32), gain_ref[...])
        out_ref[part] = grad_ref[part] + back
        return sums[0] + more[0], sums[1] + more[1]

    nothing = (jnp.zeros((1, frames_ref.shape[1]), F32),) * 2
    gain_one, shift_one = chunks(frames_ref.shape[0], norm, nothing)
    mine[0] = stats_ref[...]
    mine[0, 0:1] = gain_one
    mine[0, 3:4] = shift_one
    sends = []
    for index, target in enumerate(neighbours()):
        copy = remote_copy(
            mine.at[index], came.at[index], st_send.at[index], st_recv.at[index], target
        )
        copy.start()
        sends.append(copy)
        if index == 0:
            text.wait()
            for block in range(shards):
                rows = slice(block * 2 * own, (block + 1) * 2 * own)
                text_mine[block] = text.value(rows).astype(BF)
            text_moves += over(3, lambda other: text_mine.at[other], text_all)
            text_all[z] = text_mine[z]
        copy.wait_recv()
        mine[index + 1] = mine[index] + came[index]
    stat_moves = over(4, lambda other: mine.at[3], all_ref)
    all_ref[z] = mine[3]

    sum_third(1)
    sum_third(2)
    for copy in text_moves[shards - 1 :] + stat_moves:
        copy.wait_recv()
    text_out[...] = text_all[...].astype(F32)
    total = all_ref[0]
    for index in range(1, shards):
        total += all_ref[index]
    total_ref[...] = total
    beside(up_mine, pairs[0], up_pair, up_out)

    def ordered(first, second):
        return jnp.where(context == 0, first, second), jnp.where(context == 0, second, first)

    pairs[1].wait_recv()
    lead, trail = ordered(cross_ref[...], cross_pair[...])
    width = lead.shape[0] // 2
    for index in range(2):
        part = slice(index * width, (index + 1) * width)
        cross_out[index, :width] = lead[part]
        cross_out[index, width:] = trail[part]
    pairs[2].wait_recv()
    lead, trail = ordered(key_pair[0], key_pair[1])
    for index in range(2):
        lanes = slice(index * width, (index + 1) * width)
        key_out[index, :, :width] = lead[:, lanes]
        key_out[index, :, width:] = trail[:, lanes]
    pairs[3].wait_recv()
    lead, trail = ordered(out_pair[0], out_pair[1])
    self_out[:width] = lead
    self_out[width:] = trail
    for copy in pairs[4:]:
        copy.wait_recv()
    lead, trail = ordered(qkv_pair[0], qkv_pair[1])
    for index in range(3):
        lanes = slice(index * width, (index + 1) * width)
        qkv_out[index, :, :width] = lead[:, lanes]
        qkv_out[index, :, width:] = trail[:, lanes]
    for copy in sends + text_moves + qkv_moves + out_moves + stat_moves + pairs:
        copy.wait_send()
    text.finish()
    job.finish()


def last_step(
    part, frames, gain, grad, stats, qkv, up_a, up_b, cross, out, text, text_in, w_text, ident
):
    _, rows, width = part.shape
    shards, texts, depth = text_in.shape
    half = 2 * up_a.shape[2]
    columns = out.shape[1]
    own = texts // 8
    return call(
        last_kernel,
        "last_step",
        (
            shape(rows, width, dtype=F32),
            shape(16, width, dtype=F32),
            shape(shards, own, depth, dtype=F32),
            shape(3, depth, 2 * columns),
            shape(depth, 2 * half),
            shape(2, 2 * columns, depth),
            shape(2 * columns, depth),
            shape(2, depth, 2 * columns),
        ),
        (IN_VMEM,) * 8,
        [ANY] + [IN_VMEM] * 12,
        [
            pltpu.VMEM((4, 16, width), F32),
            pltpu.VMEM((3, 16, width), F32),
            pltpu.VMEM((shards, 16, width), F32),
            pltpu.SemaphoreType.DMA((3,)),
            pltpu.SemaphoreType.DMA((3,)),
            pltpu.SemaphoreType.DMA((5, shards - 1)),
            pltpu.SemaphoreType.DMA((5, shards - 1)),
            pltpu.VMEM((shards, depth, 3 * columns), BF),
            pltpu.VMEM((shards, columns, depth), BF),
            pltpu.VMEM((shards, texts, 2 * columns), BF),
            pltpu.VMEM((8, shards * own, depth), BF),
            pltpu.VMEM((shards, own, depth), BF),
            pltpu.VMEM((shards, own, depth), BF),
            pltpu.VMEM((2, depth, 3 * columns), BF),
            pltpu.VMEM((depth, half), BF),
            pltpu.VMEM((depth, half), BF),
            pltpu.VMEM((2 * columns, depth), BF),
            pltpu.VMEM((2, columns, depth), BF),
            pltpu.VMEM((2, depth, 2 * columns), BF),
            pltpu.SemaphoreType.DMA((7,)),
            pltpu.SemaphoreType.DMA((7,)),
            pltpu.SemaphoreType.DMA((3, shards - 1)),
            pltpu.SemaphoreType.DMA((3, shards - 1)),
        ]
        + LoadedScatter.scratch(rows, width)
        + Scatter.scratch(shards * own, depth),
        ident,
        65,
    )(part, frames, gain, grad, stats, qkv, up_a, up_b, cross, out, text, text_in, w_text)


def dots(spec, *operands):
    return jnp.einsum(spec, *operands, preferred_element_type=F32)


def layer_norm(inputs, scaling, offset):
    average = jnp.mean(inputs, axis=-1, keepdims=True)
    centred = inputs - average
    variance = jnp.mean(centred * centred, axis=-1, keepdims=True)
    return centred * lax.rsqrt(variance + EPS) * scaling + offset


def on_device(
    frames,
    text_states,
    cotangent,
    norm_gain,
    norm_bias,
    self_qkv,
    self_out,
    cross_qkv,
    cross_out,
    mlp_up,
    mlp_down,
):
    clips, rows, width = frames.shape
    context = lax.axis_index("context")
    depth = self_qkv.shape[1]
    slices = width // depth
    columns = self_qkv.shape[2] // 2
    heads = columns // HEAD_DIM
    block = clips * rows
    texts = text_states.shape[1]

    def half(weight):
        size = weight.shape[-1] // 2
        return lax.dynamic_slice_in_dim(weight, context * size, size, weight.ndim - 1)

    def over_shard(weight, tiled=True):
        return lax.all_gather(weight, "shard", axis=0, tiled=tiled)

    cross_part = half(cross_qkv)
    qkv_part = half(self_qkv)
    early = [qkv_part[0], qkv_part[1], qkv_part[2], half(self_out), cross_part[0], half(cross_out)]
    w_early = over_shard(jnp.concatenate(early, axis=1))
    w_late = over_shard(jnp.concatenate([half(mlp_up), half(mlp_down)], axis=1))
    w_text = jnp.concatenate([cross_part[1], cross_part[2]], axis=1)
    text_slices = text_states.reshape(clips * texts, slices, depth).transpose(1, 0, 2)
    w_down = over_shard(half(mlp_down))

    all_one, all_grad, text_in, text_part = first_step(
        frames.reshape(block, width),
        norm_gain,
        norm_bias,
        cotangent.reshape(block, width),
        text_slices,
        w_text,
        0,
    )
    (
        qkv, self_log, mix, my_mix, stream_one, stream_two, cross_q, cross_mix, norm_three,
        text_all, squares, plane_w,
    ) = attend_forward(
        all_one,
        w_early,
        text_part,
        frames.reshape(block, width),
        norm_gain,
        norm_bias,
        1,
    )

    grad_normed, part_three, grad_up, grad_down = feed_forward(
        norm_three, all_grad, w_late, 4
    )

    def to_shard(part):
        return lax.psum_scatter(part.astype(BF), "shard", scatter_dimension=0, tiled=True)

    grad_down = to_shard(grad_down)
    grad_up = grad_up.reshape(slices, depth, -1)
    grad_one, layer_out, stats, grad_mix, part_out, side, text_grads, up_a = rows_back(
        grad_normed,
        cotangent.reshape(block, width),
        stream_one,
        stream_two,
        cross_q,
        cross_mix,
        text_all,
        my_mix,
        norm_gain,
        norm_bias,
        plane_w,
        part_three,
        grad_up,
        3,
    )

    def slice_shards(part):
        return part.reshape(-1, slices, depth).transpose(1, 0, 2)

    grad_cross = to_shard(slice_shards(side))[0]
    part_norm, grad_w_qkv, grad_out, text_grads, grad_down, up_b = attend_backward(
        grad_mix, qkv, mix, self_log, all_one, w_early, part_out, text_grads, grad_down, grad_up, 8
    )
    (
        grad_frames, totals, grad_text, grad_w_qkv, grad_up, grad_cross, grad_out, grad_keys,
    ) = last_step(
        part_norm,
        frames.reshape(block, width),
        norm_gain[0][None],
        grad_one,
        jnp.concatenate([stats, squares], axis=0),
        grad_w_qkv.reshape(slices, depth, 3 * columns),
        up_a,
        up_b,
        grad_cross,
        slice_shards(grad_out),
        text_grads,
        text_in,
        w_text,
        11,
    )
    grad_frames = grad_frames.reshape(clips, rows, width)
    grad_text = grad_text.transpose(1, 0, 2).reshape(clips, texts // 8, width)

    squares = totals[6:10].sum(axis=1)[jnp.array([0, 2, 3, 1])]
    start = lax.axis_index("shard") * depth
    grad_gain = lax.dynamic_slice_in_dim(totals[:3], start, depth, 1)
    grad_shift = lax.dynamic_slice_in_dim(totals[3:6], start, depth, 1)
    entries = float(clips * rows * width * lax.axis_size(("shard",) + PLANE))
    return (
        layer_out.reshape(clips, rows, width),
        grad_frames,
        grad_text,
        grad_gain,
        grad_shift,
        grad_w_qkv.astype(F32),
        grad_out.transpose(1, 0).astype(F32),
        jnp.concatenate([grad_cross[:1].transpose(0, 2, 1), grad_keys]).astype(F32),
        grad_cross[1].transpose(1, 0).astype(F32),
        grad_up.astype(F32),
        grad_down.astype(F32),
        jnp.sqrt(squares / entries),
    )


def solution(mesh):
    rows = P("shard", PLANE, None)
    stack = P(None, "shard", "tensor")
    flat = P("shard", "tensor")
    return jax.shard_map(
        on_device,
        mesh=mesh,
        in_specs=(rows, P("shard"), rows, P(), P(), stack, flat, stack, flat, flat, flat),
        out_specs=(
            (rows, rows, rows, P(None, "shard"), P(None, "shard"))
            + (stack, flat, stack, flat, flat, flat, P())
        ),
        check_vma=False,
    )
```

```python
from functools import partial

import jax
import jax.numpy as jnp
from jax import lax
from jax.experimental import pallas as pl
from jax.experimental.pallas import tpu as pltpu
from jax.sharding import PartitionSpec as P

HEAD_DIM = 64
EPS = 1e-05
MASKED = -1e30
MESH = pl.DeviceIdType.MESH
BF = jnp.bfloat16
F32 = jnp.float32
PLANE = ("context", "tensor")
VMEM_LIMIT = 60 * 2**20


def place():
    return (
        lax.axis_index("shard"),
        lax.axis_index("context"),
        lax.axis_index("tensor") // 2,
        lax.axis_index("tensor") % 2,
    )


def device(z, x, y, c):
    return (z, x, 2 * y + c)


def slot(x, y, c):
    return 4 * x + 2 * y + c


def neighbours():
    z, x, y, c = place()
    return [device(z, 1 - x, y, c), device(z, x, 1 - y, c), device(z, x, y, 1 - c)]


def plane_spots():
    z, x, y, c = place()
    steps = [(a, b, d) for a in range(2) for b in range(2) for d in range(2) if a + b + d]
    return [((x + a) % 2, (y + b) % 2, (c + d) % 2) for a, b, d in steps]


def plane_others():
    z = lax.axis_index("shard")
    return [device(z, *spot) for spot in plane_spots()]


def enter(targets):
    barrier = pltpu.get_barrier_semaphore()
    for target in targets:
        pl.semaphore_signal(barrier, inc=1, device_id=target, device_id_type=MESH)
    pl.semaphore_wait(barrier, len(targets))


def remote_copy(source, target_ref, send, recv, target):
    return pltpu.make_async_remote_copy(
        src_ref=source,
        dst_ref=target_ref,
        send_sem=send,
        recv_sem=recv,
        device_id=target,
        device_id_type=MESH,
    )


class Gather:
    semaphores = 9

    def __init__(self, in_ref, out_ref, local_sem, send, recv):
        z, x, y, c = place()
        self.in_ref, self.out_ref, self.local_sem = in_ref, out_ref, local_sem
        self.send, self.recv = send, recv
        self.spot = (x, y, c)
        self.to_x, self.to_y, self.to_c = neighbours()
        self.rows = in_ref.shape[0]
        self.sends = []

    def go(self, index, owner, start, size, target, source=None):
        there = self.out_ref.at[owner, pl.ds(start, size)]
        copy = remote_copy(
            there if source is None else source,
            there,
            self.send.at[index],
            self.recv.at[index],
            target,
        )
        copy.start()
        self.sends.append(copy)

    def arrived(self, index, owner, start, size):
        there = self.out_ref.at[owner, pl.ds(start, size)]
        remote_copy(
            there, there, self.send.at[index], self.recv.at[index], self.to_x
        ).wait_recv()

    def start(self):
        me = slot(*self.spot)
        self.own = pltpu.make_async_copy(self.in_ref, self.out_ref.at[me], self.local_sem)
        self.own.start()
        for index, target in enumerate((self.to_x, self.to_y, self.to_c)):
            self.go(index, me, 0, self.rows, target, self.in_ref)

    def relay_y(self):
        x, y, c = self.spot
        owner = slot(x, 1 - y, c)
        self.arrived(1, owner, 0, self.rows)
        self.go(3, owner, 0, self.rows // 2, self.to_x)
        self.go(5, owner, 0, self.rows, self.to_c)

    def relay_x(self):
        x, y, c = self.spot
        half = self.rows // 2
        owner = slot(1 - x, y, c)
        self.arrived(0, owner, 0, self.rows)
        self.go(4, owner, half, half, self.to_y)
        self.go(6, owner, 0, self.rows, self.to_c)

    def relay_far(self):
        x, y, c = self.spot
        half = self.rows // 2
        owner = slot(1 - x, 1 - y, c)
        self.arrived(3, owner, 0, half)
        self.go(7, owner, 0, half, self.to_c)
        self.arrived(4, owner, half, half)
        self.go(8, owner, half, half, self.to_c)

    def finish(self):
        x, y, c = self.spot
        half = self.rows // 2
        self.arrived(2, slot(x, y, 1 - c), 0, self.rows)
        self.arrived(5, slot(x, 1 - y, 1 - c), 0, self.rows)
        self.arrived(6, slot(1 - x, y, 1 - c), 0, self.rows)
        self.arrived(7, slot(1 - x, 1 - y, 1 - c), 0, half)
        self.arrived(8, slot(1 - x, 1 - y, 1 - c), half, half)
        self.own.wait()
        for copy in self.sends:
            copy.wait_send()

    def rest(self):
        self.relay_y()
        self.relay_x()
        self.relay_far()
        self.finish()


class Scatter:
    @staticmethod
    def scratch(rows, columns):
        return [
            pltpu.VMEM((4, rows, columns), BF),
            pltpu.VMEM((2, rows // 2, columns), BF),
            pltpu.VMEM((2, rows, columns), BF),
            pltpu.SemaphoreType.DMA((10,)),
            pltpu.SemaphoreType.DMA((10,)),
        ]

    def __init__(self, part_ref, core, relay, final, send, recv):
        self.part_ref, self.core, self.relay, self.final = part_ref, core, relay, final
        self.send, self.recv = send, recv
        self.to_x, self.to_y, self.to_c = neighbours()
        z, x, y, c = place()
        chips = ((1 - x, 1 - y), (1 - x, y), (x, 1 - y), (x, y))
        self.mine = [slot(*chip, c) for chip in chips]
        self.theirs = [slot(*chip, 1 - c) for chip in chips]
        rows = part_ref.shape[1]
        self.low, self.high = pl.ds(0, rows // 2), pl.ds(rows // 2, rows // 2)
        self.sends = []

    def forward(self, index, source, target_ref, target):
        copy = remote_copy(
            source, target_ref, self.send.at[index], self.recv.at[index], target
        )
        copy.start()
        self.sends.append(copy)

    def arrived(self, index, ref):
        remote_copy(ref, ref, self.send.at[index], self.recv.at[index], self.to_c).wait_recv()

    def pass_core(self, index):
        source = self.part_ref.at[self.theirs[index]]
        self.forward(index, source, self.core.at[index], self.to_c)

    def add(self, index, part, more=None):
        mine = self.mine[index]
        total = self.part_ref[mine, part].astype(F32) + self.core[index, part].astype(F32)
        if more is not None:
            total += more.astype(F32)
        self.part_ref[mine, part] = total.astype(BF)
        return self.part_ref.at[mine, part]

    def far(self):
        self.arrived(0, self.core.at[0])
        self.forward(4, self.add(0, self.low), self.relay.at[0], self.to_x)
        self.forward(5, self.add(0, self.high), self.relay.at[1], self.to_y)

    def near(self):
        self.arrived(1, self.core.at[1])
        self.forward(6, self.add(1, self.low), self.final.at[0, self.low], self.to_x)
        self.arrived(2, self.core.at[2])
        self.forward(7, self.add(2, self.high), self.final.at[1, self.high], self.to_y)

    def second(self):
        low, high, final, relay = self.low, self.high, self.final, self.relay
        self.arrived(5, relay.at[1])
        self.forward(8, self.add(1, high, relay[1]), final.at[0, high], self.to_x)
        self.arrived(4, relay.at[0])
        self.forward(9, self.add(2, low, relay[0]), final.at[1, low], self.to_y)

    def wait(self):
        self.arrived(3, self.core.at[3])
        self.arrived(6, self.final.at[0, self.low])
        self.arrived(7, self.final.at[1, self.high])
        self.arrived(8, self.final.at[0, self.high])
        self.arrived(9, self.final.at[1, self.low])

    def value(self, part=slice(None)):
        total = self.part_ref[self.mine[3], part].astype(F32) + self.core[3, part].astype(F32)
        return total + self.final[0, part].astype(F32) + self.final[1, part].astype(F32)

    def total(self):
        self.wait()
        return self.value()

    def finish(self):
        for copy in self.sends:
            copy.wait_send()


class LoadedScatter(Scatter):
    steep = False

    @staticmethod
    def scratch(rows, columns):
        return [
            pltpu.VMEM((4, rows, columns), BF),
            pltpu.SemaphoreType.DMA((4,)),
        ] + Scatter.scratch(rows, columns)

    def __init__(self, in_ref, part_ref, local_sem, *scratch):
        super().__init__(part_ref, *scratch)
        self.in_ref, self.local_sem = in_ref, local_sem

    def bring(self, index):
        source = self.in_ref.at[self.theirs[index]]
        self.forward(index, source, self.core.at[index], self.to_c)
        load = pltpu.make_async_copy(
            self.in_ref.at[self.blocks[index]], self.part_ref.at[index], self.local_sem.at[index]
        )
        load.start()
        self.loads.append(load)

    def start(self):
        self.loads = []
        self.blocks, self.mine = self.mine, (0, 1, 2, 3)
        for index in range(4):
            self.bring(index)

    def first(self):
        for load in self.loads:
            load.wait()
        if not self.steep:
            self.far()
            self.near()
            return
        self.arrived(0, self.core.at[0])
        self.forward(4, self.add(0, self.low), self.relay.at[0], self.to_y)
        self.forward(5, self.add(0, self.high), self.relay.at[1], self.to_y)
        self.arrived(2, self.core.at[2])
        self.forward(7, self.add(2, self.high), self.final.at[1, self.high], self.to_y)
        self.forward(9, self.add(2, self.low), self.final.at[1, self.low], self.to_y)

    def second(self):
        if not self.steep:
            super().second()
            return
        final, relay = self.final, self.relay
        self.arrived(1, self.core.at[1])
        self.arrived(4, relay.at[0])
        self.forward(6, self.add(1, self.low, relay[0]), final.at[0, self.low], self.to_x)
        self.arrived(5, relay.at[1])
        self.forward(8, self.add(1, self.high, relay[1]), final.at[0, self.high], self.to_x)


class SteepScatter(LoadedScatter):
    steep = True


class Exchange:
    def __init__(self, in_ref, out_ref, local_sem, send, recv):
        self.in_ref, self.out_ref, self.local_sem = in_ref, out_ref, local_sem
        self.send, self.recv = send, recv
        z, x, y, c = place()
        self.me = slot(x, y, c)
        self.copies = []

    def start(self, piece, part):
        z = lax.axis_index("shard")
        own = pltpu.make_async_copy(
            self.in_ref.at[self.me, part], self.out_ref.at[self.me, part], self.local_sem.at[piece]
        )
        own.start()
        self.copies.append(own)
        for index, spot in enumerate(plane_spots()):
            copy = remote_copy(
                self.in_ref.at[slot(*spot), part],
                self.out_ref.at[self.me, part],
                self.send.at[piece, index],
                self.recv.at[piece, index],
                device(z, *spot),
            )
            copy.start()
            self.copies.append(copy)

    def finish(self, piece=None):
        copies = self.copies if piece is None else self.copies[8 * piece : 8 * piece + 8]
        for copy in copies:
            copy.wait()


ANY = pl.BlockSpec(memory_space=pl.ANY)
IN_VMEM = pl.BlockSpec(memory_space=pltpu.VMEM)


class Moves:
    def __init__(self, loads, stores):
        self.loads, self.stores = loads, stores
        for _, copy in loads:
            copy.start()
        self.begun = []

    def ready(self, *refs):
        rest = []
        for ref, copy in self.loads:
            if not refs or any(ref is wanted for wanted in refs):
                copy.wait()
            else:
                rest.append((ref, copy))
        self.loads = rest

    def store(self, *refs):
        rest = []
        for ref, copy in self.stores:
            if not refs or any(ref is wanted for wanted in refs):
                copy.start()
                self.begun.append(copy)
            else:
                rest.append((ref, copy))
        self.stores = rest

    def finish(self):
        self.ready()
        self.store()
        for copy in self.begun:
            copy.wait()


def call(kernel, name, outs, out_specs, in_specs, scratch, ident, micros):
    def run(*args):
        loaded = [i for i, spec in enumerate(in_specs) if spec is IN_VMEM]
        stored = [i for i, spec in enumerate(out_specs) if spec is IN_VMEM]
        buffers = [pltpu.VMEM(args[i].shape, args[i].dtype) for i in loaded]
        buffers += [pltpu.VMEM(outs[i].shape, outs[i].dtype) for i in stored]

        def wrapped(*refs):
            ends = len(in_specs), len(in_specs) + len(outs)
            given, made, rest = list(refs[: ends[0]]), list(refs[ends[0] : ends[1]]), refs[ends[1] :]
            sems, rest = rest[len(buffers)], (rest[: len(buffers)], rest[len(buffers) + 1 :])
            loads, stores = [], []
            for k, i in enumerate(loaded):
                copy = pltpu.make_async_copy(given[i], rest[0][k], sems.at[k])
                loads.append((rest[0][k], copy))
                given[i] = rest[0][k]
            for k, i in enumerate(stored, len(loaded)):
                copy = pltpu.make_async_copy(rest[0][k], made[i], sems.at[k])
                stores.append((rest[0][k], copy))
                made[i] = rest[0][k]
            moves = Moves(loads, stores)
            kernel(moves, *given, *made, *rest[1])
            moves.finish()

        return pl.pallas_call(
            wrapped,
            out_shape=outs,
            in_specs=[ANY] * len(in_specs),
            out_specs=(ANY,) * len(outs),
            scratch_shapes=buffers + [pltpu.SemaphoreType.DMA((len(buffers),))] + scratch,
            name=name,
            cost_estimate=pl.CostEstimate(
                flops=micros * 10**9, bytes_accessed=micros * 10**6, transcendentals=0
            ),
            compiler_params=pltpu.CompilerParams(
                collective_id=ident, has_side_effects=True, vmem_limit_bytes=VMEM_LIMIT
            ),
        )(*args)

    return run


def shape(*dims, dtype=BF):
    return jax.ShapeDtypeStruct(dims, dtype)


def gather_scratch():
    return [
        pltpu.SemaphoreType.DMA,
        pltpu.SemaphoreType.DMA((9,)),
        pltpu.SemaphoreType.DMA((9,)),
    ]


def shard_others():
    z, shards = lax.axis_index("shard"), lax.axis_size("shard")
    return [lax.rem(z + i, shards) for i in range(1, shards)]


def spread(source_of, target_ref, send, recv, others, spot):
    z = lax.axis_index("shard")
    copies = []
    for index, other in enumerate(others):
        copy = remote_copy(
            source_of(other), target_ref.at[z], send.at[index], recv.at[index],
            device(other, *spot),
        )
        copy.start()
        copies.append(copy)
    return copies


def first_kernel(
    moves, frames_ref, gain_ref, bias_ref, cot_ref, text_ref, w_text_ref,
    rows_out, cot_out, text_all, text_out,
    normed_ref, part_ref, came_ref, sends, recvs, *scratch,
):
    z = lax.axis_index("shard")
    spot = place()[1:]
    others = shard_others()
    enter(neighbours() + [device(other, *spot) for other in others])
    moves.ready()
    texts = spread(lambda other: text_ref.at[other], text_all, sends.at[0], recvs.at[0], others, spot)
    text_all[z] = text_ref[z]

    def norm(part, carry):
        normed, _ = normalise(frames_ref[part].astype(F32))
        normed_ref[part] = (normed * gain_ref[0:1] + bias_ref[0:1]).astype(BF)
        return carry

    chunks(frames_ref.shape[0], norm)
    rows, grads = Gather(normed_ref, rows_out, *scratch[:3]), Gather(cot_ref, cot_out, *scratch[3:])
    rows.start()
    for copy in texts:
        copy.wait_recv()

    def share(index, carry):
        part_ref[index] = nn(text_all[index], w_text_ref[...]).astype(BF)
        return carry

    lax.fori_loop(0, text_all.shape[0], share, 0)
    parts = spread(lambda other: part_ref.at[other], came_ref, sends.at[1], recvs.at[1], others, spot)
    came_ref[z] = part_ref[z]
    rows.relay_y()
    rows.relay_x()
    grads.start()
    rows.relay_far()
    rows.finish()
    grads.rest()
    for copy in parts:
        copy.wait_recv()
    total = came_ref[0].astype(F32)
    for index in range(1, came_ref.shape[0]):
        total += came_ref[index].astype(F32)
    text_out[...] = total.astype(BF)
    for copy in texts + parts:
        copy.wait_send()


def first_step(frames, gain, bias, cotangent, text, w_text, ident):
    rows, width = frames.shape
    shards, texts, depth = text.shape
    return call(
        first_kernel,
        "first_step",
        (
            shape(8, rows, width),
            shape(8, rows, width),
            shape(shards, texts, depth),
            shape(texts, w_text.shape[1]),
        ),
        (ANY, ANY, IN_VMEM, IN_VMEM),
        [IN_VMEM, IN_VMEM, IN_VMEM, ANY, IN_VMEM, IN_VMEM],
        [
            pltpu.VMEM((rows, width), BF),
            pltpu.VMEM((shards, texts, w_text.shape[1]), BF),
            pltpu.VMEM((shards, texts, w_text.shape[1]), BF),
            pltpu.SemaphoreType.DMA((2, shards - 1)),
            pltpu.SemaphoreType.DMA((2, shards - 1)),
        ]
        + gather_scratch() * 2,
        ident,
        60,
    )(frames, gain, bias, cotangent, text, w_text)


def feed_kernel(
    moves, own_ref, grad_ref, w_ref,
    normed_out, branch_out, up_out, down_out,
    rows_ref, grads_ref, hidden_ref, slope_ref, part_a, part_b,
    load_sem, store_sem, g_local, g_send, g_recv, *scratch,
):
    enter(neighbours())
    gather = Gather(own_ref, rows_ref, g_local, g_send, g_recv)
    gather.start()
    hidden = hidden_ref.shape[2]
    up_ref, down_ref = w_ref.at[:, pl.ds(0, hidden)], w_ref.at[:, pl.ds(hidden, hidden)]
    blocks, _, width = rows_ref.shape
    loads = []
    for block in range(blocks):
        load = pltpu.make_async_copy(grad_ref.at[block], grads_ref.at[block], load_sem.at[block])
        load.start()
        loads.append(load)
    for load in loads:
        load.wait()

    def early(block, carry):
        slope_ref[block] = nn(grads_ref[block], down_ref[...]).astype(BF)
        return carry

    moves.ready()
    lax.fori_loop(0, blocks, early, 0)

    def middle(block):
        before = nn(rows_ref[block], up_ref[...])
        share = 0.5 + 0.5 * lax.erf(before * (0.5**0.5))
        hidden_ref[block] = (before * share).astype(BF)
        slope = share + before * (jnp.exp(-0.5 * before * before) * (2.0 * jnp.pi) ** (-0.5))
        slope = (slope_ref[block].astype(F32) * slope).astype(BF)
        slope_ref[block] = slope
        part_a[block] = nt(slope, up_ref[...]).astype(BF)

    first = Scatter(part_a, *scratch)
    x, y, c = gather.spot

    def pair(cx, cy):
        def one(index, carry):
            middle(slot(cx, cy, 0) + index)
            return carry

        lax.fori_loop(0, 2, one, 0)

    gather.own.wait()
    gather.arrived(2, slot(x, y, 1 - c), 0, gather.rows)
    pair(x, y)
    first.pass_core(3)
    gather.relay_y()
    gather.relay_x()
    gather.arrived(6, slot(1 - x, y, 1 - c), 0, gather.rows)
    pair(1 - x, y)
    first.pass_core(1)
    gather.arrived(5, slot(x, 1 - y, 1 - c), 0, gather.rows)
    pair(x, 1 - y)
    first.pass_core(2)
    gather.relay_far()
    first.near()
    gather.arrived(7, slot(1 - x, 1 - y, 1 - c), 0, gather.rows // 2)
    gather.arrived(8, slot(1 - x, 1 - y, 1 - c), gather.rows // 2, gather.rows // 2)
    pair(1 - x, 1 - y)
    first.pass_core(0)
    first.far()
    for copy in gather.sends:
        copy.wait_send()

    def store(block):
        return pltpu.make_async_copy(part_b.at[block], branch_out.at[block], store_sem.at[block])

    def branch(block, carry):
        part_b[block] = nt(hidden_ref[block], down_ref[...]).astype(BF)
        store(block).start()
        return carry

    lax.fori_loop(0, blocks, branch, 0)
    first.second()
    tile = 256

    def weight(left_ref, right_ref, out_ref):
        right = right_ref[...].reshape(-1, right_ref.shape[2])

        def one(index, carry):
            lanes = pl.ds(pl.multiple_of(index * tile, tile), tile)
            left = left_ref[:, :, lanes].reshape(-1, tile)
            out_ref[lanes, :] = tn(left, right).astype(BF)
            return carry

        lax.fori_loop(0, width // tile, one, 0)

    weight(grads_ref, hidden_ref, down_out)
    moves.store(down_out)
    weight(rows_ref, slope_ref, up_out)
    moves.store(up_out)
    normed_out[...] = first.total()
    first.finish()
    for block in range(blocks):
        store(block).wait()


def feed_forward(own, grads, weights, ident):
    rows, width = own.shape
    hidden = weights.shape[1] // 2
    outs = (
        shape(rows, width, dtype=F32),
        shape(8, rows, width),
        shape(width, hidden),
        shape(width, hidden),
    )
    scratch = [
        pltpu.VMEM((8, rows, width), BF),
        pltpu.VMEM((8, rows, width), BF),
        pltpu.VMEM((8, rows, hidden), BF),
        pltpu.VMEM((8, rows, hidden), BF),
        pltpu.VMEM((8, rows, width), BF),
        pltpu.VMEM((8, rows, width), BF),
        pltpu.SemaphoreType.DMA((8,)),
        pltpu.SemaphoreType.DMA((8,)),
    ]
    return call(
        feed_kernel,
        "feed_forward",
        outs,
        (IN_VMEM, ANY, IN_VMEM, IN_VMEM),
        [ANY, ANY, IN_VMEM],
        scratch + gather_scratch() + Scatter.scratch(rows, width),
        ident,
        70,
    )(own, grads, weights)


SIDE = 256


def nt(left, right):
    return lax.dot_general(left, right, (((1,), (1,)), ((), ())), preferred_element_type=F32)


def nn(left, right):
    return lax.dot_general(left, right, (((1,), (0,)), ((), ())), preferred_element_type=F32)


def tn(left, right):
    return lax.dot_general(left, right, (((0,), (0,)), ((), ())), preferred_element_type=F32)


def turn(values):
    return jnp.transpose(values.astype(F32))


def side_by_side(ref):
    return jnp.concatenate([ref[block] for block in range(ref.shape[0])], axis=1)


def all_rows(ref):
    return ref[...].reshape(-1, ref.shape[2])


def split_columns(values, ref):
    columns = ref.shape[2]
    for block in range(ref.shape[0]):
        ref[block] = values[:, block * columns : (block + 1) * columns].astype(BF)


def causal(scores):
    keys = lax.broadcasted_iota(jnp.int32, scores.shape, 0)
    queries = lax.broadcasted_iota(jnp.int32, scores.shape, 1)
    return jnp.where(keys <= queries, scores, MASKED)


def forward_kernel(
    moves, rows_ref, side_ref, text_in, frames_ref, gain_ref, bias_ref,
    qkv_ref, log_ref, mix_ref, mine_ref, one_ref, two_ref, query_ref, cross_ref, low_ref,
    text_ref, square_ref, plane_out,
    w_own, w_out, w_query, w_cross, sum_ref, two_low_ref, store_sem,
    ex_local, ex_send, ex_recv, *scratch,
):
    enter(plane_others())
    blocks, both, _ = rows_ref.shape
    rows = both // 2
    width = mix_ref.shape[2]
    features = two_low_ref.shape[1]
    heads = width // HEAD_DIM
    length = blocks * rows
    step = SIDE // rows
    weights = (w_out, w_query, w_cross)

    def turn_own(kind):
        w_own[kind] = turn(side_ref[:, (3 + kind) * width : (4 + kind) * width]).astype(BF)

    moves.ready(side_ref)
    turn_own(0)
    jobs = [Gather(w_own.at[k], weights[k], *scratch[3 * k : 3 * k + 3]) for k in range(3)]
    text_job = Gather(text_in, text_ref, *scratch[9:])
    text_job.start()
    jobs[0].start()
    stores = []

    def keep(kind):
        copy = pltpu.make_async_copy(weights[kind], plane_out.at[kind], store_sem.at[kind])
        copy.start()
        stores.append(copy)

    def project(block, carry):
        qkv_ref[block] = nn(rows_ref[block], side_ref[:, : 3 * width]).astype(BF)
        return carry

    moves.ready()
    lax.fori_loop(0, blocks, project, 0)
    moves.store(qkv_ref)
    turn_own(1)
    turn_own(2)
    exchange = Exchange(mix_ref, mine_ref, ex_local, ex_send, ex_recv)
    for clip in range(2):
        part = pl.ds(clip * rows, rows)
        for head in range(heads):
            lanes = [pl.ds(j * width + head * HEAD_DIM, HEAD_DIM) for j in range(3)]
            key = qkv_ref[:, part, lanes[1]].reshape(length, HEAD_DIM)
            value = turn(qkv_ref[:, part, lanes[2]].reshape(length, HEAD_DIM)).astype(BF)
            for index in range(length // SIDE):
                spots = pl.ds(index * step, step)
                query = qkv_ref[spots, part, lanes[0]].reshape(SIDE, HEAD_DIM)
                query = query * jnp.asarray(HEAD_DIM ** (-0.5), BF)
                start = index * SIDE
                last = causal(nt(key[start : start + SIDE], query))
                top = jnp.max(last, axis=0, keepdims=True)
                if index:
                    early = nt(key[:start], query)
                    top = jnp.maximum(top, jnp.max(early, axis=0, keepdims=True))
                last = jnp.exp(last - top)
                total = jnp.sum(last, axis=0, keepdims=True)
                mix = nn(value[:, start : start + SIDE], last.astype(BF))
                if index:
                    early = jnp.exp(early - top)
                    total += jnp.sum(early, axis=0, keepdims=True)
                    mix += nn(value[:, :start], early.astype(BF))
                mix = jnp.transpose(mix / total).astype(BF).reshape(step, rows, HEAD_DIM)
                mix_ref[spots, part, pl.ds(head * HEAD_DIM, HEAD_DIM)] = mix
                log_ref[pl.ds(clip * heads + head, 1), pl.ds(start, SIDE)] = top + jnp.log(total)
        exchange.start(clip, part)
        if clip == 0:
            jobs[0].relay_y()
            jobs[0].relay_x()
            text_job.relay_y()
            text_job.relay_x()
    jobs[1].start()
    moves.store(mix_ref, log_ref)
    jobs[0].relay_far()
    text_job.relay_far()
    jobs[0].finish()
    text_job.finish()
    keep(0)
    exchange.finish()
    moves.store(mine_ref, text_ref)

    def apply(values_ref, kind):
        sum_ref[...] = nn(side_by_side(values_ref), all_rows(weights[kind]))

    apply(mine_ref, 0)
    nothing = jnp.zeros((1, features), F32)

    def first(part, sums):
        branch = sum_ref[part]
        total = frames_ref[part].astype(F32) + branch
        one_ref[part] = total
        normed, _ = normalise(total)
        two_low_ref[part] = (normed * gain_ref[1:2] + bias_ref[1:2]).astype(BF)
        return sums + jnp.sum(branch * branch, axis=0, keepdims=True)

    square_one = chunks(both, first, nothing)
    moves.store(one_ref)
    jobs[1].relay_y()
    jobs[1].relay_x()
    jobs[2].start()
    jobs[1].relay_far()
    jobs[1].finish()
    keep(1)

    split_columns(nt(two_low_ref[...], all_rows(w_query)), query_ref)
    texts = text_ref.shape[1] // 2

    def cross(block, carry):
        for clip in range(2):
            part = pl.ds(clip * rows, rows)
            keys = pl.ds(clip * texts, texts)
            for head in range(heads):
                here = pl.ds(head * HEAD_DIM, HEAD_DIM)
                query = query_ref[block, part, here] * jnp.asarray(HEAD_DIM ** (-0.5), BF)
                there = pl.ds(width + head * HEAD_DIM, HEAD_DIM)
                scores = nt(text_ref[block, keys, here], query)
                probs = jnp.exp(scores - jnp.max(scores, axis=0, keepdims=True))
                probs = probs / jnp.sum(probs, axis=0, keepdims=True)
                mix = nn(turn(text_ref[block, keys, there]).astype(BF), probs.astype(BF))
                cross_ref[block, part, here] = jnp.transpose(mix).astype(BF)
        return carry

    lax.fori_loop(0, blocks // 2, cross, 0)
    jobs[2].relay_y()
    jobs[2].relay_x()
    lax.fori_loop(blocks // 2, blocks, cross, 0)
    moves.store(query_ref, cross_ref)
    jobs[2].relay_far()
    jobs[2].finish()
    keep(2)
    apply(cross_ref, 2)

    def second(part, sums):
        branch = sum_ref[part]
        total = one_ref[part] + branch
        two_ref[part] = total
        normed, _ = normalise(total)
        low_ref[part] = (normed * gain_ref[2:3] + bias_ref[2:3]).astype(BF)
        return sums + jnp.sum(branch * branch, axis=0, keepdims=True)

    square_two = chunks(both, second, nothing)
    square_ref[...] = jnp.zeros_like(square_ref)
    square_ref[0:1] = square_one
    square_ref[1:2] = square_two
    for copy in stores:
        copy.wait()


def attend_forward(rows, side, text, frames, gain, bias, ident):
    blocks, block, width = rows.shape
    columns = side.shape[1] // 6
    heads = columns // HEAD_DIM
    heads_shape = shape(blocks, block, columns)
    stream = shape(block, width, dtype=F32)
    return call(
        forward_kernel,
        "attend_forward",
        (
            shape(blocks, block, 3 * columns),
            shape(2 * heads, blocks * block // 2, dtype=F32),
            heads_shape,
            heads_shape,
            stream,
            stream,
            heads_shape,
            heads_shape,
            shape(block, width),
            shape(blocks, *text.shape),
            shape(8, width, dtype=F32),
            shape(3, blocks, columns, width),
        ),
        (IN_VMEM,) * 11 + (ANY,),
        [IN_VMEM] * 2 + [ANY] + [IN_VMEM] * 3,
        [pltpu.VMEM((3, columns, width), BF)]
        + [pltpu.VMEM((blocks, columns, width), BF)] * 3
        + [
            pltpu.VMEM((block, width), F32),
            pltpu.VMEM((block, width), BF),
            pltpu.SemaphoreType.DMA((4,)),
            pltpu.SemaphoreType.DMA((2,)),
            pltpu.SemaphoreType.DMA((2, 7)),
            pltpu.SemaphoreType.DMA((2, 7)),
        ]
        + gather_scratch() * 4,
        ident,
        80,
    )(rows, side, text, frames, gain, bias)


def beside(own_ref, copy, other_ref, out_ref):
    half = own_ref.shape[1]
    context = lax.axis_index("context")
    out_ref[:, pl.ds(pl.multiple_of(context * half, half), half)] = own_ref[...]
    copy.wait_recv()
    there = pl.ds(pl.multiple_of((1 - context) * half, half), half)
    out_ref[:, there] = other_ref[...]


def backward_kernel(
    moves, grad_ref, qkv_ref, mix_ref, log_ref, rows_ref, w_ref, side_ref, text_ref, down_ref, up_ref,
    part_out, w_out, side_out, text_out, down_out, up_came,
    up_send, up_recv, out_ref, part_ref, store_sem, down_pair, pair_sem, grad_all, query_turned, ex_local, ex_send, ex_recv, *scratch,
):
    z = lax.axis_index("shard")
    spot = place()[1:]
    others = shard_others()
    enter(plane_others() + [device(other, *spot) for other in others])
    exchange = Exchange(grad_ref, grad_all, ex_local, ex_send, ex_recv)
    blocks, both, width = mix_ref.shape
    rows = both // 2
    heads = width // HEAD_DIM
    length = blocks * rows
    step = SIDE // rows
    for clip in range(2):
        exchange.start(clip, pl.ds(clip * rows, rows))
    some = pl.ds(up_came.shape[2], up_came.shape[2])
    up_moves = spread(
        lambda other: up_ref.at[other, :, some], up_came, up_send, up_recv, others, spot
    )
    up_own = pltpu.make_async_copy(up_ref.at[z, :, some], up_came.at[z], pair_sem.at[2])
    up_own.start()
    size = len(scratch) // 2
    text = LoadedScatter(text_ref, *scratch[size:])
    text.start()
    text.first()
    side = LoadedScatter(side_ref, *scratch[:size])
    side.start()
    side.first()
    moves.ready()
    for clip in range(2):
        exchange.finish(clip)
        part = pl.ds(clip * rows, rows)
        for head in range(heads):
            lanes = [pl.ds(j * width + head * HEAD_DIM, HEAD_DIM) for j in range(3)]
            query = qkv_ref[:, part, lanes[0]].reshape(length, HEAD_DIM)
            query = query * jnp.asarray(HEAD_DIM ** (-0.5), BF)
            key = qkv_ref[:, part, lanes[1]].reshape(length, HEAD_DIM)
            value = qkv_ref[:, part, lanes[2]].reshape(length, HEAD_DIM)
            key_turned = turn(key).astype(BF)
            here = pl.ds(head * HEAD_DIM, HEAD_DIM)
            grad = grad_all[:, part, here].reshape(length, HEAD_DIM)
            mixed = mix_ref[:, part, here].reshape(length, HEAD_DIM)
            inner = jnp.transpose(grad.astype(F32) * mixed.astype(F32))
            inner = jnp.sum(inner, axis=0, keepdims=True)
            logs = log_ref[pl.ds(clip * heads + head, 1), :]
            for index in range(length // SIDE):
                start = index * SIDE
                spots = pl.ds(index * step, step)
                k_part, v_part = key[start : start + SIDE], value[start : start + SIDE]
                scores = nt(k_part, query[start:])
                first = causal(scores[:, :SIDE])
                if start + SIDE < length:
                    scores = jnp.concatenate([first, scores[:, SIDE:]], axis=1)
                else:
                    scores = first
                weights = jnp.exp(scores - logs[:, start:])
                slopes = nt(v_part, grad[start:])
                slopes = (weights * (slopes - inner[:, start:])).astype(BF)
                grad_key = nn(slopes, query[start:]).astype(BF).reshape(step, rows, HEAD_DIM)
                grad_value = nn(weights.astype(BF), grad[start:]).astype(BF)
                out_ref[spots, part, lanes[1]] = grad_key
                out_ref[spots, part, lanes[2]] = grad_value.reshape(step, rows, HEAD_DIM)
                grad_query = nn(key_turned[:, start : start + SIDE], slopes)
                if index:
                    query_turned[:, start:] += grad_query
                else:
                    query_turned[...] = grad_query
            grad_query = jnp.transpose(query_turned[...]) * HEAD_DIM ** (-0.5)
            grad_query = grad_query.astype(BF).reshape(blocks, rows, HEAD_DIM)
            out_ref[:, part, lanes[0]] = grad_query
        if clip == 0:
            text.second()
            side.second()
            to_x = neighbours()[0]
            pair = remote_copy(down_ref, down_pair, pair_sem.at[0], pair_sem.at[1], to_x)
            pair.start()

    def store(block):
        return pltpu.make_async_copy(part_ref.at[block], part_out.at[block], store_sem.at[block])

    def project(block, carry):
        part_ref[block] = nt(out_ref[block], w_ref[:, : 3 * width]).astype(BF)
        store(block).start()
        return carry

    lax.fori_loop(0, blocks, project, 0)
    tile = 256
    right = out_ref[...].reshape(blocks * both, 3 * width)

    def weight(index, carry):
        lanes = pl.ds(pl.multiple_of(index * tile, tile), tile)
        left = rows_ref[:, :, lanes].reshape(blocks * both, tile)
        w_out[lanes, :] = tn(left, right).astype(BF)
        return carry

    lax.fori_loop(0, w_out.shape[0] // tile, weight, 0)
    moves.store(w_out)
    text_out[...] = text.total().astype(BF)
    side_out[...] = side.total().astype(BF)
    text.finish()
    side.finish()
    beside(down_ref, pair, down_pair, down_out)
    pair.wait_send()
    up_own.wait()
    for copy in up_moves:
        copy.wait()
    for block in range(blocks):
        store(block).wait()


def attend_backward(grad_mix, qkv, mix, logs, rows, weights, side, text, down, up, ident):
    blocks, block, columns = mix.shape
    _, side_rows, width = side.shape
    text_shape = text.shape[1:]
    return call(
        backward_kernel,
        "attend_backward",
        (
            shape(blocks, block, width),
            shape(width, 3 * columns),
            shape(side_rows, width),
            shape(*text_shape),
            shape(down.shape[0], 2 * down.shape[1]),
            shape(*up.shape[:2], up.shape[2] // 2),
        ),
        (ANY, IN_VMEM, IN_VMEM, IN_VMEM, IN_VMEM, ANY),
        [ANY] + [IN_VMEM] * 5 + [ANY, ANY, IN_VMEM, ANY],
        [
            pltpu.SemaphoreType.DMA((up.shape[0] - 1,)),
            pltpu.SemaphoreType.DMA((up.shape[0] - 1,)),
            pltpu.VMEM((blocks, block, 3 * columns), BF),
            pltpu.VMEM((blocks, block, width), BF),
            pltpu.SemaphoreType.DMA((8,)),
            pltpu.VMEM(down.shape, BF),
            pltpu.SemaphoreType.DMA((3,)),
            pltpu.VMEM((blocks, block, columns), BF),
            pltpu.VMEM((HEAD_DIM, blocks * block // 2), F32),
            pltpu.SemaphoreType.DMA((2,)),
            pltpu.SemaphoreType.DMA((2, 7)),
            pltpu.SemaphoreType.DMA((2, 7)),
        ]
        + LoadedScatter.scratch(side_rows, width)
        + LoadedScatter.scratch(*text_shape),
        ident,
        1,
    )(grad_mix, qkv, mix, logs, rows, weights, side, text, down, up)


CHUNK = 64


def chunks(rows, body, carry=None):
    def one(index, carry):
        return body(pl.ds(pl.multiple_of(index * CHUNK, CHUNK), CHUNK), carry)

    return lax.fori_loop(0, rows // CHUNK, one, 0 if carry is None else carry)


def normalise(inputs):
    average = jnp.mean(inputs, axis=-1, keepdims=True)
    centred = inputs - average
    rate = lax.rsqrt(jnp.mean(centred * centred, axis=-1, keepdims=True) + EPS)
    return centred * rate, rate


def norm_back(grads, inputs, gain):
    normed, rate = normalise(inputs)
    scaled = grads * gain
    inner = jnp.mean(scaled * normed, axis=-1, keepdims=True)
    result = rate * (scaled - jnp.mean(scaled, axis=-1, keepdims=True) - normed * inner)
    sums = (
        jnp.sum(grads * normed, axis=0, keepdims=True),
        jnp.sum(grads, axis=0, keepdims=True),
    )
    return result, sums


def rows_back_kernel(
    moves, normed_ref, cot_ref, one_ref, two_ref, query_ref, mix_ref, text_ref, my_mix_ref,
    gain_ref, bias_ref, w_ref, branch_ref, up_ref,
    grad_ref, layer_ref, stats_ref, grad_mix_ref, out_ref, side_ref, text_out, up_came,
    w_cross, w_query, w_out, low_ref, two_low_ref, back_ref, grad_cm, grad_cq, w_sem,
    up_send, up_recv, *scratch,
):
    z = lax.axis_index("shard")
    spot = place()[1:]
    others = shard_others()
    enter(neighbours() + [device(other, *spot) for other in others])
    some = pl.ds(0, up_came.shape[2])
    up_moves = spread(
        lambda other: up_ref.at[other, :, some], up_came, up_send, up_recv, others, spot
    )
    up_own = pltpu.make_async_copy(up_ref.at[z, :, some], up_came.at[z], w_sem.at[3])
    up_own.start()
    cross_job = Scatter(w_cross, *scratch[:5])
    query_job = Scatter(w_query, *scratch[5:10])
    branch_job = LoadedScatter(branch_ref, *scratch[10:])
    branch_job.start()
    blocks, columns, width = w_out.shape
    rows = low_ref.shape[0]
    heads = columns // HEAD_DIM
    loads = []
    for index, buffer in ((2, w_cross), (1, w_query), (0, w_out)):
        load = pltpu.make_async_copy(
            w_ref.at[index], buffer, w_sem.at[index]
        )
        load.start()
        loads.append(load)
    nothing = (jnp.zeros((1, width), F32),) * 2

    def third(part, sums):
        back, more = norm_back(normed_ref[part], two_ref[part], gain_ref[2:3])
        total = cot_ref[part].astype(F32) + back
        grad_ref[part] = total
        low_ref[part] = total.astype(BF)
        normed, _ = normalise(one_ref[part])
        two_low_ref[part] = (normed * gain_ref[1:2] + bias_ref[1:2]).astype(BF)
        return sums[0] + more[0], sums[1] + more[1]

    moves.ready()
    gain_three, shift_three = chunks(rows, third, nothing)
    branch_job.first()
    loads[0].wait()

    split_columns(nt(low_ref[...], all_rows(w_cross)), grad_cm)

    def cross_weight(block, carry):
        w_cross[block] = tn(mix_ref[block], low_ref[...]).astype(BF)
        return carry

    lax.fori_loop(0, blocks, cross_weight, 0)
    for index in range(4):
        cross_job.pass_core(index)
    half = rows // 2
    texts = text_ref.shape[1] // 2
    loads[1].wait()

    def cross(block, carry):
        for clip in range(2):
            part = pl.ds(clip * half, half)
            keys = pl.ds(clip * texts, texts)
            for head in range(heads):
                here = pl.ds(head * HEAD_DIM, HEAD_DIM)
                query = query_ref[block, part, here] * jnp.asarray(HEAD_DIM ** (-0.5), BF)
                there = pl.ds(columns + head * HEAD_DIM, HEAD_DIM)
                key, value = text_ref[block, keys, here], text_ref[block, keys, there]
                grad = grad_cm[block, part, here]
                scores = nt(key, query)
                weights = jnp.exp(scores - jnp.max(scores, axis=0, keepdims=True))
                weights = weights / jnp.sum(weights, axis=0, keepdims=True)
                slopes = nt(value, grad)
                inner = jnp.sum(weights * slopes, axis=0, keepdims=True)
                slopes = (weights * (slopes - inner)).astype(BF)
                grad_query = jnp.transpose(nn(turn(key).astype(BF), slopes))
                grad_cq[block, part, here] = (grad_query * HEAD_DIM ** (-0.5)).astype(BF)
                text_out[block, keys, here] = nn(slopes, query).astype(BF)
                text_out[block, keys, there] = nn(weights.astype(BF), grad).astype(BF)
        return carry

    def query_weight(block, carry):
        w_query[block] = tn(grad_cq[block], two_low_ref[...]).astype(BF)
        return carry

    branch_job.second()
    lax.fori_loop(0, blocks // 2, cross, 0)
    cross_job.far()
    cross_job.near()
    lax.fori_loop(blocks // 2, blocks, cross, 0)
    moves.store(text_out)
    back_ref[...] = nn(side_by_side(grad_cq), all_rows(w_query))
    lax.fori_loop(0, blocks, query_weight, 0)
    for index in range(4):
        query_job.pass_core(index)

    def second(part, sums):
        back, more = norm_back(back_ref[part], one_ref[part], gain_ref[1:2])
        total = grad_ref[part] + back
        grad_ref[part] = total
        low_ref[part] = total.astype(BF)
        return sums[0] + more[0], sums[1] + more[1]

    gain_two, shift_two = chunks(rows, second, nothing)
    moves.store(grad_ref)
    cross_job.second()
    query_job.far()
    query_job.near()
    loads[2].wait()

    split_columns(nt(low_ref[...], all_rows(w_out)), grad_mix_ref)

    def out_weight(block, carry):
        out_ref[block] = tn(my_mix_ref[block], low_ref[...]).astype(BF)
        return carry

    lax.fori_loop(0, blocks, out_weight, 0)
    moves.store(grad_mix_ref, out_ref)
    branch_job.wait()

    def last(part, sums):
        branch = branch_job.value(part)
        total = two_ref[part] + branch
        layer_ref[part] = total.astype(BF)
        return (
            sums[0] + jnp.sum(total * total, axis=0, keepdims=True),
            sums[1] + jnp.sum(branch * branch, axis=0, keepdims=True),
        )

    square_out, square_three = chunks(rows, last, nothing)
    rest = jnp.zeros((1, width), F32)
    for index, row in enumerate(
        (rest, gain_two, gain_three, rest, shift_two, shift_three, square_out, square_three)
    ):
        stats_ref[index : index + 1] = row
    moves.store(layer_ref, stats_ref)
    query_job.second()
    side_ref[1] = cross_job.total().astype(BF)
    side_ref[0] = query_job.total().astype(BF)
    branch_job.finish()
    cross_job.finish()
    query_job.finish()
    up_own.wait()
    for copy in up_moves:
        copy.wait()


def rows_back(
    normed, cot, one, two, query, mix, text, my_mix, gain, bias, weights, branch, up, ident
):
    rows, width = cot.shape
    blocks, _, columns = my_mix.shape
    return call(
        rows_back_kernel,
        "rows_back",
        (
            shape(rows, width, dtype=F32),
            shape(rows, width),
            shape(8, width, dtype=F32),
            shape(*my_mix.shape),
            shape(blocks, columns, width),
            shape(2, columns, width),
            shape(*text.shape),
            shape(*up.shape[:2], up.shape[2] // 2),
        ),
        (IN_VMEM,) * 7 + (ANY,),
        [IN_VMEM] * 10 + [ANY, ANY, ANY],
        [pltpu.VMEM((blocks, columns, width), BF)] * 3
        + [
            pltpu.VMEM((rows, width), BF),
            pltpu.VMEM((rows, width), BF),
            pltpu.VMEM((rows, width), F32),
            pltpu.VMEM(my_mix.shape, BF),
            pltpu.VMEM(my_mix.shape, BF),
            pltpu.SemaphoreType.DMA((4,)),
            pltpu.SemaphoreType.DMA((up.shape[0] - 1,)),
            pltpu.SemaphoreType.DMA((up.shape[0] - 1,)),
        ]
        + Scatter.scratch(columns, width) * 2
        + LoadedScatter.scratch(rows, width),
        ident,
        60,
    )(normed, cot, one, two, query, mix, text, my_mix, gain, bias, weights, branch, up)


def last_kernel(
    moves, part_ref, frames_ref, gain_ref, grad_ref, stats_ref, qkv_ref, up_a, up_b, cross_ref, out_w_ref,
    text_ref, text_in, w_text_ref,
    out_ref, total_ref, text_out, qkv_out, up_out, cross_out, self_out, key_out,
    mine, came, all_ref, st_send, st_recv, z_send, z_recv,
    qkv_came, out_came, text_came, text_part, text_mine, text_all,
    qkv_pair, up_mine, up_pair, cross_pair, out_pair, key_pair, x_send, x_recv, q_send, q_recv,
    *scratch,
):
    z = lax.axis_index("shard")
    shards = lax.axis_size("shard")
    others = shard_others()
    spot = place()[1:]
    context = spot[0]
    enter(neighbours() + [device(other, *spot) for other in others])

    def collect(copies, source_ref, came_ref, rows=slice(None)):
        for copy in copies:
            copy.wait_recv()
        total = source_ref[z, rows].astype(F32)
        for other in others:
            total += came_ref[other, rows].astype(F32)
        return total.astype(BF)

    def over(index, source_of, target_ref):
        return spread(source_of, target_ref, z_send.at[index], z_recv.at[index], others, spot)

    size = len(scratch) - 5
    text = Scatter(text_part, *scratch[size:])
    job = SteepScatter(part_ref, *scratch[:size])
    job.start()
    moves.ready()
    text_moves = over(0, lambda other: text_ref, text_came)
    out_moves = over(2, lambda other: out_w_ref.at[other], out_came)
    third = qkv_ref.shape[1] // 3
    thirds = [pl.ds(index * third, third) for index in range(3)]
    qkv_moves = []

    def send_third(index):
        for step, other in enumerate(others):
            copy = remote_copy(
                qkv_ref.at[other, thirds[index]], qkv_came.at[z, thirds[index]],
                q_send.at[index, step], q_recv.at[index, step], device(other, *spot),
            )
            copy.start()
            qkv_moves.append(copy)

    def sum_third(index):
        moves = qkv_moves[index * len(others) : (index + 1) * len(others)]
        rows = thirds[index]
        qkv_pair[0, rows] = collect(moves, qkv_ref, qkv_came, rows)
        pairs.append(swap(4 + index, qkv_pair.at[0, rows], qkv_pair.at[1, rows]))

    send_third(0)
    to_x = neighbours()[0]

    def swap(index, source, target_ref):
        copy = remote_copy(source, target_ref, x_send.at[index], x_recv.at[index], to_x)
        copy.start()
        return copy

    cross_move = swap(1, cross_ref, cross_pair)
    job.first()
    for start, up_ref in ((0, up_a), (up_a.shape[2], up_b)):
        total = up_ref[0].astype(F32)
        for index in range(1, shards):
            total += up_ref[index].astype(F32)
        up_mine[:, start : start + up_ref.shape[2]] = total.astype(BF)
    pairs = [swap(0, up_mine, up_pair), cross_move]
    text_came[z] = text_ref[...]
    for copy in text_moves:
        copy.wait_recv()
    texts = text_ref.shape[0] // 2
    own = texts // 8

    def text_back(index, carry):
        grads = nt(text_came[index], w_text_ref[...])
        rows = pl.ds(pl.multiple_of(index * 2 * own, 2 * own), 2 * own)
        for block in range(8):
            pair = [grads[k * texts + block * own : k * texts + block * own + own] for k in range(2)]
            text_part[block, rows] = jnp.concatenate(pair, axis=0).astype(BF)
        return carry

    lax.fori_loop(0, shards, text_back, 0)
    for index in range(4):
        text.pass_core(index)
    key_grad = tn(text_in[0], text_came[0])
    for index in range(1, shards):
        key_grad += tn(text_in[index], text_came[index])
    key_pair[0] = key_grad.astype(BF)
    pairs.append(swap(2, key_pair.at[0], key_pair.at[1]))
    job.second()
    text.far()
    text.near()
    out_pair[0] = collect(out_moves, out_w_ref, out_came)
    pairs.append(swap(3, out_pair.at[0], out_pair.at[1]))
    send_third(1)
    text.second()
    job.wait()
    sum_third(0)
    send_third(2)

    def norm(part, sums):
        back, more = norm_back(job.value(part), frames_ref[part].astype(F32), gain_ref[...])
        out_ref[part] = grad_ref[part] + back
        return sums[0] + more[0], sums[1] + more[1]

    nothing = (jnp.zeros((1, frames_ref.shape[1]), F32),) * 2
    gain_one, shift_one = chunks(frames_ref.shape[0], norm, nothing)
    moves.store(out_ref)
    mine[0] = stats_ref[...]
    mine[0, 0:1] = gain_one
    mine[0, 3:4] = shift_one
    sends = []
    for index, target in enumerate(neighbours()):
        copy = remote_copy(
            mine.at[index], came.at[index], st_send.at[index], st_recv.at[index], target
        )
        copy.start()
        sends.append(copy)
        if index == 0:
            text.wait()
            for block in range(shards):
                rows = slice(block * 2 * own, (block + 1) * 2 * own)
                text_mine[block] = text.value(rows).astype(BF)
            text_moves += over(3, lambda other: text_mine.at[other], text_all)
            text_all[z] = text_mine[z]
        copy.wait_recv()
        mine[index + 1] = mine[index] + came[index]
    stat_moves = over(4, lambda other: mine.at[3], all_ref)
    all_ref[z] = mine[3]

    sum_third(1)
    sum_third(2)
    for copy in text_moves[shards - 1 :] + stat_moves:
        copy.wait_recv()
    text_out[...] = text_all[...].astype(F32)
    total = all_ref[0]
    for index in range(1, shards):
        total += all_ref[index]
    total_ref[...] = total
    beside(up_mine, pairs[0], up_pair, up_out)

    def ordered(first, second):
        return jnp.where(context == 0, first, second), jnp.where(context == 0, second, first)

    pairs[1].wait_recv()
    lead, trail = ordered(cross_ref[...], cross_pair[...])
    width = lead.shape[0] // 2
    for index in range(2):
        part = slice(index * width, (index + 1) * width)
        cross_out[index, :width] = lead[part]
        cross_out[index, width:] = trail[part]
    pairs[2].wait_recv()
    lead, trail = ordered(key_pair[0], key_pair[1])
    for index in range(2):
        lanes = slice(index * width, (index + 1) * width)
        key_out[index, :, :width] = lead[:, lanes]
        key_out[index, :, width:] = trail[:, lanes]
    pairs[3].wait_recv()
    lead, trail = ordered(out_pair[0], out_pair[1])
    self_out[:width] = lead
    self_out[width:] = trail
    for copy in pairs[4:]:
        copy.wait_recv()
    lead, trail = ordered(qkv_pair[0], qkv_pair[1])
    for index in range(3):
        lanes = slice(index * width, (index + 1) * width)
        qkv_out[index, :, :width] = lead[:, lanes]
        qkv_out[index, :, width:] = trail[:, lanes]
    for copy in sends + text_moves + qkv_moves + out_moves + stat_moves + pairs:
        copy.wait_send()
    text.finish()
    job.finish()


def last_step(
    part, frames, gain, grad, stats, qkv, up_a, up_b, cross, out, text, text_in, w_text, ident
):
    _, rows, width = part.shape
    shards, texts, depth = text_in.shape
    half = 2 * up_a.shape[2]
    columns = out.shape[1]
    own = texts // 8
    return call(
        last_kernel,
        "last_step",
        (
            shape(rows, width, dtype=F32),
            shape(16, width, dtype=F32),
            shape(shards, own, depth, dtype=F32),
            shape(3, depth, 2 * columns),
            shape(depth, 2 * half),
            shape(2, 2 * columns, depth),
            shape(2 * columns, depth),
            shape(2, depth, 2 * columns),
        ),
        (IN_VMEM,) * 8,
        [ANY] + [IN_VMEM] * 12,
        [
            pltpu.VMEM((4, 16, width), F32),
            pltpu.VMEM((3, 16, width), F32),
            pltpu.VMEM((shards, 16, width), F32),
            pltpu.SemaphoreType.DMA((3,)),
            pltpu.SemaphoreType.DMA((3,)),
            pltpu.SemaphoreType.DMA((5, shards - 1)),
            pltpu.SemaphoreType.DMA((5, shards - 1)),
            pltpu.VMEM((shards, depth, 3 * columns), BF),
            pltpu.VMEM((shards, columns, depth), BF),
            pltpu.VMEM((shards, texts, 2 * columns), BF),
            pltpu.VMEM((8, shards * own, depth), BF),
            pltpu.VMEM((shards, own, depth), BF),
            pltpu.VMEM((shards, own, depth), BF),
            pltpu.VMEM((2, depth, 3 * columns), BF),
            pltpu.VMEM((depth, half), BF),
            pltpu.VMEM((depth, half), BF),
            pltpu.VMEM((2 * columns, depth), BF),
            pltpu.VMEM((2, columns, depth), BF),
            pltpu.VMEM((2, depth, 2 * columns), BF),
            pltpu.SemaphoreType.DMA((7,)),
            pltpu.SemaphoreType.DMA((7,)),
            pltpu.SemaphoreType.DMA((3, shards - 1)),
            pltpu.SemaphoreType.DMA((3, shards - 1)),
        ]
        + LoadedScatter.scratch(rows, width)
        + Scatter.scratch(shards * own, depth),
        ident,
        65,
    )(part, frames, gain, grad, stats, qkv, up_a, up_b, cross, out, text, text_in, w_text)


def dots(spec, *operands):
    return jnp.einsum(spec, *operands, preferred_element_type=F32)


def layer_norm(inputs, scaling, offset):
    average = jnp.mean(inputs, axis=-1, keepdims=True)
    centred = inputs - average
    variance = jnp.mean(centred * centred, axis=-1, keepdims=True)
    return centred * lax.rsqrt(variance + EPS) * scaling + offset


def on_device(
    frames,
    text_states,
    cotangent,
    norm_gain,
    norm_bias,
    self_qkv,
    self_out,
    cross_qkv,
    cross_out,
    mlp_up,
    mlp_down,
):
    clips, rows, width = frames.shape
    context = lax.axis_index("context")
    depth = self_qkv.shape[1]
    slices = width // depth
    columns = self_qkv.shape[2] // 2
    heads = columns // HEAD_DIM
    block = clips * rows
    texts = text_states.shape[1]

    def half(weight):
        size = weight.shape[-1] // 2
        return lax.dynamic_slice_in_dim(weight, context * size, size, weight.ndim - 1)

    def over_shard(weight, tiled=True):
        return lax.all_gather(weight, "shard", axis=0, tiled=tiled)

    cross_part = half(cross_qkv)
    qkv_part = half(self_qkv)
    early = [qkv_part[0], qkv_part[1], qkv_part[2], half(self_out), cross_part[0], half(cross_out)]
    w_early = over_shard(jnp.concatenate(early, axis=1))
    w_late = over_shard(jnp.concatenate([half(mlp_up), half(mlp_down)], axis=1))
    w_text = jnp.concatenate([cross_part[1], cross_part[2]], axis=1)
    text_slices = text_states.reshape(clips * texts, slices, depth).transpose(1, 0, 2)
    w_down = over_shard(half(mlp_down))

    all_one, all_grad, text_in, text_part = first_step(
        frames.reshape(block, width),
        norm_gain,
        norm_bias,
        cotangent.reshape(block, width),
        text_slices,
        w_text,
        0,
    )
    (
        qkv, self_log, mix, my_mix, stream_one, stream_two, cross_q, cross_mix, norm_three,
        text_all, squares, plane_w,
    ) = attend_forward(
        all_one,
        w_early,
        text_part,
        frames.reshape(block, width),
        norm_gain,
        norm_bias,
        1,
    )

    grad_normed, part_three, grad_up, grad_down = feed_forward(
        norm_three, all_grad, w_late, 4
    )

    def to_shard(part):
        return lax.psum_scatter(part.astype(BF), "shard", scatter_dimension=0, tiled=True)

    grad_down = to_shard(grad_down)
    grad_up = grad_up.reshape(slices, depth, -1)
    grad_one, layer_out, stats, grad_mix, part_out, side, text_grads, up_a = rows_back(
        grad_normed,
        cotangent.reshape(block, width),
        stream_one,
        stream_two,
        cross_q,
        cross_mix,
        text_all,
        my_mix,
        norm_gain,
        norm_bias,
        plane_w,
        part_three,
        grad_up,
        3,
    )

    def slice_shards(part):
        return part.reshape(-1, slices, depth).transpose(1, 0, 2)

    grad_cross = to_shard(slice_shards(side))[0]
    part_norm, grad_w_qkv, grad_out, text_grads, grad_down, up_b = attend_backward(
        grad_mix, qkv, mix, self_log, all_one, w_early, part_out, text_grads, grad_down, grad_up, 8
    )
    (
        grad_frames, totals, grad_text, grad_w_qkv, grad_up, grad_cross, grad_out, grad_keys,
    ) = last_step(
        part_norm,
        frames.reshape(block, width),
        norm_gain[0][None],
        grad_one,
        jnp.concatenate([stats, squares], axis=0),
        grad_w_qkv.reshape(slices, depth, 3 * columns),
        up_a,
        up_b,
        grad_cross,
        slice_shards(grad_out),
        text_grads,
        text_in,
        w_text,
        11,
    )
    grad_frames = grad_frames.reshape(clips, rows, width)
    grad_text = grad_text.transpose(1, 0, 2).reshape(clips, texts // 8, width)

    squares = totals[6:10].sum(axis=1)[jnp.array([0, 2, 3, 1])]
    start = lax.axis_index("shard") * depth
    grad_gain = lax.dynamic_slice_in_dim(totals[:3], start, depth, 1)
    grad_shift = lax.dynamic_slice_in_dim(totals[3:6], start, depth, 1)
    entries = float(clips * rows * width * lax.axis_size(("shard",) + PLANE))
    return (
        layer_out.reshape(clips, rows, width),
        grad_frames,
        grad_text,
        grad_gain,
        grad_shift,
        grad_w_qkv.astype(F32),
        grad_out.transpose(1, 0).astype(F32),
        jnp.concatenate([grad_cross[:1].transpose(0, 2, 1), grad_keys]).astype(F32),
        grad_cross[1].transpose(1, 0).astype(F32),
        grad_up.astype(F32),
        grad_down.astype(F32),
        jnp.sqrt(squares / entries),
    )


def solution(mesh):
    rows = P("shard", PLANE, None)
    stack = P(None, "shard", "tensor")
    flat = P("shard", "tensor")
    return jax.shard_map(
        on_device,
        mesh=mesh,
        in_specs=(rows, P("shard"), rows, P(), P(), stack, flat, stack, flat, flat, flat),
        out_specs=(
            (rows, rows, rows, P(None, "shard"), P(None, "shard"))
            + (stack, flat, stack, flat, flat, flat, P())
        ),
        check_vma=False,
    )
```

```python
from functools import partial

import jax
import jax.numpy as jnp
from jax import lax
from jax.experimental import pallas as pl
from jax.experimental.pallas import tpu as pltpu
from jax.sharding import PartitionSpec as P

HEAD_DIM = 64
EPS = 1e-05
MASKED = -1e30
MESH = pl.DeviceIdType.MESH
BF = jnp.bfloat16
F32 = jnp.float32
PLANE = ("context", "tensor")
VMEM_LIMIT = 60 * 2**20


def place():
    return (
        lax.axis_index("shard"),
        lax.axis_index("context"),
        lax.axis_index("tensor") // 2,
        lax.axis_index("tensor") % 2,
    )


def device(z, x, y, c):
    return (z, x, 2 * y + c)


def slot(x, y, c):
    return 4 * x + 2 * y + c


def neighbours():
    z, x, y, c = place()
    return [device(z, 1 - x, y, c), device(z, x, 1 - y, c), device(z, x, y, 1 - c)]


def plane_spots():
    z, x, y, c = place()
    steps = [(a, b, d) for a in range(2) for b in range(2) for d in range(2) if a + b + d]
    return [((x + a) % 2, (y + b) % 2, (c + d) % 2) for a, b, d in steps]


def plane_others():
    z = lax.axis_index("shard")
    return [device(z, *spot) for spot in plane_spots()]


def enter(targets):
    barrier = pltpu.get_barrier_semaphore()
    for target in targets:
        pl.semaphore_signal(barrier, inc=1, device_id=target, device_id_type=MESH)
    pl.semaphore_wait(barrier, len(targets))


def remote_copy(source, target_ref, send, recv, target):
    return pltpu.make_async_remote_copy(
        src_ref=source,
        dst_ref=target_ref,
        send_sem=send,
        recv_sem=recv,
        device_id=target,
        device_id_type=MESH,
    )


class Gather:
    semaphores = 9

    def __init__(self, in_ref, out_ref, local_sem, send, recv):
        z, x, y, c = place()
        self.in_ref, self.out_ref, self.local_sem = in_ref, out_ref, local_sem
        self.send, self.recv = send, recv
        self.spot = (x, y, c)
        self.to_x, self.to_y, self.to_c = neighbours()
        self.rows = in_ref.shape[0]
        self.sends = []

    def go(self, index, owner, start, size, target, source=None):
        there = self.out_ref.at[owner, pl.ds(start, size)]
        copy = remote_copy(
            there if source is None else source,
            there,
            self.send.at[index],
            self.recv.at[index],
            target,
        )
        copy.start()
        self.sends.append(copy)

    def arrived(self, index, owner, start, size):
        there = self.out_ref.at[owner, pl.ds(start, size)]
        remote_copy(
            there, there, self.send.at[index], self.recv.at[index], self.to_x
        ).wait_recv()

    def start(self):
        me = slot(*self.spot)
        self.own = pltpu.make_async_copy(self.in_ref, self.out_ref.at[me], self.local_sem)
        self.own.start()
        for index, target in enumerate((self.to_x, self.to_y, self.to_c)):
            self.go(index, me, 0, self.rows, target, self.in_ref)

    def relay_y(self):
        x, y, c = self.spot
        owner = slot(x, 1 - y, c)
        self.arrived(1, owner, 0, self.rows)
        self.go(3, owner, 0, self.rows // 2, self.to_x)
        self.go(5, owner, 0, self.rows, self.to_c)

    def relay_x(self):
        x, y, c = self.spot
        half = self.rows // 2
        owner = slot(1 - x, y, c)
        self.arrived(0, owner, 0, self.rows)
        self.go(4, owner, half, half, self.to_y)
        self.go(6, owner, 0, self.rows, self.to_c)

    def relay_far(self):
        x, y, c = self.spot
        half = self.rows // 2
        owner = slot(1 - x, 1 - y, c)
        self.arrived(3, owner, 0, half)
        self.go(7, owner, 0, half, self.to_c)
        self.arrived(4, owner, half, half)
        self.go(8, owner, half, half, self.to_c)

    def finish(self):
        x, y, c = self.spot
        half = self.rows // 2
        self.arrived(2, slot(x, y, 1 - c), 0, self.rows)
        self.arrived(5, slot(x, 1 - y, 1 - c), 0, self.rows)
        self.arrived(6, slot(1 - x, y, 1 - c), 0, self.rows)
        self.arrived(7, slot(1 - x, 1 - y, 1 - c), 0, half)
        self.arrived(8, slot(1 - x, 1 - y, 1 - c), half, half)
        self.own.wait()
        for copy in self.sends:
            copy.wait_send()

    def rest(self):
        self.relay_y()
        self.relay_x()
        self.relay_far()
        self.finish()


class Scatter:
    @staticmethod
    def scratch(rows, columns):
        return [
            pltpu.VMEM((4, rows, columns), BF),
            pltpu.VMEM((2, rows // 2, columns), BF),
            pltpu.VMEM((2, rows, columns), BF),
            pltpu.SemaphoreType.DMA((10,)),
            pltpu.SemaphoreType.DMA((10,)),
        ]

    def __init__(self, part_ref, core, relay, final, send, recv):
        self.part_ref, self.core, self.relay, self.final = part_ref, core, relay, final
        self.send, self.recv = send, recv
        self.to_x, self.to_y, self.to_c = neighbours()
        z, x, y, c = place()
        chips = ((1 - x, 1 - y), (1 - x, y), (x, 1 - y), (x, y))
        self.mine = [slot(*chip, c) for chip in chips]
        self.theirs = [slot(*chip, 1 - c) for chip in chips]
        rows = part_ref.shape[1]
        self.low, self.high = pl.ds(0, rows // 2), pl.ds(rows // 2, rows // 2)
        self.sends = []

    def forward(self, index, source, target_ref, target):
        copy = remote_copy(
            source, target_ref, self.send.at[index], self.recv.at[index], target
        )
        copy.start()
        self.sends.append(copy)

    def arrived(self, index, ref):
        remote_copy(ref, ref, self.send.at[index], self.recv.at[index], self.to_c).wait_recv()

    def pass_core(self, index):
        source = self.part_ref.at[self.theirs[index]]
        self.forward(index, source, self.core.at[index], self.to_c)

    def add(self, index, part, more=None):
        mine = self.mine[index]
        total = self.part_ref[mine, part].astype(F32) + self.core[index, part].astype(F32)
        if more is not None:
            total += more.astype(F32)
        self.part_ref[mine, part] = total.astype(BF)
        return self.part_ref.at[mine, part]

    def far(self):
        self.arrived(0, self.core.at[0])
        self.forward(4, self.add(0, self.low), self.relay.at[0], self.to_x)
        self.forward(5, self.add(0, self.high), self.relay.at[1], self.to_y)

    def near(self):
        self.arrived(1, self.core.at[1])
        self.forward(6, self.add(1, self.low), self.final.at[0, self.low], self.to_x)
        self.arrived(2, self.core.at[2])
        self.forward(7, self.add(2, self.high), self.final.at[1, self.high], self.to_y)

    def second(self):
        low, high, final, relay = self.low, self.high, self.final, self.relay
        self.arrived(5, relay.at[1])
        self.forward(8, self.add(1, high, relay[1]), final.at[0, high], self.to_x)
        self.arrived(4, relay.at[0])
        self.forward(9, self.add(2, low, relay[0]), final.at[1, low], self.to_y)

    def wait(self):
        self.arrived(3, self.core.at[3])
        self.arrived(6, self.final.at[0, self.low])
        self.arrived(7, self.final.at[1, self.high])
        self.arrived(8, self.final.at[0, self.high])
        self.arrived(9, self.final.at[1, self.low])

    def value(self, part=slice(None)):
        total = self.part_ref[self.mine[3], part].astype(F32) + self.core[3, part].astype(F32)
        return total + self.final[0, part].astype(F32) + self.final[1, part].astype(F32)

    def total(self):
        self.wait()
        return self.value()

    def finish(self):
        for copy in self.sends:
            copy.wait_send()


class LoadedScatter(Scatter):
    steep = False

    @staticmethod
    def scratch(rows, columns):
        return [
            pltpu.VMEM((4, rows, columns), BF),
            pltpu.SemaphoreType.DMA((4,)),
        ] + Scatter.scratch(rows, columns)

    def __init__(self, in_ref, part_ref, local_sem, *scratch):
        super().__init__(part_ref, *scratch)
        self.in_ref, self.local_sem = in_ref, local_sem

    def bring(self, index):
        source = self.in_ref.at[self.theirs[index]]
        self.forward(index, source, self.core.at[index], self.to_c)
        load = pltpu.make_async_copy(
            self.in_ref.at[self.blocks[index]], self.part_ref.at[index], self.local_sem.at[index]
        )
        load.start()
        self.loads.append(load)

    def start(self):
        self.loads = []
        self.blocks, self.mine = self.mine, (0, 1, 2, 3)
        for index in range(4):
            self.bring(index)

    def first(self):
        for load in self.loads:
            load.wait()
        if not self.steep:
            self.far()
            self.near()
            return
        self.arrived(0, self.core.at[0])
        self.forward(4, self.add(0, self.low), self.relay.at[0], self.to_y)
        self.forward(5, self.add(0, self.high), self.relay.at[1], self.to_y)
        self.arrived(2, self.core.at[2])
        self.forward(7, self.add(2, self.high), self.final.at[1, self.high], self.to_y)
        self.forward(9, self.add(2, self.low), self.final.at[1, self.low], self.to_y)

    def second(self):
        if not self.steep:
            super().second()
            return
        final, relay = self.final, self.relay
        self.arrived(1, self.core.at[1])
        self.arrived(4, relay.at[0])
        self.forward(6, self.add(1, self.low, relay[0]), final.at[0, self.low], self.to_x)
        self.arrived(5, relay.at[1])
        self.forward(8, self.add(1, self.high, relay[1]), final.at[0, self.high], self.to_x)


class SteepScatter(LoadedScatter):
    steep = True


class Exchange:
    def __init__(self, in_ref, out_ref, local_sem, send, recv):
        self.in_ref, self.out_ref, self.local_sem = in_ref, out_ref, local_sem
        self.send, self.recv = send, recv
        z, x, y, c = place()
        self.me = slot(x, y, c)
        self.copies = []

    def start(self, piece, part):
        z = lax.axis_index("shard")
        own = pltpu.make_async_copy(
            self.in_ref.at[self.me, part], self.out_ref.at[self.me, part], self.local_sem.at[piece]
        )
        own.start()
        self.copies.append(own)
        for index, spot in enumerate(plane_spots()):
            copy = remote_copy(
                self.in_ref.at[slot(*spot), part],
                self.out_ref.at[self.me, part],
                self.send.at[piece, index],
                self.recv.at[piece, index],
                device(z, *spot),
            )
            copy.start()
            self.copies.append(copy)

    def finish(self, piece=None):
        copies = self.copies if piece is None else self.copies[8 * piece : 8 * piece + 8]
        for copy in copies:
            copy.wait()


ANY = pl.BlockSpec(memory_space=pl.ANY)
IN_VMEM = pl.BlockSpec(memory_space=pltpu.VMEM)


class Moves:
    def __init__(self, loads, stores):
        self.loads, self.stores = loads, stores
        for _, copy in loads:
            copy.start()
        self.begun = []

    def ready(self, *refs):
        rest = []
        for ref, copy in self.loads:
            if not refs or any(ref is wanted for wanted in refs):
                copy.wait()
            else:
                rest.append((ref, copy))
        self.loads = rest

    def store(self, *refs):
        rest = []
        for ref, copy in self.stores:
            if not refs or any(ref is wanted for wanted in refs):
                copy.start()
                self.begun.append(copy)
            else:
                rest.append((ref, copy))
        self.stores = rest

    def finish(self):
        self.ready()
        self.store()
        for copy in self.begun:
            copy.wait()


def call(kernel, name, outs, out_specs, in_specs, scratch, ident, micros):
    def run(*args):
        loaded = [i for i, spec in enumerate(in_specs) if spec is IN_VMEM]
        stored = [i for i, spec in enumerate(out_specs) if spec is IN_VMEM]
        buffers = [pltpu.VMEM(args[i].shape, args[i].dtype) for i in loaded]
        buffers += [pltpu.VMEM(outs[i].shape, outs[i].dtype) for i in stored]

        def wrapped(*refs):
            ends = len(in_specs), len(in_specs) + len(outs)
            given, made, rest = list(refs[: ends[0]]), list(refs[ends[0] : ends[1]]), refs[ends[1] :]
            sems, rest = rest[len(buffers)], (rest[: len(buffers)], rest[len(buffers) + 1 :])
            loads, stores = [], []
            for k, i in enumerate(loaded):
                copy = pltpu.make_async_copy(given[i], rest[0][k], sems.at[k])
                loads.append((rest[0][k], copy))
                given[i] = rest[0][k]
            for k, i in enumerate(stored, len(loaded)):
                copy = pltpu.make_async_copy(rest[0][k], made[i], sems.at[k])
                stores.append((rest[0][k], copy))
                made[i] = rest[0][k]
            moves = Moves(loads, stores)
            kernel(moves, *given, *made, *rest[1])
            moves.finish()

        return pl.pallas_call(
            wrapped,
            out_shape=outs,
            in_specs=[ANY] * len(in_specs),
            out_specs=(ANY,) * len(outs),
            scratch_shapes=buffers + [pltpu.SemaphoreType.DMA((len(buffers),))] + scratch,
            name=name,
            cost_estimate=pl.CostEstimate(
                flops=micros * 10**9, bytes_accessed=micros * 10**6, transcendentals=0
            ),
            compiler_params=pltpu.CompilerParams(
                collective_id=ident, has_side_effects=True, vmem_limit_bytes=VMEM_LIMIT
            ),
        )(*args)

    return run


def shape(*dims, dtype=BF):
    return jax.ShapeDtypeStruct(dims, dtype)


def gather_scratch():
    return [
        pltpu.SemaphoreType.DMA,
        pltpu.SemaphoreType.DMA((9,)),
        pltpu.SemaphoreType.DMA((9,)),
    ]


def shard_others():
    z, shards = lax.axis_index("shard"), lax.axis_size("shard")
    return [lax.rem(z + i, shards) for i in range(1, shards)]


def spread(source_of, target_ref, send, recv, others, spot):
    z = lax.axis_index("shard")
    copies = []
    for index, other in enumerate(others):
        copy = remote_copy(
            source_of(other), target_ref.at[z], send.at[index], recv.at[index],
            device(other, *spot),
        )
        copy.start()
        copies.append(copy)
    return copies


def first_kernel(
    moves, frames_ref, gain_ref, bias_ref, cot_ref, text_ref, w_text_ref,
    rows_out, cot_out, text_all, text_out,
    normed_ref, part_ref, came_ref, some_ref, some_flat, text_plane, sends, recvs, *scratch,
):
    z = lax.axis_index("shard")
    spot = place()[1:]
    others = shard_others()
    enter(neighbours() + [device(other, *spot) for other in others])
    moves.ready()
    few = some_ref.shape[1]
    some = pl.ds(pl.multiple_of(slot(*spot) * few, few), few)
    texts = spread(
        lambda other: text_ref.at[other, some], some_ref, sends.at[0], recvs.at[0], others, spot
    )
    some_ref[z] = text_ref[z, some]

    def norm(part, carry):
        normed, _ = normalise(frames_ref[part].astype(F32))
        normed_ref[part] = (normed * gain_ref[0:1] + bias_ref[0:1]).astype(BF)
        return carry

    chunks(frames_ref.shape[0], norm)
    rows, grads = Gather(normed_ref, rows_out, *scratch[:3]), Gather(cot_ref, cot_out, *scratch[3:6])
    rows.start()
    for copy in texts:
        copy.wait_recv()
    shards, _, depth = some_ref.shape
    some_flat[...] = some_ref[...].reshape(shards * few, depth)
    meet = Gather(some_flat, text_plane, *scratch[6:])
    meet.start()
    meet.rest()

    def share(index, carry):
        rows_here = pl.ds(pl.multiple_of(index * few, few), few)
        text_all[index] = text_plane[:, rows_here].reshape(8 * few, depth)
        part_ref[index] = nn(text_all[index], w_text_ref[...]).astype(BF)
        return carry

    lax.fori_loop(0, text_all.shape[0], share, 0)
    parts = spread(lambda other: part_ref.at[other], came_ref, sends.at[1], recvs.at[1], others, spot)
    came_ref[z] = part_ref[z]
    rows.relay_y()
    rows.relay_x()
    grads.start()
    rows.relay_far()
    rows.finish()
    grads.rest()
    for copy in parts:
        copy.wait_recv()
    total = came_ref[0].astype(F32)
    for index in range(1, came_ref.shape[0]):
        total += came_ref[index].astype(F32)
    text_out[...] = total.astype(BF)
    for copy in texts + parts:
        copy.wait_send()


def first_step(frames, gain, bias, cotangent, text, w_text, ident):
    rows, width = frames.shape
    shards, texts, depth = text.shape
    return call(
        first_kernel,
        "first_step",
        (
            shape(8, rows, width),
            shape(8, rows, width),
            shape(shards, texts, depth),
            shape(texts, w_text.shape[1]),
        ),
        (ANY, ANY, IN_VMEM, IN_VMEM),
        [IN_VMEM, IN_VMEM, IN_VMEM, ANY, IN_VMEM, IN_VMEM],
        [
            pltpu.VMEM((rows, width), BF),
            pltpu.VMEM((shards, texts, w_text.shape[1]), BF),
            pltpu.VMEM((shards, texts, w_text.shape[1]), BF),
            pltpu.VMEM((shards, texts // 8, depth), BF),
            pltpu.VMEM((shards * texts // 8, depth), BF),
            pltpu.VMEM((8, shards * texts // 8, depth), BF),
            pltpu.SemaphoreType.DMA((2, shards - 1)),
            pltpu.SemaphoreType.DMA((2, shards - 1)),
        ]
        + gather_scratch() * 3,
        ident,
        60,
    )(frames, gain, bias, cotangent, text, w_text)


def feed_kernel(
    moves, own_ref, grad_ref, w_ref,
    normed_out, branch_out, up_out, down_out,
    rows_ref, grads_ref, hidden_ref, slope_ref, part_a, part_b,
    load_sem, store_sem, g_local, g_send, g_recv, *scratch,
):
    enter(neighbours())
    gather = Gather(own_ref, rows_ref, g_local, g_send, g_recv)
    gather.start()
    hidden = hidden_ref.shape[2]
    up_ref, down_ref = w_ref.at[:, pl.ds(0, hidden)], w_ref.at[:, pl.ds(hidden, hidden)]
    blocks, _, width = rows_ref.shape
    loads = []
    for block in range(blocks):
        load = pltpu.make_async_copy(grad_ref.at[block], grads_ref.at[block], load_sem.at[block])
        load.start()
        loads.append(load)
    for load in loads:
        load.wait()

    def early(block, carry):
        slope_ref[block] = nn(grads_ref[block], down_ref[...]).astype(BF)
        return carry

    moves.ready()
    lax.fori_loop(0, blocks, early, 0)

    def middle(block):
        before = nn(rows_ref[block], up_ref[...])
        share = 0.5 + 0.5 * lax.erf(before * (0.5**0.5))
        hidden_ref[block] = (before * share).astype(BF)
        slope = share + before * (jnp.exp(-0.5 * before * before) * (2.0 * jnp.pi) ** (-0.5))
        slope = (slope_ref[block].astype(F32) * slope).astype(BF)
        slope_ref[block] = slope
        part_a[block] = nt(slope, up_ref[...]).astype(BF)

    first = Scatter(part_a, *scratch)
    x, y, c = gather.spot

    def pair(cx, cy):
        def one(index, carry):
            middle(slot(cx, cy, 0) + index)
            return carry

        lax.fori_loop(0, 2, one, 0)

    gather.own.wait()
    gather.arrived(2, slot(x, y, 1 - c), 0, gather.rows)
    pair(x, y)
    first.pass_core(3)
    gather.relay_y()
    gather.relay_x()
    gather.arrived(6, slot(1 - x, y, 1 - c), 0, gather.rows)
    pair(1 - x, y)
    first.pass_core(1)
    gather.arrived(5, slot(x, 1 - y, 1 - c), 0, gather.rows)
    pair(x, 1 - y)
    first.pass_core(2)
    gather.relay_far()
    first.near()
    gather.arrived(7, slot(1 - x, 1 - y, 1 - c), 0, gather.rows // 2)
    gather.arrived(8, slot(1 - x, 1 - y, 1 - c), gather.rows // 2, gather.rows // 2)
    pair(1 - x, 1 - y)
    first.pass_core(0)
    first.far()
    for copy in gather.sends:
        copy.wait_send()

    def store(block):
        return pltpu.make_async_copy(part_b.at[block], branch_out.at[block], store_sem.at[block])

    def branch(block, carry):
        part_b[block] = nt(hidden_ref[block], down_ref[...]).astype(BF)
        store(block).start()
        return carry

    lax.fori_loop(0, blocks, branch, 0)
    first.second()
    tile = 256

    def weight(left_ref, right_ref, out_ref):
        right = right_ref[...].reshape(-1, right_ref.shape[2])

        def one(index, carry):
            lanes = pl.ds(pl.multiple_of(index * tile, tile), tile)
            left = left_ref[:, :, lanes].reshape(-1, tile)
            out_ref[lanes, :] = tn(left, right).astype(BF)
            return carry

        lax.fori_loop(0, width // tile, one, 0)

    weight(grads_ref, hidden_ref, down_out)
    moves.store(down_out)
    weight(rows_ref, slope_ref, up_out)
    moves.store(up_out)
    normed_out[...] = first.total()
    first.finish()
    for block in range(blocks):
        store(block).wait()


def feed_forward(own, grads, weights, ident):
    rows, width = own.shape
    hidden = weights.shape[1] // 2
    outs = (
        shape(rows, width, dtype=F32),
        shape(8, rows, width),
        shape(width, hidden),
        shape(width, hidden),
    )
    scratch = [
        pltpu.VMEM((8, rows, width), BF),
        pltpu.VMEM((8, rows, width), BF),
        pltpu.VMEM((8, rows, hidden), BF),
        pltpu.VMEM((8, rows, hidden), BF),
        pltpu.VMEM((8, rows, width), BF),
        pltpu.VMEM((8, rows, width), BF),
        pltpu.SemaphoreType.DMA((8,)),
        pltpu.SemaphoreType.DMA((8,)),
    ]
    return call(
        feed_kernel,
        "feed_forward",
        outs,
        (IN_VMEM, ANY, IN_VMEM, IN_VMEM),
        [ANY, ANY, IN_VMEM],
        scratch + gather_scratch() + Scatter.scratch(rows, width),
        ident,
        70,
    )(own, grads, weights)


SIDE = 256


def nt(left, right):
    return lax.dot_general(left, right, (((1,), (1,)), ((), ())), preferred_element_type=F32)


def nn(left, right):
    return lax.dot_general(left, right, (((1,), (0,)), ((), ())), preferred_element_type=F32)


def tn(left, right):
    return lax.dot_general(left, right, (((0,), (0,)), ((), ())), preferred_element_type=F32)


def turn(values):
    return jnp.transpose(values.astype(F32))


def side_by_side(ref):
    return jnp.concatenate([ref[block] for block in range(ref.shape[0])], axis=1)


def all_rows(ref):
    return ref[...].reshape(-1, ref.shape[2])


def split_columns(values, ref):
    columns = ref.shape[2]
    for block in range(ref.shape[0]):
        ref[block] = values[:, block * columns : (block + 1) * columns].astype(BF)


def causal(scores):
    keys = lax.broadcasted_iota(jnp.int32, scores.shape, 0)
    queries = lax.broadcasted_iota(jnp.int32, scores.shape, 1)
    return jnp.where(keys <= queries, scores, MASKED)


def forward_kernel(
    moves, rows_ref, side_ref, text_in, frames_ref, gain_ref, bias_ref,
    qkv_ref, log_ref, mix_ref, mine_ref, one_ref, two_ref, query_ref, cross_ref, low_ref,
    text_ref, square_ref, plane_out,
    w_own, w_out, w_query, w_cross, sum_ref, two_low_ref, store_sem,
    ex_local, ex_send, ex_recv, *scratch,
):
    enter(plane_others())
    blocks, both, _ = rows_ref.shape
    rows = both // 2
    width = mix_ref.shape[2]
    features = two_low_ref.shape[1]
    heads = width // HEAD_DIM
    length = blocks * rows
    step = SIDE // rows
    weights = (w_out, w_query, w_cross)

    def turn_own(kind):
        w_own[kind] = turn(side_ref[:, (3 + kind) * width : (4 + kind) * width]).astype(BF)

    moves.ready(side_ref)
    turn_own(0)
    jobs = [Gather(w_own.at[k], weights[k], *scratch[3 * k : 3 * k + 3]) for k in range(3)]
    text_job = Gather(text_in, text_ref, *scratch[9:])
    text_job.start()
    jobs[0].start()
    stores = []

    def keep(kind):
        copy = pltpu.make_async_copy(weights[kind], plane_out.at[kind], store_sem.at[kind])
        copy.start()
        stores.append(copy)

    def project(block, carry):
        qkv_ref[block] = nn(rows_ref[block], side_ref[:, : 3 * width]).astype(BF)
        return carry

    moves.ready()
    lax.fori_loop(0, blocks, project, 0)
    moves.store(qkv_ref)
    turn_own(1)
    turn_own(2)
    exchange = Exchange(mix_ref, mine_ref, ex_local, ex_send, ex_recv)
    for clip in range(2):
        part = pl.ds(clip * rows, rows)
        for head in range(heads):
            lanes = [pl.ds(j * width + head * HEAD_DIM, HEAD_DIM) for j in range(3)]
            key = qkv_ref[:, part, lanes[1]].reshape(length, HEAD_DIM)
            value = turn(qkv_ref[:, part, lanes[2]].reshape(length, HEAD_DIM)).astype(BF)
            for index in range(length // SIDE):
                spots = pl.ds(index * step, step)
                query = qkv_ref[spots, part, lanes[0]].reshape(SIDE, HEAD_DIM)
                query = query * jnp.asarray(HEAD_DIM ** (-0.5), BF)
                start = index * SIDE
                last = causal(nt(key[start : start + SIDE], query))
                top = jnp.max(last, axis=0, keepdims=True)
                if index:
                    early = nt(key[:start], query)
                    top = jnp.maximum(top, jnp.max(early, axis=0, keepdims=True))
                last = jnp.exp(last - top)
                total = jnp.sum(last, axis=0, keepdims=True)
                mix = nn(value[:, start : start + SIDE], last.astype(BF))
                if index:
                    early = jnp.exp(early - top)
                    total += jnp.sum(early, axis=0, keepdims=True)
                    mix += nn(value[:, :start], early.astype(BF))
                mix = jnp.transpose(mix / total).astype(BF).reshape(step, rows, HEAD_DIM)
                mix_ref[spots, part, pl.ds(head * HEAD_DIM, HEAD_DIM)] = mix
                log_ref[pl.ds(clip * heads + head, 1), pl.ds(start, SIDE)] = top + jnp.log(total)
        exchange.start(clip, part)
        if clip == 0:
            jobs[0].relay_y()
            jobs[0].relay_x()
            text_job.relay_y()
            text_job.relay_x()
    jobs[1].start()
    moves.store(mix_ref, log_ref)
    jobs[0].relay_far()
    text_job.relay_far()
    jobs[0].finish()
    text_job.finish()
    keep(0)
    exchange.finish()
    moves.store(mine_ref, text_ref)

    def apply(values_ref, kind):
        sum_ref[...] = nn(side_by_side(values_ref), all_rows(weights[kind]))

    apply(mine_ref, 0)
    nothing = jnp.zeros((1, features), F32)

    def first(part, sums):
        branch = sum_ref[part]
        total = frames_ref[part].astype(F32) + branch
        one_ref[part] = total
        normed, _ = normalise(total)
        two_low_ref[part] = (normed * gain_ref[1:2] + bias_ref[1:2]).astype(BF)
        return sums + jnp.sum(branch * branch, axis=0, keepdims=True)

    square_one = chunks(both, first, nothing)
    moves.store(one_ref)
    jobs[1].relay_y()
    jobs[1].relay_x()
    jobs[2].start()
    jobs[1].relay_far()
    jobs[1].finish()
    keep(1)

    split_columns(nt(two_low_ref[...], all_rows(w_query)), query_ref)
    texts = text_ref.shape[1] // 2

    def cross(block, carry):
        for clip in range(2):
            part = pl.ds(clip * rows, rows)
            keys = pl.ds(clip * texts, texts)
            for head in range(heads):
                here = pl.ds(head * HEAD_DIM, HEAD_DIM)
                query = query_ref[block, part, here] * jnp.asarray(HEAD_DIM ** (-0.5), BF)
                there = pl.ds(width + head * HEAD_DIM, HEAD_DIM)
                scores = nt(text_ref[block, keys, here], query)
                probs = jnp.exp(scores - jnp.max(scores, axis=0, keepdims=True))
                probs = probs / jnp.sum(probs, axis=0, keepdims=True)
                mix = nn(turn(text_ref[block, keys, there]).astype(BF), probs.astype(BF))
                cross_ref[block, part, here] = jnp.transpose(mix).astype(BF)
        return carry

    lax.fori_loop(0, blocks // 2, cross, 0)
    jobs[2].relay_y()
    jobs[2].relay_x()
    lax.fori_loop(blocks // 2, blocks, cross, 0)
    moves.store(query_ref, cross_ref)
    jobs[2].relay_far()
    jobs[2].finish()
    keep(2)
    apply(cross_ref, 2)

    def second(part, sums):
        branch = sum_ref[part]
        total = one_ref[part] + branch
        two_ref[part] = total
        normed, _ = normalise(total)
        low_ref[part] = (normed * gain_ref[2:3] + bias_ref[2:3]).astype(BF)
        return sums + jnp.sum(branch * branch, axis=0, keepdims=True)

    square_two = chunks(both, second, nothing)
    square_ref[...] = jnp.zeros_like(square_ref)
    square_ref[0:1] = square_one
    square_ref[1:2] = square_two
    for copy in stores:
        copy.wait()


def attend_forward(rows, side, text, frames, gain, bias, ident):
    blocks, block, width = rows.shape
    columns = side.shape[1] // 6
    heads = columns // HEAD_DIM
    heads_shape = shape(blocks, block, columns)
    stream = shape(block, width, dtype=F32)
    return call(
        forward_kernel,
        "attend_forward",
        (
            shape(blocks, block, 3 * columns),
            shape(2 * heads, blocks * block // 2, dtype=F32),
            heads_shape,
            heads_shape,
            stream,
            stream,
            heads_shape,
            heads_shape,
            shape(block, width),
            shape(blocks, *text.shape),
            shape(8, width, dtype=F32),
            shape(3, blocks, columns, width),
        ),
        (IN_VMEM,) * 11 + (ANY,),
        [IN_VMEM] * 2 + [ANY] + [IN_VMEM] * 3,
        [pltpu.VMEM((3, columns, width), BF)]
        + [pltpu.VMEM((blocks, columns, width), BF)] * 3
        + [
            pltpu.VMEM((block, width), F32),
            pltpu.VMEM((block, width), BF),
            pltpu.SemaphoreType.DMA((4,)),
            pltpu.SemaphoreType.DMA((2,)),
            pltpu.SemaphoreType.DMA((2, 7)),
            pltpu.SemaphoreType.DMA((2, 7)),
        ]
        + gather_scratch() * 4,
        ident,
        80,
    )(rows, side, text, frames, gain, bias)


def beside(own_ref, copy, other_ref, out_ref):
    half = own_ref.shape[1]
    context = lax.axis_index("context")
    out_ref[:, pl.ds(pl.multiple_of(context * half, half), half)] = own_ref[...]
    copy.wait_recv()
    there = pl.ds(pl.multiple_of((1 - context) * half, half), half)
    out_ref[:, there] = other_ref[...]


def backward_kernel(
    moves, grad_ref, qkv_ref, mix_ref, log_ref, rows_ref, w_ref, side_ref, text_ref, down_ref, up_ref,
    part_out, w_out, side_out, text_out, down_out, up_came,
    up_send, up_recv, out_ref, part_ref, store_sem, down_pair, pair_sem, grad_all, query_turned, ex_local, ex_send, ex_recv, *scratch,
):
    z = lax.axis_index("shard")
    spot = place()[1:]
    others = shard_others()
    enter(plane_others() + [device(other, *spot) for other in others])
    exchange = Exchange(grad_ref, grad_all, ex_local, ex_send, ex_recv)
    blocks, both, width = mix_ref.shape
    rows = both // 2
    heads = width // HEAD_DIM
    length = blocks * rows
    step = SIDE // rows
    for clip in range(2):
        exchange.start(clip, pl.ds(clip * rows, rows))
    some = pl.ds(up_came.shape[2], up_came.shape[2])
    up_moves = spread(
        lambda other: up_ref.at[other, :, some], up_came, up_send, up_recv, others, spot
    )
    up_own = pltpu.make_async_copy(up_ref.at[z, :, some], up_came.at[z], pair_sem.at[2])
    up_own.start()
    size = len(scratch) // 2
    text = LoadedScatter(text_ref, *scratch[size:])
    text.start()
    text.first()
    side = LoadedScatter(side_ref, *scratch[:size])
    side.start()
    side.first()
    moves.ready()
    for clip in range(2):
        exchange.finish(clip)
        part = pl.ds(clip * rows, rows)
        for head in range(heads):
            lanes = [pl.ds(j * width + head * HEAD_DIM, HEAD_DIM) for j in range(3)]
            query = qkv_ref[:, part, lanes[0]].reshape(length, HEAD_DIM)
            query = query * jnp.asarray(HEAD_DIM ** (-0.5), BF)
            key = qkv_ref[:, part, lanes[1]].reshape(length, HEAD_DIM)
            value = qkv_ref[:, part, lanes[2]].reshape(length, HEAD_DIM)
            key_turned = turn(key).astype(BF)
            here = pl.ds(head * HEAD_DIM, HEAD_DIM)
            grad = grad_all[:, part, here].reshape(length, HEAD_DIM)
            mixed = mix_ref[:, part, here].reshape(length, HEAD_DIM)
            inner = jnp.transpose(grad.astype(F32) * mixed.astype(F32))
            inner = jnp.sum(inner, axis=0, keepdims=True)
            logs = log_ref[pl.ds(clip * heads + head, 1), :]
            for index in range(length // SIDE):
                start = index * SIDE
                spots = pl.ds(index * step, step)
                k_part, v_part = key[start : start + SIDE], value[start : start + SIDE]
                scores = nt(k_part, query[start:])
                first = causal(scores[:, :SIDE])
                if start + SIDE < length:
                    scores = jnp.concatenate([first, scores[:, SIDE:]], axis=1)
                else:
                    scores = first
                weights = jnp.exp(scores - logs[:, start:])
                slopes = nt(v_part, grad[start:])
                slopes = (weights * (slopes - inner[:, start:])).astype(BF)
                grad_key = nn(slopes, query[start:]).astype(BF).reshape(step, rows, HEAD_DIM)
                grad_value = nn(weights.astype(BF), grad[start:]).astype(BF)
                out_ref[spots, part, lanes[1]] = grad_key
                out_ref[spots, part, lanes[2]] = grad_value.reshape(step, rows, HEAD_DIM)
                grad_query = nn(key_turned[:, start : start + SIDE], slopes)
                if index:
                    query_turned[:, start:] += grad_query
                else:
                    query_turned[...] = grad_query
            grad_query = jnp.transpose(query_turned[...]) * HEAD_DIM ** (-0.5)
            grad_query = grad_query.astype(BF).reshape(blocks, rows, HEAD_DIM)
            out_ref[:, part, lanes[0]] = grad_query
        if clip == 0:
            text.second()
            side.second()
            to_x = neighbours()[0]
            pair = remote_copy(down_ref, down_pair, pair_sem.at[0], pair_sem.at[1], to_x)
            pair.start()

    def store(block):
        return pltpu.make_async_copy(part_ref.at[block], part_out.at[block], store_sem.at[block])

    def project(block, carry):
        part_ref[block] = nt(out_ref[block], w_ref[:, : 3 * width]).astype(BF)
        store(block).start()
        return carry

    lax.fori_loop(0, blocks, project, 0)
    tile = 256
    right = out_ref[...].reshape(blocks * both, 3 * width)

    def weight(index, carry):
        lanes = pl.ds(pl.multiple_of(index * tile, tile), tile)
        left = rows_ref[:, :, lanes].reshape(blocks * both, tile)
        w_out[lanes, :] = tn(left, right).astype(BF)
        return carry

    lax.fori_loop(0, w_out.shape[0] // tile, weight, 0)
    moves.store(w_out)
    text_out[...] = text.total().astype(BF)
    into_slices(side.total().astype(BF), side_out, 0)
    text.finish()
    side.finish()
    beside(down_ref, pair, down_pair, down_out)
    pair.wait_send()
    up_own.wait()
    for copy in up_moves:
        copy.wait()
    for block in range(blocks):
        store(block).wait()


def attend_backward(grad_mix, qkv, mix, logs, rows, weights, side, text, down, up, ident):
    blocks, block, columns = mix.shape
    _, side_rows, width = side.shape
    text_shape = text.shape[1:]
    return call(
        backward_kernel,
        "attend_backward",
        (
            shape(blocks, block, width),
            shape(width, 3 * columns),
            shape(up.shape[0], side_rows, up.shape[1]),
            shape(*text_shape),
            shape(down.shape[0], 2 * down.shape[1]),
            shape(*up.shape[:2], up.shape[2] // 2),
        ),
        (ANY, IN_VMEM, IN_VMEM, IN_VMEM, IN_VMEM, ANY),
        [ANY] + [IN_VMEM] * 5 + [ANY, ANY, IN_VMEM, ANY],
        [
            pltpu.SemaphoreType.DMA((up.shape[0] - 1,)),
            pltpu.SemaphoreType.DMA((up.shape[0] - 1,)),
            pltpu.VMEM((blocks, block, 3 * columns), BF),
            pltpu.VMEM((blocks, block, width), BF),
            pltpu.SemaphoreType.DMA((8,)),
            pltpu.VMEM(down.shape, BF),
            pltpu.SemaphoreType.DMA((3,)),
            pltpu.VMEM((blocks, block, columns), BF),
            pltpu.VMEM((HEAD_DIM, blocks * block // 2), F32),
            pltpu.SemaphoreType.DMA((2,)),
            pltpu.SemaphoreType.DMA((2, 7)),
            pltpu.SemaphoreType.DMA((2, 7)),
        ]
        + LoadedScatter.scratch(side_rows, width)
        + LoadedScatter.scratch(*text_shape),
        ident,
        1,
    )(grad_mix, qkv, mix, logs, rows, weights, side, text, down, up)


CHUNK = 64


def chunks(rows, body, carry=None):
    def one(index, carry):
        return body(pl.ds(pl.multiple_of(index * CHUNK, CHUNK), CHUNK), carry)

    return lax.fori_loop(0, rows // CHUNK, one, 0 if carry is None else carry)


def normalise(inputs):
    average = jnp.mean(inputs, axis=-1, keepdims=True)
    centred = inputs - average
    rate = lax.rsqrt(jnp.mean(centred * centred, axis=-1, keepdims=True) + EPS)
    return centred * rate, rate


def norm_back(grads, inputs, gain):
    normed, rate = normalise(inputs)
    scaled = grads * gain
    inner = jnp.mean(scaled * normed, axis=-1, keepdims=True)
    result = rate * (scaled - jnp.mean(scaled, axis=-1, keepdims=True) - normed * inner)
    sums = (
        jnp.sum(grads * normed, axis=0, keepdims=True),
        jnp.sum(grads, axis=0, keepdims=True),
    )
    return result, sums


def into_slices(values, ref, start):
    shards, _, depth = ref.shape
    for index in range(shards):
        part = values[:, index * depth : (index + 1) * depth]
        ref[index, start : start + values.shape[0]] = part


def rows_back_kernel(
    moves, normed_ref, cot_ref, one_ref, two_ref, query_ref, mix_ref, text_ref, my_mix_ref,
    gain_ref, bias_ref, w_ref, branch_ref, up_ref,
    grad_ref, layer_ref, stats_ref, grad_mix_ref, out_ref, side_ref, text_out, up_came,
    w_cross, w_query, w_out, low_ref, two_low_ref, back_ref, grad_cm, grad_cq, w_sem,
    up_send, up_recv, *scratch,
):
    z = lax.axis_index("shard")
    spot = place()[1:]
    others = shard_others()
    enter(neighbours() + [device(other, *spot) for other in others])
    some = pl.ds(0, up_came.shape[2])
    up_moves = spread(
        lambda other: up_ref.at[other, :, some], up_came, up_send, up_recv, others, spot
    )
    up_own = pltpu.make_async_copy(up_ref.at[z, :, some], up_came.at[z], w_sem.at[3])
    up_own.start()
    cross_job = Scatter(w_cross, *scratch[:5])
    query_job = Scatter(w_query, *scratch[5:10])
    branch_job = LoadedScatter(branch_ref, *scratch[10:])
    branch_job.start()
    blocks, columns, width = w_out.shape
    rows = low_ref.shape[0]
    heads = columns // HEAD_DIM
    loads = []
    for index, buffer in ((2, w_cross), (1, w_query), (0, w_out)):
        load = pltpu.make_async_copy(
            w_ref.at[index], buffer, w_sem.at[index]
        )
        load.start()
        loads.append(load)
    nothing = (jnp.zeros((1, width), F32),) * 2

    def third(part, sums):
        back, more = norm_back(normed_ref[part], two_ref[part], gain_ref[2:3])
        total = cot_ref[part].astype(F32) + back
        grad_ref[part] = total
        low_ref[part] = total.astype(BF)
        normed, _ = normalise(one_ref[part])
        two_low_ref[part] = (normed * gain_ref[1:2] + bias_ref[1:2]).astype(BF)
        return sums[0] + more[0], sums[1] + more[1]

    moves.ready()
    gain_three, shift_three = chunks(rows, third, nothing)
    branch_job.first()
    loads[0].wait()

    split_columns(nt(low_ref[...], all_rows(w_cross)), grad_cm)

    def cross_weight(block, carry):
        w_cross[block] = tn(mix_ref[block], low_ref[...]).astype(BF)
        return carry

    lax.fori_loop(0, blocks, cross_weight, 0)
    for index in range(4):
        cross_job.pass_core(index)
    half = rows // 2
    texts = text_ref.shape[1] // 2
    loads[1].wait()

    def cross(block, carry):
        for clip in range(2):
            part = pl.ds(clip * half, half)
            keys = pl.ds(clip * texts, texts)
            for head in range(heads):
                here = pl.ds(head * HEAD_DIM, HEAD_DIM)
                query = query_ref[block, part, here] * jnp.asarray(HEAD_DIM ** (-0.5), BF)
                there = pl.ds(columns + head * HEAD_DIM, HEAD_DIM)
                key, value = text_ref[block, keys, here], text_ref[block, keys, there]
                grad = grad_cm[block, part, here]
                scores = nt(key, query)
                weights = jnp.exp(scores - jnp.max(scores, axis=0, keepdims=True))
                weights = weights / jnp.sum(weights, axis=0, keepdims=True)
                slopes = nt(value, grad)
                inner = jnp.sum(weights * slopes, axis=0, keepdims=True)
                slopes = (weights * (slopes - inner)).astype(BF)
                grad_query = jnp.transpose(nn(turn(key).astype(BF), slopes))
                grad_cq[block, part, here] = (grad_query * HEAD_DIM ** (-0.5)).astype(BF)
                text_out[block, keys, here] = nn(slopes, query).astype(BF)
                text_out[block, keys, there] = nn(weights.astype(BF), grad).astype(BF)
        return carry

    def query_weight(block, carry):
        w_query[block] = tn(grad_cq[block], two_low_ref[...]).astype(BF)
        return carry

    branch_job.second()
    lax.fori_loop(0, blocks // 2, cross, 0)
    cross_job.far()
    cross_job.near()
    lax.fori_loop(blocks // 2, blocks, cross, 0)
    moves.store(text_out)
    back_ref[...] = nn(side_by_side(grad_cq), all_rows(w_query))
    lax.fori_loop(0, blocks, query_weight, 0)
    for index in range(4):
        query_job.pass_core(index)

    def second(part, sums):
        back, more = norm_back(back_ref[part], one_ref[part], gain_ref[1:2])
        total = grad_ref[part] + back
        grad_ref[part] = total
        low_ref[part] = total.astype(BF)
        return sums[0] + more[0], sums[1] + more[1]

    gain_two, shift_two = chunks(rows, second, nothing)
    moves.store(grad_ref)
    cross_job.second()
    query_job.far()
    query_job.near()
    loads[2].wait()

    split_columns(nt(low_ref[...], all_rows(w_out)), grad_mix_ref)

    def out_weight(block, carry):
        out_ref[block] = tn(my_mix_ref[block], low_ref[...]).astype(BF)
        return carry

    lax.fori_loop(0, blocks, out_weight, 0)
    moves.store(grad_mix_ref, out_ref)
    branch_job.wait()

    def last(part, sums):
        branch = branch_job.value(part)
        total = two_ref[part] + branch
        layer_ref[part] = total.astype(BF)
        return (
            sums[0] + jnp.sum(total * total, axis=0, keepdims=True),
            sums[1] + jnp.sum(branch * branch, axis=0, keepdims=True),
        )

    square_out, square_three = chunks(rows, last, nothing)
    rest = jnp.zeros((1, width), F32)
    for index, row in enumerate(
        (rest, gain_two, gain_three, rest, shift_two, shift_three, square_out, square_three)
    ):
        stats_ref[index : index + 1] = row
    moves.store(layer_ref, stats_ref)
    query_job.second()
    for kind, job in ((1, cross_job), (0, query_job)):
        into_slices(job.total().astype(BF), side_ref, kind * columns)
    branch_job.finish()
    cross_job.finish()
    query_job.finish()
    up_own.wait()
    for copy in up_moves:
        copy.wait()


def rows_back(
    normed, cot, one, two, query, mix, text, my_mix, gain, bias, weights, branch, up, ident
):
    rows, width = cot.shape
    blocks, _, columns = my_mix.shape
    return call(
        rows_back_kernel,
        "rows_back",
        (
            shape(rows, width, dtype=F32),
            shape(rows, width),
            shape(8, width, dtype=F32),
            shape(*my_mix.shape),
            shape(blocks, columns, width),
            shape(up.shape[0], 2 * columns, up.shape[1]),
            shape(*text.shape),
            shape(*up.shape[:2], up.shape[2] // 2),
        ),
        (IN_VMEM,) * 7 + (ANY,),
        [IN_VMEM] * 10 + [ANY, ANY, ANY],
        [pltpu.VMEM((blocks, columns, width), BF)] * 3
        + [
            pltpu.VMEM((rows, width), BF),
            pltpu.VMEM((rows, width), BF),
            pltpu.VMEM((rows, width), F32),
            pltpu.VMEM(my_mix.shape, BF),
            pltpu.VMEM(my_mix.shape, BF),
            pltpu.SemaphoreType.DMA((4,)),
            pltpu.SemaphoreType.DMA((up.shape[0] - 1,)),
            pltpu.SemaphoreType.DMA((up.shape[0] - 1,)),
        ]
        + Scatter.scratch(columns, width) * 2
        + LoadedScatter.scratch(rows, width),
        ident,
        60,
    )(normed, cot, one, two, query, mix, text, my_mix, gain, bias, weights, branch, up)


def last_kernel(
    moves, part_ref, frames_ref, gain_ref, grad_ref, stats_ref, squares_ref, qkv_ref, up_a, up_b, cross_ref, out_w_ref,
    text_ref, text_in, w_text_ref,
    out_ref, total_ref, text_out, qkv_out, up_out, cross_out, self_out, key_out,
    mine, came, all_ref, st_send, st_recv, z_send, z_recv,
    qkv_came, out_came, text_came, text_part, text_mine, text_all,
    qkv_pair, up_mine, up_pair, cross_pair, out_pair, key_pair, x_send, x_recv, q_send, q_recv,
    *scratch,
):
    z = lax.axis_index("shard")
    shards = lax.axis_size("shard")
    others = shard_others()
    spot = place()[1:]
    context = spot[0]
    enter(neighbours() + [device(other, *spot) for other in others])

    def collect(copies, source_ref, came_ref, rows=slice(None)):
        for copy in copies:
            copy.wait_recv()
        total = source_ref[z, rows].astype(F32)
        for other in others:
            total += came_ref[other, rows].astype(F32)
        return total.astype(BF)

    def over(index, source_of, target_ref):
        return spread(source_of, target_ref, z_send.at[index], z_recv.at[index], others, spot)

    size = len(scratch) - 5
    text = Scatter(text_part, *scratch[size:])
    job = SteepScatter(part_ref, *scratch[:size])
    job.start()
    moves.ready()
    text_moves = over(0, lambda other: text_ref, text_came)
    out_moves = over(2, lambda other: out_w_ref.at[other], out_came)
    third = qkv_ref.shape[1] // 3
    thirds = [pl.ds(index * third, third) for index in range(3)]
    qkv_moves = []

    def send_third(index):
        for step, other in enumerate(others):
            copy = remote_copy(
                qkv_ref.at[other, thirds[index]], qkv_came.at[z, thirds[index]],
                q_send.at[index, step], q_recv.at[index, step], device(other, *spot),
            )
            copy.start()
            qkv_moves.append(copy)

    def sum_third(index):
        moves = qkv_moves[index * len(others) : (index + 1) * len(others)]
        rows = thirds[index]
        qkv_pair[0, rows] = collect(moves, qkv_ref, qkv_came, rows)
        pairs.append(swap(4 + index, qkv_pair.at[0, rows], qkv_pair.at[1, rows]))

    send_third(0)
    to_x = neighbours()[0]

    def swap(index, source, target_ref):
        copy = remote_copy(source, target_ref, x_send.at[index], x_recv.at[index], to_x)
        copy.start()
        return copy

    cross_move = swap(1, cross_ref, cross_pair)
    job.first()
    for start, up_ref in ((0, up_a), (up_a.shape[2], up_b)):
        total = up_ref[0].astype(F32)
        for index in range(1, shards):
            total += up_ref[index].astype(F32)
        up_mine[:, start : start + up_ref.shape[2]] = total.astype(BF)
    pairs = [swap(0, up_mine, up_pair), cross_move]
    text_came[z] = text_ref[...]
    for copy in text_moves:
        copy.wait_recv()
    texts = text_ref.shape[0] // 2
    own = texts // 8

    def text_back(index, carry):
        grads = nt(text_came[index], w_text_ref[...])
        rows = pl.ds(pl.multiple_of(index * 2 * own, 2 * own), 2 * own)
        for block in range(8):
            pair = [grads[k * texts + block * own : k * texts + block * own + own] for k in range(2)]
            text_part[block, rows] = jnp.concatenate(pair, axis=0).astype(BF)
        return carry

    lax.fori_loop(0, shards, text_back, 0)
    for index in range(4):
        text.pass_core(index)
    key_grad = tn(text_in[0], text_came[0])
    for index in range(1, shards):
        key_grad += tn(text_in[index], text_came[index])
    key_pair[0] = key_grad.astype(BF)
    pairs.append(swap(2, key_pair.at[0], key_pair.at[1]))
    job.second()
    text.far()
    text.near()
    out_pair[0] = collect(out_moves, out_w_ref, out_came)
    pairs.append(swap(3, out_pair.at[0], out_pair.at[1]))
    send_third(1)
    text.second()
    job.wait()
    sum_third(0)
    send_third(2)

    def norm(part, sums):
        back, more = norm_back(job.value(part), frames_ref[part].astype(F32), gain_ref[0:1])
        out_ref[part] = grad_ref[part] + back
        return sums[0] + more[0], sums[1] + more[1]

    nothing = (jnp.zeros((1, frames_ref.shape[1]), F32),) * 2
    gain_one, shift_one = chunks(frames_ref.shape[0], norm, nothing)
    moves.store(out_ref)
    mine[0, :8] = stats_ref[...]
    mine[0, 8:] = squares_ref[...]
    mine[0, 0:1] = gain_one
    mine[0, 3:4] = shift_one
    sends = []
    for index, target in enumerate(neighbours()):
        copy = remote_copy(
            mine.at[index], came.at[index], st_send.at[index], st_recv.at[index], target
        )
        copy.start()
        sends.append(copy)
        if index == 0:
            text.wait()
            for block in range(shards):
                rows = slice(block * 2 * own, (block + 1) * 2 * own)
                text_mine[block] = text.value(rows).astype(BF)
            text_moves += over(3, lambda other: text_mine.at[other], text_all)
            text_all[z] = text_mine[z]
        copy.wait_recv()
        mine[index + 1] = mine[index] + came[index]
    stat_moves = over(4, lambda other: mine.at[3], all_ref)
    all_ref[z] = mine[3]

    sum_third(1)
    sum_third(2)
    for copy in text_moves[shards - 1 :] + stat_moves:
        copy.wait_recv()
    text_out[...] = text_all[...].astype(F32)
    total = all_ref[0]
    for index in range(1, shards):
        total += all_ref[index]
    total_ref[...] = total
    beside(up_mine, pairs[0], up_pair, up_out)

    def ordered(first, second):
        return jnp.where(context == 0, first, second), jnp.where(context == 0, second, first)

    pairs[1].wait_recv()
    lead, trail = ordered(cross_ref[...], cross_pair[...])
    width = lead.shape[0] // 2
    for index in range(2):
        part = slice(index * width, (index + 1) * width)
        cross_out[index, :width] = lead[part]
        cross_out[index, width:] = trail[part]
    pairs[2].wait_recv()
    lead, trail = ordered(key_pair[0], key_pair[1])
    for index in range(2):
        lanes = slice(index * width, (index + 1) * width)
        key_out[index, :, :width] = lead[:, lanes]
        key_out[index, :, width:] = trail[:, lanes]
    pairs[3].wait_recv()
    lead, trail = ordered(out_pair[0], out_pair[1])
    self_out[:width] = lead
    self_out[width:] = trail
    for copy in pairs[4:]:
        copy.wait_recv()
    lead, trail = ordered(qkv_pair[0], qkv_pair[1])
    for index in range(3):
        lanes = slice(index * width, (index + 1) * width)
        qkv_out[index, :, :width] = lead[:, lanes]
        qkv_out[index, :, width:] = trail[:, lanes]
    for copy in sends + text_moves + qkv_moves + out_moves + stat_moves + pairs:
        copy.wait_send()
    text.finish()
    job.finish()


def last_step(
    part, frames, gain, grad, stats, squares, qkv, up_a, up_b, cross, out, text, text_in, w_text,
    ident,
):
    _, rows, width = part.shape
    shards, texts, depth = text_in.shape
    half = 2 * up_a.shape[2]
    columns = out.shape[1]
    own = texts // 8
    return call(
        last_kernel,
        "last_step",
        (
            shape(rows, width, dtype=F32),
            shape(16, width, dtype=F32),
            shape(shards, own, depth, dtype=F32),
            shape(3, depth, 2 * columns),
            shape(depth, 2 * half),
            shape(2, 2 * columns, depth),
            shape(2 * columns, depth),
            shape(2, depth, 2 * columns),
        ),
        (IN_VMEM,) * 8,
        [ANY] + [IN_VMEM] * 13,
        [
            pltpu.VMEM((4, 16, width), F32),
            pltpu.VMEM((3, 16, width), F32),
            pltpu.VMEM((shards, 16, width), F32),
            pltpu.SemaphoreType.DMA((3,)),
            pltpu.SemaphoreType.DMA((3,)),
            pltpu.SemaphoreType.DMA((5, shards - 1)),
            pltpu.SemaphoreType.DMA((5, shards - 1)),
            pltpu.VMEM((shards, depth, 3 * columns), BF),
            pltpu.VMEM((shards, columns, depth), BF),
            pltpu.VMEM((shards, texts, 2 * columns), BF),
            pltpu.VMEM((8, shards * own, depth), BF),
            pltpu.VMEM((shards, own, depth), BF),
            pltpu.VMEM((shards, own, depth), BF),
            pltpu.VMEM((2, depth, 3 * columns), BF),
            pltpu.VMEM((depth, half), BF),
            pltpu.VMEM((depth, half), BF),
            pltpu.VMEM((2 * columns, depth), BF),
            pltpu.VMEM((2, columns, depth), BF),
            pltpu.VMEM((2, depth, 2 * columns), BF),
            pltpu.SemaphoreType.DMA((7,)),
            pltpu.SemaphoreType.DMA((7,)),
            pltpu.SemaphoreType.DMA((3, shards - 1)),
            pltpu.SemaphoreType.DMA((3, shards - 1)),
        ]
        + LoadedScatter.scratch(rows, width)
        + Scatter.scratch(shards * own, depth),
        ident,
        65,
    )(part, frames, gain, grad, stats, squares, qkv, up_a, up_b, cross, out, text, text_in, w_text)


def dots(spec, *operands):
    return jnp.einsum(spec, *operands, preferred_element_type=F32)


def layer_norm(inputs, scaling, offset):
    average = jnp.mean(inputs, axis=-1, keepdims=True)
    centred = inputs - average
    variance = jnp.mean(centred * centred, axis=-1, keepdims=True)
    return centred * lax.rsqrt(variance + EPS) * scaling + offset


def on_device(
    frames,
    text_states,
    cotangent,
    norm_gain,
    norm_bias,
    self_qkv,
    self_out,
    cross_qkv,
    cross_out,
    mlp_up,
    mlp_down,
):
    clips, rows, width = frames.shape
    context = lax.axis_index("context")
    depth = self_qkv.shape[1]
    slices = width // depth
    columns = self_qkv.shape[2] // 2
    heads = columns // HEAD_DIM
    block = clips * rows
    texts = text_states.shape[1]

    def half(weight):
        size = weight.shape[-1] // 2
        return lax.dynamic_slice_in_dim(weight, context * size, size, weight.ndim - 1)

    def over_shard(weight, tiled=True):
        return lax.all_gather(weight, "shard", axis=0, tiled=tiled)

    cross_part = half(cross_qkv)
    qkv_part = half(self_qkv)
    early = [qkv_part[0], qkv_part[1], qkv_part[2], half(self_out), cross_part[0], half(cross_out)]
    w_early = over_shard(jnp.concatenate(early, axis=1))
    w_late = over_shard(jnp.concatenate([half(mlp_up), half(mlp_down)], axis=1))
    w_text = jnp.concatenate([cross_part[1], cross_part[2]], axis=1)
    text_slices = text_states.reshape(clips * texts, slices, depth).transpose(1, 0, 2)
    w_down = over_shard(half(mlp_down))

    all_one, all_grad, text_in, text_part = first_step(
        frames.reshape(block, width),
        norm_gain,
        norm_bias,
        cotangent.reshape(block, width),
        text_slices,
        w_text,
        0,
    )
    (
        qkv, self_log, mix, my_mix, stream_one, stream_two, cross_q, cross_mix, norm_three,
        text_all, squares, plane_w,
    ) = attend_forward(
        all_one,
        w_early,
        text_part,
        frames.reshape(block, width),
        norm_gain,
        norm_bias,
        1,
    )

    grad_normed, part_three, grad_up, grad_down = feed_forward(
        norm_three, all_grad, w_late, 4
    )

    def to_shard(part):
        return lax.psum_scatter(part.astype(BF), "shard", scatter_dimension=0, tiled=True)

    grad_down = to_shard(grad_down)
    grad_up = grad_up.reshape(slices, depth, -1)
    grad_one, layer_out, stats, grad_mix, part_out, side, text_grads, up_a = rows_back(
        grad_normed,
        cotangent.reshape(block, width),
        stream_one,
        stream_two,
        cross_q,
        cross_mix,
        text_all,
        my_mix,
        norm_gain,
        norm_bias,
        plane_w,
        part_three,
        grad_up,
        3,
    )

    grad_cross = to_shard(side)[0]
    part_norm, grad_w_qkv, grad_out, text_grads, grad_down, up_b = attend_backward(
        grad_mix, qkv, mix, self_log, all_one, w_early, part_out, text_grads, grad_down, grad_up, 8
    )
    (
        grad_frames, totals, grad_text, grad_w_qkv, grad_up, grad_cross, grad_out, grad_keys,
    ) = last_step(
        part_norm,
        frames.reshape(block, width),
        norm_gain,
        grad_one,
        stats,
        squares,
        grad_w_qkv.reshape(slices, depth, 3 * columns),
        up_a,
        up_b,
        grad_cross,
        grad_out,
        text_grads,
        text_in,
        w_text,
        11,
    )
    grad_frames = grad_frames.reshape(clips, rows, width)
    grad_text = grad_text.transpose(1, 0, 2).reshape(clips, texts // 8, width)

    squares = totals[6:10].sum(axis=1)[jnp.array([0, 2, 3, 1])]
    start = lax.axis_index("shard") * depth
    grad_gain = lax.dynamic_slice_in_dim(totals[:3], start, depth, 1)
    grad_shift = lax.dynamic_slice_in_dim(totals[3:6], start, depth, 1)
    entries = float(clips * rows * width * lax.axis_size(("shard",) + PLANE))
    return (
        layer_out.reshape(clips, rows, width),
        grad_frames,
        grad_text,
        grad_gain,
        grad_shift,
        grad_w_qkv.astype(F32),
        grad_out.transpose(1, 0).astype(F32),
        jnp.concatenate([grad_cross[:1].transpose(0, 2, 1), grad_keys]).astype(F32),
        grad_cross[1].transpose(1, 0).astype(F32),
        grad_up.astype(F32),
        grad_down.astype(F32),
        jnp.sqrt(squares / entries),
    )


def solution(mesh):
    rows = P("shard", PLANE, None)
    stack = P(None, "shard", "tensor")
    flat = P("shard", "tensor")
    return jax.shard_map(
        on_device,
        mesh=mesh,
        in_specs=(rows, P("shard"), rows, P(), P(), stack, flat, stack, flat, flat, flat),
        out_specs=(
            (rows, rows, rows, P(None, "shard"), P(None, "shard"))
            + (stack, flat, stack, flat, flat, flat, P())
        ),
        check_vma=False,
    )
```

```python
from functools import partial

import jax
import jax.numpy as jnp
from jax import lax
from jax.experimental import pallas as pl
from jax.experimental.pallas import tpu as pltpu
from jax.sharding import PartitionSpec as P

HEAD_DIM = 64
EPS = 1e-05
MASKED = -1e30
MESH = pl.DeviceIdType.MESH
BF = jnp.bfloat16
F32 = jnp.float32
PLANE = ("context", "tensor")
VMEM_LIMIT = 60 * 2**20


def place():
    return (
        lax.axis_index("shard"),
        lax.axis_index("context"),
        lax.axis_index("tensor") // 2,
        lax.axis_index("tensor") % 2,
    )


def device(z, x, y, c):
    return (z, x, 2 * y + c)


def slot(x, y, c):
    return 4 * x + 2 * y + c


def neighbours():
    z, x, y, c = place()
    return [device(z, 1 - x, y, c), device(z, x, 1 - y, c), device(z, x, y, 1 - c)]


def plane_spots():
    z, x, y, c = place()
    steps = [(a, b, d) for a in range(2) for b in range(2) for d in range(2) if a + b + d]
    return [((x + a) % 2, (y + b) % 2, (c + d) % 2) for a, b, d in steps]


def plane_others():
    z = lax.axis_index("shard")
    return [device(z, *spot) for spot in plane_spots()]


def enter(targets):
    barrier = pltpu.get_barrier_semaphore()
    for target in targets:
        pl.semaphore_signal(barrier, inc=1, device_id=target, device_id_type=MESH)
    pl.semaphore_wait(barrier, len(targets))


def remote_copy(source, target_ref, send, recv, target):
    return pltpu.make_async_remote_copy(
        src_ref=source,
        dst_ref=target_ref,
        send_sem=send,
        recv_sem=recv,
        device_id=target,
        device_id_type=MESH,
    )


class Gather:
    semaphores = 9

    def __init__(self, in_ref, out_ref, local_sem, send, recv):
        z, x, y, c = place()
        self.in_ref, self.out_ref, self.local_sem = in_ref, out_ref, local_sem
        self.send, self.recv = send, recv
        self.spot = (x, y, c)
        self.to_x, self.to_y, self.to_c = neighbours()
        self.rows = in_ref.shape[0]
        self.sends = []

    def go(self, index, owner, start, size, target, source=None):
        there = self.out_ref.at[owner, pl.ds(start, size)]
        copy = remote_copy(
            there if source is None else source,
            there,
            self.send.at[index],
            self.recv.at[index],
            target,
        )
        copy.start()
        self.sends.append(copy)

    def arrived(self, index, owner, start, size):
        there = self.out_ref.at[owner, pl.ds(start, size)]
        remote_copy(
            there, there, self.send.at[index], self.recv.at[index], self.to_x
        ).wait_recv()

    def start(self):
        me = slot(*self.spot)
        self.own = pltpu.make_async_copy(self.in_ref, self.out_ref.at[me], self.local_sem)
        self.own.start()
        for index, target in enumerate((self.to_x, self.to_y, self.to_c)):
            self.go(index, me, 0, self.rows, target, self.in_ref)

    def relay_y(self):
        x, y, c = self.spot
        owner = slot(x, 1 - y, c)
        self.arrived(1, owner, 0, self.rows)
        self.go(3, owner, 0, self.rows // 2, self.to_x)
        self.go(5, owner, 0, self.rows, self.to_c)

    def relay_x(self):
        x, y, c = self.spot
        half = self.rows // 2
        owner = slot(1 - x, y, c)
        self.arrived(0, owner, 0, self.rows)
        self.go(4, owner, half, half, self.to_y)
        self.go(6, owner, 0, self.rows, self.to_c)

    def relay_far(self):
        x, y, c = self.spot
        half = self.rows // 2
        owner = slot(1 - x, 1 - y, c)
        self.arrived(3, owner, 0, half)
        self.go(7, owner, 0, half, self.to_c)
        self.arrived(4, owner, half, half)
        self.go(8, owner, half, half, self.to_c)

    def finish(self):
        x, y, c = self.spot
        half = self.rows // 2
        self.arrived(2, slot(x, y, 1 - c), 0, self.rows)
        self.arrived(5, slot(x, 1 - y, 1 - c), 0, self.rows)
        self.arrived(6, slot(1 - x, y, 1 - c), 0, self.rows)
        self.arrived(7, slot(1 - x, 1 - y, 1 - c), 0, half)
        self.arrived(8, slot(1 - x, 1 - y, 1 - c), half, half)
        self.own.wait()
        for copy in self.sends:
            copy.wait_send()

    def rest(self):
        self.relay_y()
        self.relay_x()
        self.relay_far()
        self.finish()


class Scatter:
    @staticmethod
    def scratch(rows, columns):
        return [
            pltpu.VMEM((4, rows, columns), BF),
            pltpu.VMEM((2, rows // 2, columns), BF),
            pltpu.VMEM((2, rows, columns), BF),
            pltpu.SemaphoreType.DMA((10,)),
            pltpu.SemaphoreType.DMA((10,)),
        ]

    def __init__(self, part_ref, core, relay, final, send, recv):
        self.part_ref, self.core, self.relay, self.final = part_ref, core, relay, final
        self.send, self.recv = send, recv
        self.to_x, self.to_y, self.to_c = neighbours()
        z, x, y, c = place()
        chips = ((1 - x, 1 - y), (1 - x, y), (x, 1 - y), (x, y))
        self.mine = [slot(*chip, c) for chip in chips]
        self.theirs = [slot(*chip, 1 - c) for chip in chips]
        rows = part_ref.shape[1]
        self.low, self.high = pl.ds(0, rows // 2), pl.ds(rows // 2, rows // 2)
        self.sends = []

    def forward(self, index, source, target_ref, target):
        copy = remote_copy(
            source, target_ref, self.send.at[index], self.recv.at[index], target
        )
        copy.start()
        self.sends.append(copy)

    def arrived(self, index, ref):
        remote_copy(ref, ref, self.send.at[index], self.recv.at[index], self.to_c).wait_recv()

    def pass_core(self, index):
        source = self.part_ref.at[self.theirs[index]]
        self.forward(index, source, self.core.at[index], self.to_c)

    def add(self, index, part, more=None):
        mine = self.mine[index]
        total = self.part_ref[mine, part].astype(F32) + self.core[index, part].astype(F32)
        if more is not None:
            total += more.astype(F32)
        self.part_ref[mine, part] = total.astype(BF)
        return self.part_ref.at[mine, part]

    def far(self):
        self.arrived(0, self.core.at[0])
        self.forward(4, self.add(0, self.low), self.relay.at[0], self.to_x)
        self.forward(5, self.add(0, self.high), self.relay.at[1], self.to_y)

    def near(self):
        self.arrived(1, self.core.at[1])
        self.forward(6, self.add(1, self.low), self.final.at[0, self.low], self.to_x)
        self.arrived(2, self.core.at[2])
        self.forward(7, self.add(2, self.high), self.final.at[1, self.high], self.to_y)

    def second(self):
        low, high, final, relay = self.low, self.high, self.final, self.relay
        self.arrived(5, relay.at[1])
        self.forward(8, self.add(1, high, relay[1]), final.at[0, high], self.to_x)
        self.arrived(4, relay.at[0])
        self.forward(9, self.add(2, low, relay[0]), final.at[1, low], self.to_y)

    def wait(self):
        self.arrived(3, self.core.at[3])
        self.arrived(6, self.final.at[0, self.low])
        self.arrived(7, self.final.at[1, self.high])
        self.arrived(8, self.final.at[0, self.high])
        self.arrived(9, self.final.at[1, self.low])

    def value(self, part=slice(None)):
        total = self.part_ref[self.mine[3], part].astype(F32) + self.core[3, part].astype(F32)
        return total + self.final[0, part].astype(F32) + self.final[1, part].astype(F32)

    def total(self):
        self.wait()
        return self.value()

    def finish(self):
        for copy in self.sends:
            copy.wait_send()


class LoadedScatter(Scatter):
    steep = False

    @staticmethod
    def scratch(rows, columns):
        return [
            pltpu.VMEM((4, rows, columns), BF),
            pltpu.SemaphoreType.DMA((4,)),
        ] + Scatter.scratch(rows, columns)

    def __init__(self, in_ref, part_ref, local_sem, *scratch):
        super().__init__(part_ref, *scratch)
        self.in_ref, self.local_sem = in_ref, local_sem

    def bring(self, index):
        source = self.in_ref.at[self.theirs[index]]
        self.forward(index, source, self.core.at[index], self.to_c)
        load = pltpu.make_async_copy(
            self.in_ref.at[self.blocks[index]], self.part_ref.at[index], self.local_sem.at[index]
        )
        load.start()
        self.loads.append(load)

    def start(self):
        self.loads = []
        self.blocks, self.mine = self.mine, (0, 1, 2, 3)
        for index in range(4):
            self.bring(index)

    def first(self):
        for load in self.loads:
            load.wait()
        if not self.steep:
            self.far()
            self.near()
            return
        self.arrived(0, self.core.at[0])
        self.forward(4, self.add(0, self.low), self.relay.at[0], self.to_y)
        self.forward(5, self.add(0, self.high), self.relay.at[1], self.to_y)
        self.arrived(2, self.core.at[2])
        self.forward(7, self.add(2, self.high), self.final.at[1, self.high], self.to_y)
        self.forward(9, self.add(2, self.low), self.final.at[1, self.low], self.to_y)

    def second(self):
        if not self.steep:
            super().second()
            return
        final, relay = self.final, self.relay
        self.arrived(1, self.core.at[1])
        self.arrived(4, relay.at[0])
        self.forward(6, self.add(1, self.low, relay[0]), final.at[0, self.low], self.to_x)
        self.arrived(5, relay.at[1])
        self.forward(8, self.add(1, self.high, relay[1]), final.at[0, self.high], self.to_x)


class SteepScatter(LoadedScatter):
    steep = True


class Exchange:
    def __init__(self, in_ref, out_ref, local_sem, send, recv):
        self.in_ref, self.out_ref, self.local_sem = in_ref, out_ref, local_sem
        self.send, self.recv = send, recv
        z, x, y, c = place()
        self.me = slot(x, y, c)
        self.copies = []

    def start(self, piece, part):
        z = lax.axis_index("shard")
        own = pltpu.make_async_copy(
            self.in_ref.at[self.me, part], self.out_ref.at[self.me, part], self.local_sem.at[piece]
        )
        own.start()
        self.copies.append(own)
        for index, spot in enumerate(plane_spots()):
            copy = remote_copy(
                self.in_ref.at[slot(*spot), part],
                self.out_ref.at[self.me, part],
                self.send.at[piece, index],
                self.recv.at[piece, index],
                device(z, *spot),
            )
            copy.start()
            self.copies.append(copy)

    def finish(self, piece=None):
        copies = self.copies if piece is None else self.copies[8 * piece : 8 * piece + 8]
        for copy in copies:
            copy.wait()


ANY = pl.BlockSpec(memory_space=pl.ANY)
IN_VMEM = pl.BlockSpec(memory_space=pltpu.VMEM)


class Moves:
    def __init__(self, loads, stores):
        self.loads, self.stores = loads, stores
        for _, copy in loads:
            copy.start()
        self.begun = []

    def ready(self, *refs):
        rest = []
        for ref, copy in self.loads:
            if not refs or any(ref is wanted for wanted in refs):
                copy.wait()
            else:
                rest.append((ref, copy))
        self.loads = rest

    def store(self, *refs):
        rest = []
        for ref, copy in self.stores:
            if not refs or any(ref is wanted for wanted in refs):
                copy.start()
                self.begun.append(copy)
            else:
                rest.append((ref, copy))
        self.stores = rest

    def finish(self):
        self.ready()
        self.store()
        for copy in self.begun:
            copy.wait()


def call(kernel, name, outs, out_specs, in_specs, scratch, ident, micros):
    def run(*args):
        loaded = [i for i, spec in enumerate(in_specs) if spec is IN_VMEM]
        stored = [i for i, spec in enumerate(out_specs) if spec is IN_VMEM]
        buffers = [pltpu.VMEM(args[i].shape, args[i].dtype) for i in loaded]
        buffers += [pltpu.VMEM(outs[i].shape, outs[i].dtype) for i in stored]

        def wrapped(*refs):
            ends = len(in_specs), len(in_specs) + len(outs)
            given, made, rest = list(refs[: ends[0]]), list(refs[ends[0] : ends[1]]), refs[ends[1] :]
            sems, rest = rest[len(buffers)], (rest[: len(buffers)], rest[len(buffers) + 1 :])
            loads, stores = [], []
            for k, i in enumerate(loaded):
                copy = pltpu.make_async_copy(given[i], rest[0][k], sems.at[k])
                loads.append((rest[0][k], copy))
                given[i] = rest[0][k]
            for k, i in enumerate(stored, len(loaded)):
                copy = pltpu.make_async_copy(rest[0][k], made[i], sems.at[k])
                stores.append((rest[0][k], copy))
                made[i] = rest[0][k]
            moves = Moves(loads, stores)
            kernel(moves, *given, *made, *rest[1])
            moves.finish()

        return pl.pallas_call(
            wrapped,
            out_shape=outs,
            in_specs=[ANY] * len(in_specs),
            out_specs=(ANY,) * len(outs),
            scratch_shapes=buffers + [pltpu.SemaphoreType.DMA((len(buffers),))] + scratch,
            name=name,
            cost_estimate=pl.CostEstimate(
                flops=micros * 10**9, bytes_accessed=micros * 10**6, transcendentals=0
            ),
            compiler_params=pltpu.CompilerParams(
                collective_id=ident, has_side_effects=True, vmem_limit_bytes=VMEM_LIMIT
            ),
        )(*args)

    return run


def shape(*dims, dtype=BF):
    return jax.ShapeDtypeStruct(dims, dtype)


def gather_scratch():
    return [
        pltpu.SemaphoreType.DMA,
        pltpu.SemaphoreType.DMA((9,)),
        pltpu.SemaphoreType.DMA((9,)),
    ]


def shard_others():
    z, shards = lax.axis_index("shard"), lax.axis_size("shard")
    return [lax.rem(z + i, shards) for i in range(1, shards)]


def spread(source_of, target_ref, send, recv, others, spot):
    z = lax.axis_index("shard")
    copies = []
    for index, other in enumerate(others):
        copy = remote_copy(
            source_of(other), target_ref.at[z], send.at[index], recv.at[index],
            device(other, *spot),
        )
        copy.start()
        copies.append(copy)
    return copies


def first_kernel(
    moves, frames_ref, gain_ref, bias_ref, cot_ref, text_ref, w_text_ref,
    rows_out, cot_out, text_all, text_out,
    normed_ref, part_ref, came_ref, some_ref, some_flat, text_plane, sends, recvs, *scratch,
):
    z = lax.axis_index("shard")
    spot = place()[1:]
    others = shard_others()
    enter(neighbours() + [device(other, *spot) for other in others])
    moves.ready()
    few = some_ref.shape[1]
    some = pl.ds(pl.multiple_of(slot(*spot) * few, few), few)
    texts = spread(
        lambda other: text_ref.at[other, some], some_ref, sends.at[0], recvs.at[0], others, spot
    )
    some_ref[z] = text_ref[z, some]

    def norm(part, carry):
        normed, _ = normalise(frames_ref[part].astype(F32))
        normed_ref[part] = (normed * gain_ref[0:1] + bias_ref[0:1]).astype(BF)
        return carry

    chunks(frames_ref.shape[0], norm)
    rows, grads = Gather(normed_ref, rows_out, *scratch[:3]), Gather(cot_ref, cot_out, *scratch[3:6])
    rows.start()
    for copy in texts:
        copy.wait_recv()
    shards, _, depth = some_ref.shape
    some_flat[...] = some_ref[...].reshape(shards * few, depth)
    meet = Gather(some_flat, text_plane, *scratch[6:])
    meet.start()
    meet.rest()

    def share(index, carry):
        rows_here = pl.ds(pl.multiple_of(index * few, few), few)
        text_all[index] = text_plane[:, rows_here].reshape(8 * few, depth)
        part_ref[index] = nn(text_all[index], w_text_ref[...]).astype(BF)
        return carry

    lax.fori_loop(0, text_all.shape[0], share, 0)
    parts = spread(lambda other: part_ref.at[other], came_ref, sends.at[1], recvs.at[1], others, spot)
    came_ref[z] = part_ref[z]
    rows.relay_y()
    rows.relay_x()
    grads.start()
    rows.relay_far()
    rows.finish()
    grads.rest()
    for copy in parts:
        copy.wait_recv()
    total = came_ref[0].astype(F32)
    for index in range(1, came_ref.shape[0]):
        total += came_ref[index].astype(F32)
    text_out[...] = total.astype(BF)
    for copy in texts + parts:
        copy.wait_send()


def first_step(frames, gain, bias, cotangent, text, w_text, ident):
    rows, width = frames.shape
    shards, texts, depth = text.shape
    return call(
        first_kernel,
        "first_step",
        (
            shape(8, rows, width),
            shape(8, rows, width),
            shape(shards, texts, depth),
            shape(texts, w_text.shape[1]),
        ),
        (ANY, ANY, IN_VMEM, IN_VMEM),
        [IN_VMEM, IN_VMEM, IN_VMEM, ANY, IN_VMEM, IN_VMEM],
        [
            pltpu.VMEM((rows, width), BF),
            pltpu.VMEM((shards, texts, w_text.shape[1]), BF),
            pltpu.VMEM((shards, texts, w_text.shape[1]), BF),
            pltpu.VMEM((shards, texts // 8, depth), BF),
            pltpu.VMEM((shards * texts // 8, depth), BF),
            pltpu.VMEM((8, shards * texts // 8, depth), BF),
            pltpu.SemaphoreType.DMA((2, shards - 1)),
            pltpu.SemaphoreType.DMA((2, shards - 1)),
        ]
        + gather_scratch() * 3,
        ident,
        60,
    )(frames, gain, bias, cotangent, text, w_text)


def two(ref, block):
    return ref[pl.ds(block, 2)].reshape(2 * ref.shape[1], ref.shape[2])


def put(ref, block, values):
    ref[pl.ds(block, 2)] = values.astype(BF).reshape(2, ref.shape[1], ref.shape[2])


def feed_kernel(
    moves, own_ref, grad_ref, w_ref,
    normed_out, branch_out, up_out, down_out,
    rows_ref, grads_ref, hidden_ref, slope_ref, part_a, part_b,
    load_sem, store_sem, g_local, g_send, g_recv, *scratch,
):
    enter(neighbours())
    gather = Gather(own_ref, rows_ref, g_local, g_send, g_recv)
    gather.start()
    hidden = hidden_ref.shape[2]
    up_ref, down_ref = w_ref.at[:, pl.ds(0, hidden)], w_ref.at[:, pl.ds(hidden, hidden)]
    blocks, _, width = rows_ref.shape
    loads = []
    for block in range(blocks):
        load = pltpu.make_async_copy(grad_ref.at[block], grads_ref.at[block], load_sem.at[block])
        load.start()
        loads.append(load)
    for load in loads:
        load.wait()

    def early(index, carry):
        put(slope_ref, 2 * index, nn(two(grads_ref, 2 * index), down_ref[...]))
        return carry

    moves.ready()
    lax.fori_loop(0, blocks // 2, early, 0)

    def middle(block):
        before = nn(two(rows_ref, block), up_ref[...])
        share = 0.5 + 0.5 * lax.erf(before * (0.5**0.5))
        put(hidden_ref, block, before * share)
        slope = share + before * (jnp.exp(-0.5 * before * before) * (2.0 * jnp.pi) ** (-0.5))
        slope = (two(slope_ref, block).astype(F32) * slope).astype(BF)
        put(slope_ref, block, slope)
        put(part_a, block, nt(slope, up_ref[...]))

    first = Scatter(part_a, *scratch)
    x, y, c = gather.spot

    def pair(cx, cy):
        middle(slot(cx, cy, 0))

    gather.own.wait()
    gather.arrived(2, slot(x, y, 1 - c), 0, gather.rows)
    pair(x, y)
    first.pass_core(3)
    gather.relay_y()
    gather.relay_x()
    gather.arrived(6, slot(1 - x, y, 1 - c), 0, gather.rows)
    pair(1 - x, y)
    first.pass_core(1)
    gather.arrived(5, slot(x, 1 - y, 1 - c), 0, gather.rows)
    pair(x, 1 - y)
    first.pass_core(2)
    gather.relay_far()
    first.near()
    gather.arrived(7, slot(1 - x, 1 - y, 1 - c), 0, gather.rows // 2)
    gather.arrived(8, slot(1 - x, 1 - y, 1 - c), gather.rows // 2, gather.rows // 2)
    pair(1 - x, 1 - y)
    first.pass_core(0)
    first.far()
    for copy in gather.sends:
        copy.wait_send()

    def store(block):
        return pltpu.make_async_copy(part_b.at[block], branch_out.at[block], store_sem.at[block])

    def branch(index, carry):
        put(part_b, 2 * index, nt(two(hidden_ref, 2 * index), down_ref[...]))
        store(2 * index).start()
        store(2 * index + 1).start()
        return carry

    lax.fori_loop(0, blocks // 2, branch, 0)
    tile = 256

    def weight(left_ref, right_ref, out_ref):
        right = right_ref[...].reshape(-1, right_ref.shape[2])

        def one(index, carry):
            lanes = pl.ds(pl.multiple_of(index * tile, tile), tile)
            left = left_ref[:, :, lanes].reshape(-1, tile)
            out_ref[lanes, :] = tn(left, right).astype(BF)
            return carry

        lax.fori_loop(0, width // tile, one, 0)

    weight(grads_ref, hidden_ref, down_out)
    moves.store(down_out)
    first.second()
    weight(rows_ref, slope_ref, up_out)
    moves.store(up_out)
    normed_out[...] = first.total()
    first.finish()
    for block in range(blocks):
        store(block).wait()


def feed_forward(own, grads, weights, ident):
    rows, width = own.shape
    hidden = weights.shape[1] // 2
    outs = (
        shape(rows, width, dtype=F32),
        shape(8, rows, width),
        shape(width, hidden),
        shape(width, hidden),
    )
    scratch = [
        pltpu.VMEM((8, rows, width), BF),
        pltpu.VMEM((8, rows, width), BF),
        pltpu.VMEM((8, rows, hidden), BF),
        pltpu.VMEM((8, rows, hidden), BF),
        pltpu.VMEM((8, rows, width), BF),
        pltpu.VMEM((8, rows, width), BF),
        pltpu.SemaphoreType.DMA((8,)),
        pltpu.SemaphoreType.DMA((8,)),
    ]
    return call(
        feed_kernel,
        "feed_forward",
        outs,
        (IN_VMEM, ANY, IN_VMEM, IN_VMEM),
        [ANY, ANY, IN_VMEM],
        scratch + gather_scratch() + Scatter.scratch(rows, width),
        ident,
        70,
    )(own, grads, weights)


SIDE = 256


def nt(left, right):
    return lax.dot_general(left, right, (((1,), (1,)), ((), ())), preferred_element_type=F32)


def nn(left, right):
    return lax.dot_general(left, right, (((1,), (0,)), ((), ())), preferred_element_type=F32)


def tn(left, right):
    return lax.dot_general(left, right, (((0,), (0,)), ((), ())), preferred_element_type=F32)


def turn(values):
    return jnp.transpose(values.astype(F32))


def side_by_side(ref):
    return jnp.concatenate([ref[block] for block in range(ref.shape[0])], axis=1)


def all_rows(ref):
    return ref[...].reshape(-1, ref.shape[2])


def split_columns(values, ref):
    columns = ref.shape[2]
    for block in range(ref.shape[0]):
        ref[block] = values[:, block * columns : (block + 1) * columns].astype(BF)


def causal(scores):
    keys = lax.broadcasted_iota(jnp.int32, scores.shape, 0)
    queries = lax.broadcasted_iota(jnp.int32, scores.shape, 1)
    return jnp.where(keys <= queries, scores, MASKED)


def forward_kernel(
    moves, rows_ref, side_ref, text_in, frames_ref, gain_ref, bias_ref,
    qkv_ref, log_ref, mix_ref, mine_ref, one_ref, two_ref, query_ref, cross_ref, low_ref,
    text_ref, square_ref, plane_out,
    w_own, w_out, w_query, w_cross, sum_ref, two_low_ref, store_sem,
    ex_local, ex_send, ex_recv, *scratch,
):
    enter(plane_others())
    blocks, both, _ = rows_ref.shape
    rows = both // 2
    width = mix_ref.shape[2]
    features = two_low_ref.shape[1]
    heads = width // HEAD_DIM
    length = blocks * rows
    step = SIDE // rows
    weights = (w_out, w_query, w_cross)

    def turn_own(kind):
        w_own[kind] = turn(side_ref[:, (3 + kind) * width : (4 + kind) * width]).astype(BF)

    moves.ready(side_ref)
    turn_own(0)
    jobs = [Gather(w_own.at[k], weights[k], *scratch[3 * k : 3 * k + 3]) for k in range(3)]
    text_job = Gather(text_in, text_ref, *scratch[9:])
    text_job.start()
    jobs[0].start()
    stores = []

    def keep(kind):
        copy = pltpu.make_async_copy(weights[kind], plane_out.at[kind], store_sem.at[kind])
        copy.start()
        stores.append(copy)

    def project(index, carry):
        put(qkv_ref, 2 * index, nn(two(rows_ref, 2 * index), side_ref[:, : 3 * width]))
        return carry

    moves.ready()
    lax.fori_loop(0, blocks // 2, project, 0)
    moves.store(qkv_ref)
    turn_own(1)
    turn_own(2)
    exchange = Exchange(mix_ref, mine_ref, ex_local, ex_send, ex_recv)
    for clip in range(2):
        part = pl.ds(clip * rows, rows)
        for head in range(heads):
            lanes = [pl.ds(j * width + head * HEAD_DIM, HEAD_DIM) for j in range(3)]
            key = qkv_ref[:, part, lanes[1]].reshape(length, HEAD_DIM)
            value = turn(qkv_ref[:, part, lanes[2]].reshape(length, HEAD_DIM)).astype(BF)
            for index in range(length // SIDE):
                spots = pl.ds(index * step, step)
                query = qkv_ref[spots, part, lanes[0]].reshape(SIDE, HEAD_DIM)
                query = query * jnp.asarray(HEAD_DIM ** (-0.5), BF)
                start = index * SIDE
                last = causal(nt(key[start : start + SIDE], query))
                top = jnp.max(last, axis=0, keepdims=True)
                if index:
                    early = nt(key[:start], query)
                    top = jnp.maximum(top, jnp.max(early, axis=0, keepdims=True))
                last = jnp.exp(last - top)
                total = jnp.sum(last, axis=0, keepdims=True)
                mix = nn(value[:, start : start + SIDE], last.astype(BF))
                if index:
                    early = jnp.exp(early - top)
                    total += jnp.sum(early, axis=0, keepdims=True)
                    mix += nn(value[:, :start], early.astype(BF))
                mix = jnp.transpose(mix / total).astype(BF).reshape(step, rows, HEAD_DIM)
                mix_ref[spots, part, pl.ds(head * HEAD_DIM, HEAD_DIM)] = mix
                log_ref[pl.ds(clip * heads + head, 1), pl.ds(start, SIDE)] = top + jnp.log(total)
        exchange.start(clip, part)
        if clip == 0:
            jobs[0].relay_y()
            jobs[0].relay_x()
            text_job.relay_y()
            text_job.relay_x()
    jobs[1].start()
    moves.store(mix_ref, log_ref)
    jobs[0].relay_far()
    text_job.relay_far()
    jobs[0].finish()
    text_job.finish()
    keep(0)
    exchange.finish()
    moves.store(mine_ref, text_ref)

    def apply(values_ref, kind):
        sum_ref[...] = nn(side_by_side(values_ref), all_rows(weights[kind]))

    apply(mine_ref, 0)
    nothing = jnp.zeros((1, features), F32)

    def first(part, sums):
        branch = sum_ref[part]
        total = frames_ref[part].astype(F32) + branch
        one_ref[part] = total
        normed, _ = normalise(total)
        two_low_ref[part] = (normed * gain_ref[1:2] + bias_ref[1:2]).astype(BF)
        return sums + jnp.sum(branch * branch, axis=0, keepdims=True)

    square_one = chunks(both, first, nothing)
    moves.store(one_ref)
    jobs[1].relay_y()
    jobs[1].relay_x()
    jobs[2].start()
    jobs[1].relay_far()
    jobs[1].finish()
    keep(1)

    split_columns(nt(two_low_ref[...], all_rows(w_query)), query_ref)
    texts = text_ref.shape[1] // 2

    def cross(block, carry):
        for clip in range(2):
            part = pl.ds(clip * rows, rows)
            keys = pl.ds(clip * texts, texts)
            for head in range(heads):
                here = pl.ds(head * HEAD_DIM, HEAD_DIM)
                query = query_ref[block, part, here] * jnp.asarray(HEAD_DIM ** (-0.5), BF)
                there = pl.ds(width + head * HEAD_DIM, HEAD_DIM)
                scores = nt(text_ref[block, keys, here], query)
                probs = jnp.exp(scores - jnp.max(scores, axis=0, keepdims=True))
                probs = probs / jnp.sum(probs, axis=0, keepdims=True)
                mix = nn(turn(text_ref[block, keys, there]).astype(BF), probs.astype(BF))
                cross_ref[block, part, here] = jnp.transpose(mix).astype(BF)
        return carry

    lax.fori_loop(0, blocks // 2, cross, 0)
    jobs[2].relay_y()
    jobs[2].relay_x()
    lax.fori_loop(blocks // 2, blocks, cross, 0)
    moves.store(query_ref, cross_ref)
    jobs[2].relay_far()
    jobs[2].finish()
    keep(2)
    apply(cross_ref, 2)

    def second(part, sums):
        branch = sum_ref[part]
        total = one_ref[part] + branch
        two_ref[part] = total
        normed, _ = normalise(total)
        low_ref[part] = (normed * gain_ref[2:3] + bias_ref[2:3]).astype(BF)
        return sums + jnp.sum(branch * branch, axis=0, keepdims=True)

    square_two = chunks(both, second, nothing)
    square_ref[...] = jnp.zeros_like(square_ref)
    square_ref[0:1] = square_one
    square_ref[1:2] = square_two
    for copy in stores:
        copy.wait()


def attend_forward(rows, side, text, frames, gain, bias, ident):
    blocks, block, width = rows.shape
    columns = side.shape[1] // 6
    heads = columns // HEAD_DIM
    heads_shape = shape(blocks, block, columns)
    stream = shape(block, width, dtype=F32)
    return call(
        forward_kernel,
        "attend_forward",
        (
            shape(blocks, block, 3 * columns),
            shape(2 * heads, blocks * block // 2, dtype=F32),
            heads_shape,
            heads_shape,
            stream,
            stream,
            heads_shape,
            heads_shape,
            shape(block, width),
            shape(blocks, *text.shape),
            shape(8, width, dtype=F32),
            shape(3, blocks, columns, width),
        ),
        (IN_VMEM,) * 11 + (ANY,),
        [IN_VMEM] * 2 + [ANY] + [IN_VMEM] * 3,
        [pltpu.VMEM((3, columns, width), BF)]
        + [pltpu.VMEM((blocks, columns, width), BF)] * 3
        + [
            pltpu.VMEM((block, width), F32),
            pltpu.VMEM((block, width), BF),
            pltpu.SemaphoreType.DMA((4,)),
            pltpu.SemaphoreType.DMA((2,)),
            pltpu.SemaphoreType.DMA((2, 7)),
            pltpu.SemaphoreType.DMA((2, 7)),
        ]
        + gather_scratch() * 4,
        ident,
        80,
    )(rows, side, text, frames, gain, bias)


def beside(own_ref, copy, other_ref, out_ref):
    half = own_ref.shape[1]
    context = lax.axis_index("context")
    out_ref[:, pl.ds(pl.multiple_of(context * half, half), half)] = own_ref[...]
    copy.wait_recv()
    there = pl.ds(pl.multiple_of((1 - context) * half, half), half)
    out_ref[:, there] = other_ref[...]


def backward_kernel(
    moves, grad_ref, qkv_ref, mix_ref, log_ref, rows_ref, w_ref, side_ref, text_ref, down_ref, up_ref,
    part_out, w_out, side_out, text_out, down_out, up_came,
    up_send, up_recv, w_full, out_ref, part_ref, store_sem, down_pair, pair_sem, grad_all, query_turned, ex_local, ex_send, ex_recv, *scratch,
):
    z = lax.axis_index("shard")
    spot = place()[1:]
    others = shard_others()
    enter(plane_others() + [device(other, *spot) for other in others])
    exchange = Exchange(grad_ref, grad_all, ex_local, ex_send, ex_recv)
    blocks, both, width = mix_ref.shape
    rows = both // 2
    heads = width // HEAD_DIM
    length = blocks * rows
    step = SIDE // rows
    for clip in range(2):
        exchange.start(clip, pl.ds(clip * rows, rows))
    some = pl.ds(up_came.shape[2], up_came.shape[2])
    up_moves = spread(
        lambda other: up_ref.at[other, :, some], up_came, up_send, up_recv, others, spot
    )
    up_own = pltpu.make_async_copy(up_ref.at[z, :, some], up_came.at[z], pair_sem.at[2])
    up_own.start()
    size = len(scratch) // 2
    text = LoadedScatter(text_ref, *scratch[size:])
    text.start()
    text.first()
    side = LoadedScatter(side_ref, *scratch[:size])
    side.start()
    side.first()
    moves.ready()
    for clip in range(2):
        exchange.finish(clip)
        part = pl.ds(clip * rows, rows)
        for head in range(heads):
            lanes = [pl.ds(j * width + head * HEAD_DIM, HEAD_DIM) for j in range(3)]
            query = qkv_ref[:, part, lanes[0]].reshape(length, HEAD_DIM)
            query = query * jnp.asarray(HEAD_DIM ** (-0.5), BF)
            key = qkv_ref[:, part, lanes[1]].reshape(length, HEAD_DIM)
            value = qkv_ref[:, part, lanes[2]].reshape(length, HEAD_DIM)
            key_turned = turn(key).astype(BF)
            here = pl.ds(head * HEAD_DIM, HEAD_DIM)
            grad = grad_all[:, part, here].reshape(length, HEAD_DIM)
            mixed = mix_ref[:, part, here].reshape(length, HEAD_DIM)
            inner = jnp.transpose(grad.astype(F32) * mixed.astype(F32))
            inner = jnp.sum(inner, axis=0, keepdims=True)
            logs = log_ref[pl.ds(clip * heads + head, 1), :]
            for index in range(length // SIDE):
                start = index * SIDE
                spots = pl.ds(index * step, step)
                k_part, v_part = key[start : start + SIDE], value[start : start + SIDE]
                scores = nt(k_part, query[start:])
                first = causal(scores[:, :SIDE])
                if start + SIDE < length:
                    scores = jnp.concatenate([first, scores[:, SIDE:]], axis=1)
                else:
                    scores = first
                weights = jnp.exp(scores - logs[:, start:])
                slopes = nt(v_part, grad[start:])
                slopes = (weights * (slopes - inner[:, start:])).astype(BF)
                grad_key = nn(slopes, query[start:]).astype(BF).reshape(step, rows, HEAD_DIM)
                grad_value = nn(weights.astype(BF), grad[start:]).astype(BF)
                out_ref[spots, part, lanes[1]] = grad_key
                out_ref[spots, part, lanes[2]] = grad_value.reshape(step, rows, HEAD_DIM)
                grad_query = nn(key_turned[:, start : start + SIDE], slopes)
                if index:
                    query_turned[:, start:] += grad_query
                else:
                    query_turned[...] = grad_query
            grad_query = jnp.transpose(query_turned[...]) * HEAD_DIM ** (-0.5)
            grad_query = grad_query.astype(BF).reshape(blocks, rows, HEAD_DIM)
            out_ref[:, part, lanes[0]] = grad_query
        if clip == 0:
            text.second()
            side.second()
            to_x = neighbours()[0]
            pair = remote_copy(down_ref, down_pair, pair_sem.at[0], pair_sem.at[1], to_x)
            pair.start()

    def store(block):
        return pltpu.make_async_copy(part_ref.at[block], part_out.at[block], store_sem.at[block])

    def project(index, carry):
        put(part_ref, 2 * index, nt(two(out_ref, 2 * index), w_ref[:, : 3 * width]))
        store(2 * index).start()
        store(2 * index + 1).start()
        return carry

    lax.fori_loop(0, blocks // 2, project, 0)
    tile = 256
    right = out_ref[...].reshape(blocks * both, 3 * width)

    def weight(index, carry):
        lanes = pl.ds(pl.multiple_of(index * tile, tile), tile)
        left = rows_ref[:, :, lanes].reshape(blocks * both, tile)
        w_full[:, lanes] = jnp.transpose(tn(left, right)).astype(BF)
        return carry

    lax.fori_loop(0, w_full.shape[1] // tile, weight, 0)
    into_slices(w_full[...], w_out, 0)
    moves.store(w_out)
    text_out[...] = text.total().astype(BF)
    into_slices(side.total().astype(BF), side_out, 0)
    text.finish()
    side.finish()
    beside(down_ref, pair, down_pair, down_out)
    pair.wait_send()
    up_own.wait()
    for copy in up_moves:
        copy.wait()
    for block in range(blocks):
        store(block).wait()


def attend_backward(grad_mix, qkv, mix, logs, rows, weights, side, text, down, up, ident):
    blocks, block, columns = mix.shape
    _, side_rows, width = side.shape
    text_shape = text.shape[1:]
    return call(
        backward_kernel,
        "attend_backward",
        (
            shape(blocks, block, width),
            shape(up.shape[0], 3 * columns, up.shape[1]),
            shape(up.shape[0], side_rows, up.shape[1]),
            shape(*text_shape),
            shape(down.shape[0], 2 * down.shape[1]),
            shape(*up.shape[:2], up.shape[2] // 2),
        ),
        (ANY, IN_VMEM, IN_VMEM, IN_VMEM, IN_VMEM, ANY),
        [ANY] + [IN_VMEM] * 5 + [ANY, ANY, IN_VMEM, ANY],
        [
            pltpu.SemaphoreType.DMA((up.shape[0] - 1,)),
            pltpu.SemaphoreType.DMA((up.shape[0] - 1,)),
            pltpu.VMEM((3 * columns, width), BF),
            pltpu.VMEM((blocks, block, 3 * columns), BF),
            pltpu.VMEM((blocks, block, width), BF),
            pltpu.SemaphoreType.DMA((8,)),
            pltpu.VMEM(down.shape, BF),
            pltpu.SemaphoreType.DMA((3,)),
            pltpu.VMEM((blocks, block, columns), BF),
            pltpu.VMEM((HEAD_DIM, blocks * block // 2), F32),
            pltpu.SemaphoreType.DMA((2,)),
            pltpu.SemaphoreType.DMA((2, 7)),
            pltpu.SemaphoreType.DMA((2, 7)),
        ]
        + LoadedScatter.scratch(side_rows, width)
        + LoadedScatter.scratch(*text_shape),
        ident,
        1,
    )(grad_mix, qkv, mix, logs, rows, weights, side, text, down, up)


CHUNK = 64


def chunks(rows, body, carry=None):
    def one(index, carry):
        return body(pl.ds(pl.multiple_of(index * CHUNK, CHUNK), CHUNK), carry)

    return lax.fori_loop(0, rows // CHUNK, one, 0 if carry is None else carry)


def normalise(inputs):
    average = jnp.mean(inputs, axis=-1, keepdims=True)
    centred = inputs - average
    rate = lax.rsqrt(jnp.mean(centred * centred, axis=-1, keepdims=True) + EPS)
    return centred * rate, rate


def norm_back(grads, inputs, gain):
    normed, rate = normalise(inputs)
    scaled = grads * gain
    inner = jnp.mean(scaled * normed, axis=-1, keepdims=True)
    result = rate * (scaled - jnp.mean(scaled, axis=-1, keepdims=True) - normed * inner)
    sums = (
        jnp.sum(grads * normed, axis=0, keepdims=True),
        jnp.sum(grads, axis=0, keepdims=True),
    )
    return result, sums


def into_slices(values, ref, start):
    shards, _, depth = ref.shape
    for index in range(shards):
        part = values[:, index * depth : (index + 1) * depth]
        ref[index, start : start + values.shape[0]] = part


def rows_back_kernel(
    moves, normed_ref, cot_ref, one_ref, two_ref, query_ref, mix_ref, text_ref, my_mix_ref,
    gain_ref, bias_ref, w_ref, branch_ref, up_ref,
    grad_ref, layer_ref, stats_ref, grad_mix_ref, out_ref, side_ref, text_out, up_came,
    w_cross, w_query, w_out, low_ref, two_low_ref, back_ref, grad_cm, grad_cq, w_sem,
    up_send, up_recv, *scratch,
):
    z = lax.axis_index("shard")
    spot = place()[1:]
    others = shard_others()
    enter(neighbours() + [device(other, *spot) for other in others])
    some = pl.ds(0, up_came.shape[2])
    up_moves = spread(
        lambda other: up_ref.at[other, :, some], up_came, up_send, up_recv, others, spot
    )
    up_own = pltpu.make_async_copy(up_ref.at[z, :, some], up_came.at[z], w_sem.at[3])
    up_own.start()
    cross_job = Scatter(w_cross, *scratch[:5])
    query_job = Scatter(w_query, *scratch[5:10])
    branch_job = LoadedScatter(branch_ref, *scratch[10:])
    branch_job.start()
    blocks, columns, width = w_out.shape
    rows = low_ref.shape[0]
    heads = columns // HEAD_DIM
    loads = []
    for index, buffer in ((2, w_cross), (1, w_query), (0, w_out)):
        load = pltpu.make_async_copy(
            w_ref.at[index], buffer, w_sem.at[index]
        )
        load.start()
        loads.append(load)
    nothing = (jnp.zeros((1, width), F32),) * 2

    def third(part, sums):
        back, more = norm_back(normed_ref[part], two_ref[part], gain_ref[2:3])
        total = cot_ref[part].astype(F32) + back
        grad_ref[part] = total
        low_ref[part] = total.astype(BF)
        normed, _ = normalise(one_ref[part])
        two_low_ref[part] = (normed * gain_ref[1:2] + bias_ref[1:2]).astype(BF)
        return sums[0] + more[0], sums[1] + more[1]

    moves.ready()
    gain_three, shift_three = chunks(rows, third, nothing)
    branch_job.first()
    loads[0].wait()

    split_columns(nt(low_ref[...], all_rows(w_cross)), grad_cm)

    def cross_weight(block, carry):
        w_cross[block] = tn(mix_ref[block], low_ref[...]).astype(BF)
        return carry

    lax.fori_loop(0, blocks, cross_weight, 0)
    for index in range(4):
        cross_job.pass_core(index)
    half = rows // 2
    texts = text_ref.shape[1] // 2
    loads[1].wait()

    def cross(block, carry):
        for clip in range(2):
            part = pl.ds(clip * half, half)
            keys = pl.ds(clip * texts, texts)
            for head in range(heads):
                here = pl.ds(head * HEAD_DIM, HEAD_DIM)
                query = query_ref[block, part, here] * jnp.asarray(HEAD_DIM ** (-0.5), BF)
                there = pl.ds(columns + head * HEAD_DIM, HEAD_DIM)
                key, value = text_ref[block, keys, here], text_ref[block, keys, there]
                grad = grad_cm[block, part, here]
                scores = nt(key, query)
                weights = jnp.exp(scores - jnp.max(scores, axis=0, keepdims=True))
                weights = weights / jnp.sum(weights, axis=0, keepdims=True)
                slopes = nt(value, grad)
                inner = jnp.sum(weights * slopes, axis=0, keepdims=True)
                slopes = (weights * (slopes - inner)).astype(BF)
                grad_query = jnp.transpose(nn(turn(key).astype(BF), slopes))
                grad_cq[block, part, here] = (grad_query * HEAD_DIM ** (-0.5)).astype(BF)
                text_out[block, keys, here] = nn(slopes, query).astype(BF)
                text_out[block, keys, there] = nn(weights.astype(BF), grad).astype(BF)
        return carry

    def query_weight(block, carry):
        w_query[block] = tn(grad_cq[block], two_low_ref[...]).astype(BF)
        return carry

    branch_job.second()
    lax.fori_loop(0, blocks // 2, cross, 0)
    cross_job.far()
    cross_job.near()
    lax.fori_loop(blocks // 2, blocks, cross, 0)
    moves.store(text_out)
    back_ref[...] = nn(side_by_side(grad_cq), all_rows(w_query))
    lax.fori_loop(0, blocks, query_weight, 0)
    for index in range(4):
        query_job.pass_core(index)

    def second(part, sums):
        back, more = norm_back(back_ref[part], one_ref[part], gain_ref[1:2])
        total = grad_ref[part] + back
        grad_ref[part] = total
        low_ref[part] = total.astype(BF)
        return sums[0] + more[0], sums[1] + more[1]

    gain_two, shift_two = chunks(rows, second, nothing)
    moves.store(grad_ref)
    cross_job.second()
    query_job.far()
    query_job.near()
    loads[2].wait()

    split_columns(nt(low_ref[...], all_rows(w_out)), grad_mix_ref)

    def out_weight(block, carry):
        out_ref[block] = tn(my_mix_ref[block], low_ref[...]).astype(BF)
        return carry

    lax.fori_loop(0, blocks, out_weight, 0)
    moves.store(grad_mix_ref, out_ref)
    branch_job.wait()

    def last(part, sums):
        branch = branch_job.value(part)
        total = two_ref[part] + branch
        layer_ref[part] = total.astype(BF)
        return (
            sums[0] + jnp.sum(total * total, axis=0, keepdims=True),
            sums[1] + jnp.sum(branch * branch, axis=0, keepdims=True),
        )

    square_out, square_three = chunks(rows, last, nothing)
    rest = jnp.zeros((1, width), F32)
    for index, row in enumerate(
        (rest, gain_two, gain_three, rest, shift_two, shift_three, square_out, square_three)
    ):
        stats_ref[index : index + 1] = row
    moves.store(layer_ref, stats_ref)
    query_job.second()
    for kind, job in ((1, cross_job), (0, query_job)):
        into_slices(job.total().astype(BF), side_ref, kind * columns)
    branch_job.finish()
    cross_job.finish()
    query_job.finish()
    up_own.wait()
    for copy in up_moves:
        copy.wait()


def rows_back(
    normed, cot, one, two, query, mix, text, my_mix, gain, bias, weights, branch, up, ident
):
    rows, width = cot.shape
    blocks, _, columns = my_mix.shape
    return call(
        rows_back_kernel,
        "rows_back",
        (
            shape(rows, width, dtype=F32),
            shape(rows, width),
            shape(8, width, dtype=F32),
            shape(*my_mix.shape),
            shape(blocks, columns, width),
            shape(up.shape[0], 2 * columns, up.shape[1]),
            shape(*text.shape),
            shape(*up.shape[:2], up.shape[2] // 2),
        ),
        (IN_VMEM,) * 7 + (ANY,),
        [IN_VMEM] * 10 + [ANY, ANY, ANY],
        [pltpu.VMEM((blocks, columns, width), BF)] * 3
        + [
            pltpu.VMEM((rows, width), BF),
            pltpu.VMEM((rows, width), BF),
            pltpu.VMEM((rows, width), F32),
            pltpu.VMEM(my_mix.shape, BF),
            pltpu.VMEM(my_mix.shape, BF),
            pltpu.SemaphoreType.DMA((4,)),
            pltpu.SemaphoreType.DMA((up.shape[0] - 1,)),
            pltpu.SemaphoreType.DMA((up.shape[0] - 1,)),
        ]
        + Scatter.scratch(columns, width) * 2
        + LoadedScatter.scratch(rows, width),
        ident,
        60,
    )(normed, cot, one, two, query, mix, text, my_mix, gain, bias, weights, branch, up)


def last_kernel(
    moves, part_ref, frames_ref, gain_ref, grad_ref, stats_ref, squares_ref, qkv_ref, up_a, up_b, cross_ref, out_w_ref,
    text_ref, text_in, w_text_ref,
    out_ref, total_ref, text_out, qkv_out, up_out, cross_out, self_out, key_out,
    mine, came, all_ref, st_send, st_recv, z_send, z_recv,
    qkv_came, out_came, text_came, text_part, text_mine, text_all,
    qkv_pair, up_mine, up_pair, cross_pair, out_pair, key_pair, x_send, x_recv, q_send, q_recv,
    *scratch,
):
    z = lax.axis_index("shard")
    shards = lax.axis_size("shard")
    others = shard_others()
    spot = place()[1:]
    context = spot[0]
    enter(neighbours() + [device(other, *spot) for other in others])

    def collect(copies, source_ref, came_ref, rows=slice(None)):
        for copy in copies:
            copy.wait_recv()
        total = source_ref[z, rows].astype(F32)
        for other in others:
            total += came_ref[other, rows].astype(F32)
        return total.astype(BF)

    def over(index, source_of, target_ref):
        return spread(source_of, target_ref, z_send.at[index], z_recv.at[index], others, spot)

    size = len(scratch) - 5
    text = Scatter(text_part, *scratch[size:])
    job = SteepScatter(part_ref, *scratch[:size])
    job.start()
    moves.ready()
    text_moves = over(0, lambda other: text_ref, text_came)
    out_moves = over(2, lambda other: out_w_ref.at[other], out_came)
    third = qkv_ref.shape[1] // 3
    thirds = [pl.ds(index * third, third) for index in range(3)]
    qkv_moves = []

    def send_third(index):
        for step, other in enumerate(others):
            copy = remote_copy(
                qkv_ref.at[other, thirds[index]], qkv_came.at[z, thirds[index]],
                q_send.at[index, step], q_recv.at[index, step], device(other, *spot),
            )
            copy.start()
            qkv_moves.append(copy)

    def sum_third(index):
        moves = qkv_moves[index * len(others) : (index + 1) * len(others)]
        rows = thirds[index]
        qkv_pair[0, rows] = collect(moves, qkv_ref, qkv_came, rows)
        pairs.append(swap(4 + index, qkv_pair.at[0, rows], qkv_pair.at[1, rows]))

    send_third(0)
    to_x = neighbours()[0]

    def swap(index, source, target_ref):
        copy = remote_copy(source, target_ref, x_send.at[index], x_recv.at[index], to_x)
        copy.start()
        return copy

    cross_move = swap(1, cross_ref, cross_pair)
    job.first()
    for start, up_ref in ((0, up_a), (up_a.shape[2], up_b)):
        total = up_ref[0].astype(F32)
        for index in range(1, shards):
            total += up_ref[index].astype(F32)
        up_mine[:, start : start + up_ref.shape[2]] = total.astype(BF)
    pairs = [swap(0, up_mine, up_pair), cross_move]
    text_came[z] = text_ref[...]
    for copy in text_moves:
        copy.wait_recv()
    texts = text_ref.shape[0] // 2
    own = texts // 8

    def text_back(index, carry):
        grads = nt(text_came[index], w_text_ref[...])
        rows = pl.ds(pl.multiple_of(index * 2 * own, 2 * own), 2 * own)
        for block in range(8):
            pair = [grads[k * texts + block * own : k * texts + block * own + own] for k in range(2)]
            text_part[block, rows] = jnp.concatenate(pair, axis=0).astype(BF)
        return carry

    lax.fori_loop(0, shards, text_back, 0)
    for index in range(4):
        text.pass_core(index)
    key_grad = tn(text_in[0], text_came[0])
    for index in range(1, shards):
        key_grad += tn(text_in[index], text_came[index])
    key_pair[0] = key_grad.astype(BF)
    pairs.append(swap(2, key_pair.at[0], key_pair.at[1]))
    job.second()
    text.far()
    text.near()
    out_pair[0] = collect(out_moves, out_w_ref, out_came)
    pairs.append(swap(3, out_pair.at[0], out_pair.at[1]))
    send_third(1)
    text.second()
    job.wait()
    sum_third(0)
    send_third(2)

    def norm(part, sums):
        back, more = norm_back(job.value(part), frames_ref[part].astype(F32), gain_ref[0:1])
        out_ref[part] = grad_ref[part] + back
        return sums[0] + more[0], sums[1] + more[1]

    nothing = (jnp.zeros((1, frames_ref.shape[1]), F32),) * 2
    gain_one, shift_one = chunks(frames_ref.shape[0], norm, nothing)
    moves.store(out_ref)
    mine[0] = stats_ref[...]
    lanes = lax.broadcasted_iota(jnp.int32, gain_one.shape, 1)
    squares = (stats_ref[6:7], squares_ref[0:1], squares_ref[1:2], stats_ref[7:8])
    row = jnp.zeros_like(gain_one)
    for index, square in enumerate(squares):
        row += jnp.where(lanes == index, jnp.sum(square, axis=1, keepdims=True), 0.0)
    mine[0, 6:7] = row
    mine[0, 0:1] = gain_one
    mine[0, 3:4] = shift_one
    sends = []
    for index, target in enumerate(neighbours()):
        copy = remote_copy(
            mine.at[index], came.at[index], st_send.at[index], st_recv.at[index], target
        )
        copy.start()
        sends.append(copy)
        if index == 0:
            text.wait()
            for block in range(shards):
                rows = slice(block * 2 * own, (block + 1) * 2 * own)
                text_mine[block] = text.value(rows).astype(BF)
            text_moves += over(3, lambda other: text_mine.at[other], text_all)
            text_all[z] = text_mine[z]
        copy.wait_recv()
        mine[index + 1] = mine[index] + came[index]
    stat_moves = over(4, lambda other: mine.at[3], all_ref)
    all_ref[z] = mine[3]

    sum_third(1)
    sum_third(2)
    for copy in text_moves[shards - 1 :] + stat_moves:
        copy.wait_recv()
    text_out[...] = text_all[...].astype(F32)
    total = all_ref[0]
    for index in range(1, shards):
        total += all_ref[index]
    total_ref[...] = total
    beside(up_mine, pairs[0], up_pair, up_out)

    def ordered(first, second):
        return jnp.where(context == 0, first, second), jnp.where(context == 0, second, first)

    pairs[1].wait_recv()
    lead, trail = ordered(cross_ref[...], cross_pair[...])
    width = lead.shape[0] // 2
    for index in range(2):
        part = slice(index * width, (index + 1) * width)
        cross_out[index, :width] = lead[part]
        cross_out[index, width:] = trail[part]
    pairs[2].wait_recv()
    lead, trail = ordered(key_pair[0], key_pair[1])
    for index in range(2):
        lanes = slice(index * width, (index + 1) * width)
        key_out[index, :, :width] = lead[:, lanes]
        key_out[index, :, width:] = trail[:, lanes]
    pairs[3].wait_recv()
    lead, trail = ordered(out_pair[0], out_pair[1])
    self_out[:width] = lead
    self_out[width:] = trail
    for copy in pairs[4:]:
        copy.wait_recv()
    lead, trail = ordered(qkv_pair[0], qkv_pair[1])
    for index in range(3):
        part = slice(index * width, (index + 1) * width)
        qkv_out[index, :width] = lead[part]
        qkv_out[index, width:] = trail[part]
    for copy in sends + text_moves + qkv_moves + out_moves + stat_moves + pairs:
        copy.wait_send()
    text.finish()
    job.finish()


def last_step(
    part, frames, gain, grad, stats, squares, qkv, up_a, up_b, cross, out, text, text_in, w_text,
    ident,
):
    _, rows, width = part.shape
    shards, texts, depth = text_in.shape
    half = 2 * up_a.shape[2]
    columns = out.shape[1]
    own = texts // 8
    return call(
        last_kernel,
        "last_step",
        (
            shape(rows, width, dtype=F32),
            shape(8, width, dtype=F32),
            shape(shards, own, depth, dtype=F32),
            shape(3, 2 * columns, depth),
            shape(depth, 2 * half),
            shape(2, 2 * columns, depth),
            shape(2 * columns, depth),
            shape(2, depth, 2 * columns),
        ),
        (IN_VMEM,) * 8,
        [ANY] + [IN_VMEM] * 13,
        [
            pltpu.VMEM((4, 8, width), F32),
            pltpu.VMEM((3, 8, width), F32),
            pltpu.VMEM((shards, 8, width), F32),
            pltpu.SemaphoreType.DMA((3,)),
            pltpu.SemaphoreType.DMA((3,)),
            pltpu.SemaphoreType.DMA((5, shards - 1)),
            pltpu.SemaphoreType.DMA((5, shards - 1)),
            pltpu.VMEM((shards, 3 * columns, depth), BF),
            pltpu.VMEM((shards, columns, depth), BF),
            pltpu.VMEM((shards, texts, 2 * columns), BF),
            pltpu.VMEM((8, shards * own, depth), BF),
            pltpu.VMEM((shards, own, depth), BF),
            pltpu.VMEM((shards, own, depth), BF),
            pltpu.VMEM((2, 3 * columns, depth), BF),
            pltpu.VMEM((depth, half), BF),
            pltpu.VMEM((depth, half), BF),
            pltpu.VMEM((2 * columns, depth), BF),
            pltpu.VMEM((2, columns, depth), BF),
            pltpu.VMEM((2, depth, 2 * columns), BF),
            pltpu.SemaphoreType.DMA((7,)),
            pltpu.SemaphoreType.DMA((7,)),
            pltpu.SemaphoreType.DMA((3, shards - 1)),
            pltpu.SemaphoreType.DMA((3, shards - 1)),
        ]
        + LoadedScatter.scratch(rows, width)
        + Scatter.scratch(shards * own, depth),
        ident,
        65,
    )(part, frames, gain, grad, stats, squares, qkv, up_a, up_b, cross, out, text, text_in, w_text)


def dots(spec, *operands):
    return jnp.einsum(spec, *operands, preferred_element_type=F32)


def layer_norm(inputs, scaling, offset):
    average = jnp.mean(inputs, axis=-1, keepdims=True)
    centred = inputs - average
    variance = jnp.mean(centred * centred, axis=-1, keepdims=True)
    return centred * lax.rsqrt(variance + EPS) * scaling + offset


def on_device(
    frames,
    text_states,
    cotangent,
    norm_gain,
    norm_bias,
    self_qkv,
    self_out,
    cross_qkv,
    cross_out,
    mlp_up,
    mlp_down,
):
    clips, rows, width = frames.shape
    context = lax.axis_index("context")
    depth = self_qkv.shape[1]
    slices = width // depth
    columns = self_qkv.shape[2] // 2
    heads = columns // HEAD_DIM
    block = clips * rows
    texts = text_states.shape[1]

    def half(weight):
        size = weight.shape[-1] // 2
        return lax.dynamic_slice_in_dim(weight, context * size, size, weight.ndim - 1)

    def over_shard(weight, tiled=True):
        return lax.all_gather(weight, "shard", axis=0, tiled=tiled)

    cross_part = half(cross_qkv)
    qkv_part = half(self_qkv)
    early = [qkv_part[0], qkv_part[1], qkv_part[2], half(self_out), cross_part[0], half(cross_out)]
    w_early = over_shard(jnp.concatenate(early, axis=1))
    w_late = over_shard(jnp.concatenate([half(mlp_up), half(mlp_down)], axis=1))
    w_text = jnp.concatenate([cross_part[1], cross_part[2]], axis=1)
    text_slices = text_states.reshape(clips * texts, slices, depth).transpose(1, 0, 2)
    w_down = over_shard(half(mlp_down))

    all_one, all_grad, text_in, text_part = first_step(
        frames.reshape(block, width),
        norm_gain,
        norm_bias,
        cotangent.reshape(block, width),
        text_slices,
        w_text,
        0,
    )
    (
        qkv, self_log, mix, my_mix, stream_one, stream_two, cross_q, cross_mix, norm_three,
        text_all, squares, plane_w,
    ) = attend_forward(
        all_one,
        w_early,
        text_part,
        frames.reshape(block, width),
        norm_gain,
        norm_bias,
        1,
    )

    grad_normed, part_three, grad_up, grad_down = feed_forward(
        norm_three, all_grad, w_late, 4
    )

    def to_shard(part):
        return lax.psum_scatter(part.astype(BF), "shard", scatter_dimension=0, tiled=True)

    grad_down = to_shard(grad_down)
    grad_up = grad_up.reshape(slices, depth, -1)
    grad_one, layer_out, stats, grad_mix, part_out, side, text_grads, up_a = rows_back(
        grad_normed,
        cotangent.reshape(block, width),
        stream_one,
        stream_two,
        cross_q,
        cross_mix,
        text_all,
        my_mix,
        norm_gain,
        norm_bias,
        plane_w,
        part_three,
        grad_up,
        3,
    )

    grad_cross = to_shard(side)[0]
    part_norm, grad_w_qkv, grad_out, text_grads, grad_down, up_b = attend_backward(
        grad_mix, qkv, mix, self_log, all_one, w_early, part_out, text_grads, grad_down, grad_up, 8
    )
    (
        grad_frames, totals, grad_text, grad_w_qkv, grad_up, grad_cross, grad_out, grad_keys,
    ) = last_step(
        part_norm,
        frames.reshape(block, width),
        norm_gain,
        grad_one,
        stats,
        squares,
        grad_w_qkv,
        up_a,
        up_b,
        grad_cross,
        grad_out,
        text_grads,
        text_in,
        w_text,
        11,
    )
    grad_frames = grad_frames.reshape(clips, rows, width)
    grad_text = grad_text.transpose(1, 0, 2).reshape(clips, texts // 8, width)

    squares = totals[6, :4]
    start = lax.axis_index("shard") * depth
    grad_gain = lax.dynamic_slice_in_dim(totals[:3], start, depth, 1)
    grad_shift = lax.dynamic_slice_in_dim(totals[3:6], start, depth, 1)
    entries = float(clips * rows * width * lax.axis_size(("shard",) + PLANE))
    return (
        layer_out.reshape(clips, rows, width),
        grad_frames,
        grad_text,
        grad_gain,
        grad_shift,
        grad_w_qkv.transpose(0, 2, 1).astype(F32),
        grad_out.transpose(1, 0).astype(F32),
        jnp.concatenate([grad_cross[:1].transpose(0, 2, 1), grad_keys]).astype(F32),
        grad_cross[1].transpose(1, 0).astype(F32),
        grad_up.astype(F32),
        grad_down.astype(F32),
        jnp.sqrt(squares / entries),
    )


def solution(mesh):
    rows = P("shard", PLANE, None)
    stack = P(None, "shard", "tensor")
    flat = P("shard", "tensor")
    return jax.shard_map(
        on_device,
        mesh=mesh,
        in_specs=(rows, P("shard"), rows, P(), P(), stack, flat, stack, flat, flat, flat),
        out_specs=(
            (rows, rows, rows, P(None, "shard"), P(None, "shard"))
            + (stack, flat, stack, flat, flat, flat, P())
        ),
        check_vma=False,
    )
```

```python
from functools import partial

import jax
import jax.numpy as jnp
from jax import lax
from jax.experimental import pallas as pl
from jax.experimental.pallas import tpu as pltpu
from jax.sharding import PartitionSpec as P

HEAD_DIM = 64
EPS = 1e-05
MASKED = -1e30
MESH = pl.DeviceIdType.MESH
BF = jnp.bfloat16
F32 = jnp.float32
PLANE = ("context", "tensor")
VMEM_LIMIT = 60 * 2**20


def place():
    return (
        lax.axis_index("shard"),
        lax.axis_index("context"),
        lax.axis_index("tensor") // 2,
        lax.axis_index("tensor") % 2,
    )


def device(z, x, y, c):
    return (z, x, 2 * y + c)


def slot(x, y, c):
    return 4 * x + 2 * y + c


def neighbours():
    z, x, y, c = place()
    return [device(z, 1 - x, y, c), device(z, x, 1 - y, c), device(z, x, y, 1 - c)]


def plane_spots():
    z, x, y, c = place()
    steps = [(a, b, d) for a in range(2) for b in range(2) for d in range(2) if a + b + d]
    return [((x + a) % 2, (y + b) % 2, (c + d) % 2) for a, b, d in steps]


def plane_others():
    z = lax.axis_index("shard")
    return [device(z, *spot) for spot in plane_spots()]


def enter(targets):
    barrier = pltpu.get_barrier_semaphore()
    for target in targets:
        pl.semaphore_signal(barrier, inc=1, device_id=target, device_id_type=MESH)
    pl.semaphore_wait(barrier, len(targets))


def remote_copy(source, target_ref, send, recv, target):
    return pltpu.make_async_remote_copy(
        src_ref=source,
        dst_ref=target_ref,
        send_sem=send,
        recv_sem=recv,
        device_id=target,
        device_id_type=MESH,
    )


class Gather:
    semaphores = 9

    def __init__(self, in_ref, out_ref, local_sem, send, recv):
        z, x, y, c = place()
        self.in_ref, self.out_ref, self.local_sem = in_ref, out_ref, local_sem
        self.send, self.recv = send, recv
        self.spot = (x, y, c)
        self.to_x, self.to_y, self.to_c = neighbours()
        self.rows = in_ref.shape[0]
        self.sends = []

    def go(self, index, owner, start, size, target, source=None):
        there = self.out_ref.at[owner, pl.ds(start, size)]
        copy = remote_copy(
            there if source is None else source,
            there,
            self.send.at[index],
            self.recv.at[index],
            target,
        )
        copy.start()
        self.sends.append(copy)

    def arrived(self, index, owner, start, size):
        there = self.out_ref.at[owner, pl.ds(start, size)]
        remote_copy(
            there, there, self.send.at[index], self.recv.at[index], self.to_x
        ).wait_recv()

    def start(self):
        me = slot(*self.spot)
        self.own = pltpu.make_async_copy(self.in_ref, self.out_ref.at[me], self.local_sem)
        self.own.start()
        for index, target in enumerate((self.to_x, self.to_y, self.to_c)):
            self.go(index, me, 0, self.rows, target, self.in_ref)

    def relay_y(self):
        x, y, c = self.spot
        owner = slot(x, 1 - y, c)
        self.arrived(1, owner, 0, self.rows)
        self.go(3, owner, 0, self.rows // 2, self.to_x)
        self.go(5, owner, 0, self.rows, self.to_c)

    def relay_x(self):
        x, y, c = self.spot
        half = self.rows // 2
        owner = slot(1 - x, y, c)
        self.arrived(0, owner, 0, self.rows)
        self.go(4, owner, half, half, self.to_y)
        self.go(6, owner, 0, self.rows, self.to_c)

    def relay_far(self):
        x, y, c = self.spot
        half = self.rows // 2
        owner = slot(1 - x, 1 - y, c)
        self.arrived(3, owner, 0, half)
        self.go(7, owner, 0, half, self.to_c)
        self.arrived(4, owner, half, half)
        self.go(8, owner, half, half, self.to_c)

    def finish(self):
        x, y, c = self.spot
        half = self.rows // 2
        self.arrived(2, slot(x, y, 1 - c), 0, self.rows)
        self.arrived(5, slot(x, 1 - y, 1 - c), 0, self.rows)
        self.arrived(6, slot(1 - x, y, 1 - c), 0, self.rows)
        self.arrived(7, slot(1 - x, 1 - y, 1 - c), 0, half)
        self.arrived(8, slot(1 - x, 1 - y, 1 - c), half, half)
        self.own.wait()
        for copy in self.sends:
            copy.wait_send()

    def rest(self):
        self.relay_y()
        self.relay_x()
        self.relay_far()
        self.finish()


class Scatter:
    @staticmethod
    def scratch(rows, columns):
        return [
            pltpu.VMEM((4, rows, columns), BF),
            pltpu.VMEM((2, rows // 2, columns), BF),
            pltpu.VMEM((2, rows, columns), BF),
            pltpu.SemaphoreType.DMA((10,)),
            pltpu.SemaphoreType.DMA((10,)),
        ]

    def __init__(self, part_ref, core, relay, final, send, recv):
        self.part_ref, self.core, self.relay, self.final = part_ref, core, relay, final
        self.send, self.recv = send, recv
        self.to_x, self.to_y, self.to_c = neighbours()
        z, x, y, c = place()
        chips = ((1 - x, 1 - y), (1 - x, y), (x, 1 - y), (x, y))
        self.mine = [slot(*chip, c) for chip in chips]
        self.theirs = [slot(*chip, 1 - c) for chip in chips]
        rows = part_ref.shape[1]
        self.low, self.high = pl.ds(0, rows // 2), pl.ds(rows // 2, rows // 2)
        self.sends = []

    def forward(self, index, source, target_ref, target):
        copy = remote_copy(
            source, target_ref, self.send.at[index], self.recv.at[index], target
        )
        copy.start()
        self.sends.append(copy)

    def arrived(self, index, ref):
        remote_copy(ref, ref, self.send.at[index], self.recv.at[index], self.to_c).wait_recv()

    def pass_core(self, index):
        source = self.part_ref.at[self.theirs[index]]
        self.forward(index, source, self.core.at[index], self.to_c)

    def add(self, index, part, more=None):
        mine = self.mine[index]
        total = self.part_ref[mine, part].astype(F32) + self.core[index, part].astype(F32)
        if more is not None:
            total += more.astype(F32)
        self.part_ref[mine, part] = total.astype(BF)
        return self.part_ref.at[mine, part]

    def far(self):
        self.arrived(0, self.core.at[0])
        self.forward(4, self.add(0, self.low), self.relay.at[0], self.to_x)
        self.forward(5, self.add(0, self.high), self.relay.at[1], self.to_y)

    def near(self):
        self.arrived(1, self.core.at[1])
        self.forward(6, self.add(1, self.low), self.final.at[0, self.low], self.to_x)
        self.arrived(2, self.core.at[2])
        self.forward(7, self.add(2, self.high), self.final.at[1, self.high], self.to_y)

    def second(self):
        low, high, final, relay = self.low, self.high, self.final, self.relay
        self.arrived(5, relay.at[1])
        self.forward(8, self.add(1, high, relay[1]), final.at[0, high], self.to_x)
        self.arrived(4, relay.at[0])
        self.forward(9, self.add(2, low, relay[0]), final.at[1, low], self.to_y)

    def wait(self):
        self.arrived(3, self.core.at[3])
        self.arrived(6, self.final.at[0, self.low])
        self.arrived(7, self.final.at[1, self.high])
        self.arrived(8, self.final.at[0, self.high])
        self.arrived(9, self.final.at[1, self.low])

    def value(self, part=slice(None)):
        total = self.part_ref[self.mine[3], part].astype(F32) + self.core[3, part].astype(F32)
        return total + self.final[0, part].astype(F32) + self.final[1, part].astype(F32)

    def total(self):
        self.wait()
        return self.value()

    def finish(self):
        for copy in self.sends:
            copy.wait_send()


class LoadedScatter(Scatter):
    steep = False

    @staticmethod
    def scratch(rows, columns):
        return [
            pltpu.VMEM((4, rows, columns), BF),
            pltpu.SemaphoreType.DMA((4,)),
        ] + Scatter.scratch(rows, columns)

    def __init__(self, in_ref, part_ref, local_sem, *scratch):
        super().__init__(part_ref, *scratch)
        self.in_ref, self.local_sem = in_ref, local_sem

    def bring(self, index):
        source = self.in_ref.at[self.theirs[index]]
        self.forward(index, source, self.core.at[index], self.to_c)
        load = pltpu.make_async_copy(
            self.in_ref.at[self.blocks[index]], self.part_ref.at[index], self.local_sem.at[index]
        )
        load.start()
        self.loads.append(load)

    def start(self):
        self.loads = []
        self.blocks, self.mine = self.mine, (0, 1, 2, 3)
        for index in range(4):
            self.bring(index)

    def first(self):
        for load in self.loads:
            load.wait()
        if not self.steep:
            self.far()
            self.near()
            return
        self.arrived(0, self.core.at[0])
        self.forward(4, self.add(0, self.low), self.relay.at[0], self.to_y)
        self.forward(5, self.add(0, self.high), self.relay.at[1], self.to_y)
        self.arrived(2, self.core.at[2])
        self.forward(7, self.add(2, self.high), self.final.at[1, self.high], self.to_y)
        self.forward(9, self.add(2, self.low), self.final.at[1, self.low], self.to_y)

    def second(self):
        if not self.steep:
            super().second()
            return
        final, relay = self.final, self.relay
        self.arrived(1, self.core.at[1])
        self.arrived(4, relay.at[0])
        self.forward(6, self.add(1, self.low, relay[0]), final.at[0, self.low], self.to_x)
        self.arrived(5, relay.at[1])
        self.forward(8, self.add(1, self.high, relay[1]), final.at[0, self.high], self.to_x)


class SteepScatter(LoadedScatter):
    steep = True


class Exchange:
    def __init__(self, in_ref, out_ref, local_sem, send, recv):
        self.in_ref, self.out_ref, self.local_sem = in_ref, out_ref, local_sem
        self.send, self.recv = send, recv
        z, x, y, c = place()
        self.me = slot(x, y, c)
        self.copies = []

    def start(self, piece, part):
        z = lax.axis_index("shard")
        own = pltpu.make_async_copy(
            self.in_ref.at[self.me, part], self.out_ref.at[self.me, part], self.local_sem.at[piece]
        )
        own.start()
        self.copies.append(own)
        for index, spot in enumerate(plane_spots()):
            copy = remote_copy(
                self.in_ref.at[slot(*spot), part],
                self.out_ref.at[self.me, part],
                self.send.at[piece, index],
                self.recv.at[piece, index],
                device(z, *spot),
            )
            copy.start()
            self.copies.append(copy)

    def finish(self, piece=None):
        copies = self.copies if piece is None else self.copies[8 * piece : 8 * piece + 8]
        for copy in copies:
            copy.wait()


ANY = pl.BlockSpec(memory_space=pl.ANY)
IN_VMEM = pl.BlockSpec(memory_space=pltpu.VMEM)


class Moves:
    def __init__(self, loads, stores):
        self.loads, self.stores = loads, stores
        for _, copy in loads:
            copy.start()
        self.begun = []

    def ready(self, *refs):
        rest = []
        for ref, copy in self.loads:
            if not refs or any(ref is wanted for wanted in refs):
                copy.wait()
            else:
                rest.append((ref, copy))
        self.loads = rest

    def store(self, *refs):
        rest = []
        for ref, copy in self.stores:
            if not refs or any(ref is wanted for wanted in refs):
                copy.start()
                self.begun.append(copy)
            else:
                rest.append((ref, copy))
        self.stores = rest

    def finish(self):
        self.ready()
        self.store()
        for copy in self.begun:
            copy.wait()


def call(kernel, name, outs, out_specs, in_specs, scratch, ident, micros):
    def run(*args):
        loaded = [i for i, spec in enumerate(in_specs) if spec is IN_VMEM]
        stored = [i for i, spec in enumerate(out_specs) if spec is IN_VMEM]
        buffers = [pltpu.VMEM(args[i].shape, args[i].dtype) for i in loaded]
        buffers += [pltpu.VMEM(outs[i].shape, outs[i].dtype) for i in stored]

        def wrapped(*refs):
            ends = len(in_specs), len(in_specs) + len(outs)
            given, made, rest = list(refs[: ends[0]]), list(refs[ends[0] : ends[1]]), refs[ends[1] :]
            sems, rest = rest[len(buffers)], (rest[: len(buffers)], rest[len(buffers) + 1 :])
            loads, stores = [], []
            for k, i in enumerate(loaded):
                copy = pltpu.make_async_copy(given[i], rest[0][k], sems.at[k])
                loads.append((rest[0][k], copy))
                given[i] = rest[0][k]
            for k, i in enumerate(stored, len(loaded)):
                copy = pltpu.make_async_copy(rest[0][k], made[i], sems.at[k])
                stores.append((rest[0][k], copy))
                made[i] = rest[0][k]
            moves = Moves(loads, stores)
            kernel(moves, *given, *made, *rest[1])
            moves.finish()

        return pl.pallas_call(
            wrapped,
            out_shape=outs,
            in_specs=[ANY] * len(in_specs),
            out_specs=(ANY,) * len(outs),
            scratch_shapes=buffers + [pltpu.SemaphoreType.DMA((len(buffers),))] + scratch,
            name=name,
            cost_estimate=pl.CostEstimate(
                flops=micros * 10**9, bytes_accessed=micros * 10**6, transcendentals=0
            ),
            compiler_params=pltpu.CompilerParams(
                collective_id=ident, has_side_effects=True, vmem_limit_bytes=VMEM_LIMIT
            ),
        )(*args)

    return run


def shape(*dims, dtype=BF):
    return jax.ShapeDtypeStruct(dims, dtype)


def gather_scratch():
    return [
        pltpu.SemaphoreType.DMA,
        pltpu.SemaphoreType.DMA((9,)),
        pltpu.SemaphoreType.DMA((9,)),
    ]


def shard_others():
    z, shards = lax.axis_index("shard"), lax.axis_size("shard")
    return [lax.rem(z + i, shards) for i in range(1, shards)]


def spread(source_of, target_ref, send, recv, others, spot):
    z = lax.axis_index("shard")
    copies = []
    for index, other in enumerate(others):
        copy = remote_copy(
            source_of(other), target_ref.at[z], send.at[index], recv.at[index],
            device(other, *spot),
        )
        copy.start()
        copies.append(copy)
    return copies


def first_kernel(
    moves, frames_ref, gain_ref, bias_ref, cot_ref, text_ref, w_text_ref,
    rows_out, cot_out, text_all, text_out,
    normed_ref, part_ref, came_ref, some_ref, some_flat, text_plane, sends, recvs, *scratch,
):
    z = lax.axis_index("shard")
    spot = place()[1:]
    others = shard_others()
    enter(neighbours() + [device(other, *spot) for other in others])
    moves.ready()
    few = some_ref.shape[1]
    some = pl.ds(pl.multiple_of(slot(*spot) * few, few), few)
    texts = spread(
        lambda other: text_ref.at[other, some], some_ref, sends.at[0], recvs.at[0], others, spot
    )
    some_ref[z] = text_ref[z, some]

    def norm(part, carry):
        normed, _ = normalise(frames_ref[part].astype(F32))
        normed_ref[part] = (normed * gain_ref[0:1] + bias_ref[0:1]).astype(BF)
        return carry

    chunks(frames_ref.shape[0], norm)
    rows, grads = Gather(normed_ref, rows_out, *scratch[:3]), Gather(cot_ref, cot_out, *scratch[3:6])
    rows.start()
    for copy in texts:
        copy.wait_recv()
    shards, _, depth = some_ref.shape
    some_flat[...] = some_ref[...].reshape(shards * few, depth)
    meet = Gather(some_flat, text_plane, *scratch[6:])
    meet.start()
    meet.rest()

    def share(index, carry):
        rows_here = pl.ds(pl.multiple_of(index * few, few), few)
        text_all[index] = text_plane[:, rows_here].reshape(8 * few, depth)
        part_ref[index] = nn(text_all[index], w_text_ref[...]).astype(BF)
        return carry

    lax.fori_loop(0, text_all.shape[0], share, 0)
    parts = spread(lambda other: part_ref.at[other], came_ref, sends.at[1], recvs.at[1], others, spot)
    came_ref[z] = part_ref[z]
    rows.relay_y()
    rows.relay_x()
    grads.start()
    rows.relay_far()
    rows.finish()
    grads.rest()
    for copy in parts:
        copy.wait_recv()
    total = came_ref[0].astype(F32)
    for index in range(1, came_ref.shape[0]):
        total += came_ref[index].astype(F32)
    text_out[...] = total.astype(BF)
    for copy in texts + parts:
        copy.wait_send()


def first_step(frames, gain, bias, cotangent, text, w_text, ident):
    rows, width = frames.shape
    shards, texts, depth = text.shape
    return call(
        first_kernel,
        "first_step",
        (
            shape(8, rows, width),
            shape(8, rows, width),
            shape(shards, texts, depth),
            shape(texts, w_text.shape[1]),
        ),
        (ANY, ANY, IN_VMEM, IN_VMEM),
        [IN_VMEM, IN_VMEM, IN_VMEM, ANY, IN_VMEM, IN_VMEM],
        [
            pltpu.VMEM((rows, width), BF),
            pltpu.VMEM((shards, texts, w_text.shape[1]), BF),
            pltpu.VMEM((shards, texts, w_text.shape[1]), BF),
            pltpu.VMEM((shards, texts // 8, depth), BF),
            pltpu.VMEM((shards * texts // 8, depth), BF),
            pltpu.VMEM((8, shards * texts // 8, depth), BF),
            pltpu.SemaphoreType.DMA((2, shards - 1)),
            pltpu.SemaphoreType.DMA((2, shards - 1)),
        ]
        + gather_scratch() * 3,
        ident,
        60,
    )(frames, gain, bias, cotangent, text, w_text)


def two(ref, block):
    return ref[pl.ds(block, 2)].reshape(2 * ref.shape[1], ref.shape[2])


def put(ref, block, values):
    ref[pl.ds(block, 2)] = values.astype(BF).reshape(2, ref.shape[1], ref.shape[2])


def feed_kernel(
    moves, own_ref, grad_ref, w_ref,
    normed_out, branch_out, up_out, down_out,
    rows_ref, grads_ref, hidden_ref, slope_ref, part_a, part_b,
    load_sem, store_sem, g_local, g_send, g_recv, *scratch,
):
    enter(neighbours())
    gather = Gather(own_ref, rows_ref, g_local, g_send, g_recv)
    gather.start()
    hidden = hidden_ref.shape[2]
    up_ref, down_ref = w_ref.at[:, pl.ds(0, hidden)], w_ref.at[:, pl.ds(hidden, hidden)]
    blocks, _, width = rows_ref.shape
    loads = []
    for block in range(blocks):
        load = pltpu.make_async_copy(grad_ref.at[block], grads_ref.at[block], load_sem.at[block])
        load.start()
        loads.append(load)
    for load in loads:
        load.wait()

    def early(index, carry):
        put(slope_ref, 2 * index, nn(two(grads_ref, 2 * index), down_ref[...]))
        return carry

    moves.ready()
    lax.fori_loop(0, blocks // 2, early, 0)

    def middle(block):
        before = nn(two(rows_ref, block), up_ref[...])
        share = 0.5 + 0.5 * lax.erf(before * (0.5**0.5))
        put(hidden_ref, block, before * share)
        slope = share + before * (jnp.exp(-0.5 * before * before) * (2.0 * jnp.pi) ** (-0.5))
        slope = (two(slope_ref, block).astype(F32) * slope).astype(BF)
        put(slope_ref, block, slope)
        put(part_a, block, nt(slope, up_ref[...]))

    first = Scatter(part_a, *scratch)
    x, y, c = gather.spot

    def pair(cx, cy):
        middle(slot(cx, cy, 0))

    gather.own.wait()
    gather.arrived(2, slot(x, y, 1 - c), 0, gather.rows)
    pair(x, y)
    first.pass_core(3)
    gather.relay_y()
    gather.relay_x()
    gather.arrived(6, slot(1 - x, y, 1 - c), 0, gather.rows)
    pair(1 - x, y)
    first.pass_core(1)
    gather.arrived(5, slot(x, 1 - y, 1 - c), 0, gather.rows)
    pair(x, 1 - y)
    first.pass_core(2)
    gather.relay_far()
    first.near()
    gather.arrived(7, slot(1 - x, 1 - y, 1 - c), 0, gather.rows // 2)
    gather.arrived(8, slot(1 - x, 1 - y, 1 - c), gather.rows // 2, gather.rows // 2)
    pair(1 - x, 1 - y)
    first.pass_core(0)
    first.far()
    for copy in gather.sends:
        copy.wait_send()

    def store(block):
        return pltpu.make_async_copy(part_b.at[block], branch_out.at[block], store_sem.at[block])

    def branch(index, carry):
        put(part_b, 2 * index, nt(two(hidden_ref, 2 * index), down_ref[...]))
        store(2 * index).start()
        store(2 * index + 1).start()
        return carry

    lax.fori_loop(0, blocks // 2, branch, 0)
    tile = 256

    def weight(left_ref, right_ref, out_ref):
        right = right_ref[...].reshape(-1, right_ref.shape[2])

        def one(index, carry):
            lanes = pl.ds(pl.multiple_of(index * tile, tile), tile)
            left = left_ref[:, :, lanes].reshape(-1, tile)
            out_ref[lanes, :] = tn(left, right).astype(BF)
            return carry

        lax.fori_loop(0, width // tile, one, 0)

    weight(grads_ref, hidden_ref, down_out)
    moves.store(down_out)
    first.second()
    weight(rows_ref, slope_ref, up_out)
    moves.store(up_out)
    normed_out[...] = first.total()
    first.finish()
    for block in range(blocks):
        store(block).wait()


def feed_forward(own, grads, weights, ident):
    rows, width = own.shape
    hidden = weights.shape[1] // 2
    outs = (
        shape(rows, width, dtype=F32),
        shape(8, rows, width),
        shape(width, hidden),
        shape(width, hidden),
    )
    scratch = [
        pltpu.VMEM((8, rows, width), BF),
        pltpu.VMEM((8, rows, width), BF),
        pltpu.VMEM((8, rows, hidden), BF),
        pltpu.VMEM((8, rows, hidden), BF),
        pltpu.VMEM((8, rows, width), BF),
        pltpu.VMEM((8, rows, width), BF),
        pltpu.SemaphoreType.DMA((8,)),
        pltpu.SemaphoreType.DMA((8,)),
    ]
    return call(
        feed_kernel,
        "feed_forward",
        outs,
        (IN_VMEM, ANY, IN_VMEM, IN_VMEM),
        [ANY, ANY, IN_VMEM],
        scratch + gather_scratch() + Scatter.scratch(rows, width),
        ident,
        70,
    )(own, grads, weights)


SIDE = 256


def nt(left, right):
    return lax.dot_general(left, right, (((1,), (1,)), ((), ())), preferred_element_type=F32)


def nn(left, right):
    return lax.dot_general(left, right, (((1,), (0,)), ((), ())), preferred_element_type=F32)


def tn(left, right):
    return lax.dot_general(left, right, (((0,), (0,)), ((), ())), preferred_element_type=F32)


def turn(values):
    return jnp.transpose(values.astype(F32))


def side_by_side(ref):
    return jnp.concatenate([ref[block] for block in range(ref.shape[0])], axis=1)


def all_rows(ref):
    return ref[...].reshape(-1, ref.shape[2])


def split_columns(values, ref):
    columns = ref.shape[2]
    for block in range(ref.shape[0]):
        ref[block] = values[:, block * columns : (block + 1) * columns].astype(BF)


def causal(scores):
    keys = lax.broadcasted_iota(jnp.int32, scores.shape, 0)
    queries = lax.broadcasted_iota(jnp.int32, scores.shape, 1)
    return jnp.where(keys <= queries, scores, MASKED)


def forward_kernel(
    moves, rows_ref, side_ref, text_in, frames_ref, gain_ref, bias_ref,
    qkv_ref, log_ref, mix_ref, mine_ref, one_ref, two_ref, query_ref, cross_ref, low_ref,
    text_ref, square_ref, plane_out,
    w_own, w_out, w_query, w_cross, sum_ref, two_low_ref, store_sem,
    ex_local, ex_send, ex_recv, *scratch,
):
    enter(plane_others())
    blocks, both, _ = rows_ref.shape
    rows = both // 2
    width = mix_ref.shape[2]
    features = two_low_ref.shape[1]
    heads = width // HEAD_DIM
    length = blocks * rows
    step = SIDE // rows
    weights = (w_out, w_query, w_cross)

    def turn_own(kind):
        w_own[kind] = turn(side_ref[:, (3 + kind) * width : (4 + kind) * width]).astype(BF)

    moves.ready(side_ref)
    turn_own(0)
    jobs = [Gather(w_own.at[k], weights[k], *scratch[3 * k : 3 * k + 3]) for k in range(3)]
    text_job = Gather(text_in, text_ref, *scratch[9:])
    text_job.start()
    jobs[0].start()
    stores = []

    def keep(kind):
        copy = pltpu.make_async_copy(weights[kind], plane_out.at[kind], store_sem.at[kind])
        copy.start()
        stores.append(copy)

    def project(index, carry):
        put(qkv_ref, 2 * index, nn(two(rows_ref, 2 * index), side_ref[:, : 3 * width]))
        return carry

    moves.ready()
    lax.fori_loop(0, blocks // 2, project, 0)
    moves.store(qkv_ref)
    turn_own(1)
    turn_own(2)
    exchange = Exchange(mix_ref, mine_ref, ex_local, ex_send, ex_recv)
    for clip in range(2):
        part = pl.ds(clip * rows, rows)
        for head in range(heads):
            lanes = [pl.ds(j * width + head * HEAD_DIM, HEAD_DIM) for j in range(3)]
            key = qkv_ref[:, part, lanes[1]].reshape(length, HEAD_DIM)
            value = turn(qkv_ref[:, part, lanes[2]].reshape(length, HEAD_DIM)).astype(BF)
            for index in range(length // SIDE):
                spots = pl.ds(index * step, step)
                query = qkv_ref[spots, part, lanes[0]].reshape(SIDE, HEAD_DIM)
                query = query * jnp.asarray(HEAD_DIM ** (-0.5), BF)
                start = index * SIDE
                last = causal(nt(key[start : start + SIDE], query))
                top = jnp.max(last, axis=0, keepdims=True)
                if index:
                    early = nt(key[:start], query)
                    top = jnp.maximum(top, jnp.max(early, axis=0, keepdims=True))
                last = jnp.exp(last - top)
                total = jnp.sum(last, axis=0, keepdims=True)
                mix = nn(value[:, start : start + SIDE], last.astype(BF))
                if index:
                    early = jnp.exp(early - top)
                    total += jnp.sum(early, axis=0, keepdims=True)
                    mix += nn(value[:, :start], early.astype(BF))
                mix = jnp.transpose(mix / total).astype(BF).reshape(step, rows, HEAD_DIM)
                mix_ref[spots, part, pl.ds(head * HEAD_DIM, HEAD_DIM)] = mix
                log_ref[pl.ds(clip * heads + head, 1), pl.ds(start, SIDE)] = top + jnp.log(total)
        exchange.start(clip, part)
        if clip == 0:
            jobs[0].relay_y()
            jobs[0].relay_x()
            text_job.relay_y()
            text_job.relay_x()
    jobs[1].start()
    moves.store(mix_ref, log_ref)
    jobs[0].relay_far()
    text_job.relay_far()
    jobs[0].finish()
    text_job.finish()
    keep(0)
    exchange.finish()
    moves.store(mine_ref, text_ref)

    def apply(values_ref, kind):
        sum_ref[...] = nn(side_by_side(values_ref), all_rows(weights[kind]))

    apply(mine_ref, 0)
    nothing = jnp.zeros((1, features), F32)

    def first(part, sums):
        branch = sum_ref[part]
        total = frames_ref[part].astype(F32) + branch
        one_ref[part] = total
        normed, _ = normalise(total)
        two_low_ref[part] = (normed * gain_ref[1:2] + bias_ref[1:2]).astype(BF)
        return sums + jnp.sum(branch * branch, axis=0, keepdims=True)

    square_one = chunks(both, first, nothing)
    moves.store(one_ref)
    jobs[1].relay_y()
    jobs[1].relay_x()
    jobs[2].start()
    jobs[1].relay_far()
    jobs[1].finish()
    keep(1)

    split_columns(nt(two_low_ref[...], all_rows(w_query)), query_ref)
    texts = text_ref.shape[1] // 2

    def cross(block, carry):
        for clip in range(2):
            part = pl.ds(clip * rows, rows)
            keys = pl.ds(clip * texts, texts)
            for head in range(heads):
                here = pl.ds(head * HEAD_DIM, HEAD_DIM)
                query = query_ref[block, part, here] * jnp.asarray(HEAD_DIM ** (-0.5), BF)
                there = pl.ds(width + head * HEAD_DIM, HEAD_DIM)
                scores = nt(text_ref[block, keys, here], query)
                probs = jnp.exp(scores - jnp.max(scores, axis=0, keepdims=True))
                probs = probs / jnp.sum(probs, axis=0, keepdims=True)
                mix = nn(turn(text_ref[block, keys, there]).astype(BF), probs.astype(BF))
                cross_ref[block, part, here] = jnp.transpose(mix).astype(BF)
        return carry

    lax.fori_loop(0, blocks // 2, cross, 0)
    jobs[2].relay_y()
    jobs[2].relay_x()
    lax.fori_loop(blocks // 2, blocks, cross, 0)
    moves.store(query_ref, cross_ref)
    jobs[2].relay_far()
    jobs[2].finish()
    keep(2)
    apply(cross_ref, 2)

    def second(part, sums):
        branch = sum_ref[part]
        total = one_ref[part] + branch
        two_ref[part] = total
        normed, _ = normalise(total)
        low_ref[part] = (normed * gain_ref[2:3] + bias_ref[2:3]).astype(BF)
        return sums + jnp.sum(branch * branch, axis=0, keepdims=True)

    square_two = chunks(both, second, nothing)
    square_ref[...] = jnp.zeros_like(square_ref)
    square_ref[0:1] = square_one
    square_ref[1:2] = square_two
    for copy in stores:
        copy.wait()


def attend_forward(rows, side, text, frames, gain, bias, ident):
    blocks, block, width = rows.shape
    columns = side.shape[1] // 6
    heads = columns // HEAD_DIM
    heads_shape = shape(blocks, block, columns)
    stream = shape(block, width, dtype=F32)
    return call(
        forward_kernel,
        "attend_forward",
        (
            shape(blocks, block, 3 * columns),
            shape(2 * heads, blocks * block // 2, dtype=F32),
            heads_shape,
            heads_shape,
            stream,
            stream,
            heads_shape,
            heads_shape,
            shape(block, width),
            shape(blocks, *text.shape),
            shape(8, width, dtype=F32),
            shape(3, blocks, columns, width),
        ),
        (IN_VMEM,) * 11 + (ANY,),
        [IN_VMEM] * 2 + [ANY] + [IN_VMEM] * 3,
        [pltpu.VMEM((3, columns, width), BF)]
        + [pltpu.VMEM((blocks, columns, width), BF)] * 3
        + [
            pltpu.VMEM((block, width), F32),
            pltpu.VMEM((block, width), BF),
            pltpu.SemaphoreType.DMA((4,)),
            pltpu.SemaphoreType.DMA((2,)),
            pltpu.SemaphoreType.DMA((2, 7)),
            pltpu.SemaphoreType.DMA((2, 7)),
        ]
        + gather_scratch() * 4,
        ident,
        80,
    )(rows, side, text, frames, gain, bias)


def beside(own_ref, copy, other_ref, out_ref):
    half = own_ref.shape[1]
    context = lax.axis_index("context")
    out_ref[:, pl.ds(pl.multiple_of(context * half, half), half)] = own_ref[...]
    copy.wait_recv()
    there = pl.ds(pl.multiple_of((1 - context) * half, half), half)
    out_ref[:, there] = other_ref[...]


def backward_kernel(
    moves, grad_ref, qkv_ref, mix_ref, log_ref, rows_ref, w_ref, side_ref, text_ref, down_ref, up_ref,
    part_out, w_out, side_out, text_out, down_out, up_came,
    up_send, up_recv, t_send, t_recv, w_full, out_ref, part_ref, store_sem, down_pair, pair_sem, grad_all, query_turned, ex_local, ex_send, ex_recv, *scratch,
):
    z = lax.axis_index("shard")
    spot = place()[1:]
    others = shard_others()
    enter(plane_others() + [device(other, *spot) for other in others])
    exchange = Exchange(grad_ref, grad_all, ex_local, ex_send, ex_recv)
    blocks, both, width = mix_ref.shape
    rows = both // 2
    heads = width // HEAD_DIM
    length = blocks * rows
    step = SIDE // rows
    for clip in range(2):
        exchange.start(clip, pl.ds(clip * rows, rows))
    some = pl.ds(2 * up_came.shape[2], up_came.shape[2])
    up_moves = spread(
        lambda other: up_ref.at[other, :, some], up_came, up_send, up_recv, others, spot
    )
    up_own = pltpu.make_async_copy(up_ref.at[z, :, some], up_came.at[z], pair_sem.at[2])
    up_own.start()
    size = len(scratch) // 2
    text = LoadedScatter(text_ref, *scratch[size:])
    text.start()
    text.first()
    side = LoadedScatter(side_ref, *scratch[:size])
    side.start()
    side.first()
    moves.ready()
    for clip in range(2):
        exchange.finish(clip)
        part = pl.ds(clip * rows, rows)
        for head in range(heads):
            lanes = [pl.ds(j * width + head * HEAD_DIM, HEAD_DIM) for j in range(3)]
            query = qkv_ref[:, part, lanes[0]].reshape(length, HEAD_DIM)
            query = query * jnp.asarray(HEAD_DIM ** (-0.5), BF)
            key = qkv_ref[:, part, lanes[1]].reshape(length, HEAD_DIM)
            value = qkv_ref[:, part, lanes[2]].reshape(length, HEAD_DIM)
            key_turned = turn(key).astype(BF)
            here = pl.ds(head * HEAD_DIM, HEAD_DIM)
            grad = grad_all[:, part, here].reshape(length, HEAD_DIM)
            mixed = mix_ref[:, part, here].reshape(length, HEAD_DIM)
            inner = jnp.transpose(grad.astype(F32) * mixed.astype(F32))
            inner = jnp.sum(inner, axis=0, keepdims=True)
            logs = log_ref[pl.ds(clip * heads + head, 1), :]
            for index in range(length // SIDE):
                start = index * SIDE
                spots = pl.ds(index * step, step)
                k_part, v_part = key[start : start + SIDE], value[start : start + SIDE]
                scores = nt(k_part, query[start:])
                first = causal(scores[:, :SIDE])
                if start + SIDE < length:
                    scores = jnp.concatenate([first, scores[:, SIDE:]], axis=1)
                else:
                    scores = first
                weights = jnp.exp(scores - logs[:, start:])
                slopes = nt(v_part, grad[start:])
                slopes = (weights * (slopes - inner[:, start:])).astype(BF)
                grad_key = nn(slopes, query[start:]).astype(BF).reshape(step, rows, HEAD_DIM)
                grad_value = nn(weights.astype(BF), grad[start:]).astype(BF)
                out_ref[spots, part, lanes[1]] = grad_key
                out_ref[spots, part, lanes[2]] = grad_value.reshape(step, rows, HEAD_DIM)
                grad_query = nn(key_turned[:, start : start + SIDE], slopes)
                if index:
                    query_turned[:, start:] += grad_query
                else:
                    query_turned[...] = grad_query
            grad_query = jnp.transpose(query_turned[...]) * HEAD_DIM ** (-0.5)
            grad_query = grad_query.astype(BF).reshape(blocks, rows, HEAD_DIM)
            out_ref[:, part, lanes[0]] = grad_query
        if clip == 0:
            text.second()
            side.second()
            to_x = neighbours()[0]
            pair = remote_copy(down_ref, down_pair, pair_sem.at[0], pair_sem.at[1], to_x)
            pair.start()

    def store(block):
        return pltpu.make_async_copy(part_ref.at[block], part_out.at[block], store_sem.at[block])

    def project(index, carry):
        put(part_ref, 2 * index, nt(two(out_ref, 2 * index), w_ref[:, : 3 * width]))
        store(2 * index).start()
        store(2 * index + 1).start()
        return carry

    lax.fori_loop(0, blocks // 2, project, 0)
    text_out[z] = text.total().astype(BF)
    text_moves = spread(lambda other: text_out.at[z], text_out, t_send, t_recv, others, spot)
    tile = 256
    right = out_ref[...].reshape(blocks * both, 3 * width)

    def weight(index, carry):
        lanes = pl.ds(pl.multiple_of(index * tile, tile), tile)
        left = rows_ref[:, :, lanes].reshape(blocks * both, tile)
        w_full[:, lanes] = jnp.transpose(tn(left, right)).astype(BF)
        return carry

    lax.fori_loop(0, w_full.shape[1] // tile, weight, 0)
    into_slices(w_full[...], w_out, 0)
    moves.store(w_out)
    into_slices(side.total().astype(BF), side_out, 0)
    text.finish()
    side.finish()
    beside(down_ref, pair, down_pair, down_out)
    pair.wait_send()
    up_own.wait()
    for copy in up_moves + text_moves:
        copy.wait()
    for block in range(blocks):
        store(block).wait()


def attend_backward(grad_mix, qkv, mix, logs, rows, weights, side, text, down, up, ident):
    blocks, block, columns = mix.shape
    _, side_rows, width = side.shape
    text_shape = text.shape[1:]
    return call(
        backward_kernel,
        "attend_backward",
        (
            shape(blocks, block, width),
            shape(up.shape[0], 3 * columns, up.shape[1]),
            shape(up.shape[0], side_rows, up.shape[1]),
            shape(up.shape[0], *text_shape),
            shape(down.shape[0], 2 * down.shape[1]),
            shape(*up.shape[:2], up.shape[2] // 3),
        ),
        (ANY, IN_VMEM, IN_VMEM, IN_VMEM, IN_VMEM, ANY),
        [ANY] + [IN_VMEM] * 5 + [ANY, ANY, IN_VMEM, ANY],
        [
            pltpu.SemaphoreType.DMA((up.shape[0] - 1,)),
            pltpu.SemaphoreType.DMA((up.shape[0] - 1,)),
            pltpu.SemaphoreType.DMA((up.shape[0] - 1,)),
            pltpu.SemaphoreType.DMA((up.shape[0] - 1,)),
            pltpu.VMEM((3 * columns, width), BF),
            pltpu.VMEM((blocks, block, 3 * columns), BF),
            pltpu.VMEM((blocks, block, width), BF),
            pltpu.SemaphoreType.DMA((8,)),
            pltpu.VMEM(down.shape, BF),
            pltpu.SemaphoreType.DMA((3,)),
            pltpu.VMEM((blocks, block, columns), BF),
            pltpu.VMEM((HEAD_DIM, blocks * block // 2), F32),
            pltpu.SemaphoreType.DMA((2,)),
            pltpu.SemaphoreType.DMA((2, 7)),
            pltpu.SemaphoreType.DMA((2, 7)),
        ]
        + LoadedScatter.scratch(side_rows, width)
        + LoadedScatter.scratch(*text_shape),
        ident,
        1,
    )(grad_mix, qkv, mix, logs, rows, weights, side, text, down, up)


CHUNK = 64


def chunks(rows, body, carry=None):
    def one(index, carry):
        return body(pl.ds(pl.multiple_of(index * CHUNK, CHUNK), CHUNK), carry)

    return lax.fori_loop(0, rows // CHUNK, one, 0 if carry is None else carry)


def normalise(inputs):
    average = jnp.mean(inputs, axis=-1, keepdims=True)
    centred = inputs - average
    rate = lax.rsqrt(jnp.mean(centred * centred, axis=-1, keepdims=True) + EPS)
    return centred * rate, rate


def norm_back(grads, inputs, gain):
    normed, rate = normalise(inputs)
    scaled = grads * gain
    inner = jnp.mean(scaled * normed, axis=-1, keepdims=True)
    result = rate * (scaled - jnp.mean(scaled, axis=-1, keepdims=True) - normed * inner)
    sums = (
        jnp.sum(grads * normed, axis=0, keepdims=True),
        jnp.sum(grads, axis=0, keepdims=True),
    )
    return result, sums


def into_slices(values, ref, start):
    shards, _, depth = ref.shape
    for index in range(shards):
        part = values[:, index * depth : (index + 1) * depth]
        ref[index, start : start + values.shape[0]] = part


def rows_back_kernel(
    moves, normed_ref, cot_ref, one_ref, two_ref, query_ref, mix_ref, text_ref, my_mix_ref,
    gain_ref, bias_ref, w_ref, branch_ref, up_ref,
    grad_ref, layer_ref, stats_ref, grad_mix_ref, out_ref, side_ref, text_out, up_came,
    w_cross, w_query, w_out, low_ref, two_low_ref, back_ref, grad_cm, grad_cq, w_sem,
    up_send, up_recv, *scratch,
):
    z = lax.axis_index("shard")
    spot = place()[1:]
    others = shard_others()
    enter(neighbours() + [device(other, *spot) for other in others])
    some = pl.ds(0, up_came.shape[2])
    up_moves = spread(
        lambda other: up_ref.at[other, :, some], up_came, up_send, up_recv, others, spot
    )
    up_own = pltpu.make_async_copy(up_ref.at[z, :, some], up_came.at[z], w_sem.at[3])
    up_own.start()
    cross_job = Scatter(w_cross, *scratch[:5])
    query_job = Scatter(w_query, *scratch[5:10])
    branch_job = LoadedScatter(branch_ref, *scratch[10:])
    branch_job.start()
    blocks, columns, width = w_out.shape
    rows = low_ref.shape[0]
    heads = columns // HEAD_DIM
    loads = []
    for index, buffer in ((2, w_cross), (1, w_query), (0, w_out)):
        load = pltpu.make_async_copy(
            w_ref.at[index], buffer, w_sem.at[index]
        )
        load.start()
        loads.append(load)
    nothing = (jnp.zeros((1, width), F32),) * 2

    def third(part, sums):
        back, more = norm_back(normed_ref[part], two_ref[part], gain_ref[2:3])
        total = cot_ref[part].astype(F32) + back
        grad_ref[part] = total
        low_ref[part] = total.astype(BF)
        normed, _ = normalise(one_ref[part])
        two_low_ref[part] = (normed * gain_ref[1:2] + bias_ref[1:2]).astype(BF)
        return sums[0] + more[0], sums[1] + more[1]

    moves.ready()
    gain_three, shift_three = chunks(rows, third, nothing)
    branch_job.first()
    loads[0].wait()

    split_columns(nt(low_ref[...], all_rows(w_cross)), grad_cm)

    def cross_weight(block, carry):
        w_cross[block] = tn(mix_ref[block], low_ref[...]).astype(BF)
        return carry

    lax.fori_loop(0, blocks, cross_weight, 0)
    for index in range(4):
        cross_job.pass_core(index)
    half = rows // 2
    texts = text_ref.shape[1] // 2
    loads[1].wait()

    def cross(block, carry):
        for clip in range(2):
            part = pl.ds(clip * half, half)
            keys = pl.ds(clip * texts, texts)
            for head in range(heads):
                here = pl.ds(head * HEAD_DIM, HEAD_DIM)
                query = query_ref[block, part, here] * jnp.asarray(HEAD_DIM ** (-0.5), BF)
                there = pl.ds(columns + head * HEAD_DIM, HEAD_DIM)
                key, value = text_ref[block, keys, here], text_ref[block, keys, there]
                grad = grad_cm[block, part, here]
                scores = nt(key, query)
                weights = jnp.exp(scores - jnp.max(scores, axis=0, keepdims=True))
                weights = weights / jnp.sum(weights, axis=0, keepdims=True)
                slopes = nt(value, grad)
                inner = jnp.sum(weights * slopes, axis=0, keepdims=True)
                slopes = (weights * (slopes - inner)).astype(BF)
                grad_query = jnp.transpose(nn(turn(key).astype(BF), slopes))
                grad_cq[block, part, here] = (grad_query * HEAD_DIM ** (-0.5)).astype(BF)
                text_out[block, keys, here] = nn(slopes, query).astype(BF)
                text_out[block, keys, there] = nn(weights.astype(BF), grad).astype(BF)
        return carry

    def query_weight(block, carry):
        w_query[block] = tn(grad_cq[block], two_low_ref[...]).astype(BF)
        return carry

    branch_job.second()
    lax.fori_loop(0, blocks // 2, cross, 0)
    cross_job.far()
    cross_job.near()
    lax.fori_loop(blocks // 2, blocks, cross, 0)
    moves.store(text_out)
    back_ref[...] = nn(side_by_side(grad_cq), all_rows(w_query))
    lax.fori_loop(0, blocks, query_weight, 0)
    for index in range(4):
        query_job.pass_core(index)

    def second(part, sums):
        back, more = norm_back(back_ref[part], one_ref[part], gain_ref[1:2])
        total = grad_ref[part] + back
        grad_ref[part] = total
        low_ref[part] = total.astype(BF)
        return sums[0] + more[0], sums[1] + more[1]

    gain_two, shift_two = chunks(rows, second, nothing)
    moves.store(grad_ref)
    cross_job.second()
    query_job.far()
    query_job.near()
    loads[2].wait()

    split_columns(nt(low_ref[...], all_rows(w_out)), grad_mix_ref)

    def out_weight(block, carry):
        out_ref[block] = tn(my_mix_ref[block], low_ref[...]).astype(BF)
        return carry

    lax.fori_loop(0, blocks, out_weight, 0)
    moves.store(grad_mix_ref, out_ref)
    branch_job.wait()

    def last(part, sums):
        branch = branch_job.value(part)
        total = two_ref[part] + branch
        layer_ref[part] = total.astype(BF)
        return (
            sums[0] + jnp.sum(total * total, axis=0, keepdims=True),
            sums[1] + jnp.sum(branch * branch, axis=0, keepdims=True),
        )

    square_out, square_three = chunks(rows, last, nothing)
    rest = jnp.zeros((1, width), F32)
    for index, row in enumerate(
        (rest, gain_two, gain_three, rest, shift_two, shift_three, square_out, square_three)
    ):
        stats_ref[index : index + 1] = row
    moves.store(layer_ref, stats_ref)
    query_job.second()
    for kind, job in ((1, cross_job), (0, query_job)):
        into_slices(job.total().astype(BF), side_ref, kind * columns)
    branch_job.finish()
    cross_job.finish()
    query_job.finish()
    up_own.wait()
    for copy in up_moves:
        copy.wait()


def rows_back(
    normed, cot, one, two, query, mix, text, my_mix, gain, bias, weights, branch, up, ident
):
    rows, width = cot.shape
    blocks, _, columns = my_mix.shape
    return call(
        rows_back_kernel,
        "rows_back",
        (
            shape(rows, width, dtype=F32),
            shape(rows, width),
            shape(8, width, dtype=F32),
            shape(*my_mix.shape),
            shape(blocks, columns, width),
            shape(up.shape[0], 2 * columns, up.shape[1]),
            shape(*text.shape),
            shape(*up.shape[:2], 2 * up.shape[2] // 3),
        ),
        (IN_VMEM,) * 7 + (ANY,),
        [IN_VMEM] * 10 + [ANY, ANY, ANY],
        [pltpu.VMEM((blocks, columns, width), BF)] * 3
        + [
            pltpu.VMEM((rows, width), BF),
            pltpu.VMEM((rows, width), BF),
            pltpu.VMEM((rows, width), F32),
            pltpu.VMEM(my_mix.shape, BF),
            pltpu.VMEM(my_mix.shape, BF),
            pltpu.SemaphoreType.DMA((4,)),
            pltpu.SemaphoreType.DMA((up.shape[0] - 1,)),
            pltpu.SemaphoreType.DMA((up.shape[0] - 1,)),
        ]
        + Scatter.scratch(columns, width) * 2
        + LoadedScatter.scratch(rows, width),
        ident,
        60,
    )(normed, cot, one, two, query, mix, text, my_mix, gain, bias, weights, branch, up)


def last_kernel(
    moves, part_ref, frames_ref, gain_ref, grad_ref, stats_ref, squares_ref, qkv_ref, up_a, up_b, cross_ref, out_w_ref,
    text_came, text_in, w_text_ref,
    out_ref, total_ref, text_out, qkv_out, up_out, cross_out, self_out, key_out,
    mine, came, all_ref, st_send, st_recv, z_send, z_recv,
    qkv_came, out_came, text_part, text_mine, text_all,
    qkv_pair, up_mine, up_pair, cross_pair, out_pair, key_pair, x_send, x_recv, q_send, q_recv,
    *scratch,
):
    z = lax.axis_index("shard")
    shards = lax.axis_size("shard")
    others = shard_others()
    spot = place()[1:]
    context = spot[0]
    enter(neighbours() + [device(other, *spot) for other in others])

    def collect(copies, source_ref, came_ref, rows=slice(None)):
        for copy in copies:
            copy.wait_recv()
        total = source_ref[z, rows].astype(F32)
        for other in others:
            total += came_ref[other, rows].astype(F32)
        return total.astype(BF)

    def over(index, source_of, target_ref):
        return spread(source_of, target_ref, z_send.at[index], z_recv.at[index], others, spot)

    size = len(scratch) - 5
    text = Scatter(text_part, *scratch[size:])
    job = SteepScatter(part_ref, *scratch[:size])
    job.start()
    moves.ready(out_w_ref, qkv_ref, cross_ref)
    out_moves = over(2, lambda other: out_w_ref.at[other], out_came)
    third = qkv_ref.shape[1] // 3
    thirds = [pl.ds(index * third, third) for index in range(3)]
    qkv_moves = []

    def send_third(index):
        for step, other in enumerate(others):
            copy = remote_copy(
                qkv_ref.at[other, thirds[index]], qkv_came.at[z, thirds[index]],
                q_send.at[index, step], q_recv.at[index, step], device(other, *spot),
            )
            copy.start()
            qkv_moves.append(copy)

    def sum_third(index):
        moves = qkv_moves[index * len(others) : (index + 1) * len(others)]
        rows = thirds[index]
        qkv_pair[0, rows] = collect(moves, qkv_ref, qkv_came, rows)
        pairs.append(swap(4 + index, qkv_pair.at[0, rows], qkv_pair.at[1, rows]))

    send_third(0)
    to_x = neighbours()[0]

    def swap(index, source, target_ref):
        copy = remote_copy(source, target_ref, x_send.at[index], x_recv.at[index], to_x)
        copy.start()
        return copy

    cross_move = swap(1, cross_ref, cross_pair)
    job.first()
    moves.ready()
    for start, up_ref in ((0, up_a), (up_a.shape[2], up_b)):
        total = up_ref[0].astype(F32)
        for index in range(1, shards):
            total += up_ref[index].astype(F32)
        up_mine[:, start : start + up_ref.shape[2]] = total.astype(BF)
    pairs = [swap(0, up_mine, up_pair), cross_move]
    texts = text_came.shape[1] // 2
    own = texts // 8

    def text_back(index, carry):
        grads = nt(text_came[index], w_text_ref[...])
        rows = pl.ds(pl.multiple_of(index * 2 * own, 2 * own), 2 * own)
        for block in range(8):
            pair = [grads[k * texts + block * own : k * texts + block * own + own] for k in range(2)]
            text_part[block, rows] = jnp.concatenate(pair, axis=0).astype(BF)
        return carry

    lax.fori_loop(0, shards, text_back, 0)
    for index in range(4):
        text.pass_core(index)
    key_grad = tn(text_in[0], text_came[0])
    for index in range(1, shards):
        key_grad += tn(text_in[index], text_came[index])
    key_pair[0] = key_grad.astype(BF)
    pairs.append(swap(2, key_pair.at[0], key_pair.at[1]))
    job.second()
    text.far()
    text.near()
    out_pair[0] = collect(out_moves, out_w_ref, out_came)
    pairs.append(swap(3, out_pair.at[0], out_pair.at[1]))
    send_third(1)
    text.second()
    job.wait()
    sum_third(0)
    send_third(2)

    def norm(part, sums):
        back, more = norm_back(job.value(part), frames_ref[part].astype(F32), gain_ref[0:1])
        out_ref[part] = grad_ref[part] + back
        return sums[0] + more[0], sums[1] + more[1]

    nothing = (jnp.zeros((1, frames_ref.shape[1]), F32),) * 2
    gain_one, shift_one = chunks(frames_ref.shape[0], norm, nothing)
    moves.store(out_ref)
    mine[0] = stats_ref[...]
    lanes = lax.broadcasted_iota(jnp.int32, gain_one.shape, 1)
    squares = (stats_ref[6:7], squares_ref[0:1], squares_ref[1:2], stats_ref[7:8])
    row = jnp.zeros_like(gain_one)
    for index, square in enumerate(squares):
        row += jnp.where(lanes == index, jnp.sum(square, axis=1, keepdims=True), 0.0)
    mine[0, 6:7] = row
    mine[0, 0:1] = gain_one
    mine[0, 3:4] = shift_one
    sends = []
    for index, target in enumerate(neighbours()):
        copy = remote_copy(
            mine.at[index], came.at[index], st_send.at[index], st_recv.at[index], target
        )
        copy.start()
        sends.append(copy)
        if index == 0:
            text.wait()
            for block in range(shards):
                rows = slice(block * 2 * own, (block + 1) * 2 * own)
                text_mine[block] = text.value(rows).astype(BF)
            text_moves = over(3, lambda other: text_mine.at[other], text_all)
            text_all[z] = text_mine[z]
        copy.wait_recv()
        mine[index + 1] = mine[index] + came[index]
    stat_moves = over(4, lambda other: mine.at[3], all_ref)
    all_ref[z] = mine[3]

    sum_third(1)
    sum_third(2)
    for copy in text_moves + stat_moves:
        copy.wait_recv()
    text_out[...] = text_all[...].astype(F32)
    total = all_ref[0]
    for index in range(1, shards):
        total += all_ref[index]
    total_ref[...] = total
    beside(up_mine, pairs[0], up_pair, up_out)

    def ordered(first, second):
        return jnp.where(context == 0, first, second), jnp.where(context == 0, second, first)

    pairs[1].wait_recv()
    lead, trail = ordered(cross_ref[...], cross_pair[...])
    width = lead.shape[0] // 2
    for index in range(2):
        part = slice(index * width, (index + 1) * width)
        cross_out[index, :width] = lead[part]
        cross_out[index, width:] = trail[part]
    pairs[2].wait_recv()
    lead, trail = ordered(key_pair[0], key_pair[1])
    for index in range(2):
        lanes = slice(index * width, (index + 1) * width)
        key_out[index, :, :width] = lead[:, lanes]
        key_out[index, :, width:] = trail[:, lanes]
    pairs[3].wait_recv()
    lead, trail = ordered(out_pair[0], out_pair[1])
    self_out[:width] = lead
    self_out[width:] = trail
    for copy in pairs[4:]:
        copy.wait_recv()
    lead, trail = ordered(qkv_pair[0], qkv_pair[1])
    for index in range(3):
        part = slice(index * width, (index + 1) * width)
        qkv_out[index, :width] = lead[part]
        qkv_out[index, width:] = trail[part]
    for copy in sends + text_moves + qkv_moves + out_moves + stat_moves + pairs:
        copy.wait_send()
    text.finish()
    job.finish()


def last_step(
    part, frames, gain, grad, stats, squares, qkv, up_a, up_b, cross, out, text, text_in, w_text,
    ident,
):
    _, rows, width = part.shape
    shards, texts, depth = text_in.shape
    half = up_a.shape[2] + up_b.shape[2]
    columns = out.shape[1]
    own = texts // 8
    return call(
        last_kernel,
        "last_step",
        (
            shape(rows, width, dtype=F32),
            shape(8, width, dtype=F32),
            shape(shards, own, depth, dtype=F32),
            shape(3, 2 * columns, depth),
            shape(depth, 2 * half),
            shape(2, 2 * columns, depth),
            shape(2 * columns, depth),
            shape(2, depth, 2 * columns),
        ),
        (IN_VMEM,) * 8,
        [ANY] + [IN_VMEM] * 13,
        [
            pltpu.VMEM((4, 8, width), F32),
            pltpu.VMEM((3, 8, width), F32),
            pltpu.VMEM((shards, 8, width), F32),
            pltpu.SemaphoreType.DMA((3,)),
            pltpu.SemaphoreType.DMA((3,)),
            pltpu.SemaphoreType.DMA((5, shards - 1)),
            pltpu.SemaphoreType.DMA((5, shards - 1)),
            pltpu.VMEM((shards, 3 * columns, depth), BF),
            pltpu.VMEM((shards, columns, depth), BF),
            pltpu.VMEM((8, shards * own, depth), BF),
            pltpu.VMEM((shards, own, depth), BF),
            pltpu.VMEM((shards, own, depth), BF),
            pltpu.VMEM((2, 3 * columns, depth), BF),
            pltpu.VMEM((depth, half), BF),
            pltpu.VMEM((depth, half), BF),
            pltpu.VMEM((2 * columns, depth), BF),
            pltpu.VMEM((2, columns, depth), BF),
            pltpu.VMEM((2, depth, 2 * columns), BF),
            pltpu.SemaphoreType.DMA((7,)),
            pltpu.SemaphoreType.DMA((7,)),
            pltpu.SemaphoreType.DMA((3, shards - 1)),
            pltpu.SemaphoreType.DMA((3, shards - 1)),
        ]
        + LoadedScatter.scratch(rows, width)
        + Scatter.scratch(shards * own, depth),
        ident,
        65,
    )(part, frames, gain, grad, stats, squares, qkv, up_a, up_b, cross, out, text, text_in, w_text)


def dots(spec, *operands):
    return jnp.einsum(spec, *operands, preferred_element_type=F32)


def layer_norm(inputs, scaling, offset):
    average = jnp.mean(inputs, axis=-1, keepdims=True)
    centred = inputs - average
    variance = jnp.mean(centred * centred, axis=-1, keepdims=True)
    return centred * lax.rsqrt(variance + EPS) * scaling + offset


def on_device(
    frames,
    text_states,
    cotangent,
    norm_gain,
    norm_bias,
    self_qkv,
    self_out,
    cross_qkv,
    cross_out,
    mlp_up,
    mlp_down,
):
    clips, rows, width = frames.shape
    context = lax.axis_index("context")
    depth = self_qkv.shape[1]
    slices = width // depth
    columns = self_qkv.shape[2] // 2
    heads = columns // HEAD_DIM
    block = clips * rows
    texts = text_states.shape[1]

    def half(weight):
        size = weight.shape[-1] // 2
        return lax.dynamic_slice_in_dim(weight, context * size, size, weight.ndim - 1)

    def over_shard(weight, tiled=True):
        return lax.all_gather(weight, "shard", axis=0, tiled=tiled)

    cross_part = half(cross_qkv)
    qkv_part = half(self_qkv)
    early = [qkv_part[0], qkv_part[1], qkv_part[2], half(self_out), cross_part[0], half(cross_out)]
    w_early = over_shard(jnp.concatenate(early, axis=1))
    w_late = over_shard(jnp.concatenate([half(mlp_up), half(mlp_down)], axis=1))
    w_text = jnp.concatenate([cross_part[1], cross_part[2]], axis=1)
    text_slices = text_states.reshape(clips * texts, slices, depth).transpose(1, 0, 2)
    w_down = over_shard(half(mlp_down))

    all_one, all_grad, text_in, text_part = first_step(
        frames.reshape(block, width),
        norm_gain,
        norm_bias,
        cotangent.reshape(block, width),
        text_slices,
        w_text,
        0,
    )
    (
        qkv, self_log, mix, my_mix, stream_one, stream_two, cross_q, cross_mix, norm_three,
        text_all, squares, plane_w,
    ) = attend_forward(
        all_one,
        w_early,
        text_part,
        frames.reshape(block, width),
        norm_gain,
        norm_bias,
        1,
    )

    grad_normed, part_three, grad_up, grad_down = feed_forward(
        norm_three, all_grad, w_late, 4
    )

    def to_shard(part):
        return lax.psum_scatter(part.astype(BF), "shard", scatter_dimension=0, tiled=True)

    grad_down = to_shard(grad_down)
    grad_up = grad_up.reshape(slices, depth, -1)
    grad_one, layer_out, stats, grad_mix, part_out, side, text_grads, up_a = rows_back(
        grad_normed,
        cotangent.reshape(block, width),
        stream_one,
        stream_two,
        cross_q,
        cross_mix,
        text_all,
        my_mix,
        norm_gain,
        norm_bias,
        plane_w,
        part_three,
        grad_up,
        3,
    )

    grad_cross = to_shard(side)[0]
    part_norm, grad_w_qkv, grad_out, text_grads, grad_down, up_b = attend_backward(
        grad_mix, qkv, mix, self_log, all_one, w_early, part_out, text_grads, grad_down, grad_up, 8
    )
    (
        grad_frames, totals, grad_text, grad_w_qkv, grad_up, grad_cross, grad_out, grad_keys,
    ) = last_step(
        part_norm,
        frames.reshape(block, width),
        norm_gain,
        grad_one,
        stats,
        squares,
        grad_w_qkv,
        up_a,
        up_b,
        grad_cross,
        grad_out,
        text_grads,
        text_in,
        w_text,
        11,
    )
    grad_frames = grad_frames.reshape(clips, rows, width)
    grad_text = grad_text.transpose(1, 0, 2).reshape(clips, texts // 8, width)

    squares = totals[6, :4]
    start = lax.axis_index("shard") * depth
    grad_gain = lax.dynamic_slice_in_dim(totals[:3], start, depth, 1)
    grad_shift = lax.dynamic_slice_in_dim(totals[3:6], start, depth, 1)
    entries = float(clips * rows * width * lax.axis_size(("shard",) + PLANE))
    return (
        layer_out.reshape(clips, rows, width),
        grad_frames,
        grad_text,
        grad_gain,
        grad_shift,
        grad_w_qkv.transpose(0, 2, 1).astype(F32),
        grad_out.transpose(1, 0).astype(F32),
        jnp.concatenate([grad_cross[:1].transpose(0, 2, 1), grad_keys]).astype(F32),
        grad_cross[1].transpose(1, 0).astype(F32),
        grad_up.astype(F32),
        grad_down.astype(F32),
        jnp.sqrt(squares / entries),
    )


def solution(mesh):
    rows = P("shard", PLANE, None)
    stack = P(None, "shard", "tensor")
    flat = P("shard", "tensor")
    return jax.shard_map(
        on_device,
        mesh=mesh,
        in_specs=(rows, P("shard"), rows, P(), P(), stack, flat, stack, flat, flat, flat),
        out_specs=(
            (rows, rows, rows, P(None, "shard"), P(None, "shard"))
            + (stack, flat, stack, flat, flat, flat, P())
        ),
        check_vma=False,
    )
```
